32 devices in a mesh: batch: 4 (over y, core), rows: 8 (over z, x).
Axes of the slice: x: 2, y: 2, z: 4, core: 2. Of those that a mesh axis runs over, the one named last changes fastest.
Arguments:
- features_0: bfloat16 [4, 48, 128, 256], P('batch', None, 'rows'), may hold values from -6 to 6
- features_1: bfloat16 [4, 96, 64, 128], P('batch', None, 'rows'), may hold values from -6 to 6
- features_2: bfloat16 [4, 192, 32, 64], P('batch', None, 'rows'), may hold values from -6 to 6
- features_3: bfloat16 [4, 384, 16, 32], P('batch', None, 'rows'), may hold values from -6 to 6
- block_0: bfloat16 [2, 3, 3, 48, 48], replicated, may hold values from -0.3125 to 0.3125
- block_1: bfloat16 [2, 3, 3, 96, 96], replicated, may hold values from -0.21875 to 0.21875
- block_2: bfloat16 [2, 3, 3, 192, 192], replicated, may hold values from -0.15625 to 0.15625
- block_3: bfloat16 [2, 3, 3, 384, 384], replicated, may hold values from -0.109375 to 0.109375
- unite_1: bfloat16 [48, 96], replicated, may hold values from -0.625 to 0.625
- unite_2: bfloat16 [48, 192], replicated, may hold values from -0.4375 to 0.4375
- unite_3: bfloat16 [48, 384], replicated, may hold values from -0.3125 to 0.3125
- norm_gains: float32 [2, 720], replicated, may hold values from 0.5 to 1.5
- norm_shifts: float32 [2, 720], replicated, may hold values from -3 to 3
- unite_gains: float32 [3, 48], replicated, may hold values from 0.5 to 1.5
- unite_shifts: float32 [3, 48], replicated, may hold values from -3 to 3
- output_grad: bfloat16 [4, 48, 128, 256], P('batch', None, 'rows'), may hold values from -6 to 6
- heights: int32 [4], replicated, may hold values from 8 to 128, as said below
- widths: int32 [4], replicated, may hold values from 8 to 256, as said below
- item_slot: int32 [4], replicated, may hold values from 0 to 3, each once
Outputs:
- united: bfloat16 [4, 48, 128, 256], P('batch', None, 'rows')
- grad_features_0: bfloat16 [4, 48, 128, 256], P('batch', None, 'rows')
- grad_features_1: bfloat16 [4, 96, 64, 128], P('batch', None, 'rows')
- grad_features_2: bfloat16 [4, 192, 32, 64], P('batch', None, 'rows')
- grad_features_3: bfloat16 [4, 384, 16, 32], P('batch', None, 'rows')
- grad_block_0: float32 [2, 3, 3, 48, 48], P(None, None, None, 'batch')
- grad_block_1: float32 [2, 3, 3, 96, 96], P(None, None, None, 'batch')
- grad_block_2: float32 [2, 3, 3, 192, 192], P(None, None, None, 'batch')
- grad_block_3: float32 [2, 3, 3, 384, 384], P(None, None, None, 'batch')
- grad_unite_1: float32 [48, 96], P('batch')
- grad_unite_2: float32 [48, 192], P('batch')
- grad_unite_3: float32 [48, 384], P('batch')
- grad_norm_gains: float32 [2, 720], replicated
- grad_norm_shifts: float32 [2, 720], replicated
- grad_unite_gains: float32 [3, 48], replicated
- grad_unite_shifts: float32 [3, 48], replicated
The draws below stay inside these ranges and needn't reach their ends.
Inputs may be any that keep to these rules, and one draw needn't show every extreme that they name: `heights`: multiples of 8; in every draw some items are whole, with all 128 rows and all 256 columns. `widths`: multiples of 8. `item_slot`: a permutation of the slots.
All inputs are finite; a program needn't handle non-finite values.
Results may differ from the reference program's by a relative error of at most 0.018.
Values may be sent and summed in bfloat16 or wider, within the bound.
A program may use at most 128 MiB of HBM per device.

```python
import jax
import jax.numpy as jnp
from jax import lax

CHANNELS = 48
COLUMNS = 256
HEIGHT = 128
ITEMS = 4


def crop_units(key):
    full_rows = HEIGHT // 8
    full_cols = COLUMNS // 8
    key_rows, key_cols, key_whole = jax.random.split(key, 3)
    row_units = jax.random.randint(key_rows, (ITEMS,), 1, full_rows + 1)
    col_units = jax.random.randint(key_cols, (ITEMS,), 1, full_cols + 1)
    offset = jax.random.randint(key_whole, (), 0, 4)
    whole = (jnp.arange(ITEMS) + offset) % 4 == 0
    return (jnp.where(whole, full_rows, row_units) * 8, jnp.where(whole, full_cols, col_units) * 8)


def draw_heights(key, part):
    shared = crop_units(key)
    return shared[0].astype(jnp.int32)


def draw_widths(key, part):
    shared = crop_units(key)
    return shared[1].astype(jnp.int32)


def shard_levels(own_key, dims, cuts, least, top_value):
    loudness = 1.0
    for axis_at, parts in cuts:
        steps = jax.random.uniform(jax.random.fold_in(jax.random.fold_in(own_key, 6), axis_at), (parts,), jnp.float32, least / len(cuts), top_value / len(cuts))
        loudness = loudness * jnp.repeat(jnp.exp(steps), dims[axis_at] // parts).reshape((-1,) + (1,) * (len(dims) - 1 - axis_at))
    return loudness


def centred(own_key, dims, scale, most, pieces=(), kind=jnp.bfloat16):
    level = shard_levels(own_key, dims, pieces, -0.22, 0.18) if pieces else 1.0
    drawn = jax.random.normal(own_key, dims, jnp.float32) * scale * level
    return jnp.minimum(jnp.maximum(drawn, -most), most).astype(kind)


def setup_inputs(seed: int = 0) -> dict:
    splits = jax.random.split(jax.random.key(seed), 20)
    return {
        "features_0": centred(splits[0], (ITEMS, CHANNELS, HEIGHT, COLUMNS), 1.0, 6.0, ((0, 4), (2, 8))),
        "features_1": centred(splits[1], (ITEMS, 2 * CHANNELS, HEIGHT // 2, COLUMNS // 2), 1.0, 6.0, ((0, 4), (2, 8))),
        "features_2": centred(splits[2], (ITEMS, 4 * CHANNELS, HEIGHT // 4, COLUMNS // 4), 1.0, 6.0, ((0, 4), (2, 8))),
        "features_3": centred(splits[3], (ITEMS, 8 * CHANNELS, HEIGHT // 8, COLUMNS // 8), 1.0, 6.0, ((0, 4), (2, 8))),
        "block_0": centred(splits[4], (2, 3, 3, CHANNELS, CHANNELS), (9 * CHANNELS) ** -0.5, 0.3125),
        "block_1": centred(splits[5], (2, 3, 3, 2 * CHANNELS, 2 * CHANNELS), (18 * CHANNELS) ** -0.5, 0.21875),
        "block_2": centred(splits[6], (2, 3, 3, 4 * CHANNELS, 4 * CHANNELS), (36 * CHANNELS) ** -0.5, 0.15625),
        "block_3": centred(splits[7], (2, 3, 3, 8 * CHANNELS, 8 * CHANNELS), (72 * CHANNELS) ** -0.5, 0.109375),
        "unite_1": centred(splits[8], (CHANNELS, 2 * CHANNELS), (2 * CHANNELS) ** -0.5, 0.625),
        "unite_2": centred(splits[9], (CHANNELS, 4 * CHANNELS), (4 * CHANNELS) ** -0.5, 0.4375),
        "unite_3": centred(splits[10], (CHANNELS, 8 * CHANNELS), (8 * CHANNELS) ** -0.5, 0.3125),
        "norm_gains": jnp.clip(1.0 + 0.1 * jax.random.normal(splits[11], (2, 15 * CHANNELS), jnp.float32), 0.5, 1.5),
        "norm_shifts": centred(splits[12], (2, 15 * CHANNELS), 0.5, 3.0, (), jnp.float32),
        "unite_gains": jnp.clip(1.0 + 0.1 * jax.random.normal(splits[13], (3, CHANNELS), jnp.float32), 0.5, 1.5),
        "unite_shifts": centred(splits[14], (3, CHANNELS), 0.5, 3.0, (), jnp.float32),
        "output_grad": centred(splits[15], (ITEMS, CHANNELS, HEIGHT, COLUMNS), 1.0, 6.0, ((0, 4), (2, 8))),
        "heights": draw_heights(jax.random.fold_in(splits[19], 71), 0),
        "widths": draw_widths(jax.random.fold_in(splits[19], 71), 0),
        "item_slot": jax.random.permutation(splits[18], ITEMS).astype(jnp.int32),
    }


EPSILON = 1e-05

@jax.custom_vjp
def low(v):
    return lax.optimization_barrier(v.astype(jnp.bfloat16)).astype(jnp.float32)

@jax.custom_vjp
def low_back(v):
    return v

def low_keep(v):
    return (low(v), None)

def low_pass(kept, grad):
    return (grad,)

def back_keep(v):
    return (v, None)

def back_low(kept, grad):
    return (low(grad),)
low.defvjp(low_keep, low_pass)
low_back.defvjp(back_keep, back_low)

def blend_table(out_len, in_len, scale, out_start, in_start, in_count):
    out_index = out_start + jnp.arange(out_len, dtype=jnp.int32)
    numerator = 2 * out_index + 1 - scale
    lower_index = jnp.where(numerator < 0, 0, numerator // (2 * scale)).astype(jnp.int32)
    fraction = jnp.where(numerator < 0, 0, numerator - lower_index * 2 * scale).astype(jnp.float32) / (2.0 * scale)
    upper_index = jnp.minimum(lower_index + 1, in_len - 1)
    source = in_start + jnp.arange(in_count, dtype=jnp.int32)
    near_part = (source[None, :] == lower_index[:, None]).astype(jnp.float32)
    far_part = (source[None, :] == upper_index[:, None]).astype(jnp.float32)
    return (1.0 - fraction)[:, None] * near_part + fraction[:, None] * far_part

def level_mask(heights, widths, item_slot, level):
    scale = 2 ** level
    slots = jnp.arange(ITEMS, dtype=jnp.int32)
    matches = (item_slot[None, :] == slots[:, None]).astype(jnp.int32)
    slot_rows = lax.optimization_barrier(jnp.sum(matches * heights[None, :], axis=1)) // scale
    slot_cols = lax.optimization_barrier(jnp.sum(matches * widths[None, :], axis=1)) // scale
    row_index = jnp.arange(HEIGHT // scale, dtype=jnp.int32)
    col_index = jnp.arange(COLUMNS // scale, dtype=jnp.int32)
    inside = (row_index[None, :, None] < slot_rows[:, None, None]) & (col_index[None, None, :] < slot_cols[:, None, None])
    return inside.astype(jnp.float32)[:, None]

def expand(vector):
    return vector[None, :, None, None]

def batch_norm(values, mask, count, gain, shift):
    mean = lax.optimization_barrier(jnp.sum(values * mask, axis=(0, 2, 3))) / count
    centered = values - expand(mean)
    variance = lax.optimization_barrier(jnp.sum(mask * centered * centered, axis=(0, 2, 3))) / count
    normed = centered * expand(lax.rsqrt(variance + EPSILON))
    return (expand(gain) * normed + expand(shift)) * mask

def conv_same(values, kernel):
    return lax.conv_general_dilated(values, kernel.transpose(2, 3, 0, 1), (1, 1), ((1, 1), (1, 1)), dimension_numbers=('NCHW', 'OIHW', 'NCHW'), precision=lax.Precision.HIGHEST)

def upsample(values, level):
    scale = 2 ** level
    row_table = blend_table(HEIGHT, HEIGHT // scale, scale, 0, 0, HEIGHT // scale)
    col_table = blend_table(COLUMNS, COLUMNS // scale, scale, 0, 0, COLUMNS // scale)
    rows_up = jnp.einsum('gr,ncrw->ncgw', row_table, values, precision=lax.Precision.HIGHEST)
    return jnp.einsum('ncgw,hw->ncgh', rows_up, col_table, precision=lax.Precision.HIGHEST)

def reference(features_0, features_1, features_2, features_3, block_0, block_1, block_2, block_3, unite_1, unite_2, unite_3, norm_gains, norm_shifts, unite_gains, unite_shifts, output_grad, heights, widths, item_slot):
    masks = [level_mask(heights, widths, item_slot, level) for level in range(4)]
    counts = [jnp.sum(heights // 2 ** level * (widths // 2 ** level)).astype(jnp.float32) for level in range(4)]

    def forward(inputs, blocks, unites, gains, shifts, fgains, fshifts):
        branches = []
        for level in range(4):
            lower_bound = CHANNELS * (2 ** level - 1)
            upper_bound = CHANNELS * (2 ** (level + 1) - 1)
            start = inputs[level] * masks[level]
            first_out = low_back(conv_same(start, blocks[level][0]))
            first_act = jax.nn.silu(batch_norm(first_out, masks[level], counts[level], gains[0, lower_bound:upper_bound], shifts[0, lower_bound:upper_bound]))
            second_out = low_back(conv_same(low(first_act), blocks[level][1]))
            second_pre = batch_norm(second_out, masks[level], counts[level], gains[1, lower_bound:upper_bound], shifts[1, lower_bound:upper_bound]) + start
            branches.append(jax.nn.silu(second_pre))
        total = branches[0]
        for level in range(1, 4):
            unite_out = low_back(jnp.einsum('oc,nchw->nohw', unites[level - 1], low(branches[level]), precision=lax.Precision.HIGHEST))
            unite_norm = batch_norm(unite_out, masks[level], counts[level], fgains[level - 1], fshifts[level - 1])
            total = total + upsample(unite_norm, level)
        return jax.nn.silu(total) * masks[0]
    inputs = tuple((value.astype(jnp.float32) for value in (features_0, features_1, features_2, features_3)))
    blocks = tuple((value.astype(jnp.float32) for value in (block_0, block_1, block_2, block_3)))
    unites = tuple((value.astype(jnp.float32) for value in (unite_1, unite_2, unite_3)))
    result, pullback = jax.vjp(forward, inputs, blocks, unites, norm_gains, norm_shifts, unite_gains, unite_shifts)
    grads = pullback(output_grad.astype(jnp.float32))
    grad_inputs, grad_blocks, grad_unites = (grads[0], grads[1], grads[2])
    return (result.astype(jnp.bfloat16), grad_inputs[0].astype(jnp.bfloat16), grad_inputs[1].astype(jnp.bfloat16), grad_inputs[2].astype(jnp.bfloat16), grad_inputs[3].astype(jnp.bfloat16), grad_blocks[0], grad_blocks[1], grad_blocks[2], grad_blocks[3], grad_unites[0], grad_unites[1], grad_unites[2], grads[3], grads[4], grads[5], grads[6])
```

```python
import functools

import jax
import jax.numpy as jnp
import numpy as np
from jax import lax
from jax.experimental import pallas as pl
from jax.experimental.pallas import tpu as pltpu
from jax.sharding import PartitionSpec as P

EPSILON = 1e-05
LEVELS = 4
MESH = pl.DeviceIdType.MESH
F32 = jnp.float32
BF16 = jnp.bfloat16

MEAN1, RSTD1, GAIN1, SHIFT1, MEAN2, RSTD2, GAIN2, SHIFT2, LOCAL, CA, CB, CC, N_COLS = range(13)
UMEAN, URSTD, UGAIN, USHIFT, ULOCAL, UA, UB, UC, N_UCOLS = range(9)


class Sizes:
    def __init__(self, features):
        self.chan = [f.shape[1] for f in features]
        self.rows = [f.shape[2] for f in features]
        self.width = [f.shape[3] for f in features]
        self.own = [r * w for r, w in zip(self.rows, self.width)]
        self.flat = [(r + 2) * w for r, w in zip(self.rows, self.width)]
        self.off = [sum(self.chan[:l]) for l in range(LEVELS)]
        self.total = sum(self.chan)
        self.blocks = -(-self.total // 128)
        self.uchan = self.chan[0]
        self.utotal = 3 * self.uchan
        self.ublocks = -(-self.utotal // 128)
        self.rim_rows = [c * w // 128 for c, w in zip(self.chan, self.width)]
        self.rim_off = [sum(self.rim_rows[:l]) for l in range(LEVELS)]
        self.rim_total = sum(self.rim_rows)
        self.chunk = []
        for c, n, w in zip(self.chan, self.flat, self.width):
            lanes = max(x for x in range(128, 641, 128) if n % x == 0 and x % w == 0)
            rows = max(r for r in (16, 32, 48) if c % r == 0 and r * lanes <= 12288)
            self.chunk.append((rows, lanes))


def blend(scale, rows):
    out = []
    for g in range(rows):
        num = 2 * g + 1 - scale
        low = num // (2 * scale)
        out.append((low + 1, (num - 2 * scale * low) / (2.0 * scale)))
    return out


def column_table(width, fine):
    scale = fine // width
    group = max(1, 128 // width)
    span = max(128, width)
    table = np.zeros((span, group * fine), np.float32)
    for r in range(group):
        for g in range(fine):
            num = 2 * g + 1 - scale
            low = 0 if num < 0 else num // (2 * scale)
            frac = 0.0 if num < 0 else (num - 2 * scale * low) / (2.0 * scale)
            high = min(low + 1, width - 1)
            table[r * width + low, r * fine + g] += 1.0 - frac
            table[r * width + high, r * fine + g] += frac
    return table


def sigmoid(v):
    return jax.nn.sigmoid(v)


def main_kernel(sz, nb, nk, *refs):
    it = iter(refs)
    take = lambda n: [next(it) for _ in range(n)]
    heights, widths, slots = take(3)
    feats = take(4)
    (ograd,) = take(1)
    wfwd = take(4)
    wbwd = take(4)
    unites = take(3)
    unites_t = take(3)
    (params,) = take(1)
    tables = take(3)
    tables_t = take(3)
    (united_ref,) = take(1)
    gfeat = take(4)
    gker = take(4)
    gunite = take(3)
    (totals_ref,) = take(1)
    x3 = take(4)
    a3 = take(4)
    g3 = take(4)
    t3 = take(4)
    xf = take(4)
    y1 = take(4)
    y2 = take(4)
    p1 = take(4)
    br = take(3)
    uo = take(3)
    up = take(3)
    (cols, ucols, stat_a, stat_b, ustat_a, ustat_b, n_a, n_b, un_a, un_b) = take(10)
    masks = take(4)
    (rec_a, rec_b, rim_s, rim_r, mid_s, mid_r) = take(6)
    (sa_send, sa_recv, sb_send, sb_recv, rim_send, rim_recv) = take(6)

    C, R, W, N, NP, OFF = sz.chan, sz.rows, sz.width, sz.own, sz.flat, sz.off
    me_b = lax.axis_index("batch")
    me_k = lax.axis_index("rows")

    def peer_b(j):
        return lax.rem(me_b + j, nb)

    def peer_k(j):
        return lax.rem(me_k + j, nk)

    barrier = pltpu.get_barrier_semaphore()
    for j in range(1, nb):
        pl.semaphore_signal(barrier, inc=1, device_id=(peer_b(j), me_k), device_id_type=MESH)
    for j in range(1, nk):
        pl.semaphore_signal(barrier, inc=1, device_id=(me_b, peer_k(j)), device_id_type=MESH)
    pl.semaphore_wait(barrier, nb + nk - 2)

    my_h = jnp.int32(0)
    my_w = jnp.int32(0)
    slot_h, slot_w = [], []
    for b in range(nb):
        h = jnp.int32(0)
        w = jnp.int32(0)
        for i in range(nb):
            hit = (slots[i] == b).astype(jnp.int32)
            h = h + hit * heights[i]
            w = w + hit * widths[i]
        slot_h.append(h)
        slot_w.append(w)
        mine = (me_b == b).astype(jnp.int32)
        my_h = my_h + mine * h
        my_w = my_w + mine * w

    count = []
    for l in range(LEVELS):
        c = jnp.int32(0)
        for b in range(nb):
            c = c + lax.shift_right_logical(slot_h[b], l) * lax.shift_right_logical(slot_w[b], l)
        count.append(c.astype(F32))
    inv_local = []
    for l in range(LEVELS):
        inside = jnp.clip(lax.shift_right_logical(my_h, l) - me_k * R[l], 0, R[l])
        own = inside * lax.shift_right_logical(my_w, l)
        inv_local.append(1.0 / jnp.maximum(own, 1).astype(F32))
        lane = lax.broadcasted_iota(jnp.int32, (1, NP[l]), 1)
        log_w = W[l].bit_length() - 1
        row = me_k * R[l] + lax.shift_right_logical(lane, log_w) - 1
        col = lane & (W[l] - 1)
        valid = (row >= 0) & (row < lax.shift_right_logical(my_h, l))
        valid = valid & (col < lax.shift_right_logical(my_w, l))
        masks[l][0:1, :] = jnp.where(valid, 1.0, 0.0)
        masks[l][1:2, :] = jnp.where(valid & (lane >= W[l]) & (lane < W[l] + N[l]), 1.0, 0.0)

    place = lax.broadcasted_iota(jnp.int32, (8, 128), 0) * 128 + lax.broadcasted_iota(
        jnp.int32, (8, 128), 1
    )

    def by_level(values):
        out = jnp.full((8, 128), values[3])
        for l in (2, 1, 0):
            out = jnp.where(place < OFF[l + 1], jnp.full((8, 128), values[l]), out)
        return out

    def by_unite(values):
        out = jnp.full((8, 128), values[2])
        for j in (1, 0):
            out = jnp.where(place < (j + 1) * sz.uchan, jnp.full((8, 128), values[j]), out)
        return out

    inv_count = 1.0 / by_level(count)
    inv_ucount = 1.0 / by_unite(count[1:])
    for chooser, levels, na_ref, nb_ref in (
        (by_level, range(4), n_a, n_b),
        (by_unite, range(1, 4), un_a, un_b),
    ):
        span = chooser([jnp.int32(R[l]) for l in levels])
        hv = [chooser([lax.shift_right_logical(h, l) for l in levels]) for h in slot_h]
        wv = [chooser([lax.shift_right_logical(w, l) for l in levels]) for w in slot_w]
        for b in range(nb):
            na_ref[b] = (jnp.clip(hv[b] - me_k * span, 0, span) * wv[b]).astype(F32)
        for k in range(nk):
            n = jnp.zeros((8, 128), jnp.int32)
            for b in range(nb):
                n = n + jnp.clip(hv[b] - k * span, 0, span) * wv[b]
            nb_ref[k] = n.astype(F32)

    def tile(v, lanes):
        return v if lanes == 128 else jnp.concatenate([v] * (lanes // 128), axis=1)

    def col(slot, l, r0, rc, lanes):
        return tile(cols[slot, pl.ds(pl.multiple_of(OFF[l] + r0, 16), rc), :], lanes)

    def ucol(slot, j, lanes):
        return tile(ucols[slot, j * sz.uchan : (j + 1) * sz.uchan, :], lanes)

    def to_columns(packed, ref, slot_list, blocks):
        full = jnp.concatenate(packed + [jnp.zeros((128 - 8 * len(packed), 128), F32)], axis=0)
        turned = full.T
        for i, slot in enumerate(slot_list):
            for k in range(blocks):
                ref[slot, 128 * k : 128 * k + 128, :] = jnp.broadcast_to(
                    turned[:, 8 * i + k : 8 * i + k + 1], (128, 128)
                )

    to_columns([params[8 * i : 8 * i + 8] for i in range(4)], cols, [GAIN1, SHIFT1, GAIN2, SHIFT2], sz.blocks)
    to_columns([params[8 * i : 8 * i + 8] for i in range(4, 6)], ucols, [UGAIN, USHIFT], sz.ublocks)
    gain1_p, gain2_p, ugain_p = params[0:8], params[16:24], params[32:40]
    stat_a[...] = jnp.zeros_like(stat_a)
    stat_b[...] = jnp.zeros_like(stat_b)
    ustat_a[...] = jnp.zeros_like(ustat_a)
    ustat_b[...] = jnp.zeros_like(ustat_b)

    def fold(v):
        out = v[:, 0:128]
        for i in range(1, v.shape[1] // 128):
            out = out + v[:, 128 * i : 128 * i + 128]
        return out

    lane128 = lax.broadcasted_iota(jnp.int32, (1, 128), 1)

    def record(a_ref, b_ref, blocks):
        out = jnp.zeros((128, 128), F32)
        for base, ref in ((0, a_ref), (8, b_ref)):
            for k in range(blocks):
                s = jnp.sum(ref[128 * k : 128 * k + 128, :], axis=1, keepdims=True)
                out = jnp.where(lane128 == base + k, s, out)
        return out.T[0:16]

    def spread(e, which, rec):
        copies = []
        if which == 0:
            ref, send, recv, n, me = rec_a, sa_send, sa_recv, nb, me_b
        else:
            ref, send, recv, n, me = rec_b, sb_send, sb_recv, nk, me_k
        ref[e, me] = rec
        for j in range(1, n):
            target = (peer_b(j), me_k) if which == 0 else (me_b, peer_k(j))
            copy = pltpu.make_async_remote_copy(
                src_ref=ref.at[e, me],
                dst_ref=ref.at[e, me],
                send_sem=send.at[e, j],
                recv_sem=recv.at[e, me],
                device_id=target,
                device_id_type=MESH,
            )
            copy.start()
            copies.append(copy)
        for j in range(1, n):
            other = peer_b(j) if which == 0 else peer_k(j)
            pltpu.make_async_remote_copy(
                src_ref=ref.at[e, me],
                dst_ref=ref.at[e, other],
                send_sem=send.at[e, j],
                recv_sem=recv.at[e, other],
                device_id=(me_b, me_k),
                device_id_type=MESH,
            ).wait_recv()
        for copy in copies:
            copy.wait_send()

    def gather_moments(e, rec, na_ref, nb_ref):
        for which, n, ref, n_ref in ((0, nb, rec_a, na_ref), (1, nk, rec_b, nb_ref)):
            spread(e, which, rec)
            total = jnp.zeros((8, 128), F32)
            size = jnp.zeros((8, 128), F32)
            for i in range(n):
                total = total + ref[e, i, 0:8]
                size = size + n_ref[i]
            mean = total / jnp.maximum(size, 1.0)
            spread_sum = jnp.zeros((8, 128), F32)
            for i in range(n):
                delta = ref[e, i, 0:8] / jnp.maximum(n_ref[i], 1.0) - mean
                spread_sum = spread_sum + (ref[e, i, 8:16] + n_ref[i] * delta * delta)
            rec = jnp.concatenate([total, spread_sum], axis=0)
        return rec

    def gather_sums(e, rec):
        for which, n, ref in ((0, nb, rec_a), (1, nk, rec_b)):
            spread(e, which, rec)
            rec = jnp.zeros((16, 128), F32)
            for i in range(n):
                rec = rec + ref[e, i]
        return rec

    def rim_copies(slot, src, dst):
        up = pltpu.make_async_remote_copy(
            src_ref=src.at[0],
            dst_ref=dst.at[1],
            send_sem=rim_send.at[slot, 0],
            recv_sem=rim_recv.at[slot, 1],
            device_id=(me_b, lax.rem(me_k + nk - 1, nk)),
            device_id_type=MESH,
        )
        down = pltpu.make_async_remote_copy(
            src_ref=src.at[1],
            dst_ref=dst.at[0],
            send_sem=rim_send.at[slot, 1],
            recv_sem=rim_recv.at[slot, 0],
            device_id=(me_b, lax.rem(me_k + 1, nk)),
            device_id_type=MESH,
        )
        return up, down

    def rims_start(slot, src, dst):
        up, down = rim_copies(slot, src, dst)

        @pl.when(me_k > 0)
        def _():
            up.start()

        @pl.when(me_k < nk - 1)
        def _():
            down.start()

    def rims_wait(slot, src, dst):
        up, down = rim_copies(slot, src, dst)

        @pl.when(me_k > 0)
        def _():
            down.wait_recv()
            up.wait_send()

        @pl.when(me_k < nk - 1)
        def _():
            up.wait_recv()
            down.wait_send()

    def pack_row(ref, l, lane0):
        if W[l] >= 128:
            return jnp.concatenate(
                [ref[:, lane0 + 128 * i : lane0 + 128 * i + 128] for i in range(W[l] // 128)], axis=0
            )
        group = 128 // W[l]
        rows = C[l] // group
        base, shift = lane0 // 128 * 128, lane0 % 128
        out = None
        for g in range(group):
            v = ref[g * rows : (g + 1) * rows, base : base + 128]
            turn = (g * W[l] - shift) % 128
            v = pltpu.roll(v, turn, 1) if turn else v
            out = v if out is None else jnp.where(lane128 >= g * W[l], v, out)
        return out

    def unpack_row(ref, l, lane0, q):
        if W[l] >= 128:
            for i in range(W[l] // 128):
                ref[:, lane0 + 128 * i : lane0 + 128 * i + 128] = q[i * C[l] : (i + 1) * C[l]]
            return
        group = 128 // W[l]
        rows = C[l] // group
        base, shift = lane0 // 128 * 128, lane0 % 128
        here = (lane128 >= shift) & (lane128 < shift + W[l])
        for g in range(group):
            turn = (shift - g * W[l]) % 128
            v = pltpu.roll(q, turn, 1) if turn else q
            old = ref[g * rows : (g + 1) * rows, base : base + 128]
            ref[g * rows : (g + 1) * rows, base : base + 128] = jnp.where(here, v, old)

    def pack_rims(slot, arrays):
        for l in range(LEVELS):
            at = slice(sz.rim_off[l], sz.rim_off[l] + sz.rim_rows[l])
            rim_s[slot, 0, at, :] = pack_row(arrays[l], l, W[l]).astype(BF16)
            rim_s[slot, 1, at, :] = pack_row(arrays[l], l, N[l]).astype(BF16)

    def unpack_rims(slot, arrays):
        for l in range(LEVELS):
            at = slice(sz.rim_off[l], sz.rim_off[l] + sz.rim_rows[l])
            unpack_row(arrays[l], l, 0, rim_r[slot, 0, at, :].astype(F32))
            unpack_row(arrays[l], l, W[l] + N[l], rim_r[slot, 1, at, :].astype(F32))

    def each(l, body):
        rc, lanes = sz.chunk[l]

        def step(i, _):
            body(pl.multiple_of(i * rc, rc), rc, lanes)
            return 0

        lax.fori_loop(0, C[l] // rc, step, 0)

    def lane_chunks(l, lanes):
        return [(i, i + lanes) for i in range(0, NP[l], lanes)]

    def stack_columns(ref, l, r0, rc, a, b, v):
        lanes = b - a
        at = lax.broadcasted_iota(jnp.int32, (1, lanes), 1) & (W[l] - 1)
        left = jnp.where(at == 0, 0.0, pltpu.roll(v, 1, 1))
        right = jnp.where(at == W[l] - 1, 0.0, pltpu.roll(v, lanes - 1, 1))
        for u, part in enumerate((left, v, right)):
            ref[pl.ds(pl.multiple_of(u * C[l] + r0, 16), rc), a:b] = part.astype(BF16)

    def stack_rows(ref, l, r0, rc, v):
        for t in range(3):
            turn = ((t - 1) * W[l]) % NP[l]
            part = pltpu.roll(v, turn, 1) if turn else v
            ref[pl.ds(pl.multiple_of(t * C[l] + r0, 16), rc), :] = part.astype(BF16)

    def conv(l, w_ref, which, src, dst):
        c = C[l]
        if W[l] % 128 == 0:
            span = min(1024, N[l])

            def step(i, _):
                acc = None
                for t in range(3):
                    at = pl.ds(pl.multiple_of(i * span + t * W[l], 128), span)
                    part = jnp.dot(
                        w_ref[which, t * c : (t + 1) * c, :], src[:, at], preferred_element_type=F32
                    )
                    acc = part if acc is None else acc + part
                dst[:, pl.ds(pl.multiple_of(i * span + W[l], 128), span)] = acc
                return 0

            lax.fori_loop(0, N[l] // span, step, 0)
        else:
            rows = 96

            def step(i, _):
                acc = None
                for t in range(3):
                    at = pl.ds(pl.multiple_of(t * c + i * rows, 16), rows)
                    part = jnp.dot(w_ref[which, at, :], src[...], preferred_element_type=F32)
                    turn = ((1 - t) * W[l]) % NP[l]
                    part = pltpu.roll(part, turn, 1) if turn else part
                    acc = part if acc is None else acc + part
                dst[pl.ds(pl.multiple_of(i * rows, 16), rows), :] = acc
                return 0

            lax.fori_loop(0, c // rows, step, 0)

    def kernel_grad(l, which, src):
        c = C[l]
        span = 96 if W[l] < 128 else 3 * c

        def step(i, _):
            at = pl.ds(pl.multiple_of(i * span, 16), span)
            gker[l][which, at, :] = lax.dot_general(
                t3[l][at, :], src[...], (((1,), (1,)), ((), ())), preferred_element_type=F32
            ).astype(BF16)
            return 0

        lax.fori_loop(0, 3 * c // span, step, 0)

    def moments(arrays):
        for l in range(LEVELS):

            def body(r0, rc, lanes, l=l):
                acc = jnp.zeros((rc, 128), F32)
                for a, b in lane_chunks(l, lanes):
                    m = masks[l][1:2, a:b] > 0
                    acc = acc + fold(jnp.where(m, arrays[l][pl.ds(r0, rc), a:b], 0.0))
                stat_a[pl.ds(pl.multiple_of(OFF[l] + r0, 16), rc), :] = acc

            each(l, body)
        for l in range(LEVELS):
            at = slice(OFF[l], OFF[l] + C[l])
            s = jnp.sum(stat_a[at, :], axis=1, keepdims=True) * inv_local[l]
            cols[LOCAL, at, :] = jnp.broadcast_to(s, (C[l], 128))
        for l in range(LEVELS):

            def body(r0, rc, lanes, l=l):
                acc = jnp.zeros((rc, 128), F32)
                mean = col(LOCAL, l, r0, rc, lanes)
                for a, b in lane_chunks(l, lanes):
                    m = masks[l][1:2, a:b] > 0
                    d = jnp.where(m, arrays[l][pl.ds(r0, rc), a:b] - mean, 0.0)
                    acc = acc + fold(d * d)
                stat_b[pl.ds(pl.multiple_of(OFF[l] + r0, 16), rc), :] = acc

            each(l, body)
        return record(stat_a, stat_b, sz.blocks)

    for l in range(LEVELS):

        def body(r0, rc, lanes, l=l):
            for a, b in lane_chunks(l, lanes):
                xf[l][pl.ds(r0, rc), a:b] = feats[l][pl.ds(r0, rc), a:b].astype(F32)

        each(l, body)
    pack_rims(0, xf)
    rims_start(0, rim_s.at[0], rim_r.at[0])
    rims_wait(0, rim_s.at[0], rim_r.at[0])
    unpack_rims(0, xf)
    for l in range(LEVELS):

        def body(r0, rc, lanes, l=l):
            for a, b in lane_chunks(l, lanes):
                m = masks[l][0:1, a:b] > 0
                stack_columns(x3[l], l, r0, rc, a, b, jnp.where(m, xf[l][pl.ds(r0, rc), a:b], 0.0))

        each(l, body)

    for l in range(LEVELS):
        conv(l, wfwd[l], 0, x3[l], y1[l])
    pack_rims(1, y1)
    rims_start(1, rim_s.at[1], rim_r.at[1])
    got = gather_moments(0, moments(y1), n_a, n_b)
    rims_wait(1, rim_s.at[1], rim_r.at[1])
    mean1_p = got[0:8] * inv_count
    rstd1_p = lax.rsqrt(got[8:16] * inv_count + EPSILON)
    to_columns([mean1_p, rstd1_p], cols, [MEAN1, RSTD1], sz.blocks)
    unpack_rims(1, y1)

    def first_pre(l, r0, rc, a, b, lanes):
        hat = (y1[l][pl.ds(r0, rc), a:b] - col(MEAN1, l, r0, rc, lanes)) * col(RSTD1, l, r0, rc, lanes)
        return hat, hat * col(GAIN1, l, r0, rc, lanes) + col(SHIFT1, l, r0, rc, lanes)

    for l in range(LEVELS):

        def body(r0, rc, lanes, l=l):
            for a, b in lane_chunks(l, lanes):
                m = masks[l][0:1, a:b] > 0
                _, pre = first_pre(l, r0, rc, a, b, lanes)
                stack_columns(a3[l], l, r0, rc, a, b, jnp.where(m, pre * sigmoid(pre), 0.0))

        each(l, body)

    for l in range(LEVELS):
        conv(l, wfwd[l], 1, a3[l], y2[l])
    pack_rims(2, y2)
    rims_start(2, rim_s.at[2], rim_r.at[2])
    got = gather_moments(1, moments(y2), n_a, n_b)
    rims_wait(2, rim_s.at[2], rim_r.at[2])
    mean2_p = got[0:8] * inv_count
    rstd2_p = lax.rsqrt(got[8:16] * inv_count + EPSILON)
    to_columns([mean2_p, rstd2_p], cols, [MEAN2, RSTD2], sz.blocks)
    unpack_rims(2, y2)

    def second_hat(l, r0, rc, a, b, lanes):
        return (y2[l][pl.ds(r0, rc), a:b] - col(MEAN2, l, r0, rc, lanes)) * col(RSTD2, l, r0, rc, lanes)

    def start_part(l, r0, rc, a, b):
        return x3[l][pl.ds(pl.multiple_of(C[l] + r0, 16), rc), a:b].astype(F32)

    for l in range(LEVELS):

        def body(r0, rc, lanes, l=l):
            for a, b in lane_chunks(l, lanes):
                m = masks[l][0:1, a:b] > 0
                hat = second_hat(l, r0, rc, a, b, lanes)
                pre = hat * col(GAIN2, l, r0, rc, lanes) + col(SHIFT2, l, r0, rc, lanes)
                pre = jnp.where(m, pre, 0.0) + start_part(l, r0, rc, a, b)
                p1[l][pl.ds(r0, rc), a:b] = pre
                if l:
                    br[l - 1][pl.ds(r0, rc), a:b] = (pre * sigmoid(pre)).astype(BF16)

        each(l, body)

    UC_ = sz.uchan
    for j in range(3):
        l = j + 1
        uo[j][...] = jnp.dot(unites[j][...], br[j][...], preferred_element_type=F32)
    for j in range(3):
        l = j + 1
        m = masks[l][1:2, :] > 0
        v = jnp.where(m, uo[j][...], 0.0)
        part = fold(v)
        ustat_a[j * UC_ : (j + 1) * UC_, :] = part
        mean = jnp.sum(part, axis=1, keepdims=True) * inv_local[l]
        d = jnp.where(m, uo[j][...] - mean, 0.0)
        ustat_b[j * UC_ : (j + 1) * UC_, :] = fold(d * d)
    got = gather_moments(2, record(ustat_a, ustat_b, sz.ublocks), un_a, un_b)
    umean_p = got[0:8] * inv_ucount
    urstd_p = lax.rsqrt(got[8:16] * inv_ucount + EPSILON)
    to_columns([umean_p, urstd_p], ucols, [UMEAN, URSTD], sz.ublocks)

    at_top = me_k == 0
    at_bottom = me_k == nk - 1
    fine = W[0]
    split = lambda v: (v.astype(BF16), (v - v.astype(BF16).astype(F32)).astype(BF16))

    def edge(l, n):
        lane = lax.broadcasted_iota(jnp.int32, (1, n), 1)
        return lane

    for j in range(3):
        l = j + 1
        m = masks[l][0:1, :] > 0
        hat = (uo[j][...] - ucol(UMEAN, j, NP[l])) * ucol(URSTD, j, NP[l])
        uo[j][...] = hat
        norm = jnp.where(m, hat * ucol(UGAIN, j, NP[l]) + ucol(USHIFT, j, NP[l]), 0.0)
        lane = edge(l, NP[l])
        norm = jnp.where((lane < W[l]) & at_top, pltpu.roll(norm, NP[l] - W[l], 1), norm)
        norm = jnp.where((lane >= W[l] + N[l]) & at_bottom, pltpu.roll(norm, W[l], 1), norm)
        hi, lo = split(norm)
        both = jnp.concatenate([hi, lo], axis=0)
        span = max(128, W[l])
        width = tables[j].shape[1]
        for i in range(NP[l] // span):
            wide = jnp.dot(both[:, span * i : span * i + span], tables[j][...], preferred_element_type=F32)
            up[j][:, width * i : width * i + width] = wide[0:UC_] + wide[UC_:]

    blends = [blend(2 ** (j + 1), R[0]) for j in range(3)]

    def total_body(r0, rc, lanes):
        rows = pl.ds(r0, rc)
        coarse = [{}, {}, {}]
        have = [{}, {}, {}]
        for g in range(R[0]):
            a, b = (g + 1) * fine, (g + 2) * fine
            pre = p1[0][rows, a:b]
            total = pre * sigmoid(pre)
            for j in range(3):
                low, frac = blends[j][g]
                for i in (low, low + 1):
                    if i not in have[j]:
                        have[j][i] = up[j][rows, i * fine : (i + 1) * fine]
                total = total + ((1.0 - frac) * have[j][low] + frac * have[j][low + 1])
            m = masks[0][1:2, a:b] > 0
            sig = sigmoid(total)
            united_ref[rows, g * fine : (g + 1) * fine] = jnp.where(m, total * sig, 0.0).astype(BF16)
            slope = sig * (1.0 + total * (1.0 - sig))
            grad = jnp.where(m, ograd[rows, g * fine : (g + 1) * fine].astype(F32) * slope, 0.0)
            xf[0][rows, a:b] = grad
            for j in range(3):
                low, frac = blends[j][g]
                for i, weight in ((low, 1.0 - frac), (low + 1, frac)):
                    coarse[j][i] = weight * grad if i not in coarse[j] else coarse[j][i] + weight * grad
                done = [i for i in coarse[j] if g + 1 == R[0] or i < blends[j][g + 1][0]]
                for i in done:
                    up[j][rows, i * fine : (i + 1) * fine] = coarse[j].pop(i)

    def total_step(i, _):
        total_body(pl.multiple_of(i * 16, 16), 16, fine)
        return 0

    lax.fori_loop(0, UC_ // 16, total_step, 0)

    ud = []
    for j in range(3):
        l = j + 1
        span = max(128, W[l])
        width = tables[j].shape[1]
        parts = []
        for i in range(NP[l] // span):
            hi, lo = split(up[j][:, width * i : width * i + width])
            both = jnp.concatenate([hi, lo], axis=0)
            narrow = jnp.dot(both, tables_t[j][...], preferred_element_type=F32)
            parts.append(narrow[0:UC_] + narrow[UC_:])
        d = parts[0] if len(parts) == 1 else jnp.concatenate(parts, axis=1)
        lane = edge(l, NP[l])
        fold_top = jnp.where((lane >= W[l]) & (lane < 2 * W[l]) & at_top, pltpu.roll(d, W[l], 1), 0.0)
        fold_bottom = jnp.where(
            (lane >= N[l]) & (lane < W[l] + N[l]) & at_bottom, pltpu.roll(d, NP[l] - W[l], 1), 0.0
        )
        d = d + fold_top + fold_bottom
        d = jnp.where(masks[l][0:1, :] > 0, d, 0.0)
        ustat_a[j * UC_ : (j + 1) * UC_, :] = fold(d * uo[j][...])
        ustat_b[j * UC_ : (j + 1) * UC_, :] = fold(d)
        up[j][:, 0 : NP[l]] = d
    at = 0
    lay = []
    for j in range(3):
        l = j + 1
        n = max(2 * W[l], 128)
        lay.append((at, n))
        mid_s[0, :, at : at + n] = up[j][:, 0:n].astype(BF16)
        mid_s[1, :, at : at + n] = up[j][:, NP[l] - n : NP[l]].astype(BF16)
        at += n
    mid_s[0, :, at : at + fine] = xf[0][:, fine : 2 * fine].astype(BF16)
    mid_s[1, :, at : at + fine] = xf[0][:, N[0] : N[0] + fine].astype(BF16)
    rims_start(3, mid_s, mid_r)
    got4 = gather_sums(3, record(ustat_a, ustat_b, sz.ublocks))
    totals_ref[0] = got4
    rims_wait(3, mid_s, mid_r)
    scale_p = urstd_p * ugain_p
    to_columns(
        [scale_p, got4[8:16] * inv_ucount, got4[0:8] * inv_ucount], ucols, [UA, UB, UC], sz.ublocks
    )
    xf[0][:, 0:fine] = mid_r[0, :, at : at + fine].astype(F32)
    xf[0][:, N[0] + fine : NP[0]] = mid_r[1, :, at : at + fine].astype(F32)
    for j in range(3):
        l = j + 1
        start, n = lay[j]
        lane = edge(l, n)
        above = mid_r[0, :, start : start + n].astype(F32)
        below = mid_r[1, :, start : start + n].astype(F32)
        if NP[l] == n:
            above, below = pltpu.roll(above, n // 2, 1), pltpu.roll(below, n // 2, 1)
            d = up[j][:, 0:n]
            d = d + jnp.where((lane < 2 * W[l]) & (me_k > 0), above, 0.0)
            d = d + jnp.where((lane >= n - 2 * W[l]) & (me_k < nk - 1), below, 0.0)
            up[j][:, 0:n] = d
        else:
            up[j][:, 0:n] = up[j][:, 0:n] + jnp.where((lane >= 0) & (me_k > 0), above, 0.0)
            up[j][:, NP[l] - n : NP[l]] = up[j][:, NP[l] - n : NP[l]] + jnp.where(
                (lane >= 0) & (me_k < nk - 1), below, 0.0
            )
    for j in range(3):
        l = j + 1
        d = up[j][:, 0 : NP[l]]
        g = ucol(UA, j, NP[l]) * (d - ucol(UB, j, NP[l]) - uo[j][...] * ucol(UC, j, NP[l]))
        g = jnp.where(masks[l][0:1, :] > 0, g, 0.0)
        low = g.astype(BF16)
        xf[l][...] = jnp.dot(unites_t[j][...], low, preferred_element_type=F32)
        own = jnp.where(masks[l][1:2, :] > 0, g, 0.0).astype(BF16)
        gunite[j][...] = lax.dot_general(
            own, br[j][...], (((1,), (1,)), ((), ())), preferred_element_type=F32
        ).astype(BF16)

    for l in range(LEVELS):

        def body(r0, rc, lanes, l=l):
            acc_g = jnp.zeros((rc, 128), F32)
            acc_s = jnp.zeros((rc, 128), F32)
            for a, b in lane_chunks(l, lanes):
                m = masks[l][1:2, a:b] > 0
                pre = p1[l][pl.ds(r0, rc), a:b]
                sig = sigmoid(pre)
                d = xf[l][pl.ds(r0, rc), a:b] * (sig * (1.0 + pre * (1.0 - sig)))
                xf[l][pl.ds(r0, rc), a:b] = d
                d = jnp.where(m, d, 0.0)
                acc_s = acc_s + fold(d)
                acc_g = acc_g + fold(jnp.where(m, d * second_hat(l, r0, rc, a, b, lanes), 0.0))
            at = pl.ds(pl.multiple_of(OFF[l] + r0, 16), rc)
            stat_a[at, :] = acc_g
            stat_b[at, :] = acc_s

        each(l, body)
    got5 = gather_sums(4, record(stat_a, stat_b, sz.blocks))
    totals_ref[1] = got5
    to_columns(
        [rstd2_p * gain2_p, got5[8:16] * inv_count, got5[0:8] * inv_count], cols, [CA, CB, CC], sz.blocks
    )

    def store_gradient(l, r0, rc, parts):
        v = parts[0] if len(parts) == 1 else jnp.concatenate(parts, axis=1)
        stack_rows(t3[l], l, r0, rc, jnp.where(masks[l][1:2, :] > 0, v, 0.0))

    for l in range(LEVELS):

        def body(r0, rc, lanes, l=l):
            parts = []
            for a, b in lane_chunks(l, lanes):
                m = masks[l][0:1, a:b] > 0
                hat = second_hat(l, r0, rc, a, b, lanes)
                d = xf[l][pl.ds(r0, rc), a:b]
                g = col(CA, l, r0, rc, lanes) * (
                    d - col(CB, l, r0, rc, lanes) - hat * col(CC, l, r0, rc, lanes)
                )
                g = jnp.where(m, g, 0.0)
                stack_columns(g3[l], l, r0, rc, a, b, g)
                parts.append(g)
            store_gradient(l, r0, rc, parts)

        each(l, body)

    for l in range(LEVELS):
        conv(l, wbwd[l], 1, g3[l], p1[l])
    for l in range(LEVELS):

        def body(r0, rc, lanes, l=l):
            acc_g = jnp.zeros((rc, 128), F32)
            acc_s = jnp.zeros((rc, 128), F32)
            for a, b in lane_chunks(l, lanes):
                m = masks[l][1:2, a:b] > 0
                hat, pre = first_pre(l, r0, rc, a, b, lanes)
                sig = sigmoid(pre)
                d = p1[l][pl.ds(r0, rc), a:b] * (sig * (1.0 + pre * (1.0 - sig)))
                d = jnp.where(m, d, 0.0)
                p1[l][pl.ds(r0, rc), a:b] = d
                acc_s = acc_s + fold(d)
                acc_g = acc_g + fold(jnp.where(m, d * hat, 0.0))
            at = pl.ds(pl.multiple_of(OFF[l] + r0, 16), rc)
            stat_a[at, :] = acc_g
            stat_b[at, :] = acc_s

        each(l, body)
    pack_rims(3, p1)
    rims_start(4, rim_s.at[3], rim_r.at[3])
    for l in range(LEVELS):
        kernel_grad(l, 1, a3[l])
    got6 = gather_sums(5, record(stat_a, stat_b, sz.blocks))
    totals_ref[2] = got6
    rims_wait(4, rim_s.at[3], rim_r.at[3])
    to_columns(
        [rstd1_p * gain1_p, got6[8:16] * inv_count, got6[0:8] * inv_count], cols, [CA, CB, CC], sz.blocks
    )
    unpack_rims(3, p1)
    for l in range(LEVELS):

        def body(r0, rc, lanes, l=l):
            parts = []
            for a, b in lane_chunks(l, lanes):
                m = masks[l][0:1, a:b] > 0
                hat, _ = first_pre(l, r0, rc, a, b, lanes)
                d = p1[l][pl.ds(r0, rc), a:b]
                g = col(CA, l, r0, rc, lanes) * (
                    d - col(CB, l, r0, rc, lanes) - hat * col(CC, l, r0, rc, lanes)
                )
                g = jnp.where(m, g, 0.0)
                stack_columns(g3[l], l, r0, rc, a, b, g)
                parts.append(g)
            store_gradient(l, r0, rc, parts)

        each(l, body)

    for l in range(LEVELS):
        conv(l, wbwd[l], 0, g3[l], y1[l])
    for l in range(LEVELS):

        def body(r0, rc, lanes, l=l):
            for a, b in lane_chunks(l, lanes):
                m = masks[l][1:2, a:b] > 0
                v = y1[l][pl.ds(r0, rc), a:b] + xf[l][pl.ds(r0, rc), a:b]
                gfeat[l][pl.ds(r0, rc), a:b] = jnp.where(m, v, 0.0).astype(BF16)

        each(l, body)
    for l in range(LEVELS):
        kernel_grad(l, 0, x3[l])


def body(*args):
    features = args[0:4]
    blocks = args[4:8]
    unites = args[8:11]
    norm_gains, norm_shifts, unite_gains, unite_shifts, output_grad, heights, widths, item_slot = args[11:]
    sz = Sizes(features)
    nb = lax.axis_size("batch")
    nk = lax.axis_size("rows")
    C, R, W, N, NP = sz.chan, sz.rows, sz.width, sz.own, sz.flat

    flat = [
        jnp.pad(f.reshape(C[l], N[l]), ((0, 0), (W[l], W[l]))) for l, f in enumerate(features)
    ]
    ograd = output_grad.reshape(C[0], N[0])
    wfwd = [
        b.transpose(0, 1, 3, 2, 4).reshape(2, 3 * C[l], 3 * C[l]) for l, b in enumerate(blocks)
    ]
    wbwd = [
        b[:, ::-1, ::-1].transpose(0, 1, 4, 2, 3).reshape(2, 3 * C[l], 3 * C[l])
        for l, b in enumerate(blocks)
    ]

    def packed(row):
        return jnp.pad(row, (0, 1024 - row.shape[0])).reshape(8, 128)

    params = jnp.concatenate(
        [
            packed(norm_gains[0]),
            packed(norm_shifts[0]),
            packed(norm_gains[1]),
            packed(norm_shifts[1]),
            packed(unite_gains.reshape(-1)),
            packed(unite_shifts.reshape(-1)),
        ],
        axis=0,
    )
    tables = [column_table(W[l], W[0]) for l in range(1, 4)]
    operands = [heights, widths, item_slot, *flat, ograd, *wfwd, *wbwd, *unites]
    operands += [u.T for u in unites] + [params]
    operands += [jnp.asarray(t, BF16) for t in tables] + [jnp.asarray(t.T, BF16) for t in tables]

    shape = jax.ShapeDtypeStruct
    outs = [shape((C[0], N[0]), BF16)]
    outs += [shape((C[l], NP[l]), BF16) for l in range(4)]
    outs += [shape((2, 3 * C[l], 3 * C[l]), BF16) for l in range(4)]
    outs += [shape((sz.uchan, C[l]), BF16) for l in range(1, 4)]
    outs += [shape((3, 16, 128), F32)]
    vm = pltpu.VMEM
    scratch = []
    for _ in range(4):
        scratch += [vm((3 * C[l], NP[l]), BF16) for l in range(4)]
    for _ in range(4):
        scratch += [vm((C[l], NP[l]), F32) for l in range(4)]
    scratch += [vm((C[l], NP[l]), BF16) for l in range(1, 4)]
    scratch += [vm((sz.uchan, NP[l]), F32) for l in range(1, 4)]
    scratch += [vm((sz.uchan, (R[l] + 2) * W[0]), F32) for l in range(1, 4)]
    scratch += [
        vm((N_COLS, sz.blocks * 128, 128), F32),
        vm((N_UCOLS, sz.ublocks * 128, 128), F32),
        vm((sz.blocks * 128, 128), F32),
        vm((sz.blocks * 128, 128), F32),
        vm((sz.ublocks * 128, 128), F32),
        vm((sz.ublocks * 128, 128), F32),
        vm((nb, 8, 128), F32),
        vm((nk, 8, 128), F32),
        vm((nb, 8, 128), F32),
        vm((nk, 8, 128), F32),
    ]
    scratch += [vm((8, NP[l]), F32) for l in range(4)]
    mid = sum(max(2 * W[l], 128) for l in range(1, 4)) + W[0]
    scratch += [
        vm((6, nb, 16, 128), F32),
        vm((6, nk, 16, 128), F32),
        vm((4, 2, sz.rim_total, 128), BF16),
        vm((4, 2, sz.rim_total, 128), BF16),
        vm((2, sz.uchan, mid), BF16),
        vm((2, sz.uchan, mid), BF16),
        pltpu.SemaphoreType.DMA((6, nb)),
        pltpu.SemaphoreType.DMA((6, nb)),
        pltpu.SemaphoreType.DMA((6, nk)),
        pltpu.SemaphoreType.DMA((6, nk)),
        pltpu.SemaphoreType.DMA((5, 2)),
        pltpu.SemaphoreType.DMA((5, 2)),
    ]
    in_vmem = pl.BlockSpec(memory_space=pltpu.VMEM)
    in_smem = pl.BlockSpec(memory_space=pltpu.SMEM)
    got = pl.pallas_call(
        functools.partial(main_kernel, sz, nb, nk),
        out_shape=outs,
        in_specs=[in_smem] * 3 + [in_vmem] * (len(operands) - 3),
        out_specs=[in_vmem] * len(outs),
        scratch_shapes=scratch,
        compiler_params=pltpu.CompilerParams(
            collective_id=0, has_side_effects=True, vmem_limit_bytes=60 * 2**20
        ),
    )(*operands)

    united = got[0].reshape(1, C[0], R[0], W[0])
    grad_inputs = [
        got[1 + l][:, W[l] : W[l] + N[l]].reshape(1, C[l], R[l], W[l]) for l in range(4)
    ]
    sums = []
    for l in range(4):
        part = got[5 + l].reshape(2, 3, C[l], 3, C[l])
        part = lax.psum(part, "rows")
        part = lax.psum_scatter(part, "batch", scatter_dimension=2, tiled=True)
        sums.append(part.transpose(0, 1, 3, 2, 4).astype(F32))
    for j in range(3):
        part = lax.psum(got[9 + j], "rows")
        sums.append(lax.psum_scatter(part, "batch", scatter_dimension=0, tiled=True).astype(F32))
    totals = got[12].reshape(3, 2, 1024)
    grad_norm_gains = totals[2:0:-1, 0, : sz.total]
    grad_norm_shifts = totals[2:0:-1, 1, : sz.total]
    grad_unite_gains = totals[0, 0, : sz.utotal].reshape(3, -1)
    grad_unite_shifts = totals[0, 1, : sz.utotal].reshape(3, -1)
    return (
        united,
        *grad_inputs,
        *sums,
        grad_norm_gains,
        grad_norm_shifts,
        grad_unite_gains,
        grad_unite_shifts,
    )


def solution(mesh):
    image = P("batch", None, "rows", None)
    kernel = P(None, None, None, "batch", None)
    return jax.shard_map(
        body,
        mesh=mesh,
        in_specs=(image,) * 4 + (P(),) * 11 + (image,) + (P(),) * 3,
        out_specs=(image,) * 5 + (kernel,) * 4 + (P("batch", None),) * 3 + (P(),) * 4,
        check_vma=False,
    )
```

```python
import functools

import jax
import jax.numpy as jnp
import numpy as np
from jax import lax
from jax.experimental import pallas as pl
from jax.experimental.pallas import tpu as pltpu
from jax.sharding import PartitionSpec as P

EPSILON = 1e-05
LEVELS = 4
MESH = pl.DeviceIdType.MESH
F32 = jnp.float32
BF16 = jnp.bfloat16

MEAN, RSTD, GAIN1, SHIFT1, GAIN2, SHIFT2, LOCAL, N_COLS = range(8)
CA, CB, CC = MEAN, RSTD, LOCAL
UMEAN, URSTD, UGAIN, USHIFT, ULOCAL, UA, UB, UC, N_UCOLS = range(9)


class Sizes:
    def __init__(self, features, nb, nk):
        self.chan = [f.shape[1] for f in features]
        self.rows = [f.shape[2] for f in features]
        self.width = [f.shape[3] for f in features]
        self.own = [r * w for r, w in zip(self.rows, self.width)]
        self.flat = [(r + 2) * w for r, w in zip(self.rows, self.width)]
        self.off = [sum(self.chan[:l]) for l in range(LEVELS)]
        self.total = sum(self.chan)
        self.blocks = -(-self.total // 128)
        self.uchan = self.chan[0]
        self.utotal = 3 * self.uchan
        self.ublocks = -(-self.utotal // 128)
        self.rim_rows = [c * w // 128 for c, w in zip(self.chan, self.width)]
        self.rim_off = [sum(self.rim_rows[:l]) for l in range(LEVELS)]
        self.rim_total = sum(self.rim_rows)
        self.chunk = []
        for c, n, w in zip(self.chan, self.flat, self.width):
            lanes = max(x for x in range(128, 641, 128) if n % x == 0 and x % w == 0)
            rows = max(r for r in (16, 32, 48) if c % r == 0 and r * lanes <= 12288)
            self.chunk.append((rows, lanes))
        self.nc = 2 if nb % 2 == 0 else 1
        self.nx = 2 if nk % 2 == 0 else 1
        self.ny = nb // self.nc
        self.nz = nk // self.nx
        self.gather = nb * nk <= 32 and self.nx == 2 and self.nc == 2 and self.own[3] == 64
        self.sum_levels = [0, 1, 2]
        self.stacked = [l for l in range(3 if self.gather else 4) if self.width[l] < 128]
        self.spots = {}
        at = 0
        for l in self.sum_levels:
            rows = -(-3 * self.chan[l] // nb // 16) * 16
            for i in range(-(-3 * self.chan[l] // 128)):
                self.spots[l, i] = (at, rows)
                at += rows
        for j in range(3):
            rows = -(-self.uchan // nb // 16) * 16
            for i in range(-(-self.chan[j + 1] // 128)):
                self.spots["u", j, i] = (at, rows)
                at += rows
        self.part = -(-at // (nk * 16)) * 16
        self.sum_rows = self.part * nk


def blend(scale, rows):
    out = []
    for g in range(rows):
        num = 2 * g + 1 - scale
        low = num // (2 * scale)
        out.append((low + 1, (num - 2 * scale * low) / (2.0 * scale)))
    return out


def column_table(width, fine):
    scale = fine // width
    group = max(1, 128 // width)
    span = max(128, width)
    table = np.zeros((span, group * fine), np.float32)
    for r in range(group):
        for g in range(fine):
            num = 2 * g + 1 - scale
            low = 0 if num < 0 else num // (2 * scale)
            frac = 0.0 if num < 0 else (num - 2 * scale * low) / (2.0 * scale)
            high = min(low + 1, width - 1)
            table[r * width + low, r * fine + g] += 1.0 - frac
            table[r * width + high, r * fine + g] += frac
    return table


def sigmoid(v):
    return jax.nn.sigmoid(v)


def main_kernel(sz, nb, nk, *refs):
    it = iter(refs)
    take = lambda n: [next(it) for _ in range(n)]
    heights, widths, slots = take(3)
    feats = take(4)
    (ograd,) = take(1)
    blocks = take(4)
    unites = take(3)
    norm_gains, norm_shifts, unite_gains, unite_shifts = take(4)
    tables = take(3)
    tables_t = take(3)
    (united_ref,) = take(1)
    gfeat = take(4)
    (sums_ref,) = take(1)
    (coarse_ref,) = take(1)
    (totals_ref,) = take(1)
    raw = take(3 if sz.gather else 4)
    wide = take(4)
    (stage,) = take(1)
    x3 = take(4)
    a3 = take(4)
    g3 = take(4)
    t3 = dict(zip(sz.stacked, take(len(sz.stacked))))
    cstage, cstage_sem = take(2)
    (kg,) = take(1)
    gun = take(3)
    xf = take(4)
    y1 = take(4)
    y2 = take(4)
    p1 = take(4)
    br = take(3)
    uo = take(3)
    up = take(3)
    (cols, ucols, stat_a, stat_b, ustat_a, ustat_b, n_a, n_b, un_a, un_b) = take(10)
    masks = take(4)
    (rec_a, rec_b, rim_s, rim_r, mid_s, mid_r) = take(6)
    (sa_send, sa_recv, sb_send, sb_recv, rim_send, rim_recv) = take(6)
    raw_sem, wide_sem = take(2)
    prow, urow = take(2)
    part_a, got_a, got_b, got_c, got_d, out_sem = take(6)
    (ra_send, ra_recv, rb_send, rb_recv, rc_send, rc_recv, rd_send, rd_recv) = take(8)
    if sz.gather:
        xg, gs, gr, x3g, t3g = take(5)
        (xg_send, xg_recv, g1_send, g1_recv, g2_send, g2_recv) = take(6)

    C, R, W, N, NP, OFF = sz.chan, sz.rows, sz.width, sz.own, sz.flat, sz.off
    me_b = lax.axis_index("batch")
    me_k = lax.axis_index("rows")

    def peer_b(j):
        return lax.rem(me_b + j, nb)

    def peer_k(j):
        return lax.rem(me_k + j, nk)

    def raw_copy(l, which):
        if l == 3 and sz.gather:
            dst = x3g.at[0:3, :, 0 : C[3]]
        else:
            dst = raw[l]
        return pltpu.make_async_copy(blocks[l].at[which], dst, raw_sem.at[l, which])

    def wide_copies(which):
        c = C[3]
        return [
            pltpu.make_async_copy(
                blocks[3].at[which, t, u * c : (u + 1) * c, :],
                wide[3].at[which, t * c : (t + 1) * c, u * c : (u + 1) * c],
                wide_sem.at[which, 3 * t + u],
            )
            for t in range(3)
            for u in range(3)
        ]

    for l in range(3):
        raw_copy(l, 0).start()
    for which in range(2):
        for copy in wide_copies(which):
            copy.start()
    raw_copy(3, 0).start()

    def widen(which):
        for copy in wide_copies(which):
            copy.wait()
        for l in range(3):
            raw_copy(l, which).wait()
            c = C[l]
            for t in range(3):
                wide[l][which, t * c : (t + 1) * c, :] = jnp.concatenate(
                    [raw[l][t, u * c : (u + 1) * c, :] for u in range(3)], axis=1
                )

    def turn(which):
        raw_copy(3, which).wait()
        for l in range(LEVELS):
            for t in range(3):
                if l == 3 and sz.gather:
                    v = x3g[t, :, 0 : C[3]]
                else:
                    v = raw[l][t]
                wide[l][which, t * C[l] : (t + 1) * C[l], :] = v.T
        if which == 0:
            for l in range(LEVELS):
                raw_copy(l, 1).start()

    barrier = pltpu.get_barrier_semaphore()
    for j in range(1, nb):
        pl.semaphore_signal(barrier, inc=1, device_id=(peer_b(j), me_k), device_id_type=MESH)
    for j in range(1, nk):
        pl.semaphore_signal(barrier, inc=1, device_id=(me_b, peer_k(j)), device_id_type=MESH)
    pl.semaphore_wait(barrier, nb + nk - 2)

    my_h = jnp.int32(0)
    my_w = jnp.int32(0)
    slot_h, slot_w = [], []
    for b in range(nb):
        h = jnp.int32(0)
        w = jnp.int32(0)
        for i in range(nb):
            hit = (slots[i] == b).astype(jnp.int32)
            h = h + hit * heights[i]
            w = w + hit * widths[i]
        slot_h.append(h)
        slot_w.append(w)
        mine = (me_b == b).astype(jnp.int32)
        my_h = my_h + mine * h
        my_w = my_w + mine * w

    count = []
    for l in range(LEVELS):
        c = jnp.int32(0)
        for b in range(nb):
            c = c + lax.shift_right_logical(slot_h[b], l) * lax.shift_right_logical(slot_w[b], l)
        count.append(c.astype(F32))
    inv_local = []
    for l in range(LEVELS):
        inside = jnp.clip(lax.shift_right_logical(my_h, l) - me_k * R[l], 0, R[l])
        own = inside * lax.shift_right_logical(my_w, l)
        inv_local.append(1.0 / jnp.maximum(own, 1).astype(F32))
        lane = lax.broadcasted_iota(jnp.int32, (1, NP[l]), 1)
        log_w = W[l].bit_length() - 1
        row = me_k * R[l] + lax.shift_right_logical(lane, log_w) - 1
        col = lane & (W[l] - 1)
        valid = (row >= 0) & (row < lax.shift_right_logical(my_h, l))
        valid = valid & (col < lax.shift_right_logical(my_w, l))
        masks[l][0:1, :] = jnp.where(valid, 1.0, 0.0)
        masks[l][1:2, :] = jnp.where(valid & (lane >= W[l]) & (lane < W[l] + N[l]), 1.0, 0.0)

    place = lax.broadcasted_iota(jnp.int32, (8, 128), 0) * 128 + lax.broadcasted_iota(
        jnp.int32, (8, 128), 1
    )

    def by_level(values):
        out = jnp.full((8, 128), values[3])
        for l in (2, 1, 0):
            out = jnp.where(place < OFF[l + 1], jnp.full((8, 128), values[l]), out)
        return out

    def by_unite(values):
        out = jnp.full((8, 128), values[2])
        for j in (1, 0):
            out = jnp.where(place < (j + 1) * sz.uchan, jnp.full((8, 128), values[j]), out)
        return out

    inv_count = 1.0 / by_level(count)
    inv_ucount = 1.0 / by_unite(count[1:])
    for chooser, levels, na_ref, nb_ref in (
        (by_level, range(4), n_a, n_b),
        (by_unite, range(1, 4), un_a, un_b),
    ):
        span = chooser([jnp.int32(R[l]) for l in levels])
        hv = [chooser([lax.shift_right_logical(h, l) for l in levels]) for h in slot_h]
        wv = [chooser([lax.shift_right_logical(w, l) for l in levels]) for w in slot_w]
        for b in range(nb):
            na_ref[b] = (jnp.clip(hv[b] - me_k * span, 0, span) * wv[b]).astype(F32)
        for k in range(nk):
            n = jnp.zeros((8, 128), jnp.int32)
            for b in range(nb):
                n = n + jnp.clip(hv[b] - k * span, 0, span) * wv[b]
            nb_ref[k] = n.astype(F32)

    def tile(v, lanes):
        return v if lanes == 128 else jnp.concatenate([v] * (lanes // 128), axis=1)

    def col(slot, l, r0, rc, lanes):
        return tile(cols[slot, pl.ds(pl.multiple_of(OFF[l] + r0, 16), rc), :], lanes)

    def ucol(slot, j, lanes):
        return tile(ucols[slot, j * sz.uchan : (j + 1) * sz.uchan, :], lanes)

    def to_columns(packed, ref, slot_list, blocks):
        full = jnp.concatenate(packed + [jnp.zeros((128 - 8 * len(packed), 128), F32)], axis=0)
        turned = full.T
        for i, slot in enumerate(slot_list):
            for k in range(blocks):
                ref[slot, 128 * k : 128 * k + 128, :] = jnp.broadcast_to(
                    turned[:, 8 * i + k : 8 * i + k + 1], (128, 128)
                )

    prow[...] = jnp.zeros_like(prow)
    urow[...] = jnp.zeros_like(urow)
    for i in range(2):
        prow[2 * i : 2 * i + 1, 0 : sz.total] = norm_gains[i : i + 1, :]
        prow[2 * i + 1 : 2 * i + 2, 0 : sz.total] = norm_shifts[i : i + 1, :]
    for j in range(3):
        at = slice(j * sz.uchan, (j + 1) * sz.uchan)
        urow[0:1, at] = unite_gains[j : j + 1, :]
        urow[1:2, at] = unite_shifts[j : j + 1, :]
    standing = prow[...].T
    for i, slot in enumerate((GAIN1, SHIFT1, GAIN2, SHIFT2)):
        cols[slot] = jnp.broadcast_to(standing[:, i : i + 1], (sz.blocks * 128, 128))
    standing = urow[...].T
    for i, slot in enumerate((UGAIN, USHIFT)):
        ucols[slot] = jnp.broadcast_to(standing[:, i : i + 1], (sz.ublocks * 128, 128))

    def packed(ref, i, blocks):
        rows = [ref[i : i + 1, 128 * k : 128 * k + 128] for k in range(blocks)]
        return jnp.concatenate(rows + [jnp.zeros((8 - blocks, 128), F32)], axis=0)

    gain1_p, gain2_p = packed(prow, 0, sz.blocks), packed(prow, 2, sz.blocks)
    ugain_p = packed(urow, 0, sz.ublocks)
    stat_a[...] = jnp.zeros_like(stat_a)
    stat_b[...] = jnp.zeros_like(stat_b)
    ustat_a[...] = jnp.zeros_like(ustat_a)
    ustat_b[...] = jnp.zeros_like(ustat_b)

    def fold(v):
        out = v[:, 0:128]
        for i in range(1, v.shape[1] // 128):
            out = out + v[:, 128 * i : 128 * i + 128]
        return out

    lane128 = lax.broadcasted_iota(jnp.int32, (1, 128), 1)

    def record(a_ref, b_ref, blocks):
        out = jnp.zeros((128, 128), F32)
        for base, ref in ((0, a_ref), (8, b_ref)):
            for k in range(blocks):
                s = jnp.sum(ref[128 * k : 128 * k + 128, :], axis=1, keepdims=True)
                out = jnp.where(lane128 == base + k, s, out)
        return out.T[0:16]

    def spread(e, which, rec, meanwhile):
        copies = []
        if which == 0:
            ref, send, recv, n, me = rec_a, sa_send, sa_recv, nb, me_b
        else:
            ref, send, recv, n, me = rec_b, sb_send, sb_recv, nk, me_k
        ref[e, me] = rec
        for j in range(1, n):
            target = (peer_b(j), me_k) if which == 0 else (me_b, peer_k(j))
            copy = pltpu.make_async_remote_copy(
                src_ref=ref.at[e, me],
                dst_ref=ref.at[e, me],
                send_sem=send.at[e, j],
                recv_sem=recv.at[e, me],
                device_id=target,
                device_id_type=MESH,
            )
            copy.start()
            copies.append(copy)
        if meanwhile is not None:
            meanwhile()
        for j in range(1, n):
            other = peer_b(j) if which == 0 else peer_k(j)
            pltpu.make_async_remote_copy(
                src_ref=ref.at[e, me],
                dst_ref=ref.at[e, other],
                send_sem=send.at[e, j],
                recv_sem=recv.at[e, other],
                device_id=(me_b, me_k),
                device_id_type=MESH,
            ).wait_recv()
        for copy in copies:
            copy.wait_send()

    def gather_moments(e, rec, na_ref, nb_ref, meanwhile=(None, None)):
        for which, n, ref, n_ref in ((0, nb, rec_a, na_ref), (1, nk, rec_b, nb_ref)):
            spread(e, which, rec, meanwhile[which])
            total = jnp.zeros((8, 128), F32)
            size = jnp.zeros((8, 128), F32)
            for i in range(n):
                total = total + ref[e, i, 0:8]
                size = size + n_ref[i]
            mean = total / jnp.maximum(size, 1.0)
            spread_sum = jnp.zeros((8, 128), F32)
            for i in range(n):
                delta = ref[e, i, 0:8] / jnp.maximum(n_ref[i], 1.0) - mean
                spread_sum = spread_sum + (ref[e, i, 8:16] + n_ref[i] * delta * delta)
            rec = jnp.concatenate([total, spread_sum], axis=0)
        return rec

    def gather_sums(e, rec, meanwhile=(None, None)):
        for which, n, ref in ((0, nb, rec_a), (1, nk, rec_b)):
            spread(e, which, rec, meanwhile[which])
            rec = jnp.zeros((16, 128), F32)
            for i in range(n):
                rec = rec + ref[e, i]
        return rec

    def rim_copies(slot, src, dst):
        up = pltpu.make_async_remote_copy(
            src_ref=src.at[0],
            dst_ref=dst.at[1],
            send_sem=rim_send.at[slot, 0],
            recv_sem=rim_recv.at[slot, 1],
            device_id=(me_b, lax.rem(me_k + nk - 1, nk)),
            device_id_type=MESH,
        )
        down = pltpu.make_async_remote_copy(
            src_ref=src.at[1],
            dst_ref=dst.at[0],
            send_sem=rim_send.at[slot, 1],
            recv_sem=rim_recv.at[slot, 0],
            device_id=(me_b, lax.rem(me_k + 1, nk)),
            device_id_type=MESH,
        )
        return up, down

    def rims_start(slot, src, dst):
        up, down = rim_copies(slot, src, dst)

        @pl.when(me_k > 0)
        def _():
            up.start()

        @pl.when(me_k < nk - 1)
        def _():
            down.start()

    def rims_wait(slot, src, dst):
        up, down = rim_copies(slot, src, dst)

        @pl.when(me_k > 0)
        def _():
            down.wait_recv()
            up.wait_send()

        @pl.when(me_k < nk - 1)
        def _():
            up.wait_recv()
            down.wait_send()

    def pack_row(ref, l, lane0):
        if W[l] >= 128:
            return jnp.concatenate(
                [ref[:, lane0 + 128 * i : lane0 + 128 * i + 128] for i in range(W[l] // 128)], axis=0
            )
        group = 128 // W[l]
        rows = C[l] // group
        base, shift = lane0 // 128 * 128, lane0 % 128
        out = None
        for g in range(group):
            v = ref[g * rows : (g + 1) * rows, base : base + 128]
            turn = (g * W[l] - shift) % 128
            v = pltpu.roll(v, turn, 1) if turn else v
            out = v if out is None else jnp.where(lane128 >= g * W[l], v, out)
        return out

    def unpack_row(ref, l, lane0, q):
        if W[l] >= 128:
            for i in range(W[l] // 128):
                ref[:, lane0 + 128 * i : lane0 + 128 * i + 128] = q[i * C[l] : (i + 1) * C[l]]
            return
        group = 128 // W[l]
        rows = C[l] // group
        base, shift = lane0 // 128 * 128, lane0 % 128
        here = (lane128 >= shift) & (lane128 < shift + W[l])
        for g in range(group):
            turn = (shift - g * W[l]) % 128
            v = pltpu.roll(q, turn, 1) if turn else q
            old = ref[g * rows : (g + 1) * rows, base : base + 128]
            ref[g * rows : (g + 1) * rows, base : base + 128] = jnp.where(here, v, old)

    def pack_rims(slot, arrays):
        for l in range(LEVELS):
            at = slice(sz.rim_off[l], sz.rim_off[l] + sz.rim_rows[l])
            rim_s[0, at, :] = pack_row(arrays[l], l, W[l]).astype(BF16)
            rim_s[1, at, :] = pack_row(arrays[l], l, N[l]).astype(BF16)

    def unpack_rims(slot, arrays):
        for l in range(LEVELS):
            at = slice(sz.rim_off[l], sz.rim_off[l] + sz.rim_rows[l])
            unpack_row(arrays[l], l, 0, rim_r[slot, 0, at, :].astype(F32))
            unpack_row(arrays[l], l, W[l] + N[l], rim_r[slot, 1, at, :].astype(F32))

    def each(l, body):
        rc, lanes = sz.chunk[l]

        def step(i, _):
            body(pl.multiple_of(i * rc, rc), rc, lanes)
            return 0

        lax.fori_loop(0, C[l] // rc, step, 0)

    def lane_chunks(l, lanes):
        return [(i, i + lanes) for i in range(0, NP[l], lanes)]

    def stack_columns(ref, l, r0, rc, a, b, v, back=False):
        lanes = b - a
        at = lax.broadcasted_iota(jnp.int32, (1, lanes), 1) & (W[l] - 1)
        left = jnp.where(at == 0, 0.0, pltpu.roll(v, 1, 1))
        right = jnp.where(at == W[l] - 1, 0.0, pltpu.roll(v, lanes - 1, 1))
        for u, part in enumerate((right, v, left) if back else (left, v, right)):
            ref[pl.ds(pl.multiple_of(u * C[l] + r0, 16), rc), a:b] = part.astype(BF16)

    def stack_rows(ref, l, r0, rc, v):
        for t in range(3):
            turn = ((t - 1) * W[l]) % NP[l]
            part = pltpu.roll(v, turn, 1) if turn else v
            ref[pl.ds(pl.multiple_of(t * C[l] + r0, 16), rc), :] = part.astype(BF16)

    def conv(l, w, which, src, dst, sign=1):
        c = C[l]
        if W[l] % 128 == 0:
            span = min(1024, N[l])

            def step(i, _):
                acc = None
                for t in range(3):
                    at = pl.ds(pl.multiple_of(i * span + (1 + sign * (t - 1)) * W[l], 128), span)
                    part = jnp.dot(
                        w[l][which, t * c : (t + 1) * c, :], src[l][:, at], preferred_element_type=F32
                    )
                    acc = part if acc is None else acc + part
                dst[l][:, pl.ds(pl.multiple_of(i * span + W[l], 128), span)] = acc
                return 0

            lax.fori_loop(0, N[l] // span, step, 0)
        else:
            rows = 96

            def step(i, _):
                acc = None
                for t in range(3):
                    at = pl.ds(pl.multiple_of(t * c + i * rows, 16), rows)
                    part = jnp.dot(w[l][which, at, :], src[l][...], preferred_element_type=F32)
                    turn = (sign * (1 - t) * W[l]) % NP[l]
                    part = pltpu.roll(part, turn, 1) if turn else part
                    acc = part if acc is None else acc + part
                dst[l][pl.ds(pl.multiple_of(i * rows, 16), rows), :] = acc
                return 0

            lax.fori_loop(0, c // rows, step, 0)

    def kernel_grad(l, src):
        c = C[l]
        if W[l] % 128 == 0:
            for t in range(3):
                kg[t * c : (t + 1) * c, 0 : 3 * c] = lax.dot_general(
                    g3[l][c : 2 * c, W[l] : W[l] + N[l]],
                    src[l][:, t * W[l] : t * W[l] + N[l]],
                    (((1,), (1,)), ((), ())),
                    preferred_element_type=F32,
                )
            return
        span = 96

        def step(i, _):
            at = pl.ds(pl.multiple_of(i * span, 16), span)
            kg[at, 0 : 3 * c] = lax.dot_general(
                t3[l][at, :], src[l][...], (((1,), (1,)), ((), ())), preferred_element_type=F32
            )
            return 0

        lax.fori_loop(0, 3 * c // span, step, 0)

    nc, ny, nx, nz = sz.nc, sz.ny, sz.nx, sz.nz
    my_core, my_y = lax.rem(me_b, nc), lax.div(me_b, nc)
    my_x, my_z = lax.rem(me_k, nx), lax.div(me_k, nx)

    def others(n, me):
        return [lax.rem(me + j, n) for j in range(1, n)]

    def remote(src, dst, send, recv, target):
        return pltpu.make_async_remote_copy(
            src_ref=src, dst_ref=dst, send_sem=send, recv_sem=recv, device_id=target, device_id_type=MESH
        )

    def sum_pack(c, l):
        n = C[l] // nb
        for q in range(nb):
            dst = part_a.at[c, q % nc, q // nc]
            for i in range(-(-3 * C[l] // 128)):
                at, rows = sz.spots[l, i]
                lanes = slice(128 * i, 128 * i + 128)
                parts = [kg[t * C[l] + q * n : t * C[l] + q * n + n, lanes] for t in range(3)]
                if rows > 3 * n:
                    parts.append(jnp.zeros((rows - 3 * n, 128), F32))
                dst[at : at + rows, :] = jnp.concatenate(parts, axis=0).astype(BF16)

    def sum_pack_unites():
        n = sz.uchan // nb
        for q in range(nb):
            dst = part_a.at[1, q % nc, q // nc]
            for j in range(3):
                for i in range(-(-C[j + 1] // 128)):
                    at, rows = sz.spots["u", j, i]
                    v = gun[j][q * n : q * n + n, 128 * i : 128 * i + 128]
                    if rows > n:
                        v = jnp.concatenate([v, jnp.zeros((rows - n, 128), F32)], axis=0)
                    dst[at : at + rows, :] = v.astype(BF16)

    def core_copies(c):
        out = []
        for other in others(nc, my_core):
            target = (my_y * nc + other, me_k)
            out.append(remote(part_a.at[c, other], got_a.at[c], ra_send.at[c], ra_recv.at[c], target))
        return out

    def y_copies(c, sending):
        out = []
        for other in others(ny, my_y):
            target = (other * nc + my_core, me_k)
            if sending:
                src, dst, sem = part_a.at[c, my_core, other], got_b.at[c, my_y], rb_recv.at[c, my_y]
            else:
                src, dst, sem = part_a.at[c, my_core, other], got_b.at[c, other], rb_recv.at[c, other]
            out.append(remote(src, dst, rb_send.at[c, other], sem, target))
        return out

    def row_copies(c, sending):
        out = []
        for other in others(nk, me_k):
            slot = me_k if sending else other
            out.append(
                remote(
                    part_a.at[c, my_core, my_y, pl.ds(pl.multiple_of(other * sz.part, 16), sz.part), :],
                    got_c.at[c, slot], rc_send.at[c, other], rc_recv.at[c, slot], (me_b, other)
                )
            )
        return out

    def back_copies(c, sending):
        out = []
        for other in others(nk, me_k):
            slot = me_k if sending else other
            out.append(
                remote(
                    got_d.at[c, me_k], got_d.at[c, slot], rd_send.at[c, other], rd_recv.at[c, slot], (me_b, other)
                )
            )
        return out

    def finish(pair):
        sent, received = pair
        for copy in received:
            copy.wait_recv()
        for copy in sent:
            copy.wait_send()

    def sum_first(c, src):
        for l in sz.sum_levels:
            kernel_grad(l, src)
            sum_pack(c, l)
        if c == 1:
            sum_pack_unites()
        for copy in core_copies(c):
            copy.start()

    def sum_second(c):
        copies = core_copies(c)
        finish((copies, copies))
        for y in range(ny):
            v = part_a[c, my_core, y].astype(F32)
            if nc > 1:
                v = v + got_a[c, y].astype(F32)
            part_a[c, my_core, y] = v.astype(BF16)
        for copy in y_copies(c, True):
            copy.start()

    def sum_third(c):
        finish((y_copies(c, True), y_copies(c, False)))
        got_b[c, my_y] = part_a[c, my_core, my_y]
        for k in range(nk):
            at = slice(k * sz.part, (k + 1) * sz.part)
            v = got_b[c, 0, at, :].astype(F32)
            for y in range(1, ny):
                v = v + got_b[c, y, at, :].astype(F32)
            part_a[c, my_core, my_y, at, :] = v.astype(BF16)
        for copy in row_copies(c, True):
            copy.start()

    def sum_fourth(c):
        finish((row_copies(c, True), row_copies(c, False)))
        mine = pl.ds(pl.multiple_of(me_k * sz.part, 16), sz.part)
        got_c[c, me_k] = part_a[c, my_core, my_y, mine, :]
        v = got_c[c, 0].astype(F32)
        for k in range(1, nk):
            v = v + got_c[c, k].astype(F32)
        got_d[c, me_k] = v.astype(BF16)
        for copy in back_copies(c, True):
            copy.start()

    def sum_last(c):
        finish((back_copies(c, True), back_copies(c, False)))
        pltpu.make_async_copy(got_d.at[c], sums_ref.at[c], out_sem.at[c]).start()

    c3 = C[3] // nb
    half = c3 // 2

    def pack_pixels(ref):
        parts = []
        for q in range(nb):
            at = C[3] + q * c3
            low = pltpu.roll(ref[at : at + half, :].astype(F32), 128 - W[3], 1)
            high = pltpu.roll(ref[at + half : at + c3, :].astype(F32), 64 - W[3], 1)
            parts.append(jnp.where(lane128 < 64, low, high))
        return jnp.concatenate(parts, axis=0).astype(BF16)

    def unpack_pixels(first, second):
        first, second = first.astype(F32), second.astype(F32)
        low = jnp.where(lane128 < 64, first, pltpu.roll(second, 64, 1))
        high = jnp.where(lane128 < 64, pltpu.roll(first, 64, 1), second)
        return low, high

    def gather_copies(c, step, sending):
        if not sz.gather:
            return []
        n, me = ((nz, my_z), (nx, my_x), (ny, my_y), (nc, my_core))[step]
        out = []
        for other in others(n, me):
            slot = me if sending else other
            if step == 0:
                ref, target = xg.at[c, my_core, my_y, my_x, slot], (me_b, other * nx + my_x)
            elif step == 1:
                ref, target = xg.at[c, my_core, my_y, slot], (me_b, my_z * nx + other)
            elif step == 2:
                ref, target = xg.at[c, my_core, slot], (other * nc + my_core, me_k)
            else:
                ref, target = xg.at[c, slot], (my_y * nc + other, me_k)
            out.append(remote(ref, ref, xg_send.at[c, step, other], xg_recv.at[c, step, slot], target))
        return out

    def gather_start(c, step):
        for copy in gather_copies(c, step, True):
            copy.start()

    def gather_wait(c, step):
        finish((gather_copies(c, step, True), gather_copies(c, step, False)))

    def gather_begin(c, ref):
        if sz.gather:
            xg[c, my_core, my_y, my_x, my_z] = pack_pixels(ref[3])
            gather_start(c, 0)

    def gather_next(c, step):
        gather_wait(c, step)
        gather_start(c, step + 1)

    def grad_copies(c, step, sending):
        out = []
        if step == 0:
            for other in others(nb, me_b):
                slot = me_b if sending else other
                src = gs.at[c, other]
                out.append(
                    remote(src, gr.at[c, me_k, slot], g1_send.at[c, other], g1_recv.at[c, slot], (other, me_k))
                )
        else:
            for other in others(nk, me_k):
                slot = me_k if sending else other
                ref = gr.at[c, slot]
                out.append(remote(gr.at[c, me_k], ref, g2_send.at[c, other], g2_recv.at[c, slot], (me_b, other)))
        return out

    def grad_begin(c):
        if sz.gather:
            v = pack_pixels(g3[3])
            for q in range(nb):
                gs[c, q] = v[q * half : (q + 1) * half]
            for copy in grad_copies(c, 0, True):
                copy.start()

    def grad_next(c):
        if sz.gather:
            finish((grad_copies(c, 0, True), grad_copies(c, 0, False)))
            gr[c, me_k, me_b] = gs[c, me_b]
            for copy in grad_copies(c, 1, True):
                copy.start()

    image = nz * 128

    def coarse_inputs(c):
        if not sz.gather:
            return
        gather_wait(c, 3)
        at = lane128 & (W[3] - 1)

        def item(b, _):
            def group(q, _):
                for z in range(nz):
                    rows = pl.ds(pl.multiple_of(q * half, 16), half)
                    core, y = lax.rem(b, nc), lax.div(b, nc)
                    pair = unpack_pixels(xg[c, core, y, 0, z, rows, :], xg[c, core, y, 1, z, rows, :])
                    for i, v in enumerate(pair):
                        left = jnp.where(at == 0, 0.0, pltpu.roll(v, 1, 1))
                        right = jnp.where(at == W[3] - 1, 0.0, pltpu.roll(v, 127, 1))
                        for u, part in enumerate((left, v, right)):
                            spot = pl.ds(pl.multiple_of(u * C[3] + q * c3 + i * half, 16), half)
                            x3g[b, spot, 128 * z : 128 * z + 128] = part.astype(BF16)
                return 0

            lax.fori_loop(0, nb, group, 0)
            return 0

        lax.fori_loop(0, nb, item, 0)

    def coarse_copy(c, i):
        at = pl.ds(i * c3 if isinstance(i, int) else pl.multiple_of(i * c3, 16), c3)
        slot = i % 2 if isinstance(i, int) else lax.rem(i, 2)
        return pltpu.make_async_copy(cstage.at[slot], coarse_ref.at[c, at, :], cstage_sem.at[slot])

    def coarse_local(c, src):
        def step(i, _):
            at = pl.ds(pl.multiple_of(i * c3, 16), c3)
            cstage[0] = lax.dot_general(
                t3[3][at, :], src[3][...], (((1,), (1,)), ((), ())), preferred_element_type=F32
            )
            copy = pltpu.make_async_copy(cstage.at[0], coarse_ref.at[c, at, :], cstage_sem.at[0])
            copy.start()
            copy.wait()
            return 0

        lax.fori_loop(0, 3 * nb, step, 0)

    def coarse_gradient(c):
        if not sz.gather:
            coarse_local(c, a3 if c else x3)
            return
        finish((grad_copies(c, 1, True), grad_copies(c, 1, False)))
        lane = lax.broadcasted_iota(jnp.int32, (1, image), 1)

        def item(b, _):
            low, high = [], []
            for z in range(nz):
                first, second = unpack_pixels(gr[c, nx * z, b], gr[c, nx * z + 1, b])
                low.append(first)
                high.append(second)
            for i, parts in enumerate((low, high)):
                v = jnp.concatenate(parts, axis=1) if nz > 1 else parts[0]
                up_ = jnp.where(lane >= image - W[3], 0.0, pltpu.roll(v, image - W[3], 1))
                down = jnp.where(lane < W[3], 0.0, pltpu.roll(v, W[3], 1))
                for t, part in enumerate((up_, v, down)):
                    spot = t * c3 + i * half
                    t3g[b, spot : spot + half, :] = part.astype(BF16)
            return 0

        lax.fori_loop(0, nb, item, 0)

        def step(i, _):
            at = pl.ds(pl.multiple_of(i * c3, 16), c3)
            acc = None
            for b in range(nb):
                part = lax.dot_general(
                    t3g[b, at, :], x3g[b, :, 0:image], (((1,), (1,)), ((), ())), preferred_element_type=F32
                )
                acc = part if acc is None else acc + part
            slot = lax.rem(i, 2)

            @pl.when(i >= 2)
            def _():
                coarse_copy(c, i - 2).wait()

            cstage[slot] = acc
            coarse_copy(c, i).start()
            return 0

        lax.fori_loop(0, 3, step, 0)
        coarse_copy(c, 1).wait()
        coarse_copy(c, 2).wait()

    def moments(arrays):
        for l in range(LEVELS):

            def body(r0, rc, lanes, l=l):
                acc = jnp.zeros((rc, 128), F32)
                for a, b in lane_chunks(l, lanes):
                    m = masks[l][1:2, a:b] > 0
                    acc = acc + fold(jnp.where(m, arrays[l][pl.ds(r0, rc), a:b], 0.0))
                stat_a[pl.ds(pl.multiple_of(OFF[l] + r0, 16), rc), :] = acc

            each(l, body)
        for l in range(LEVELS):
            at = slice(OFF[l], OFF[l] + C[l])
            s = jnp.sum(stat_a[at, :], axis=1, keepdims=True) * inv_local[l]
            cols[LOCAL, at, :] = jnp.broadcast_to(s, (C[l], 128))
        for l in range(LEVELS):

            def body(r0, rc, lanes, l=l):
                acc = jnp.zeros((rc, 128), F32)
                mean = col(LOCAL, l, r0, rc, lanes)
                for a, b in lane_chunks(l, lanes):
                    m = masks[l][1:2, a:b] > 0
                    d = jnp.where(m, arrays[l][pl.ds(r0, rc), a:b] - mean, 0.0)
                    acc = acc + fold(d * d)
                stat_b[pl.ds(pl.multiple_of(OFF[l] + r0, 16), rc), :] = acc

            each(l, body)
        return record(stat_a, stat_b, sz.blocks)

    def halves(l):
        return max(1, W[l] // 128)

    def to_stage(ref, src):
        for h in range(src.shape[1] // 128):
            ref[h] = src[:, 128 * h : 128 * h + 128].astype(F32)

    for l in range(LEVELS):
        if W[l] >= 128:
            to_stage(stage, feats[l])
            for r in range(R[l]):
                for h in range(halves(l)):
                    a = (r + 1) * W[l] + 128 * h
                    xf[l][:, a : a + 128] = stage[h, pl.ds(r, C[l], stride=R[l]), :]
        else:
            v = feats[l][...].astype(F32)
            v = jnp.concatenate([v, jnp.zeros((NP[l] - N[l], C[l]), F32)], axis=0)
            xf[l][...] = pltpu.roll(v.T, W[l], 1)
    pack_rims(0, xf)
    rims_start(0, rim_s, rim_r.at[0])
    to_stage(stage, ograd)
    widen(0)
    rims_wait(0, rim_s, rim_r.at[0])
    unpack_rims(0, xf)
    for l in range(LEVELS):

        def body(r0, rc, lanes, l=l):
            for a, b in lane_chunks(l, lanes):
                m = masks[l][0:1, a:b] > 0
                stack_columns(x3[l], l, r0, rc, a, b, jnp.where(m, xf[l][pl.ds(r0, rc), a:b], 0.0))

        each(l, body)

    gather_begin(0, x3)
    for l in range(LEVELS):
        conv(l, wide, 0, x3, y1)
    pack_rims(1, y1)
    rims_start(1, rim_s, rim_r.at[1])

    def while_first():
        gather_next(0, 0)
        turn(0)

    got = gather_moments(0, moments(y1), n_a, n_b, (while_first, lambda: widen(1)))
    rims_wait(1, rim_s, rim_r.at[1])
    mean1_p = got[0:8] * inv_count
    rstd1_p = lax.rsqrt(got[8:16] * inv_count + EPSILON)
    to_columns([mean1_p, rstd1_p], cols, [MEAN, RSTD], sz.blocks)
    unpack_rims(1, y1)

    def pre_of(hat, gain, shift, l, r0, rc, lanes):
        return hat * col(gain, l, r0, rc, lanes) + col(shift, l, r0, rc, lanes)

    for l in range(LEVELS):

        def body(r0, rc, lanes, l=l):
            for a, b in lane_chunks(l, lanes):
                m = masks[l][0:1, a:b] > 0
                hat = (y1[l][pl.ds(r0, rc), a:b] - col(MEAN, l, r0, rc, lanes)) * col(RSTD, l, r0, rc, lanes)
                y1[l][pl.ds(r0, rc), a:b] = hat
                pre = pre_of(hat, GAIN1, SHIFT1, l, r0, rc, lanes)
                stack_columns(a3[l], l, r0, rc, a, b, jnp.where(m, pre * sigmoid(pre), 0.0))

        each(l, body)

    gather_begin(1, a3)
    for l in range(LEVELS):
        conv(l, wide, 1, a3, y2)
    pack_rims(2, y2)
    rims_start(2, rim_s, rim_r.at[2])

    def while_second():
        gather_next(0, 1)
        gather_next(1, 0)

    got = gather_moments(1, moments(y2), n_a, n_b, (while_second, lambda: turn(1)))
    rims_wait(2, rim_s, rim_r.at[2])
    mean2_p = got[0:8] * inv_count
    rstd2_p = lax.rsqrt(got[8:16] * inv_count + EPSILON)
    to_columns([mean2_p, rstd2_p], cols, [MEAN, RSTD], sz.blocks)
    unpack_rims(2, y2)

    def start_part(l, r0, rc, a, b):
        return x3[l][pl.ds(pl.multiple_of(C[l] + r0, 16), rc), a:b].astype(F32)

    for l in range(LEVELS):

        def body(r0, rc, lanes, l=l):
            for a, b in lane_chunks(l, lanes):
                m = masks[l][0:1, a:b] > 0
                hat = (y2[l][pl.ds(r0, rc), a:b] - col(MEAN, l, r0, rc, lanes)) * col(RSTD, l, r0, rc, lanes)
                y2[l][pl.ds(r0, rc), a:b] = hat
                pre = pre_of(hat, GAIN2, SHIFT2, l, r0, rc, lanes)
                pre = jnp.where(m, pre, 0.0) + start_part(l, r0, rc, a, b)
                p1[l][pl.ds(r0, rc), a:b] = pre
                if l:
                    br[l - 1][pl.ds(r0, rc), a:b] = (pre * sigmoid(pre)).astype(BF16)

        each(l, body)

    UC_ = sz.uchan
    for j in range(3):
        l = j + 1
        uo[j][...] = jnp.dot(unites[j][...], br[j][...], preferred_element_type=F32)
    for j in range(3):
        l = j + 1
        m = masks[l][1:2, :] > 0
        v = jnp.where(m, uo[j][...], 0.0)
        part = fold(v)
        ustat_a[j * UC_ : (j + 1) * UC_, :] = part
        mean = jnp.sum(part, axis=1, keepdims=True) * inv_local[l]
        d = jnp.where(m, uo[j][...] - mean, 0.0)
        ustat_b[j * UC_ : (j + 1) * UC_, :] = fold(d * d)

    def while_unite():
        gather_next(0, 2)
        gather_next(1, 1)

    got = gather_moments(2, record(ustat_a, ustat_b, sz.ublocks), un_a, un_b, (while_unite, None))
    umean_p = got[0:8] * inv_ucount
    urstd_p = lax.rsqrt(got[8:16] * inv_ucount + EPSILON)
    to_columns([umean_p, urstd_p], ucols, [UMEAN, URSTD], sz.ublocks)

    at_top = me_k == 0
    at_bottom = me_k == nk - 1
    fine = W[0]
    split = lambda v: (v.astype(BF16), (v - v.astype(BF16).astype(F32)).astype(BF16))

    def edge(l, n):
        lane = lax.broadcasted_iota(jnp.int32, (1, n), 1)
        return lane

    for j in range(3):
        l = j + 1
        m = masks[l][0:1, :] > 0
        hat = (uo[j][...] - ucol(UMEAN, j, NP[l])) * ucol(URSTD, j, NP[l])
        uo[j][...] = hat
        norm = jnp.where(m, hat * ucol(UGAIN, j, NP[l]) + ucol(USHIFT, j, NP[l]), 0.0)
        lane = edge(l, NP[l])
        norm = jnp.where((lane < W[l]) & at_top, pltpu.roll(norm, NP[l] - W[l], 1), norm)
        norm = jnp.where((lane >= W[l] + N[l]) & at_bottom, pltpu.roll(norm, W[l], 1), norm)
        hi, lo = split(norm)
        both = jnp.concatenate([hi, lo], axis=0)
        span = max(128, W[l])
        width = tables[j].shape[1]
        for i in range(NP[l] // span):
            broad = jnp.dot(both[:, span * i : span * i + span], tables[j][...], preferred_element_type=F32)
            up[j][:, width * i : width * i + width] = broad[0:UC_] + broad[UC_:]

    blends = [blend(2 ** (j + 1), R[0]) for j in range(3)]

    def total_body(r0, rc, lanes):
        rows = pl.ds(r0, rc)
        coarse = [{}, {}, {}]
        have = [{}, {}, {}]
        for g in range(R[0]):
            a, b = (g + 1) * fine, (g + 2) * fine
            pre = p1[0][rows, a:b]
            total = pre * sigmoid(pre)
            for j in range(3):
                low, frac = blends[j][g]
                for i in (low, low + 1):
                    if i not in have[j]:
                        have[j][i] = up[j][rows, i * fine : (i + 1) * fine]
                total = total + ((1.0 - frac) * have[j][low] + frac * have[j][low + 1])
            m = masks[0][1:2, a:b] > 0
            sig = sigmoid(total)
            out = jnp.where(m, total * sig, 0.0)
            slope = sig * (1.0 + total * (1.0 - sig))
            spots = [(h, pl.ds(r0 * R[0] + g, rc, stride=R[0])) for h in range(halves(0))]
            grad = jnp.concatenate([stage[h, at, :] for h, at in spots], axis=1)
            grad = jnp.where(m, grad * slope, 0.0)
            for h, at in spots:
                stage[h, at, :] = out[:, 128 * h : 128 * h + 128]
            xf[0][rows, a:b] = grad
            for j in range(3):
                low, frac = blends[j][g]
                for i, weight in ((low, 1.0 - frac), (low + 1, frac)):
                    coarse[j][i] = weight * grad if i not in coarse[j] else coarse[j][i] + weight * grad
                done = [i for i in coarse[j] if g + 1 == R[0] or i < blends[j][g + 1][0]]
                for i in done:
                    up[j][rows, i * fine : (i + 1) * fine] = coarse[j].pop(i)

    def total_step(i, _):
        total_body(pl.multiple_of(i * 16, 16), 16, fine)
        return 0

    lax.fori_loop(0, UC_ // 16, total_step, 0)
    for h in range(halves(0)):
        united_ref[:, 128 * h : 128 * h + 128] = stage[h].astype(BF16)

    ud = []
    for j in range(3):
        l = j + 1
        span = max(128, W[l])
        width = tables[j].shape[1]
        parts = []
        for i in range(NP[l] // span):
            hi, lo = split(up[j][:, width * i : width * i + width])
            both = jnp.concatenate([hi, lo], axis=0)
            narrow = jnp.dot(both, tables_t[j][...], preferred_element_type=F32)
            parts.append(narrow[0:UC_] + narrow[UC_:])
        d = parts[0] if len(parts) == 1 else jnp.concatenate(parts, axis=1)
        lane = edge(l, NP[l])
        fold_top = jnp.where((lane >= W[l]) & (lane < 2 * W[l]) & at_top, pltpu.roll(d, W[l], 1), 0.0)
        fold_bottom = jnp.where(
            (lane >= N[l]) & (lane < W[l] + N[l]) & at_bottom, pltpu.roll(d, NP[l] - W[l], 1), 0.0
        )
        d = d + fold_top + fold_bottom
        d = jnp.where(masks[l][0:1, :] > 0, d, 0.0)
        ustat_a[j * UC_ : (j + 1) * UC_, :] = fold(d * uo[j][...])
        ustat_b[j * UC_ : (j + 1) * UC_, :] = fold(d)
        up[j][:, 0 : NP[l]] = d
    at = 0
    lay = []
    for j in range(3):
        l = j + 1
        n = max(2 * W[l], 128)
        lay.append((at, n))
        mid_s[0, :, at : at + n] = up[j][:, 0:n].astype(BF16)
        mid_s[1, :, at : at + n] = up[j][:, NP[l] - n : NP[l]].astype(BF16)
        at += n
    mid_s[0, :, at : at + fine] = xf[0][:, fine : 2 * fine].astype(BF16)
    mid_s[1, :, at : at + fine] = xf[0][:, N[0] : N[0] + fine].astype(BF16)
    rims_start(3, mid_s, mid_r)
    got4 = gather_sums(3, record(ustat_a, ustat_b, sz.ublocks), (lambda: gather_next(1, 2), None))
    totals_ref[0] = got4
    rims_wait(3, mid_s, mid_r)
    scale_p = urstd_p * ugain_p
    to_columns(
        [scale_p, got4[8:16] * inv_ucount, got4[0:8] * inv_ucount], ucols, [UA, UB, UC], sz.ublocks
    )
    xf[0][:, 0:fine] = mid_r[0, :, at : at + fine].astype(F32)
    xf[0][:, N[0] + fine : NP[0]] = mid_r[1, :, at : at + fine].astype(F32)
    for j in range(3):
        l = j + 1
        start, n = lay[j]
        lane = edge(l, n)
        above = mid_r[0, :, start : start + n].astype(F32)
        below = mid_r[1, :, start : start + n].astype(F32)
        if NP[l] == n:
            above, below = pltpu.roll(above, n // 2, 1), pltpu.roll(below, n // 2, 1)
            d = up[j][:, 0:n]
            d = d + jnp.where((lane < 2 * W[l]) & (me_k > 0), above, 0.0)
            d = d + jnp.where((lane >= n - 2 * W[l]) & (me_k < nk - 1), below, 0.0)
            up[j][:, 0:n] = d
        else:
            up[j][:, 0:n] = up[j][:, 0:n] + jnp.where((lane >= 0) & (me_k > 0), above, 0.0)
            up[j][:, NP[l] - n : NP[l]] = up[j][:, NP[l] - n : NP[l]] + jnp.where(
                (lane >= 0) & (me_k < nk - 1), below, 0.0
            )
    for j in range(3):
        l = j + 1
        d = up[j][:, 0 : NP[l]]
        g = ucol(UA, j, NP[l]) * (d - ucol(UB, j, NP[l]) - uo[j][...] * ucol(UC, j, NP[l]))
        g = jnp.where(masks[l][0:1, :] > 0, g, 0.0)
        low = g.astype(BF16)
        xf[l][...] = jnp.dot(unites[j][...].T, low, preferred_element_type=F32)
        own = jnp.where(masks[l][1:2, :] > 0, g, 0.0).astype(BF16)
        gun[j][:, 0 : C[l]] = lax.dot_general(
            own, br[j][...], (((1,), (1,)), ((), ())), preferred_element_type=F32
        )

    for l in range(LEVELS):

        def body(r0, rc, lanes, l=l):
            acc_g = jnp.zeros((rc, 128), F32)
            acc_s = jnp.zeros((rc, 128), F32)
            for a, b in lane_chunks(l, lanes):
                m = masks[l][1:2, a:b] > 0
                pre = p1[l][pl.ds(r0, rc), a:b]
                sig = sigmoid(pre)
                d = xf[l][pl.ds(r0, rc), a:b] * (sig * (1.0 + pre * (1.0 - sig)))
                xf[l][pl.ds(r0, rc), a:b] = d
                d = jnp.where(m, d, 0.0)
                acc_s = acc_s + fold(d)
                acc_g = acc_g + fold(jnp.where(m, d * y2[l][pl.ds(r0, rc), a:b], 0.0))
            at = pl.ds(pl.multiple_of(OFF[l] + r0, 16), rc)
            stat_a[at, :] = acc_g
            stat_b[at, :] = acc_s

        each(l, body)
    got5 = gather_sums(4, record(stat_a, stat_b, sz.blocks), (lambda: coarse_inputs(1), None))
    totals_ref[1] = got5
    to_columns(
        [rstd2_p * gain2_p, got5[8:16] * inv_count, got5[0:8] * inv_count], cols, [CA, CB, CC], sz.blocks
    )

    def store_gradient(l, r0, rc, parts):
        v = parts[0] if len(parts) == 1 else jnp.concatenate(parts, axis=1)
        if l not in sz.stacked:
            return
        stack_rows(t3[l], l, r0, rc, jnp.where(masks[l][1:2, :] > 0, v, 0.0))

    for l in range(LEVELS):

        def body(r0, rc, lanes, l=l):
            parts = []
            for a, b in lane_chunks(l, lanes):
                m = masks[l][0:1, a:b] > 0
                hat = y2[l][pl.ds(r0, rc), a:b]
                d = xf[l][pl.ds(r0, rc), a:b]
                g = col(CA, l, r0, rc, lanes) * (
                    d - col(CB, l, r0, rc, lanes) - hat * col(CC, l, r0, rc, lanes)
                )
                g = jnp.where(m, g, 0.0)
                stack_columns(g3[l], l, r0, rc, a, b, g, back=True)
                parts.append(g)
            store_gradient(l, r0, rc, parts)

        each(l, body)

    grad_begin(1)

    for l in range(LEVELS):
        conv(l, wide, 1, g3, p1, -1)
    for l in range(LEVELS):

        def body(r0, rc, lanes, l=l):
            acc_g = jnp.zeros((rc, 128), F32)
            acc_s = jnp.zeros((rc, 128), F32)
            for a, b in lane_chunks(l, lanes):
                m = masks[l][1:2, a:b] > 0
                hat = y1[l][pl.ds(r0, rc), a:b]
                pre = pre_of(hat, GAIN1, SHIFT1, l, r0, rc, lanes)
                sig = sigmoid(pre)
                d = p1[l][pl.ds(r0, rc), a:b] * (sig * (1.0 + pre * (1.0 - sig)))
                d = jnp.where(m, d, 0.0)
                p1[l][pl.ds(r0, rc), a:b] = d
                acc_s = acc_s + fold(d)
                acc_g = acc_g + fold(jnp.where(m, d * hat, 0.0))
            at = pl.ds(pl.multiple_of(OFF[l] + r0, 16), rc)
            stat_a[at, :] = acc_g
            stat_b[at, :] = acc_s

        each(l, body)
    pack_rims(3, p1)
    rims_start(4, rim_s, rim_r.at[3])

    def while_back():
        grad_next(1)
        sum_first(1, a3)

    def while_back_rows():
        coarse_gradient(1)
        coarse_inputs(0)

    got6 = gather_sums(5, record(stat_a, stat_b, sz.blocks), (while_back, while_back_rows))
    totals_ref[2] = got6
    rims_wait(4, rim_s, rim_r.at[3])
    to_columns(
        [rstd1_p * gain1_p, got6[8:16] * inv_count, got6[0:8] * inv_count], cols, [CA, CB, CC], sz.blocks
    )
    unpack_rims(3, p1)
    for l in (3, 0, 1, 2):

        def body(r0, rc, lanes, l=l):
            parts = []
            for a, b in lane_chunks(l, lanes):
                m = masks[l][0:1, a:b] > 0
                hat = y1[l][pl.ds(r0, rc), a:b]
                d = p1[l][pl.ds(r0, rc), a:b]
                g = col(CA, l, r0, rc, lanes) * (
                    d - col(CB, l, r0, rc, lanes) - hat * col(CC, l, r0, rc, lanes)
                )
                g = jnp.where(m, g, 0.0)
                stack_columns(g3[l], l, r0, rc, a, b, g, back=True)
                parts.append(g)
            store_gradient(l, r0, rc, parts)

        each(l, body)
        if l == 3:
            grad_begin(0)

    sum_first(0, x3)
    sum_second(1)
    grad_next(0)

    def features_out(l):
        if W[l] < 128:
            v = jnp.where(masks[l][1:2, :] > 0, y1[l][...] + xf[l][...], 0.0)
            gfeat[l][...] = pltpu.roll(v, NP[l] - W[l], 1).T[0 : N[l]].astype(BF16)
            return

        def body(r0, rc, lanes):
            for r in range(R[l]):
                for h in range(halves(l)):
                    a = (r + 1) * W[l] + 128 * h
                    m = masks[l][1:2, a : a + 128] > 0
                    v = y1[l][pl.ds(r0, rc), a : a + 128] + xf[l][pl.ds(r0, rc), a : a + 128]
                    stage[h, pl.ds(r0 * R[l] + r, rc, stride=R[l]), :] = jnp.where(m, v, 0.0)

        each(l, body)
        for h in range(halves(l)):
            gfeat[l][:, 128 * h : 128 * h + 128] = stage[h].astype(BF16)

    for l in (0, 1):
        conv(l, wide, 0, g3, y1, -1)
        features_out(l)
    sum_second(0)
    sum_third(1)
    for l in (2, 3):
        conv(l, wide, 0, g3, y1, -1)
        features_out(l)
    sum_fourth(1)
    sum_third(0)
    coarse_gradient(0)
    sum_fourth(0)
    sum_last(1)
    sum_last(0)
    for c in range(2):
        pltpu.make_async_copy(got_d.at[c], sums_ref.at[c], out_sem.at[c]).wait()


def last_kernel(sz, nb, *refs):
    it = iter(refs)
    take = lambda n: [next(it) for _ in range(n)]
    maps = take(5)
    sums, totals = take(2)
    (coarse,) = take(1)
    maps_out = take(5)
    kernels = take(4)
    unites = take(3)
    norm_gains, norm_shifts, unite_gains, unite_shifts = take(4)
    (sem,) = take(1)
    copies = [pltpu.make_async_copy(a, b, sem.at[i]) for i, (a, b) in enumerate(zip(maps, maps_out))]
    for copy in copies:
        copy.start()
    C = sz.chan
    for l in range(LEVELS):
        n = C[l] // nb
        for c in range(2):
            if l in sz.sum_levels:
                parts = []
                for i in range(-(-3 * C[l] // 128)):
                    at, rows = sz.spots[l, i]
                    parts.append(sums[c, at : at + rows, :].astype(F32))
                v = jnp.concatenate(parts, axis=1)
            for t in range(3):
                for u in range(3):
                    if l in sz.sum_levels:
                        kernels[l][c, t, u] = v[t * n : (t + 1) * n, u * C[l] : (u + 1) * C[l]]
                    else:
                        kernels[l][c, t, u] = coarse[c, t * n : (t + 1) * n, u * C[l] : (u + 1) * C[l]]
    n = sz.uchan // nb
    for j in range(3):
        width = C[j + 1]
        for i in range(-(-width // 128)):
            at, _ = sz.spots["u", j, i]
            m = min(128, width - 128 * i)
            unites[j][:, 128 * i : 128 * i + m] = sums[1, at : at + n, 0:m].astype(F32)
    for row, which in ((0, 2), (1, 1)):
        for k in range(sz.blocks):
            m = min(128, sz.total - 128 * k)
            for ref, base in ((norm_gains, 0), (norm_shifts, 8)):
                ref[row : row + 1, 128 * k : 128 * k + m] = totals[which, base + k : base + k + 1, 0:m]
    for ref, base in ((unite_gains, 0), (unite_shifts, 8)):
        v = jnp.concatenate([totals[0, base + k : base + k + 1, :] for k in range(sz.ublocks)], axis=1)
        for j in range(3):
            ref[j : j + 1, :] = v[:, j * sz.uchan : (j + 1) * sz.uchan]
    for copy in copies:
        copy.wait()


def body(*args):
    features = args[0:4]
    blocks = args[4:8]
    unites = args[8:11]
    norm_gains, norm_shifts, unite_gains, unite_shifts, output_grad, heights, widths, item_slot = args[11:]
    nb = lax.axis_size("batch")
    nk = lax.axis_size("rows")
    sz = Sizes(features, nb, nk)
    C, R, W, N, NP = sz.chan, sz.rows, sz.width, sz.own, sz.flat

    flat = [
        f.reshape(C[l] * R[l], W[l]) if W[l] >= 128 else f.transpose(0, 2, 3, 1).reshape(N[l], C[l])
        for l, f in enumerate(features)
    ]
    ograd = output_grad.reshape(C[0] * R[0], W[0])
    blocks = [b.reshape(2, 3, 3 * C[l], C[l]) for l, b in enumerate(blocks)]

    tables = [column_table(W[l], W[0]) for l in range(1, 4)]
    operands = [heights, widths, item_slot, *flat, ograd, *blocks, *unites]
    operands += [norm_gains, norm_shifts, unite_gains, unite_shifts]
    operands += [jnp.asarray(t, BF16) for t in tables] + [jnp.asarray(t.T, BF16) for t in tables]

    shape = jax.ShapeDtypeStruct
    map_shapes = [(C[0] * R[0], W[0])]
    map_shapes += [(C[l] * R[l], W[l]) if W[l] >= 128 else (N[l], C[l]) for l in range(4)]
    outs = [shape(m, BF16) for m in map_shapes]
    outs += [shape((2, nk, sz.part, 128), BF16)]
    outs += [shape((2, 3 * C[3] // nb if sz.gather else 3 * C[3], 3 * C[3]), F32)]
    outs += [shape((3, 16, 128), F32)]
    vm = pltpu.VMEM
    scratch = [
        vm((3, 3 * C[l], C[l]), BF16) for l in range(3 if sz.gather else 4)
    ]
    scratch += [vm((2, 3 * C[l], 3 * C[l]), BF16) for l in range(4)]
    scratch += [vm((max(1, W[0] // 128), C[0] * R[0], 128), F32)]
    for _ in range(3):
        scratch += [vm((3 * C[l], NP[l]), BF16) for l in range(4)]
    scratch += [vm((3 * C[l], NP[l]), BF16) for l in sz.stacked]
    scratch += [vm((2, C[3] // nb, 3 * C[3]), F32), pltpu.SemaphoreType.DMA((2,))]
    top = C[sz.sum_levels[-1]]
    scratch += [vm((3 * top, -(-3 * top // 128) * 128), F32)]
    scratch += [vm((sz.uchan, -(-C[l] // 128) * 128), F32) for l in range(1, 4)]
    for _ in range(4):
        scratch += [vm((C[l], NP[l]), F32) for l in range(4)]
    scratch += [vm((C[l], NP[l]), BF16) for l in range(1, 4)]
    scratch += [vm((sz.uchan, NP[l]), F32) for l in range(1, 4)]
    scratch += [vm((sz.uchan, (R[l] + 2) * W[0]), F32) for l in range(1, 4)]
    scratch += [
        vm((N_COLS, sz.blocks * 128, 128), F32),
        vm((N_UCOLS, sz.ublocks * 128, 128), F32),
        vm((sz.blocks * 128, 128), F32),
        vm((sz.blocks * 128, 128), F32),
        vm((sz.ublocks * 128, 128), F32),
        vm((sz.ublocks * 128, 128), F32),
        vm((nb, 8, 128), F32),
        vm((nk, 8, 128), F32),
        vm((nb, 8, 128), F32),
        vm((nk, 8, 128), F32),
    ]
    scratch += [vm((8, NP[l]), F32) for l in range(4)]
    mid = sum(max(2 * W[l], 128) for l in range(1, 4)) + W[0]
    scratch += [
        vm((6, nb, 16, 128), F32),
        vm((6, nk, 16, 128), F32),
        vm((2, sz.rim_total, 128), BF16),
        vm((4, 2, sz.rim_total, 128), BF16),
        vm((2, sz.uchan, mid), BF16),
        vm((2, sz.uchan, mid), BF16),
        pltpu.SemaphoreType.DMA((6, nb)),
        pltpu.SemaphoreType.DMA((6, nb)),
        pltpu.SemaphoreType.DMA((6, nk)),
        pltpu.SemaphoreType.DMA((6, nk)),
        pltpu.SemaphoreType.DMA((5, 2)),
        pltpu.SemaphoreType.DMA((5, 2)),
        pltpu.SemaphoreType.DMA((4, 2)),
        pltpu.SemaphoreType.DMA((2, 9)),
        vm((8, sz.blocks * 128), F32),
        vm((8, sz.ublocks * 128), F32),
        vm((2, sz.nc, sz.ny, sz.sum_rows, 128), BF16),
        vm((2, sz.ny, sz.sum_rows, 128), BF16),
        vm((2, sz.ny, sz.sum_rows, 128), BF16),
        vm((2, nk, sz.part, 128), BF16),
        vm((2, nk, sz.part, 128), BF16),
        pltpu.SemaphoreType.DMA((2,)),
    ]
    sems = pltpu.SemaphoreType.DMA
    scratch += [sems((2,)), sems((2,))] + [sems((2, sz.ny))] * 2 + [sems((2, nk))] * 4
    if sz.gather:
        half = C[3] // nb // 2
        most = max(sz.nz, sz.nx, sz.ny, sz.nc)
        scratch += [
            vm((2, sz.nc, sz.ny, sz.nx, sz.nz, C[3] // 2, 128), BF16),
            vm((2, nb, half, 128), BF16),
            vm((2, nk, nb, half, 128), BF16),
            vm((max(3, nb), 3 * C[3], max(C[3], 128 * sz.nz)), BF16),
            vm((nb, 3 * C[3] // nb, 128 * sz.nz), BF16),
            sems((2, 4, most)),
            sems((2, 4, most)),
            sems((2, nb)),
            sems((2, nb)),
            sems((2, nk)),
            sems((2, nk)),
        ]
    in_vmem = pl.BlockSpec(memory_space=pltpu.VMEM)
    in_smem = pl.BlockSpec(memory_space=pltpu.SMEM)
    got = pl.pallas_call(
        functools.partial(main_kernel, sz, nb, nk),
        out_shape=outs,
        in_specs=[in_smem] * 3
        + [in_vmem] * 5
        + [pl.BlockSpec(memory_space=pl.ANY)] * 4
        + [in_vmem] * (len(operands) - 12),
        out_specs=[in_vmem] * 5
        + [pl.BlockSpec(memory_space=pl.ANY)] * 2
        + [in_vmem],
        scratch_shapes=scratch,
        compiler_params=pltpu.CompilerParams(
            collective_id=0, has_side_effects=True, vmem_limit_bytes=60 * 2**20
        ),
    )(*operands)

    maps, sums, totals = got[0:5], got[5], got[-1]
    coarse = got[6]
    if not sz.gather:
        coarse = coarse.astype(BF16).reshape(2, 3, C[3], 3 * C[3])
        coarse = lax.psum(coarse, "rows")
        coarse = lax.psum_scatter(coarse, "batch", scatter_dimension=2, tiled=True)
        coarse = coarse.astype(F32).reshape(2, 3 * C[3] // nb, 3 * C[3])
    in_any = pl.BlockSpec(memory_space=pl.ANY)
    outs = [shape(m, BF16) for m in map_shapes]
    outs += [shape((2, 3, 3, C[l] // nb, C[l]), F32) for l in range(4)]
    outs += [shape((sz.uchan // nb, C[l]), F32) for l in range(1, 4)]
    outs += [shape((2, sz.total), F32)] * 2 + [shape((3, sz.uchan), F32)] * 2
    outs = pl.pallas_call(
        functools.partial(last_kernel, sz, nb),
        out_shape=outs,
        in_specs=[in_vmem] * 8,
        out_specs=[in_any] * 5 + [in_vmem] * (len(outs) - 5),
        scratch_shapes=[pltpu.SemaphoreType.DMA((5,))],
        compiler_params=pltpu.CompilerParams(vmem_limit_bytes=60 * 2**20),
    )(*maps, sums.reshape(2, sz.sum_rows, 128), totals, coarse)
    shaped = []
    for i, m in enumerate(outs[0:5]):
        l = max(i - 1, 0)
        if W[l] >= 128:
            shaped.append(m.reshape(1, C[l], R[l], W[l]))
        else:
            shaped.append(m.reshape(1, R[l], W[l], C[l]).transpose(0, 3, 1, 2))
    return (*shaped, *outs[5:])


def solution(mesh):
    image = P("batch", None, "rows", None)
    kernel = P(None, None, None, "batch", None)
    return jax.shard_map(
        body,
        mesh=mesh,
        in_specs=(image,) * 4 + (P(),) * 11 + (image,) + (P(),) * 3,
        out_specs=(image,) * 5 + (kernel,) * 4 + (P("batch", None),) * 3 + (P(),) * 4,
        check_vma=False,
    )
```

```python
import functools

import jax
import jax.numpy as jnp
import numpy as np
from jax import lax
from jax.experimental import pallas as pl
from jax.experimental.pallas import tpu as pltpu
from jax.sharding import PartitionSpec as P

EPSILON = 1e-05
LEVELS = 4
MESH = pl.DeviceIdType.MESH
F32 = jnp.float32
BF16 = jnp.bfloat16

MEAN, RSTD, GAIN1, SHIFT1, GAIN2, SHIFT2, LOCAL, N_COLS = range(8)
CA, CB, CC = MEAN, RSTD, LOCAL
UMEAN, URSTD, UGAIN, USHIFT, ULOCAL, UA, UB, UC, N_UCOLS = range(9)


class Sizes:
    def __init__(self, features, nb, nk):
        self.chan = [f.shape[1] for f in features]
        self.rows = [f.shape[2] for f in features]
        self.width = [f.shape[3] for f in features]
        self.own = [r * w for r, w in zip(self.rows, self.width)]
        self.flat = [(r + 2) * w for r, w in zip(self.rows, self.width)]
        self.off = [sum(self.chan[:l]) for l in range(LEVELS)]
        self.total = sum(self.chan)
        self.blocks = -(-self.total // 128)
        self.uchan = self.chan[0]
        self.utotal = 3 * self.uchan
        self.ublocks = -(-self.utotal // 128)
        self.rim_rows = [c * w // 128 for c, w in zip(self.chan, self.width)]
        self.rim_off = [sum(self.rim_rows[:l]) for l in range(LEVELS)]
        self.rim_total = sum(self.rim_rows)
        self.chunk = []
        for c, n, w in zip(self.chan, self.flat, self.width):
            lanes = max(x for x in range(128, 641, 128) if n % x == 0 and x % w == 0)
            rows = max(r for r in (16, 32, 48) if c % r == 0 and r * lanes <= 12288)
            self.chunk.append((rows, lanes))
        self.nc = 2 if nb % 2 == 0 else 1
        self.nx = 2 if nk % 2 == 0 else 1
        self.ny = nb // self.nc
        self.nz = nk // self.nx
        self.gather = nb * nk <= 32 and self.nx == 2 and self.nc == 2 and self.own[3] == 64
        self.pair = self.gather and self.chan[2] // nb % 16 == 0 and self.own[2] % 128 == 0
        self.sum_levels = [0, 1] if self.pair else [0, 1, 2]
        self.stacked = [l for l in range(3 if self.gather else 4) if self.width[l] < 128]
        self.stacked = [l for l in self.stacked if not (self.pair and l == 2)]
        self.spots = {}
        at = 0

        def place(key, values, width):
            nonlocal at
            rows = -(-values // 16) * 16
            for i in range(-(-width // 128)):
                self.spots[(*key, i)] = (at, rows)
                at += rows

        for l in self.sum_levels:
            place((l,), 3 * self.chan[l] // nb, 3 * self.chan[l])
        for j in range(3):
            place(("u", j), self.uchan // nb, self.chan[j + 1])
        self.batch_rows = at
        if self.pair:
            place((2,), 3 * self.chan[2] // nb, 3 * self.chan[2])
        self.part = -(-at // (nk * 16)) * 16
        self.sum_rows = self.part * nk


def blend(scale, rows):
    out = []
    for g in range(rows):
        num = 2 * g + 1 - scale
        low = num // (2 * scale)
        out.append((low + 1, (num - 2 * scale * low) / (2.0 * scale)))
    return out


def column_table(width, fine):
    scale = fine // width
    group = max(1, 128 // width)
    span = max(128, width)
    table = np.zeros((span, group * fine), np.float32)
    for r in range(group):
        for g in range(fine):
            num = 2 * g + 1 - scale
            low = 0 if num < 0 else num // (2 * scale)
            frac = 0.0 if num < 0 else (num - 2 * scale * low) / (2.0 * scale)
            high = min(low + 1, width - 1)
            table[r * width + low, r * fine + g] += 1.0 - frac
            table[r * width + high, r * fine + g] += frac
    return table


def sigmoid(v):
    return jax.nn.sigmoid(v)


def main_kernel(sz, nb, nk, *refs):
    it = iter(refs)
    take = lambda n: [next(it) for _ in range(n)]
    heights, widths, slots = take(3)
    feats = take(4)
    (ograd,) = take(1)
    blocks = take(4)
    unites = take(3)
    norm_gains, norm_shifts, unite_gains, unite_shifts = take(4)
    tables = take(3)
    tables_t = take(3)
    (united_ref,) = take(1)
    gfeat = take(4)
    (sums_ref,) = take(1)
    (coarse_ref,) = take(1)
    (totals_ref,) = take(1)
    raw = take(3 if sz.gather else 4)
    wide = take(4)
    (stage,) = take(1)
    x3 = take(4)
    a3 = take(4)
    g3 = take(4)
    t3 = dict(zip(sz.stacked, take(len(sz.stacked))))
    cstage, cstage_sem = take(2)
    (kg,) = take(1)
    gun = take(3)
    xf = take(4)
    y1 = take(4)
    y2 = take(4)
    p1 = take(4)
    br = take(3)
    uo = take(3)
    up = take(3)
    (cols, ucols, stat_a, stat_b, ustat_a, ustat_b, n_a, n_b, un_a, un_b) = take(10)
    masks = take(4)
    (rec_a, rec_b, rim_s, rim_r, mid_s, mid_r) = take(6)
    (sa_send, sa_recv, sb_send, sb_recv, rim_send, rim_recv) = take(6)
    raw_sem, wide_sem = take(2)
    prow, urow = take(2)
    part_a, got_a, got_b, part_s, got_x, got_z, got_d, out_sem = take(8)
    (ra_send, ra_recv, rb_send, rb_recv, rx_send, rx_recv, rz_send, rz_recv) = take(8)
    (dz_send, dz_recv, dx_send, dx_recv) = take(4)
    if sz.gather:
        xg, gs, gr, x3g, t3g = take(5)
        (xg_send, xg_recv, g1_send, g1_recv, g2_send, g2_recv, g3_send, g3_recv) = take(8)
    if sz.pair:
        xb, x3b, gsb, gb, t3b = take(5)
        (xb_send, xb_recv, gb_send, gb_recv) = take(4)

    C, R, W, N, NP, OFF = sz.chan, sz.rows, sz.width, sz.own, sz.flat, sz.off
    me_b = lax.axis_index("batch")
    me_k = lax.axis_index("rows")

    def peer_b(j):
        return lax.rem(me_b + j, nb)

    def peer_k(j):
        return lax.rem(me_k + j, nk)

    def raw_copy(l, which):
        if l == 3 and sz.gather:
            dst = x3g.at[0:3, :, 0 : C[3]]
        else:
            dst = raw[l]
        return pltpu.make_async_copy(blocks[l].at[which], dst, raw_sem.at[l, which])

    def wide_copies(which):
        c = C[3]
        return [
            pltpu.make_async_copy(
                blocks[3].at[which, t, u * c : (u + 1) * c, :],
                wide[3].at[which, t * c : (t + 1) * c, u * c : (u + 1) * c],
                wide_sem.at[which, 3 * t + u],
            )
            for t in range(3)
            for u in range(3)
        ]

    for l in range(3):
        raw_copy(l, 0).start()
    for which in range(2):
        for copy in wide_copies(which):
            copy.start()
    raw_copy(3, 0).start()

    def widen(which):
        for copy in wide_copies(which):
            copy.wait()
        for l in range(3):
            raw_copy(l, which).wait()
            c = C[l]
            for t in range(3):
                wide[l][which, t * c : (t + 1) * c, :] = jnp.concatenate(
                    [raw[l][t, u * c : (u + 1) * c, :] for u in range(3)], axis=1
                )

    def turn(which):
        raw_copy(3, which).wait()
        for l in range(LEVELS):
            for t in range(3):
                if l == 3 and sz.gather:
                    v = x3g[t, :, 0 : C[3]]
                else:
                    v = raw[l][t]
                wide[l][which, t * C[l] : (t + 1) * C[l], :] = v.T
        if which == 0:
            for l in range(LEVELS):
                raw_copy(l, 1).start()

    barrier = pltpu.get_barrier_semaphore()
    for j in range(1, nb):
        pl.semaphore_signal(barrier, inc=1, device_id=(peer_b(j), me_k), device_id_type=MESH)
    for j in range(1, nk):
        pl.semaphore_signal(barrier, inc=1, device_id=(me_b, peer_k(j)), device_id_type=MESH)

    my_h = jnp.int32(0)
    my_w = jnp.int32(0)
    slot_h, slot_w = [], []
    for b in range(nb):
        h = jnp.int32(0)
        w = jnp.int32(0)
        for i in range(nb):
            hit = (slots[i] == b).astype(jnp.int32)
            h = h + hit * heights[i]
            w = w + hit * widths[i]
        slot_h.append(h)
        slot_w.append(w)
        mine = (me_b == b).astype(jnp.int32)
        my_h = my_h + mine * h
        my_w = my_w + mine * w

    count = []
    for l in range(LEVELS):
        c = jnp.int32(0)
        for b in range(nb):
            c = c + lax.shift_right_logical(slot_h[b], l) * lax.shift_right_logical(slot_w[b], l)
        count.append(c.astype(F32))
    inv_local = []
    for l in range(LEVELS):
        inside = jnp.clip(lax.shift_right_logical(my_h, l) - me_k * R[l], 0, R[l])
        own = inside * lax.shift_right_logical(my_w, l)
        inv_local.append(1.0 / jnp.maximum(own, 1).astype(F32))
        lane = lax.broadcasted_iota(jnp.int32, (1, NP[l]), 1)
        log_w = W[l].bit_length() - 1
        row = me_k * R[l] + lax.shift_right_logical(lane, log_w) - 1
        col = lane & (W[l] - 1)
        valid = (row >= 0) & (row < lax.shift_right_logical(my_h, l))
        valid = valid & (col < lax.shift_right_logical(my_w, l))
        masks[l][0:1, :] = jnp.where(valid, 1.0, 0.0)
        masks[l][1:2, :] = jnp.where(valid & (lane >= W[l]) & (lane < W[l] + N[l]), 1.0, 0.0)

    place = lax.broadcasted_iota(jnp.int32, (8, 128), 0) * 128 + lax.broadcasted_iota(
        jnp.int32, (8, 128), 1
    )

    def by_level(values):
        out = jnp.full((8, 128), values[3])
        for l in (2, 1, 0):
            out = jnp.where(place < OFF[l + 1], jnp.full((8, 128), values[l]), out)
        return out

    def by_unite(values):
        out = jnp.full((8, 128), values[2])
        for j in (1, 0):
            out = jnp.where(place < (j + 1) * sz.uchan, jnp.full((8, 128), values[j]), out)
        return out

    inv_count = 1.0 / by_level(count)
    inv_ucount = 1.0 / by_unite(count[1:])
    for chooser, levels, na_ref, nb_ref in (
        (by_level, range(4), n_a, n_b),
        (by_unite, range(1, 4), un_a, un_b),
    ):
        span = chooser([jnp.int32(R[l]) for l in levels])
        hv = [chooser([lax.shift_right_logical(h, l) for l in levels]) for h in slot_h]
        wv = [chooser([lax.shift_right_logical(w, l) for l in levels]) for w in slot_w]
        for b in range(nb):
            na_ref[b] = (jnp.clip(hv[b] - me_k * span, 0, span) * wv[b]).astype(F32)
        for k in range(nk):
            n = jnp.zeros((8, 128), jnp.int32)
            for b in range(nb):
                n = n + jnp.clip(hv[b] - k * span, 0, span) * wv[b]
            nb_ref[k] = n.astype(F32)

    def tile(v, lanes):
        return v if lanes == 128 else jnp.concatenate([v] * (lanes // 128), axis=1)

    def col(slot, l, r0, rc, lanes):
        return tile(cols[slot, pl.ds(pl.multiple_of(OFF[l] + r0, 16), rc), :], lanes)

    def ucol(slot, j, lanes):
        return tile(ucols[slot, j * sz.uchan : (j + 1) * sz.uchan, :], lanes)

    def to_columns(packed, ref, slot_list, spans):
        full = jnp.concatenate(packed + [jnp.zeros((128 - 8 * len(packed), 128), F32)], axis=0)
        standing = full.T
        for i, slot in enumerate(slot_list):
            for lo, hi in spans:
                for k in range(lo // 128, -(-hi // 128)):
                    a, b = max(lo, 128 * k), min(hi, 128 * k + 128)
                    v = standing[a - 128 * k : b - 128 * k, 8 * i + k : 8 * i + k + 1]
                    ref[slot, a:b, :] = jnp.broadcast_to(v, (b - a, 128))

    FINE, COARSE = (0,), (1, 2, 3)
    spans_of = {FINE: [(0, C[0])], COARSE: [(C[0], sz.total)]}
    u_spans = [(0, sz.utotal)]

    prow[...] = jnp.zeros_like(prow)
    urow[...] = jnp.zeros_like(urow)
    for i in range(2):
        prow[2 * i : 2 * i + 1, 0 : sz.total] = norm_gains[i : i + 1, :]
        prow[2 * i + 1 : 2 * i + 2, 0 : sz.total] = norm_shifts[i : i + 1, :]
    for j in range(3):
        at = slice(j * sz.uchan, (j + 1) * sz.uchan)
        urow[0:1, at] = unite_gains[j : j + 1, :]
        urow[1:2, at] = unite_shifts[j : j + 1, :]
    standing = prow[...].T
    for i, slot in enumerate((GAIN1, SHIFT1, GAIN2, SHIFT2)):
        cols[slot] = jnp.broadcast_to(standing[:, i : i + 1], (sz.blocks * 128, 128))
    standing = urow[...].T
    for i, slot in enumerate((UGAIN, USHIFT)):
        ucols[slot] = jnp.broadcast_to(standing[:, i : i + 1], (sz.ublocks * 128, 128))

    def packed(ref, i, blocks):
        rows = [ref[i : i + 1, 128 * k : 128 * k + 128] for k in range(blocks)]
        return jnp.concatenate(rows + [jnp.zeros((8 - blocks, 128), F32)], axis=0)

    gain1_p, gain2_p = packed(prow, 0, sz.blocks), packed(prow, 2, sz.blocks)
    ugain_p = packed(urow, 0, sz.ublocks)
    stat_a[...] = jnp.zeros_like(stat_a)
    stat_b[...] = jnp.zeros_like(stat_b)
    ustat_a[...] = jnp.zeros_like(ustat_a)
    ustat_b[...] = jnp.zeros_like(ustat_b)

    def fold(v):
        out = v[:, 0:128]
        for i in range(1, v.shape[1] // 128):
            out = out + v[:, 128 * i : 128 * i + 128]
        return out

    lane128 = lax.broadcasted_iota(jnp.int32, (1, 128), 1)

    def record(a_ref, b_ref, spans):
        out = jnp.zeros((128, 128), F32)
        for base, ref in ((0, a_ref), (8, b_ref)):
            for lo, hi in spans:
                for k in range(lo // 128, -(-hi // 128)):
                    s = jnp.sum(ref[128 * k : 128 * k + 128, :], axis=1, keepdims=True)
                    out = jnp.where(lane128 == base + k, s, out)
        return out.T[0:16]

    def record_copies(e, which, sending):
        if which == 0:
            ref, send, recv, n, me = rec_a, sa_send, sa_recv, nb, me_b
        else:
            ref, send, recv, n, me = rec_b, sb_send, sb_recv, nk, me_k
        out = []
        for j in range(1, n):
            other = lax.rem(me + j, n)
            slot = me if sending else other
            out.append(
                pltpu.make_async_remote_copy(
                    src_ref=ref.at[e, me],
                    dst_ref=ref.at[e, slot],
                    send_sem=send.at[e, other],
                    recv_sem=recv.at[e, slot],
                    device_id=(other, me_k) if which == 0 else (me_b, other),
                    device_id_type=MESH,
                )
            )
        return out

    def record_send(e, which, rec):
        if which == 0:
            rec_a[e, me_b] = rec
        else:
            rec_b[e, me_k] = rec
        for copy in record_copies(e, which, True):
            copy.start()

    def record_total(e, which, sizes):
        for copy in record_copies(e, which, False):
            copy.wait_recv()
        for copy in record_copies(e, which, True):
            copy.wait_send()
        ref, n = ((rec_a, nb), (rec_b, nk))[which]
        if sizes is None:
            out = ref[e, 0]
            for i in range(1, n):
                out = out + ref[e, i]
            return out
        total = jnp.zeros((8, 128), F32)
        size = jnp.zeros((8, 128), F32)
        for i in range(n):
            total = total + ref[e, i, 0:8]
            size = size + sizes[which][i]
        mean = total / jnp.maximum(size, 1.0)
        spread_sum = jnp.zeros((8, 128), F32)
        for i in range(n):
            delta = ref[e, i, 0:8] / jnp.maximum(sizes[which][i], 1.0) - mean
            spread_sum = spread_sum + (ref[e, i, 8:16] + sizes[which][i] * delta * delta)
        return jnp.concatenate([total, spread_sum], axis=0)

    def ex_start(e, rec):
        record_send(e, 0, rec)

    def ex_mid(e, sizes=None):
        record_send(e, 1, record_total(e, 0, sizes))

    def ex_end(e, sizes=None):
        return record_total(e, 1, sizes)

    def rim_copies(slot, src, dst):
        up = pltpu.make_async_remote_copy(
            src_ref=src(0),
            dst_ref=dst(1),
            send_sem=rim_send.at[slot, 0],
            recv_sem=rim_recv.at[slot, 1],
            device_id=(me_b, lax.rem(me_k + nk - 1, nk)),
            device_id_type=MESH,
        )
        down = pltpu.make_async_remote_copy(
            src_ref=src(1),
            dst_ref=dst(0),
            send_sem=rim_send.at[slot, 1],
            recv_sem=rim_recv.at[slot, 0],
            device_id=(me_b, lax.rem(me_k + 1, nk)),
            device_id_type=MESH,
        )
        return up, down

    def rims_start(slot, src, dst):
        up, down = rim_copies(slot, src, dst)

        @pl.when(me_k > 0)
        def _():
            up.start()

        @pl.when(me_k < nk - 1)
        def _():
            down.start()

    def rims_wait(slot, src, dst):
        up, down = rim_copies(slot, src, dst)

        @pl.when(me_k > 0)
        def _():
            down.wait_recv()
            up.wait_send()

        @pl.when(me_k < nk - 1)
        def _():
            up.wait_recv()
            down.wait_send()

    def pack_row(ref, l, lane0):
        if W[l] >= 128:
            return jnp.concatenate(
                [ref[:, lane0 + 128 * i : lane0 + 128 * i + 128] for i in range(W[l] // 128)], axis=0
            )
        group = 128 // W[l]
        rows = C[l] // group
        base, shift = lane0 // 128 * 128, lane0 % 128
        out = None
        for g in range(group):
            v = ref[g * rows : (g + 1) * rows, base : base + 128]
            turn = (g * W[l] - shift) % 128
            v = pltpu.roll(v, turn, 1) if turn else v
            out = v if out is None else jnp.where(lane128 >= g * W[l], v, out)
        return out

    def unpack_row(ref, l, lane0, q):
        if W[l] >= 128:
            for i in range(W[l] // 128):
                ref[:, lane0 + 128 * i : lane0 + 128 * i + 128] = q[i * C[l] : (i + 1) * C[l]]
            return
        group = 128 // W[l]
        rows = C[l] // group
        base, shift = lane0 // 128 * 128, lane0 % 128
        here = (lane128 >= shift) & (lane128 < shift + W[l])
        for g in range(group):
            turn = (shift - g * W[l]) % 128
            v = pltpu.roll(q, turn, 1) if turn else q
            old = ref[g * rows : (g + 1) * rows, base : base + 128]
            ref[g * rows : (g + 1) * rows, base : base + 128] = jnp.where(here, v, old)

    def rim_span(group):
        first, last = group[0], group[-1]
        return slice(sz.rim_off[first], sz.rim_off[last] + sz.rim_rows[last])

    def rims_of(slot, group):
        at = rim_span(group)
        number = 2 * slot + (0 if group == FINE else 1)
        return number, lambda i: rim_s.at[i, at, :], lambda i: rim_r.at[slot, i, at, :]

    def send_rims(slot, group, arrays):
        for l in group:
            at = rim_span((l,))
            rim_s[0, at, :] = pack_row(arrays[l], l, W[l]).astype(BF16)
            rim_s[1, at, :] = pack_row(arrays[l], l, N[l]).astype(BF16)
        rims_start(*rims_of(slot, group))

    def take_rims(slot, group, arrays):
        rims_wait(*rims_of(slot, group))
        for l in group:
            at = rim_span((l,))
            unpack_row(arrays[l], l, 0, rim_r[slot, 0, at, :].astype(F32))
            unpack_row(arrays[l], l, W[l] + N[l], rim_r[slot, 1, at, :].astype(F32))

    def each(l, body):
        rc, lanes = sz.chunk[l]

        def step(i, _):
            body(pl.multiple_of(i * rc, rc), rc, lanes)
            return 0

        lax.fori_loop(0, C[l] // rc, step, 0)

    def lane_chunks(l, lanes):
        return [(i, i + lanes) for i in range(0, NP[l], lanes)]

    def stack_columns(ref, l, r0, rc, a, b, v, back=False):
        lanes = b - a
        at = lax.broadcasted_iota(jnp.int32, (1, lanes), 1) & (W[l] - 1)
        left = jnp.where(at == 0, 0.0, pltpu.roll(v, 1, 1))
        right = jnp.where(at == W[l] - 1, 0.0, pltpu.roll(v, lanes - 1, 1))
        for u, part in enumerate((right, v, left) if back else (left, v, right)):
            ref[pl.ds(pl.multiple_of(u * C[l] + r0, 16), rc), a:b] = part.astype(BF16)

    def stack_rows(ref, l, r0, rc, v):
        for t in range(3):
            turn = ((t - 1) * W[l]) % NP[l]
            part = pltpu.roll(v, turn, 1) if turn else v
            ref[pl.ds(pl.multiple_of(t * C[l] + r0, 16), rc), :] = part.astype(BF16)

    def conv(l, w, which, src, dst, sign=1):
        c = C[l]
        if W[l] % 128 == 0:
            span = min(1024, N[l])

            def step(i, _):
                acc = None
                for t in range(3):
                    at = pl.ds(pl.multiple_of(i * span + (1 + sign * (t - 1)) * W[l], 128), span)
                    part = jnp.dot(
                        w[l][which, t * c : (t + 1) * c, :], src[l][:, at], preferred_element_type=F32
                    )
                    acc = part if acc is None else acc + part
                dst[l][:, pl.ds(pl.multiple_of(i * span + W[l], 128), span)] = acc
                return 0

            lax.fori_loop(0, N[l] // span, step, 0)
        else:
            rows = 96

            def step(i, _):
                acc = None
                for t in range(3):
                    at = pl.ds(pl.multiple_of(t * c + i * rows, 16), rows)
                    part = jnp.dot(w[l][which, at, :], src[l][...], preferred_element_type=F32)
                    turn = (sign * (1 - t) * W[l]) % NP[l]
                    part = pltpu.roll(part, turn, 1) if turn else part
                    acc = part if acc is None else acc + part
                dst[l][pl.ds(pl.multiple_of(i * rows, 16), rows), :] = acc
                return 0

            lax.fori_loop(0, c // rows, step, 0)

    def kernel_grad(l, src):
        c = C[l]
        if W[l] % 128 == 0:
            for t in range(3):
                kg[t * c : (t + 1) * c, 0 : 3 * c] = lax.dot_general(
                    g3[l][c : 2 * c, W[l] : W[l] + N[l]],
                    src[l][:, t * W[l] : t * W[l] + N[l]],
                    (((1,), (1,)), ((), ())),
                    preferred_element_type=F32,
                )
            return
        span = 96

        def step(i, _):
            at = pl.ds(pl.multiple_of(i * span, 16), span)
            kg[at, 0 : 3 * c] = lax.dot_general(
                t3[l][at, :], src[l][...], (((1,), (1,)), ((), ())), preferred_element_type=F32
            )
            return 0

        lax.fori_loop(0, 3 * c // span, step, 0)

    nc, ny, nx, nz = sz.nc, sz.ny, sz.nx, sz.nz
    my_core, my_y = lax.rem(me_b, nc), lax.div(me_b, nc)
    my_x, my_z = lax.rem(me_k, nx), lax.div(me_k, nx)

    def others(n, me):
        return [lax.rem(me + j, n) for j in range(1, n)]

    def remote(src, dst, send, recv, target):
        return pltpu.make_async_remote_copy(
            src_ref=src, dst_ref=dst, send_sem=send, recv_sem=recv, device_id=target, device_id_type=MESH
        )

    def sum_pack(c, l):
        n = C[l] // nb
        for q in range(nb):
            dst = part_a.at[c, q % nc, q // nc]
            for i in range(-(-3 * C[l] // 128)):
                at, rows = sz.spots[l, i]
                lanes = slice(128 * i, 128 * i + 128)
                parts = [kg[t * C[l] + q * n : t * C[l] + q * n + n, lanes] for t in range(3)]
                if rows > 3 * n:
                    parts.append(jnp.zeros((rows - 3 * n, 128), F32))
                dst[at : at + rows, :] = jnp.concatenate(parts, axis=0).astype(BF16)

    def sum_pack_unites():
        n = sz.uchan // nb
        for q in range(nb):
            dst = part_a.at[1, q % nc, q // nc]
            for j in range(3):
                for i in range(-(-C[j + 1] // 128)):
                    at, rows = sz.spots["u", j, i]
                    v = gun[j][q * n : q * n + n, 128 * i : 128 * i + 128]
                    if rows > n:
                        v = jnp.concatenate([v, jnp.zeros((rows - n, 128), F32)], axis=0)
                    dst[at : at + rows, :] = v.astype(BF16)

    def core_copies(c):
        out = []
        for other in others(nc, my_core):
            target = (my_y * nc + other, me_k)
            out.append(remote(part_a.at[c, other], got_a.at[c], ra_send.at[c], ra_recv.at[c], target))
        return out

    def y_copies(c, sending):
        out = []
        for other in others(ny, my_y):
            target = (other * nc + my_core, me_k)
            if sending:
                src, dst, sem = part_a.at[c, my_core, other], got_b.at[c, my_y], rb_recv.at[c, my_y]
            else:
                src, dst, sem = part_a.at[c, my_core, other], got_b.at[c, other], rb_recv.at[c, other]
            out.append(remote(src, dst, rb_send.at[c, other], sem, target))
        return out

    def part_at(x, z, n=1):
        return pl.ds(pl.multiple_of((x * nz + z) * sz.part, 16), n * sz.part)

    def x_copies(c):
        out = []
        for other in others(nx, my_x):
            src = part_s.at[c, part_at(other, 0, nz), :]
            target = (me_b, my_z * nx + other)
            out.append(remote(src, got_x.at[c], rx_send.at[c], rx_recv.at[c], target))
        return out

    def z_copies(c, sending):
        out = []
        for other in others(nz, my_z):
            slot = my_z if sending else other
            src = part_s.at[c, part_at(my_x, other), :]
            target = (me_b, other * nx + my_x)
            out.append(remote(src, got_z.at[c, slot], rz_send.at[c, other], rz_recv.at[c, slot], target))
        return out

    def back_z_copies(c, sending):
        out = []
        for other in others(nz, my_z):
            slot = my_z if sending else other
            src, dst = got_d.at[c, part_at(my_x, my_z), :], got_d.at[c, part_at(my_x, slot), :]
            target = (me_b, other * nx + my_x)
            out.append(remote(src, dst, dz_send.at[c, other], dz_recv.at[c, slot], target))
        return out

    def back_x_copies(c, sending):
        out = []
        for other in others(nx, my_x):
            slot = my_x if sending else other
            src, dst = got_d.at[c, part_at(my_x, 0, nz), :], got_d.at[c, part_at(slot, 0, nz), :]
            target = (me_b, my_z * nx + other)
            out.append(remote(src, dst, dx_send.at[c], dx_recv.at[c], target))
        return out

    def finish(pair):
        sent, received = pair
        for copy in received:
            copy.wait_recv()
        for copy in sent:
            copy.wait_send()

    def sum_level(c, l, src):
        kernel_grad(l, src)
        sum_pack(c, l)

    def sum_first(c):
        for copy in core_copies(c):
            copy.start()

    def sum_second(c):
        copies = core_copies(c)
        finish((copies, copies))
        for y in range(ny):
            v = part_a[c, my_core, y].astype(F32)
            if nc > 1:
                v = v + got_a[c, y].astype(F32)
            part_a[c, my_core, y] = v.astype(BF16)
        for copy in y_copies(c, True):
            copy.start()

    def sum_third(c):
        finish((y_copies(c, True), y_copies(c, False)))
        got_b[c, my_y] = part_a[c, my_core, my_y]
        v = got_b[c, 0].astype(F32)
        for y in range(1, ny):
            v = v + got_b[c, y].astype(F32)
        part_s[c, 0 : sz.batch_rows, :] = v.astype(BF16)
        for copy in x_copies(c):
            copy.start()

    def sum_fourth(c):
        copies = x_copies(c)
        finish((copies, copies))
        mine = part_at(my_x, 0, nz)
        if nx > 1:
            v = part_s[c, mine, :].astype(F32) + got_x[c].astype(F32)
            part_s[c, mine, :] = v.astype(BF16)
        for copy in z_copies(c, True):
            copy.start()

    def sum_fifth(c):
        finish((z_copies(c, True), z_copies(c, False)))
        got_z[c, my_z] = part_s[c, part_at(my_x, my_z), :]
        v = got_z[c, 0].astype(F32)
        for z in range(1, nz):
            v = v + got_z[c, z].astype(F32)
        got_d[c, part_at(my_x, my_z), :] = v.astype(BF16)
        for copy in back_z_copies(c, True):
            copy.start()

    def sum_sixth(c):
        finish((back_z_copies(c, True), back_z_copies(c, False)))
        for copy in back_x_copies(c, True):
            copy.start()

    def sum_last(c):
        finish((back_x_copies(c, True), back_x_copies(c, False)))
        pltpu.make_async_copy(got_d.at[c], sums_ref.at[c], out_sem.at[c]).start()

    c2 = C[2] // nb

    def pair_copies(c, step, sending):
        if not sz.pair:
            return []
        n, me = ((ny, my_y), (nc, my_core))[step]
        out = []
        for other in others(n, me):
            slot = me if sending else other
            if step == 0:
                ref, target = xb.at[c, my_core, slot], (other * nc + my_core, me_k)
            else:
                ref, target = xb.at[c, slot], (my_y * nc + other, me_k)
            out.append(remote(ref, ref, xb_send.at[c, step, other], xb_recv.at[c, step, slot], target))
        return out

    def pair_begin(c, ref):
        if sz.pair:
            xb[c, my_core, my_y] = ref[2][C[2] : 2 * C[2], :]
            for copy in pair_copies(c, 0, True):
                copy.start()

    def pair_next(c):
        finish((pair_copies(c, 0, True), pair_copies(c, 0, False)))
        for copy in pair_copies(c, 1, True):
            copy.start()

    def pair_inputs(c):
        if not sz.pair:
            return
        finish((pair_copies(c, 1, True), pair_copies(c, 1, False)))
        at = lax.broadcasted_iota(jnp.int32, (1, NP[2]), 1) & (W[2] - 1)

        def item(b, _):
            def group(q, _):
                rows = pl.ds(pl.multiple_of(q * c2, 16), c2)
                v = xb[c, lax.rem(b, nc), lax.div(b, nc), rows, :].astype(F32)
                left = jnp.where(at == 0, 0.0, pltpu.roll(v, 1, 1))
                right = jnp.where(at == W[2] - 1, 0.0, pltpu.roll(v, NP[2] - 1, 1))
                for u, part in enumerate((left, v, right)):
                    x3b[b, pl.ds(pl.multiple_of(u * C[2] + q * c2, 16), c2), :] = part.astype(BF16)
                return 0

            lax.fori_loop(0, nb, group, 0)
            return 0

        lax.fori_loop(0, nb, item, 0)

    def pair_grad_copies(c, sending):
        out = []
        for other in others(nb, me_b):
            slot = me_b if sending else other
            out.append(
                remote(gsb.at[c, other], gb.at[c, slot], gb_send.at[c, other], gb_recv.at[c, slot], (other, me_k))
            )
        return out

    def pair_grad_begin(c):
        if sz.pair:
            for q in range(nb):
                v = g3[2][C[2] + q * c2 : C[2] + (q + 1) * c2, :].astype(F32)
                gsb[c, q] = pltpu.roll(v, NP[2] - W[2], 1)[:, 0 : N[2]].astype(BF16)
            for copy in pair_grad_copies(c, True):
                copy.start()

    def pair_gradient(c):
        if not sz.pair:
            return
        finish((pair_grad_copies(c, True), pair_grad_copies(c, False)))
        gb[c, me_b] = gsb[c, me_b]

        def item(b, _):
            v = jnp.concatenate([gb[c, b].astype(F32), jnp.zeros((c2, NP[2] - N[2]), F32)], axis=1)
            for t in range(3):
                part = pltpu.roll(v, t * W[2], 1) if t else v
                t3b[b, t * c2 : (t + 1) * c2, :] = part.astype(BF16)
            return 0

        lax.fori_loop(0, nb, item, 0)
        acc = None
        for b in range(nb):
            part = lax.dot_general(t3b[b], x3b[b], (((1,), (1,)), ((), ())), preferred_element_type=F32)
            acc = part if acc is None else acc + part
        for i in range(-(-3 * C[2] // 128)):
            at, rows = sz.spots[2, i]
            m = min(128, 3 * C[2] - 128 * i)
            part_s[c, at : at + rows, 0:m] = acc[:, 128 * i : 128 * i + m].astype(BF16)

    c3 = C[3] // nb
    half = c3 // 2

    def pack_pixels(ref):
        parts = []
        for q in range(nb):
            at = C[3] + q * c3
            low = pltpu.roll(ref[at : at + half, :].astype(F32), 128 - W[3], 1)
            high = pltpu.roll(ref[at + half : at + c3, :].astype(F32), 64 - W[3], 1)
            parts.append(jnp.where(lane128 < 64, low, high))
        return jnp.concatenate(parts, axis=0).astype(BF16)

    def unpack_pixels(first, second):
        first, second = first.astype(F32), second.astype(F32)
        low = jnp.where(lane128 < 64, first, pltpu.roll(second, 64, 1))
        high = jnp.where(lane128 < 64, pltpu.roll(first, 64, 1), second)
        return low, high

    def gather_copies(c, step, sending):
        if not sz.gather:
            return []
        n, me = ((nz, my_z), (nx, my_x), (ny, my_y), (nc, my_core))[step]
        out = []
        for other in others(n, me):
            slot = me if sending else other
            if step == 0:
                ref, target = xg.at[c, my_core, my_y, my_x, slot], (me_b, other * nx + my_x)
            elif step == 1:
                ref, target = xg.at[c, my_core, my_y, slot], (me_b, my_z * nx + other)
            elif step == 2:
                ref, target = xg.at[c, my_core, slot], (other * nc + my_core, me_k)
            else:
                ref, target = xg.at[c, slot], (my_y * nc + other, me_k)
            out.append(remote(ref, ref, xg_send.at[c, step, other], xg_recv.at[c, step, slot], target))
        return out

    def gather_start(c, step):
        for copy in gather_copies(c, step, True):
            copy.start()

    def gather_wait(c, step):
        finish((gather_copies(c, step, True), gather_copies(c, step, False)))

    def gather_begin(c, ref):
        if sz.gather:
            xg[c, my_core, my_y, my_x, my_z] = pack_pixels(ref[3])
            gather_start(c, 0)

    def gather_next(c, step):
        gather_wait(c, step)
        gather_start(c, step + 1)

    def grad_copies(c, step, sending):
        out = []
        if step == 0:
            for other in others(nb, me_b):
                slot = me_b if sending else other
                src = gs.at[c, other]
                out.append(
                    remote(src, gr.at[c, my_x, my_z, slot], g1_send.at[c, other], g1_recv.at[c, slot], (other, me_k))
                )
        elif step == 1:
            for other in others(nz, my_z):
                slot = my_z if sending else other
                src, dst = gr.at[c, my_x, my_z], gr.at[c, my_x, slot]
                target = (me_b, other * nx + my_x)
                out.append(remote(src, dst, g2_send.at[c, other], g2_recv.at[c, slot], target))
        else:
            for other in others(nx, my_x):
                slot = my_x if sending else other
                src, dst = gr.at[c, my_x], gr.at[c, slot]
                target = (me_b, my_z * nx + other)
                out.append(remote(src, dst, g3_send.at[c], g3_recv.at[c], target))
        return out

    def grad_begin(c):
        if sz.gather:
            v = pack_pixels(g3[3])
            for q in range(nb):
                gs[c, q] = v[q * half : (q + 1) * half]
            for copy in grad_copies(c, 0, True):
                copy.start()

    def grad_next(c):
        if sz.gather:
            finish((grad_copies(c, 0, True), grad_copies(c, 0, False)))
            gr[c, my_x, my_z, me_b] = gs[c, me_b]
            for copy in grad_copies(c, 1, True):
                copy.start()

    def grad_third(c):
        if sz.gather:
            finish((grad_copies(c, 1, True), grad_copies(c, 1, False)))
            for copy in grad_copies(c, 2, True):
                copy.start()

    image = nz * 128

    def coarse_inputs(c):
        if not sz.gather:
            return
        gather_wait(c, 3)
        at = lane128 & (W[3] - 1)

        def item(b, _):
            def group(q, _):
                for z in range(nz):
                    rows = pl.ds(pl.multiple_of(q * half, 16), half)
                    core, y = lax.rem(b, nc), lax.div(b, nc)
                    pair = unpack_pixels(xg[c, core, y, 0, z, rows, :], xg[c, core, y, 1, z, rows, :])
                    for i, v in enumerate(pair):
                        left = jnp.where(at == 0, 0.0, pltpu.roll(v, 1, 1))
                        right = jnp.where(at == W[3] - 1, 0.0, pltpu.roll(v, 127, 1))
                        for u, part in enumerate((left, v, right)):
                            spot = pl.ds(pl.multiple_of(u * C[3] + q * c3 + i * half, 16), half)
                            x3g[b, spot, 128 * z : 128 * z + 128] = part.astype(BF16)
                return 0

            lax.fori_loop(0, nb, group, 0)
            return 0

        lax.fori_loop(0, nb, item, 0)

    def coarse_copy(c, i):
        at = pl.ds(i * c3 if isinstance(i, int) else pl.multiple_of(i * c3, 16), c3)
        slot = i % 2 if isinstance(i, int) else lax.rem(i, 2)
        return pltpu.make_async_copy(cstage.at[slot], coarse_ref.at[c, at, :], cstage_sem.at[slot])

    def coarse_local(c, src):
        def step(i, _):
            at = pl.ds(pl.multiple_of(i * c3, 16), c3)
            cstage[0] = lax.dot_general(
                t3[3][at, :], src[3][...], (((1,), (1,)), ((), ())), preferred_element_type=F32
            )
            copy = pltpu.make_async_copy(cstage.at[0], coarse_ref.at[c, at, :], cstage_sem.at[0])
            copy.start()
            copy.wait()
            return 0

        lax.fori_loop(0, 3 * nb, step, 0)

    def coarse_gradient(c):
        if not sz.gather:
            coarse_local(c, a3 if c else x3)
            return
        finish((grad_copies(c, 2, True), grad_copies(c, 2, False)))
        lane = lax.broadcasted_iota(jnp.int32, (1, image), 1)

        def item(b, _):
            low, high = [], []
            for z in range(nz):
                first, second = unpack_pixels(gr[c, 0, z, b], gr[c, 1, z, b])
                low.append(first)
                high.append(second)
            for i, parts in enumerate((low, high)):
                v = jnp.concatenate(parts, axis=1) if nz > 1 else parts[0]
                up_ = jnp.where(lane >= image - W[3], 0.0, pltpu.roll(v, image - W[3], 1))
                down = jnp.where(lane < W[3], 0.0, pltpu.roll(v, W[3], 1))
                for t, part in enumerate((up_, v, down)):
                    spot = t * c3 + i * half
                    t3g[b, spot : spot + half, :] = part.astype(BF16)
            return 0

        lax.fori_loop(0, nb, item, 0)

        def step(i, _):
            at = pl.ds(pl.multiple_of(i * c3, 16), c3)
            acc = None
            for b in range(nb):
                part = lax.dot_general(
                    t3g[b, at, :], x3g[b, :, 0:image], (((1,), (1,)), ((), ())), preferred_element_type=F32
                )
                acc = part if acc is None else acc + part
            slot = lax.rem(i, 2)

            @pl.when(i >= 2)
            def _():
                coarse_copy(c, i - 2).wait()

            cstage[slot] = acc
            coarse_copy(c, i).start()
            return 0

        lax.fori_loop(0, 3, step, 0)
        coarse_copy(c, 1).wait()
        coarse_copy(c, 2).wait()

    def moments(arrays, group):
        for l in group:

            def body(r0, rc, lanes, l=l):
                acc = jnp.zeros((rc, 128), F32)
                for a, b in lane_chunks(l, lanes):
                    m = masks[l][1:2, a:b] > 0
                    acc = acc + fold(jnp.where(m, arrays[l][pl.ds(r0, rc), a:b], 0.0))
                stat_a[pl.ds(pl.multiple_of(OFF[l] + r0, 16), rc), :] = acc

            each(l, body)
        for l in group:
            at = slice(OFF[l], OFF[l] + C[l])
            s = jnp.sum(stat_a[at, :], axis=1, keepdims=True) * inv_local[l]
            cols[LOCAL, at, :] = jnp.broadcast_to(s, (C[l], 128))
        for l in group:

            def body(r0, rc, lanes, l=l):
                acc = jnp.zeros((rc, 128), F32)
                mean = col(LOCAL, l, r0, rc, lanes)
                for a, b in lane_chunks(l, lanes):
                    m = masks[l][1:2, a:b] > 0
                    d = jnp.where(m, arrays[l][pl.ds(r0, rc), a:b] - mean, 0.0)
                    acc = acc + fold(d * d)
                stat_b[pl.ds(pl.multiple_of(OFF[l] + r0, 16), rc), :] = acc

            each(l, body)
        return record(stat_a, stat_b, spans_of[group])

    def mean_rstd(got, group):
        mean, rstd = got[0:8] * inv_count, lax.rsqrt(got[8:16] * inv_count + EPSILON)
        to_columns([mean, rstd], cols, [MEAN, RSTD], spans_of[group])
        return rstd

    def halves(l):
        return max(1, W[l] // 128)

    def to_stage(ref, src):
        for h in range(src.shape[1] // 128):
            ref[h] = src[:, 128 * h : 128 * h + 128].astype(F32)

    for l in range(LEVELS):
        if W[l] >= 128:
            to_stage(stage, feats[l])
            for r in range(R[l]):
                for h in range(halves(l)):
                    a = (r + 1) * W[l] + 128 * h
                    xf[l][:, a : a + 128] = stage[h, pl.ds(r, C[l], stride=R[l]), :]
        else:
            v = feats[l][...].astype(F32)
            v = jnp.concatenate([v, jnp.zeros((NP[l] - N[l], C[l]), F32)], axis=0)
            xf[l][...] = pltpu.roll(v.T, W[l], 1)
    pl.semaphore_wait(barrier, nb + nk - 2)
    send_rims(0, COARSE, xf)
    send_rims(0, FINE, xf)
    to_stage(stage, ograd)
    widen(0)

    def stack_start(l):
        def body(r0, rc, lanes):
            for a, b in lane_chunks(l, lanes):
                m = masks[l][0:1, a:b] > 0
                stack_columns(x3[l], l, r0, rc, a, b, jnp.where(m, xf[l][pl.ds(r0, rc), a:b], 0.0))

        each(l, body)

    def pre_of(hat, gain, shift, l, r0, rc, lanes):
        return hat * col(gain, l, r0, rc, lanes) + col(shift, l, r0, rc, lanes)

    def first_act(l):
        def body(r0, rc, lanes):
            for a, b in lane_chunks(l, lanes):
                m = masks[l][0:1, a:b] > 0
                hat = (y1[l][pl.ds(r0, rc), a:b] - col(MEAN, l, r0, rc, lanes)) * col(RSTD, l, r0, rc, lanes)
                y1[l][pl.ds(r0, rc), a:b] = hat
                pre = pre_of(hat, GAIN1, SHIFT1, l, r0, rc, lanes)
                stack_columns(a3[l], l, r0, rc, a, b, jnp.where(m, pre * sigmoid(pre), 0.0))

        each(l, body)

    def second_act(l):
        def body(r0, rc, lanes):
            for a, b in lane_chunks(l, lanes):
                m = masks[l][0:1, a:b] > 0
                hat = (y2[l][pl.ds(r0, rc), a:b] - col(MEAN, l, r0, rc, lanes)) * col(RSTD, l, r0, rc, lanes)
                y2[l][pl.ds(r0, rc), a:b] = hat
                pre = pre_of(hat, GAIN2, SHIFT2, l, r0, rc, lanes)
                start = x3[l][pl.ds(pl.multiple_of(C[l] + r0, 16), rc), a:b].astype(F32)
                pre = jnp.where(m, pre, 0.0) + start
                p1[l][pl.ds(r0, rc), a:b] = pre
                if l:
                    br[l - 1][pl.ds(r0, rc), a:b] = (pre * sigmoid(pre)).astype(BF16)

        each(l, body)

    def second_sums(l):
        def body(r0, rc, lanes):
            acc_g = jnp.zeros((rc, 128), F32)
            acc_s = jnp.zeros((rc, 128), F32)
            for a, b in lane_chunks(l, lanes):
                m = masks[l][1:2, a:b] > 0
                pre = p1[l][pl.ds(r0, rc), a:b]
                sig = sigmoid(pre)
                d = xf[l][pl.ds(r0, rc), a:b] * (sig * (1.0 + pre * (1.0 - sig)))
                xf[l][pl.ds(r0, rc), a:b] = d
                d = jnp.where(m, d, 0.0)
                acc_s = acc_s + fold(d)
                acc_g = acc_g + fold(jnp.where(m, d * y2[l][pl.ds(r0, rc), a:b], 0.0))
            at = pl.ds(pl.multiple_of(OFF[l] + r0, 16), rc)
            stat_a[at, :] = acc_g
            stat_b[at, :] = acc_s

        each(l, body)

    def first_sums(l):
        def body(r0, rc, lanes):
            acc_g = jnp.zeros((rc, 128), F32)
            acc_s = jnp.zeros((rc, 128), F32)
            for a, b in lane_chunks(l, lanes):
                m = masks[l][1:2, a:b] > 0
                hat = y1[l][pl.ds(r0, rc), a:b]
                pre = pre_of(hat, GAIN1, SHIFT1, l, r0, rc, lanes)
                sig = sigmoid(pre)
                d = p1[l][pl.ds(r0, rc), a:b] * (sig * (1.0 + pre * (1.0 - sig)))
                d = jnp.where(m, d, 0.0)
                p1[l][pl.ds(r0, rc), a:b] = d
                acc_s = acc_s + fold(d)
                acc_g = acc_g + fold(jnp.where(m, d * hat, 0.0))
            at = pl.ds(pl.multiple_of(OFF[l] + r0, 16), rc)
            stat_a[at, :] = acc_g
            stat_b[at, :] = acc_s

        each(l, body)

    def norm_grad(l, hats, grads):
        def body(r0, rc, lanes):
            parts = []
            for a, b in lane_chunks(l, lanes):
                m = masks[l][0:1, a:b] > 0
                hat = hats[l][pl.ds(r0, rc), a:b]
                d = grads[l][pl.ds(r0, rc), a:b]
                g = col(CA, l, r0, rc, lanes) * (
                    d - col(CB, l, r0, rc, lanes) - hat * col(CC, l, r0, rc, lanes)
                )
                g = jnp.where(m, g, 0.0)
                stack_columns(g3[l], l, r0, rc, a, b, g, back=True)
                parts.append(g)
            if l in sz.stacked:
                v = parts[0] if len(parts) == 1 else jnp.concatenate(parts, axis=1)
                stack_rows(t3[l], l, r0, rc, jnp.where(masks[l][1:2, :] > 0, v, 0.0))

        each(l, body)

    def norm_columns(scale, got, group):
        to_columns(
            [scale, got[8:16] * inv_count, got[0:8] * inv_count], cols, [CA, CB, CC], spans_of[group]
        )

    def features_out(l):
        if W[l] < 128:
            v = jnp.where(masks[l][1:2, :] > 0, y1[l][...] + xf[l][...], 0.0)
            gfeat[l][...] = pltpu.roll(v, NP[l] - W[l], 1).T[0 : N[l]].astype(BF16)
            return

        def body(r0, rc, lanes):
            for r in range(R[l]):
                for h in range(halves(l)):
                    a = (r + 1) * W[l] + 128 * h
                    m = masks[l][1:2, a : a + 128] > 0
                    v = y1[l][pl.ds(r0, rc), a : a + 128] + xf[l][pl.ds(r0, rc), a : a + 128]
                    stage[h, pl.ds(r0 * R[l] + r, rc, stride=R[l]), :] = jnp.where(m, v, 0.0)

        each(l, body)
        for h in range(halves(l)):
            gfeat[l][:, 128 * h : 128 * h + 128] = stage[h].astype(BF16)

    sizes, u_sizes = (n_a, n_b), (un_a, un_b)
    fine_place = place < C[0]

    take_rims(0, COARSE, xf)
    for l in COARSE:
        stack_start(l)
    gather_begin(0, x3)
    for l in COARSE:
        conv(l, wide, 0, x3, y1)
    send_rims(1, COARSE, y1)
    ex_start(0, moments(y1, COARSE))
    take_rims(0, FINE, xf)
    stack_start(0)
    conv(0, wide, 0, x3, y1)
    send_rims(1, FINE, y1)
    ex_mid(0, sizes)
    ex_start(1, moments(y1, FINE))
    pair_begin(0, x3)
    turn(0)
    ex_mid(1, sizes)
    gather_next(0, 0)
    widen(1)
    rstd1_c = mean_rstd(ex_end(0, sizes), COARSE)
    take_rims(1, COARSE, y1)
    for l in COARSE:
        first_act(l)

    gather_begin(1, a3)
    for l in COARSE:
        conv(l, wide, 1, a3, y2)
    send_rims(2, COARSE, y2)
    ex_start(2, moments(y2, COARSE))
    rstd1_f = mean_rstd(ex_end(1, sizes), FINE)
    take_rims(1, FINE, y1)
    first_act(0)
    ex_mid(2, sizes)
    conv(0, wide, 1, a3, y2)
    send_rims(2, FINE, y2)
    ex_start(4, moments(y2, FINE))
    pair_begin(1, a3)
    pair_next(0)
    rstd2_c = mean_rstd(ex_end(2, sizes), COARSE)
    take_rims(2, COARSE, y2)
    for l in COARSE:
        second_act(l)

    UC_ = sz.uchan
    for j in range(3):
        l = j + 1
        uo[j][...] = jnp.dot(unites[j][...], br[j][...], preferred_element_type=F32)
    for j in range(3):
        l = j + 1
        m = masks[l][1:2, :] > 0
        v = jnp.where(m, uo[j][...], 0.0)
        part = fold(v)
        ustat_a[j * UC_ : (j + 1) * UC_, :] = part
        mean = jnp.sum(part, axis=1, keepdims=True) * inv_local[l]
        d = jnp.where(m, uo[j][...] - mean, 0.0)
        ustat_b[j * UC_ : (j + 1) * UC_, :] = fold(d * d)
    ex_start(3, record(ustat_a, ustat_b, u_spans))
    ex_mid(4, sizes)
    gather_next(0, 1)
    turn(1)
    ex_mid(3, u_sizes)
    gather_next(1, 0)
    pair_next(1)
    rstd2_f = mean_rstd(ex_end(4, sizes), FINE)
    take_rims(2, FINE, y2)
    second_act(0)
    got = ex_end(3, u_sizes)
    umean_p = got[0:8] * inv_ucount
    urstd_p = lax.rsqrt(got[8:16] * inv_ucount + EPSILON)
    to_columns([umean_p, urstd_p], ucols, [UMEAN, URSTD], u_spans)

    at_top = me_k == 0
    at_bottom = me_k == nk - 1
    fine = W[0]
    split = lambda v: (v.astype(BF16), (v - v.astype(BF16).astype(F32)).astype(BF16))

    def edge(l, n):
        return lax.broadcasted_iota(jnp.int32, (1, n), 1)

    for j in range(3):
        l = j + 1
        m = masks[l][0:1, :] > 0
        hat = (uo[j][...] - ucol(UMEAN, j, NP[l])) * ucol(URSTD, j, NP[l])
        uo[j][...] = hat
        norm = jnp.where(m, hat * ucol(UGAIN, j, NP[l]) + ucol(USHIFT, j, NP[l]), 0.0)
        lane = edge(l, NP[l])
        norm = jnp.where((lane < W[l]) & at_top, pltpu.roll(norm, NP[l] - W[l], 1), norm)
        norm = jnp.where((lane >= W[l] + N[l]) & at_bottom, pltpu.roll(norm, W[l], 1), norm)
        hi, lo = split(norm)
        both = jnp.concatenate([hi, lo], axis=0)
        span = max(128, W[l])
        width = tables[j].shape[1]
        for i in range(NP[l] // span):
            broad = jnp.dot(both[:, span * i : span * i + span], tables[j][...], preferred_element_type=F32)
            up[j][:, width * i : width * i + width] = broad[0:UC_] + broad[UC_:]

    blends = [blend(2 ** (j + 1), R[0]) for j in range(3)]

    def total_body(r0, rc, lanes):
        rows = pl.ds(r0, rc)
        coarse = [{}, {}, {}]
        have = [{}, {}, {}]
        for g in range(R[0]):
            a, b = (g + 1) * fine, (g + 2) * fine
            pre = p1[0][rows, a:b]
            total = pre * sigmoid(pre)
            for j in range(3):
                low, frac = blends[j][g]
                for i in (low, low + 1):
                    if i not in have[j]:
                        have[j][i] = up[j][rows, i * fine : (i + 1) * fine]
                total = total + ((1.0 - frac) * have[j][low] + frac * have[j][low + 1])
            m = masks[0][1:2, a:b] > 0
            sig = sigmoid(total)
            out = jnp.where(m, total * sig, 0.0)
            slope = sig * (1.0 + total * (1.0 - sig))
            spots = [(h, pl.ds(r0 * R[0] + g, rc, stride=R[0])) for h in range(halves(0))]
            grad = jnp.concatenate([stage[h, at, :] for h, at in spots], axis=1)
            grad = jnp.where(m, grad * slope, 0.0)
            for h, at in spots:
                stage[h, at, :] = out[:, 128 * h : 128 * h + 128]
            xf[0][rows, a:b] = grad
            for j in range(3):
                low, frac = blends[j][g]
                for i, weight in ((low, 1.0 - frac), (low + 1, frac)):
                    coarse[j][i] = weight * grad if i not in coarse[j] else coarse[j][i] + weight * grad
                done = [i for i in coarse[j] if g + 1 == R[0] or i < blends[j][g + 1][0]]
                for i in done:
                    up[j][rows, i * fine : (i + 1) * fine] = coarse[j].pop(i)

    def total_step(i, _):
        total_body(pl.multiple_of(i * 16, 16), 16, fine)
        return 0

    lax.fori_loop(0, UC_ // 16, total_step, 0)
    for h in range(halves(0)):
        united_ref[:, 128 * h : 128 * h + 128] = stage[h].astype(BF16)

    for j in range(3):
        l = j + 1
        span = max(128, W[l])
        width = tables[j].shape[1]
        parts = []
        for i in range(NP[l] // span):
            hi, lo = split(up[j][:, width * i : width * i + width])
            both = jnp.concatenate([hi, lo], axis=0)
            narrow = jnp.dot(both, tables_t[j][...], preferred_element_type=F32)
            parts.append(narrow[0:UC_] + narrow[UC_:])
        d = parts[0] if len(parts) == 1 else jnp.concatenate(parts, axis=1)
        lane = edge(l, NP[l])
        fold_top = jnp.where((lane >= W[l]) & (lane < 2 * W[l]) & at_top, pltpu.roll(d, W[l], 1), 0.0)
        fold_bottom = jnp.where(
            (lane >= N[l]) & (lane < W[l] + N[l]) & at_bottom, pltpu.roll(d, NP[l] - W[l], 1), 0.0
        )
        d = d + fold_top + fold_bottom
        d = jnp.where(masks[l][0:1, :] > 0, d, 0.0)
        ustat_a[j * UC_ : (j + 1) * UC_, :] = fold(d * uo[j][...])
        ustat_b[j * UC_ : (j + 1) * UC_, :] = fold(d)
        up[j][:, 0 : NP[l]] = d
    at = 0
    lay = []
    for j in range(3):
        l = j + 1
        n = max(2 * W[l], 128)
        lay.append((at, n))
        mid_s[0, :, at : at + n] = up[j][:, 0:n].astype(BF16)
        mid_s[1, :, at : at + n] = up[j][:, NP[l] - n : NP[l]].astype(BF16)
        at += n
    mid_s[0, :, at : at + fine] = xf[0][:, fine : 2 * fine].astype(BF16)
    mid_s[1, :, at : at + fine] = xf[0][:, N[0] : N[0] + fine].astype(BF16)
    rims_start(8, lambda i: mid_s.at[i], lambda i: mid_r.at[i])
    ex_start(5, record(ustat_a, ustat_b, u_spans))
    second_sums(0)
    ex_mid(5)
    ex_start(6, record(stat_a, stat_b, spans_of[FINE]))
    gather_next(1, 1)
    got = ex_end(5)
    totals_ref[0] = got
    rims_wait(8, lambda i: mid_s.at[i], lambda i: mid_r.at[i])
    to_columns(
        [urstd_p * ugain_p, got[8:16] * inv_ucount, got[0:8] * inv_ucount], ucols, [UA, UB, UC], u_spans
    )
    for i, lane0 in ((0, 0), (1, W[0] + N[0])):
        pre = p1[0][:, lane0 : lane0 + fine]
        sig = sigmoid(pre)
        slope = sig * (1.0 + pre * (1.0 - sig))
        xf[0][:, lane0 : lane0 + fine] = mid_r[i, :, at : at + fine].astype(F32) * slope
    for j in range(3):
        l = j + 1
        start, n = lay[j]
        lane = edge(l, n)
        above = mid_r[0, :, start : start + n].astype(F32)
        below = mid_r[1, :, start : start + n].astype(F32)
        if NP[l] == n:
            above, below = pltpu.roll(above, n // 2, 1), pltpu.roll(below, n // 2, 1)
            d = up[j][:, 0:n]
            d = d + jnp.where((lane < 2 * W[l]) & (me_k > 0), above, 0.0)
            d = d + jnp.where((lane >= n - 2 * W[l]) & (me_k < nk - 1), below, 0.0)
            up[j][:, 0:n] = d
        else:
            up[j][:, 0:n] = up[j][:, 0:n] + jnp.where((lane >= 0) & (me_k > 0), above, 0.0)
            up[j][:, NP[l] - n : NP[l]] = up[j][:, NP[l] - n : NP[l]] + jnp.where(
                (lane >= 0) & (me_k < nk - 1), below, 0.0
            )
    for j in range(3):
        l = j + 1
        d = up[j][:, 0 : NP[l]]
        g = ucol(UA, j, NP[l]) * (d - ucol(UB, j, NP[l]) - uo[j][...] * ucol(UC, j, NP[l]))
        g = jnp.where(masks[l][0:1, :] > 0, g, 0.0)
        low = g.astype(BF16)
        xf[l][...] = jnp.dot(unites[j][...].T, low, preferred_element_type=F32)
        own = jnp.where(masks[l][1:2, :] > 0, g, 0.0).astype(BF16)
        gun[j][:, 0 : C[l]] = lax.dot_general(
            own, br[j][...], (((1,), (1,)), ((), ())), preferred_element_type=F32
        )

    for l in COARSE:
        second_sums(l)
    ex_start(7, record(stat_a, stat_b, spans_of[COARSE]))
    ex_mid(6)
    got_f = ex_end(6)
    norm_columns(rstd2_f * gain2_p, got_f, FINE)
    norm_grad(0, y2, xf)
    ex_mid(7)
    conv(0, wide, 1, g3, p1, -1)
    first_sums(0)
    send_rims(3, FINE, p1)
    ex_start(8, record(stat_a, stat_b, spans_of[FINE]))
    sum_level(1, 0, a3)
    sum_pack_unites()
    got = ex_end(7)
    totals_ref[1] = jnp.where(jnp.concatenate([fine_place] * 2, axis=0), got_f, got)
    norm_columns(rstd2_c * gain2_p, got, COARSE)
    norm_grad(2, y2, xf)
    pair_grad_begin(1)
    norm_grad(3, y2, xf)
    grad_begin(1)
    norm_grad(1, y2, xf)

    for l in COARSE:
        conv(l, wide, 1, g3, p1, -1)
    for l in COARSE:
        first_sums(l)
    send_rims(3, COARSE, p1)
    ex_start(9, record(stat_a, stat_b, spans_of[COARSE]))
    for l in sz.sum_levels[1:]:
        sum_level(1, l, a3)
    sum_first(1)
    ex_mid(8)
    pair_inputs(1)
    ex_mid(9)
    sum_second(1)
    grad_next(1)
    pair_gradient(1)
    gather_next(0, 2)
    gather_next(1, 2)
    got_f = ex_end(8)
    take_rims(3, FINE, p1)
    norm_columns(rstd1_f * gain1_p, got_f, FINE)
    norm_grad(0, y1, p1)
    sum_third(1)
    sum_level(0, 0, x3)
    grad_third(1)
    got = ex_end(9)
    totals_ref[2] = jnp.where(jnp.concatenate([fine_place] * 2, axis=0), got_f, got)
    take_rims(3, COARSE, p1)
    norm_columns(rstd1_c * gain1_p, got, COARSE)
    norm_grad(2, y1, p1)
    pair_grad_begin(0)
    norm_grad(3, y1, p1)
    grad_begin(0)
    norm_grad(1, y1, p1)
    for l in sz.sum_levels[1:]:
        sum_level(0, l, x3)
    sum_first(0)
    sum_fourth(1)

    pair_inputs(0)
    sum_second(0)
    conv(0, wide, 0, g3, y1, -1)
    features_out(0)
    sum_fifth(1)
    pair_gradient(0)
    sum_third(0)
    grad_next(0)
    conv(1, wide, 0, g3, y1, -1)
    features_out(1)
    sum_sixth(1)
    sum_fourth(0)
    for l in (2, 3):
        conv(l, wide, 0, g3, y1, -1)
        features_out(l)
    grad_third(0)
    sum_fifth(0)
    coarse_inputs(1)
    coarse_gradient(1)
    sum_sixth(0)
    coarse_inputs(0)
    coarse_gradient(0)
    sum_last(1)
    sum_last(0)
    for c in range(2):
        pltpu.make_async_copy(got_d.at[c], sums_ref.at[c], out_sem.at[c]).wait()


def last_kernel(sz, nb, *refs):
    it = iter(refs)
    take = lambda n: [next(it) for _ in range(n)]
    maps = take(5)
    sums, totals = take(2)
    (coarse,) = take(1)
    maps_out = take(5)
    kernels = take(4)
    unites = take(3)
    norm_gains, norm_shifts, unite_gains, unite_shifts = take(4)
    (sem,) = take(1)
    copies = [pltpu.make_async_copy(a, b, sem.at[i]) for i, (a, b) in enumerate(zip(maps, maps_out))]
    for copy in copies:
        copy.start()
    C = sz.chan
    for l in range(LEVELS):
        n = C[l] // nb
        for c in range(2):
            if (l, 0) in sz.spots:
                parts = []
                for i in range(-(-3 * C[l] // 128)):
                    at, rows = sz.spots[l, i]
                    parts.append(sums[c, at : at + rows, :].astype(F32))
                v = jnp.concatenate(parts, axis=1)
            for t in range(3):
                for u in range(3):
                    if (l, 0) in sz.spots:
                        kernels[l][c, t, u] = v[t * n : (t + 1) * n, u * C[l] : (u + 1) * C[l]]
                    else:
                        kernels[l][c, t, u] = coarse[c, t * n : (t + 1) * n, u * C[l] : (u + 1) * C[l]]
    n = sz.uchan // nb
    for j in range(3):
        width = C[j + 1]
        for i in range(-(-width // 128)):
            at, _ = sz.spots["u", j, i]
            m = min(128, width - 128 * i)
            unites[j][:, 128 * i : 128 * i + m] = sums[1, at : at + n, 0:m].astype(F32)
    for row, which in ((0, 2), (1, 1)):
        for k in range(sz.blocks):
            m = min(128, sz.total - 128 * k)
            for ref, base in ((norm_gains, 0), (norm_shifts, 8)):
                ref[row : row + 1, 128 * k : 128 * k + m] = totals[which, base + k : base + k + 1, 0:m]
    for ref, base in ((unite_gains, 0), (unite_shifts, 8)):
        v = jnp.concatenate([totals[0, base + k : base + k + 1, :] for k in range(sz.ublocks)], axis=1)
        for j in range(3):
            ref[j : j + 1, :] = v[:, j * sz.uchan : (j + 1) * sz.uchan]
    for copy in copies:
        copy.wait()


def body(*args):
    features = args[0:4]
    blocks = args[4:8]
    unites = args[8:11]
    norm_gains, norm_shifts, unite_gains, unite_shifts, output_grad, heights, widths, item_slot = args[11:]
    nb = lax.axis_size("batch")
    nk = lax.axis_size("rows")
    sz = Sizes(features, nb, nk)
    C, R, W, N, NP = sz.chan, sz.rows, sz.width, sz.own, sz.flat

    flat = [
        f.reshape(C[l] * R[l], W[l]) if W[l] >= 128 else f.transpose(0, 2, 3, 1).reshape(N[l], C[l])
        for l, f in enumerate(features)
    ]
    ograd = output_grad.reshape(C[0] * R[0], W[0])
    blocks = [b.reshape(2, 3, 3 * C[l], C[l]) for l, b in enumerate(blocks)]

    tables = [column_table(W[l], W[0]) for l in range(1, 4)]
    operands = [heights, widths, item_slot, *flat, ograd, *blocks, *unites]
    operands += [norm_gains, norm_shifts, unite_gains, unite_shifts]
    operands += [jnp.asarray(t, BF16) for t in tables] + [jnp.asarray(t.T, BF16) for t in tables]

    shape = jax.ShapeDtypeStruct
    map_shapes = [(C[0] * R[0], W[0])]
    map_shapes += [(C[l] * R[l], W[l]) if W[l] >= 128 else (N[l], C[l]) for l in range(4)]
    outs = [shape(m, BF16) for m in map_shapes]
    outs += [shape((2, sz.sum_rows, 128), BF16)]
    outs += [shape((2, 3 * C[3] // nb if sz.gather else 3 * C[3], 3 * C[3]), F32)]
    outs += [shape((3, 16, 128), F32)]
    vm = pltpu.VMEM
    scratch = [
        vm((3, 3 * C[l], C[l]), BF16) for l in range(3 if sz.gather else 4)
    ]
    scratch += [vm((2, 3 * C[l], 3 * C[l]), BF16) for l in range(4)]
    scratch += [vm((max(1, W[0] // 128), C[0] * R[0], 128), F32)]
    for _ in range(3):
        scratch += [vm((3 * C[l], NP[l]), BF16) for l in range(4)]
    scratch += [vm((3 * C[l], NP[l]), BF16) for l in sz.stacked]
    scratch += [vm((2, C[3] // nb, 3 * C[3]), F32), pltpu.SemaphoreType.DMA((2,))]
    top = C[sz.sum_levels[-1]]
    scratch += [vm((3 * top, -(-3 * top // 128) * 128), F32)]
    scratch += [vm((sz.uchan, -(-C[l] // 128) * 128), F32) for l in range(1, 4)]
    for _ in range(4):
        scratch += [vm((C[l], NP[l]), F32) for l in range(4)]
    scratch += [vm((C[l], NP[l]), BF16) for l in range(1, 4)]
    scratch += [vm((sz.uchan, NP[l]), F32) for l in range(1, 4)]
    scratch += [vm((sz.uchan, (R[l] + 2) * W[0]), F32) for l in range(1, 4)]
    scratch += [
        vm((N_COLS, sz.blocks * 128, 128), F32),
        vm((N_UCOLS, sz.ublocks * 128, 128), F32),
        vm((sz.blocks * 128, 128), F32),
        vm((sz.blocks * 128, 128), F32),
        vm((sz.ublocks * 128, 128), F32),
        vm((sz.ublocks * 128, 128), F32),
        vm((nb, 8, 128), F32),
        vm((nk, 8, 128), F32),
        vm((nb, 8, 128), F32),
        vm((nk, 8, 128), F32),
    ]
    scratch += [vm((8, NP[l]), F32) for l in range(4)]
    mid = sum(max(2 * W[l], 128) for l in range(1, 4)) + W[0]
    scratch += [
        vm((10, nb, 16, 128), F32),
        vm((10, nk, 16, 128), F32),
        vm((2, sz.rim_total, 128), BF16),
        vm((4, 2, sz.rim_total, 128), BF16),
        vm((2, sz.uchan, mid), BF16),
        vm((2, sz.uchan, mid), BF16),
        pltpu.SemaphoreType.DMA((10, nb)),
        pltpu.SemaphoreType.DMA((10, nb)),
        pltpu.SemaphoreType.DMA((10, nk)),
        pltpu.SemaphoreType.DMA((10, nk)),
        pltpu.SemaphoreType.DMA((9, 2)),
        pltpu.SemaphoreType.DMA((9, 2)),
        pltpu.SemaphoreType.DMA((4, 2)),
        pltpu.SemaphoreType.DMA((2, 9)),
        vm((8, sz.blocks * 128), F32),
        vm((8, sz.ublocks * 128), F32),
        vm((2, sz.nc, sz.ny, sz.batch_rows, 128), BF16),
        vm((2, sz.ny, sz.batch_rows, 128), BF16),
        vm((2, sz.ny, sz.batch_rows, 128), BF16),
        vm((2, sz.sum_rows, 128), BF16),
        vm((2, sz.nz * sz.part, 128), BF16),
        vm((2, sz.nz, sz.part, 128), BF16),
        vm((2, sz.sum_rows, 128), BF16),
        pltpu.SemaphoreType.DMA((2,)),
    ]
    sems = pltpu.SemaphoreType.DMA
    scratch += [sems((2,))] * 2 + [sems((2, sz.ny))] * 2 + [sems((2,))] * 2 + [sems((2, sz.nz))] * 4
    scratch += [sems((2,))] * 2
    if sz.gather:
        half = C[3] // nb // 2
        most = max(sz.nz, sz.nx, sz.ny, sz.nc)
        scratch += [
            vm((2, sz.nc, sz.ny, sz.nx, sz.nz, C[3] // 2, 128), BF16),
            vm((2, nb, half, 128), BF16),
            vm((2, sz.nx, sz.nz, nb, half, 128), BF16),
            vm((max(3, nb), 3 * C[3], max(C[3], 128 * sz.nz)), BF16),
            vm((nb, 3 * C[3] // nb, 128 * sz.nz), BF16),
            sems((2, 4, most)),
            sems((2, 4, most)),
            sems((2, nb)),
            sems((2, nb)),
            sems((2, sz.nz)),
            sems((2, sz.nz)),
            sems((2,)),
            sems((2,)),
        ]
    if sz.pair:
        c2 = C[2] // nb
        scratch += [
            vm((2, sz.nc, sz.ny, C[2], NP[2]), BF16),
            vm((nb, 3 * C[2], NP[2]), BF16),
            vm((2, nb, c2, N[2]), BF16),
            vm((2, nb, c2, N[2]), BF16),
            vm((nb, 3 * c2, NP[2]), BF16),
            sems((2, 2, max(sz.ny, sz.nc))),
            sems((2, 2, max(sz.ny, sz.nc))),
            sems((2, nb)),
            sems((2, nb)),
        ]
    in_vmem = pl.BlockSpec(memory_space=pltpu.VMEM)
    in_smem = pl.BlockSpec(memory_space=pltpu.SMEM)
    got = pl.pallas_call(
        functools.partial(main_kernel, sz, nb, nk),
        out_shape=outs,
        in_specs=[in_smem] * 3
        + [in_vmem] * 5
        + [pl.BlockSpec(memory_space=pl.ANY)] * 4
        + [in_vmem] * (len(operands) - 12),
        out_specs=[in_vmem] * 5
        + [pl.BlockSpec(memory_space=pl.ANY)] * 2
        + [in_vmem],
        scratch_shapes=scratch,
        compiler_params=pltpu.CompilerParams(
            collective_id=0, has_side_effects=True, vmem_limit_bytes=60 * 2**20
        ),
    )(*operands)

    maps, sums, totals = got[0:5], got[5], got[-1]
    coarse = got[6]
    if not sz.gather:
        coarse = coarse.astype(BF16).reshape(2, 3, C[3], 3 * C[3])
        coarse = lax.psum(coarse, "rows")
        coarse = lax.psum_scatter(coarse, "batch", scatter_dimension=2, tiled=True)
        coarse = coarse.astype(F32).reshape(2, 3 * C[3] // nb, 3 * C[3])
    in_any = pl.BlockSpec(memory_space=pl.ANY)
    outs = [shape(m, BF16) for m in map_shapes]
    outs += [shape((2, 3, 3, C[l] // nb, C[l]), F32) for l in range(4)]
    outs += [shape((sz.uchan // nb, C[l]), F32) for l in range(1, 4)]
    outs += [shape((2, sz.total), F32)] * 2 + [shape((3, sz.uchan), F32)] * 2
    outs = pl.pallas_call(
        functools.partial(last_kernel, sz, nb),
        out_shape=outs,
        in_specs=[in_vmem] * 8,
        out_specs=[in_any] * 5 + [in_vmem] * (len(outs) - 5),
        scratch_shapes=[pltpu.SemaphoreType.DMA((5,))],
        compiler_params=pltpu.CompilerParams(vmem_limit_bytes=60 * 2**20),
    )(*maps, sums, totals, coarse)
    shaped = []
    for i, m in enumerate(outs[0:5]):
        l = max(i - 1, 0)
        if W[l] >= 128:
            shaped.append(m.reshape(1, C[l], R[l], W[l]))
        else:
            shaped.append(m.reshape(1, R[l], W[l], C[l]).transpose(0, 3, 1, 2))
    return (*shaped, *outs[5:])


def solution(mesh):
    image = P("batch", None, "rows", None)
    kernel = P(None, None, None, "batch", None)
    return jax.shard_map(
        body,
        mesh=mesh,
        in_specs=(image,) * 4 + (P(),) * 11 + (image,) + (P(),) * 3,
        out_specs=(image,) * 5 + (kernel,) * 4 + (P("batch", None),) * 3 + (P(),) * 4,
        check_vma=False,
    )
```

```python
import functools

import jax
import jax.numpy as jnp
import numpy as np
from jax import lax
from jax.experimental import pallas as pl
from jax.experimental.pallas import tpu as pltpu
from jax.sharding import PartitionSpec as P

EPSILON = 1e-05
LEVELS = 4
MESH = pl.DeviceIdType.MESH
F32 = jnp.float32
BF16 = jnp.bfloat16

MEAN, RSTD, GAIN1, SHIFT1, GAIN2, SHIFT2, LOCAL, N_COLS = range(8)
CA, CB, CC = MEAN, RSTD, LOCAL
UMEAN, URSTD, UGAIN, USHIFT, ULOCAL, UA, UB, UC, N_UCOLS = range(9)


class Sizes:
    def __init__(self, features, nb, nk):
        self.chan = [f.shape[1] for f in features]
        self.rows = [f.shape[2] for f in features]
        self.width = [f.shape[3] for f in features]
        self.own = [r * w for r, w in zip(self.rows, self.width)]
        self.flat = [(r + 2) * w for r, w in zip(self.rows, self.width)]
        self.off = [sum(self.chan[:l]) for l in range(LEVELS)]
        self.total = sum(self.chan)
        self.blocks = -(-self.total // 128)
        self.uchan = self.chan[0]
        self.utotal = 3 * self.uchan
        self.ublocks = -(-self.utotal // 128)
        self.rim_rows = [c * w // 128 for c, w in zip(self.chan, self.width)]
        self.rim_off = [sum(self.rim_rows[:l]) for l in range(LEVELS)]
        self.rim_total = sum(self.rim_rows)
        self.chunk = []
        for c, n, w in zip(self.chan, self.flat, self.width):
            lanes = max(x for x in range(128, 641, 128) if n % x == 0 and x % w == 0)
            rows = max(r for r in (16, 32, 48) if c % r == 0 and r * lanes <= 12288)
            self.chunk.append((rows, lanes))
        self.nc = 2 if nb % 2 == 0 else 1
        self.nx = 2 if nk % 2 == 0 else 1
        self.ny = nb // self.nc
        self.nz = nk // self.nx
        self.gather = nb * nk <= 32 and self.nx == 2 and self.nc == 2 and self.own[3] == 64
        self.pair = self.gather and self.chan[2] // nb % 16 == 0 and self.chan[2] % 128 == 64
        self.sum_levels = [0, 1] if self.pair else [0, 1, 2]
        self.stacked = [l for l in range(3 if self.gather else 4) if self.width[l] < 128]
        self.stacked = [l for l in self.stacked if not (self.pair and l == 2)]
        self.spots = {}
        at = 0

        def place(key, values, width):
            nonlocal at
            rows = -(-values // 16) * 16
            for i in range(-(-width // 128)):
                self.spots[(*key, i)] = (at, rows)
                at += rows

        place((0,), 3 * self.chan[0] // nb, 3 * self.chan[0])
        for j in range(3):
            place(("u", j), self.uchan // nb, self.chan[j + 1])
        self.early_rows = at
        for l in self.sum_levels[1:]:
            place((l,), 3 * self.chan[l] // nb, 3 * self.chan[l])
        self.batch_rows = at
        if self.pair:
            rows = 9 * self.chan[2] // nb
            for i in range(self.chan[2] // 128):
                self.spots[2, i] = (at, rows)
                at += rows
            rows = -(-rows // 32) * 16
            self.spots[2, self.chan[2] // 128] = (at, rows)
            at += rows
        self.part = -(-at // (nk * 16)) * 16
        self.sum_rows = self.part * nk


def blend(scale, rows):
    out = []
    for g in range(rows):
        num = 2 * g + 1 - scale
        low = num // (2 * scale)
        out.append((low + 1, (num - 2 * scale * low) / (2.0 * scale)))
    return out


def column_table(width, fine):
    scale = fine // width
    group = max(1, 128 // width)
    span = max(128, width)
    table = np.zeros((span, group * fine), np.float32)
    for r in range(group):
        for g in range(fine):
            num = 2 * g + 1 - scale
            low = 0 if num < 0 else num // (2 * scale)
            frac = 0.0 if num < 0 else (num - 2 * scale * low) / (2.0 * scale)
            high = min(low + 1, width - 1)
            table[r * width + low, r * fine + g] += 1.0 - frac
            table[r * width + high, r * fine + g] += frac
    return table


def sigmoid(v):
    return jax.nn.sigmoid(v)


def main_kernel(sz, nb, nk, *refs):
    it = iter(refs)
    take = lambda n: [next(it) for _ in range(n)]
    heights, widths, slots = take(3)
    feats = take(4)
    (ograd,) = take(1)
    blocks = take(4)
    unites = take(3)
    norm_gains, norm_shifts, unite_gains, unite_shifts = take(4)
    tables = take(3)
    tables_t = take(3)
    (united_ref,) = take(1)
    gfeat = take(4)
    (sums_ref,) = take(1)
    (coarse_ref,) = take(1)
    (totals_ref,) = take(1)
    raw = take(3 if sz.gather else 4)
    wide = take(4)
    (stage,) = take(1)
    x3 = take(4)
    a3 = take(4)
    g3 = take(4)
    t3 = dict(zip(sz.stacked, take(len(sz.stacked))))
    cstage, cstage_sem = take(2)
    (kg,) = take(1)
    gun = take(3)
    xf = take(4)
    y1 = take(4)
    y2 = take(4)
    p1 = take(4)
    br = take(3)
    uo = take(3)
    up = take(3)
    (cols, ucols, stat_a, stat_b, ustat_a, ustat_b, n_a, n_b, un_a, un_b) = take(10)
    masks = take(4)
    (rec_a, rec_b, rim_s, rim_r, mid_s, mid_r) = take(6)
    (sa_send, sa_recv, sb_send, sb_recv, rim_send, rim_recv) = take(6)
    raw_sem, wide_sem = take(2)
    prow, urow = take(2)
    part_a, got_a, part_s, got_x, got_z, got_d, out_sem = take(7)
    (ra_send, ra_recv, rx_send, rx_recv, rz_send, rz_recv) = take(6)
    (dz_send, dz_recv, dx_send, dx_recv) = take(4)
    if sz.gather:
        xg, xi, gs, gr, g9 = take(5)
        (xg_send, xg_recv, g1_send, g1_recv, g2_send, g2_recv, g3_send, g3_recv) = take(8)
    if sz.pair:
        xb, gsb, gb, g9b = take(4)
        (xb_send, xb_recv, gb_send, gb_recv) = take(4)

    C, R, W, N, NP, OFF = sz.chan, sz.rows, sz.width, sz.own, sz.flat, sz.off
    me_b = lax.axis_index("batch")
    me_k = lax.axis_index("rows")

    def peer_b(j):
        return lax.rem(me_b + j, nb)

    def peer_k(j):
        return lax.rem(me_k + j, nk)

    def raw_copy(l, which):
        if l == 3 and sz.gather:
            dst = g9.at[:, :, 0 : C[3]]
        else:
            dst = raw[l]
        return pltpu.make_async_copy(blocks[l].at[which], dst, raw_sem.at[l, which])

    def wide_copies(which):
        c = C[3]
        return [
            pltpu.make_async_copy(
                blocks[3].at[which, t, u * c : (u + 1) * c, :],
                wide[3].at[which, t * c : (t + 1) * c, u * c : (u + 1) * c],
                wide_sem.at[which, 3 * t + u],
            )
            for t in range(3)
            for u in range(3)
        ]

    for l in range(3):
        raw_copy(l, 0).start()
    for which in range(2):
        for copy in wide_copies(which):
            copy.start()
    raw_copy(3, 0).start()

    def widen(which):
        for copy in wide_copies(which):
            copy.wait()
        for l in range(3):
            raw_copy(l, which).wait()
            c = C[l]
            for t in range(3):
                wide[l][which, t * c : (t + 1) * c, :] = jnp.concatenate(
                    [raw[l][t, u * c : (u + 1) * c, :] for u in range(3)], axis=1
                )

    def turn(which):
        raw_copy(3, which).wait()
        for l in range(LEVELS):
            for t in range(3):
                if l == 3 and sz.gather:
                    v = g9[t, :, 0 : C[3]]
                else:
                    v = raw[l][t]
                wide[l][which, t * C[l] : (t + 1) * C[l], :] = v.T
        if which == 0:
            for l in range(LEVELS):
                raw_copy(l, 1).start()

    barrier = pltpu.get_barrier_semaphore()
    for j in range(1, nb):
        pl.semaphore_signal(barrier, inc=1, device_id=(peer_b(j), me_k), device_id_type=MESH)
    for j in range(1, nk):
        pl.semaphore_signal(barrier, inc=1, device_id=(me_b, peer_k(j)), device_id_type=MESH)

    my_h = jnp.int32(0)
    my_w = jnp.int32(0)
    slot_h, slot_w = [], []
    for b in range(nb):
        h = jnp.int32(0)
        w = jnp.int32(0)
        for i in range(nb):
            hit = (slots[i] == b).astype(jnp.int32)
            h = h + hit * heights[i]
            w = w + hit * widths[i]
        slot_h.append(h)
        slot_w.append(w)
        mine = (me_b == b).astype(jnp.int32)
        my_h = my_h + mine * h
        my_w = my_w + mine * w

    count = []
    for l in range(LEVELS):
        c = jnp.int32(0)
        for b in range(nb):
            c = c + lax.shift_right_logical(slot_h[b], l) * lax.shift_right_logical(slot_w[b], l)
        count.append(c.astype(F32))
    inv_local = []
    for l in range(LEVELS):
        inside = jnp.clip(lax.shift_right_logical(my_h, l) - me_k * R[l], 0, R[l])
        own = inside * lax.shift_right_logical(my_w, l)
        inv_local.append(1.0 / jnp.maximum(own, 1).astype(F32))
        lane = lax.broadcasted_iota(jnp.int32, (1, NP[l]), 1)
        log_w = W[l].bit_length() - 1
        row = me_k * R[l] + lax.shift_right_logical(lane, log_w) - 1
        col = lane & (W[l] - 1)
        valid = (row >= 0) & (row < lax.shift_right_logical(my_h, l))
        valid = valid & (col < lax.shift_right_logical(my_w, l))
        masks[l][0:1, :] = jnp.where(valid, 1.0, 0.0)
        masks[l][1:2, :] = jnp.where(valid & (lane >= W[l]) & (lane < W[l] + N[l]), 1.0, 0.0)

    place = lax.broadcasted_iota(jnp.int32, (8, 128), 0) * 128 + lax.broadcasted_iota(
        jnp.int32, (8, 128), 1
    )

    def by_level(values):
        out = jnp.full((8, 128), values[3])
        for l in (2, 1, 0):
            out = jnp.where(place < OFF[l + 1], jnp.full((8, 128), values[l]), out)
        return out

    def by_unite(values):
        out = jnp.full((8, 128), values[2])
        for j in (1, 0):
            out = jnp.where(place < (j + 1) * sz.uchan, jnp.full((8, 128), values[j]), out)
        return out

    inv_count = 1.0 / by_level(count)
    inv_ucount = 1.0 / by_unite(count[1:])
    for chooser, levels, na_ref, nb_ref in (
        (by_level, range(4), n_a, n_b),
        (by_unite, range(1, 4), un_a, un_b),
    ):
        span = chooser([jnp.int32(R[l]) for l in levels])
        hv = [chooser([lax.shift_right_logical(h, l) for l in levels]) for h in slot_h]
        wv = [chooser([lax.shift_right_logical(w, l) for l in levels]) for w in slot_w]
        for b in range(nb):
            na_ref[b] = (jnp.clip(hv[b] - me_k * span, 0, span) * wv[b]).astype(F32)
        for k in range(nk):
            n = jnp.zeros((8, 128), jnp.int32)
            for b in range(nb):
                n = n + jnp.clip(hv[b] - k * span, 0, span) * wv[b]
            nb_ref[k] = n.astype(F32)

    def tile(v, lanes):
        return v if lanes == 128 else jnp.concatenate([v] * (lanes // 128), axis=1)

    def col(slot, l, r0, rc, lanes):
        return tile(cols[slot, pl.ds(pl.multiple_of(OFF[l] + r0, 16), rc), :], lanes)

    def ucol(slot, j, lanes):
        return tile(ucols[slot, j * sz.uchan : (j + 1) * sz.uchan, :], lanes)

    def to_columns(packed, ref, slot_list, spans):
        full = jnp.concatenate(packed + [jnp.zeros((128 - 8 * len(packed), 128), F32)], axis=0)
        standing = full.T
        for i, slot in enumerate(slot_list):
            for lo, hi in spans:
                for k in range(lo // 128, -(-hi // 128)):
                    a, b = max(lo, 128 * k), min(hi, 128 * k + 128)
                    v = standing[a - 128 * k : b - 128 * k, 8 * i + k : 8 * i + k + 1]
                    ref[slot, a:b, :] = jnp.broadcast_to(v, (b - a, 128))

    FINE, COARSE = (0,), (1, 2, 3)
    spans_of = {FINE: [(0, C[0])], COARSE: [(C[0], sz.total)]}
    u_spans = [(0, sz.utotal)]

    prow[...] = jnp.zeros_like(prow)
    urow[...] = jnp.zeros_like(urow)
    for i in range(2):
        prow[2 * i : 2 * i + 1, 0 : sz.total] = norm_gains[i : i + 1, :]
        prow[2 * i + 1 : 2 * i + 2, 0 : sz.total] = norm_shifts[i : i + 1, :]
    for j in range(3):
        at = slice(j * sz.uchan, (j + 1) * sz.uchan)
        urow[0:1, at] = unite_gains[j : j + 1, :]
        urow[1:2, at] = unite_shifts[j : j + 1, :]
    standing = prow[...].T
    for i, slot in enumerate((GAIN1, SHIFT1, GAIN2, SHIFT2)):
        cols[slot] = jnp.broadcast_to(standing[:, i : i + 1], (sz.blocks * 128, 128))
    standing = urow[...].T
    for i, slot in enumerate((UGAIN, USHIFT)):
        ucols[slot] = jnp.broadcast_to(standing[:, i : i + 1], (sz.ublocks * 128, 128))

    def packed(ref, i, blocks):
        rows = [ref[i : i + 1, 128 * k : 128 * k + 128] for k in range(blocks)]
        return jnp.concatenate(rows + [jnp.zeros((8 - blocks, 128), F32)], axis=0)

    gain1_p, gain2_p = packed(prow, 0, sz.blocks), packed(prow, 2, sz.blocks)
    ugain_p = packed(urow, 0, sz.ublocks)
    stat_a[...] = jnp.zeros_like(stat_a)
    stat_b[...] = jnp.zeros_like(stat_b)
    ustat_a[...] = jnp.zeros_like(ustat_a)
    ustat_b[...] = jnp.zeros_like(ustat_b)

    def fold(v):
        out = v[:, 0:128]
        for i in range(1, v.shape[1] // 128):
            out = out + v[:, 128 * i : 128 * i + 128]
        return out

    lane128 = lax.broadcasted_iota(jnp.int32, (1, 128), 1)

    def record(a_ref, b_ref, spans):
        out = jnp.zeros((128, 128), F32)
        for base, ref in ((0, a_ref), (8, b_ref)):
            for lo, hi in spans:
                for k in range(lo // 128, -(-hi // 128)):
                    s = jnp.sum(ref[128 * k : 128 * k + 128, :], axis=1, keepdims=True)
                    out = jnp.where(lane128 == base + k, s, out)
        return out.T[0:16]

    def record_copies(e, which, sending):
        if which == 0:
            ref, send, recv, n, me = rec_a, sa_send, sa_recv, nb, me_b
        else:
            ref, send, recv, n, me = rec_b, sb_send, sb_recv, nk, me_k
        out = []
        for j in range(1, n):
            other = lax.rem(me + j, n)
            slot = me if sending else other
            out.append(
                pltpu.make_async_remote_copy(
                    src_ref=ref.at[e, me],
                    dst_ref=ref.at[e, slot],
                    send_sem=send.at[e, other],
                    recv_sem=recv.at[e, slot],
                    device_id=(other, me_k) if which == 0 else (me_b, other),
                    device_id_type=MESH,
                )
            )
        return out

    def record_send(e, which, rec):
        if which == 0:
            rec_a[e, me_b] = rec
        else:
            rec_b[e, me_k] = rec
        for copy in record_copies(e, which, True):
            copy.start()

    def record_total(e, which, sizes):
        for copy in record_copies(e, which, False):
            copy.wait_recv()
        for copy in record_copies(e, which, True):
            copy.wait_send()
        ref, n = ((rec_a, nb), (rec_b, nk))[which]
        if sizes is None:
            out = ref[e, 0]
            for i in range(1, n):
                out = out + ref[e, i]
            return out
        total = jnp.zeros((8, 128), F32)
        size = jnp.zeros((8, 128), F32)
        for i in range(n):
            total = total + ref[e, i, 0:8]
            size = size + sizes[which][i]
        mean = total / jnp.maximum(size, 1.0)
        spread_sum = jnp.zeros((8, 128), F32)
        for i in range(n):
            delta = ref[e, i, 0:8] / jnp.maximum(sizes[which][i], 1.0) - mean
            spread_sum = spread_sum + (ref[e, i, 8:16] + sizes[which][i] * delta * delta)
        return jnp.concatenate([total, spread_sum], axis=0)

    def ex_start(e, rec):
        record_send(e, 0, rec)

    def ex_mid(e, sizes=None):
        record_send(e, 1, record_total(e, 0, sizes))

    def ex_end(e, sizes=None):
        return record_total(e, 1, sizes)

    def rim_copies(slot, src, dst):
        up = pltpu.make_async_remote_copy(
            src_ref=src(0),
            dst_ref=dst(1),
            send_sem=rim_send.at[slot, 0],
            recv_sem=rim_recv.at[slot, 1],
            device_id=(me_b, lax.rem(me_k + nk - 1, nk)),
            device_id_type=MESH,
        )
        down = pltpu.make_async_remote_copy(
            src_ref=src(1),
            dst_ref=dst(0),
            send_sem=rim_send.at[slot, 1],
            recv_sem=rim_recv.at[slot, 0],
            device_id=(me_b, lax.rem(me_k + 1, nk)),
            device_id_type=MESH,
        )
        return up, down

    def rims_start(slot, src, dst):
        up, down = rim_copies(slot, src, dst)

        @pl.when(me_k > 0)
        def _():
            up.start()

        @pl.when(me_k < nk - 1)
        def _():
            down.start()

    def rims_wait(slot, src, dst):
        up, down = rim_copies(slot, src, dst)

        @pl.when(me_k > 0)
        def _():
            down.wait_recv()
            up.wait_send()

        @pl.when(me_k < nk - 1)
        def _():
            up.wait_recv()
            down.wait_send()

    def pack_row(ref, l, lane0):
        if W[l] >= 128:
            return jnp.concatenate(
                [ref[:, lane0 + 128 * i : lane0 + 128 * i + 128] for i in range(W[l] // 128)], axis=0
            )
        group = 128 // W[l]
        rows = C[l] // group
        base, shift = lane0 // 128 * 128, lane0 % 128
        out = None
        for g in range(group):
            v = ref[g * rows : (g + 1) * rows, base : base + 128]
            turn = (g * W[l] - shift) % 128
            v = pltpu.roll(v, turn, 1) if turn else v
            out = v if out is None else jnp.where(lane128 >= g * W[l], v, out)
        return out

    def unpack_row(ref, l, lane0, q):
        if W[l] >= 128:
            for i in range(W[l] // 128):
                ref[:, lane0 + 128 * i : lane0 + 128 * i + 128] = q[i * C[l] : (i + 1) * C[l]]
            return
        group = 128 // W[l]
        rows = C[l] // group
        base, shift = lane0 // 128 * 128, lane0 % 128
        here = (lane128 >= shift) & (lane128 < shift + W[l])
        for g in range(group):
            turn = (shift - g * W[l]) % 128
            v = pltpu.roll(q, turn, 1) if turn else q
            old = ref[g * rows : (g + 1) * rows, base : base + 128]
            ref[g * rows : (g + 1) * rows, base : base + 128] = jnp.where(here, v, old)

    def rim_span(group):
        first, last = group[0], group[-1]
        return slice(sz.rim_off[first], sz.rim_off[last] + sz.rim_rows[last])

    def rims_of(slot, group):
        at = rim_span(group)
        number = 2 * slot + (0 if group == FINE else 1)
        return number, lambda i: rim_s.at[i, at, :], lambda i: rim_r.at[slot, i, at, :]

    def send_rims(slot, group, arrays):
        for l in group:
            at = rim_span((l,))
            rim_s[0, at, :] = pack_row(arrays[l], l, W[l]).astype(BF16)
            rim_s[1, at, :] = pack_row(arrays[l], l, N[l]).astype(BF16)
        rims_start(*rims_of(slot, group))

    def take_rims(slot, group, arrays):
        rims_wait(*rims_of(slot, group))
        for l in group:
            at = rim_span((l,))
            unpack_row(arrays[l], l, 0, rim_r[slot, 0, at, :].astype(F32))
            unpack_row(arrays[l], l, W[l] + N[l], rim_r[slot, 1, at, :].astype(F32))

    def each(l, body):
        rc, lanes = sz.chunk[l]

        def step(i, _):
            body(pl.multiple_of(i * rc, rc), rc, lanes)
            return 0

        count = C[l] // rc
        lax.fori_loop(0, count, step, 0, unroll=max(k for k in range(1, 9) if count % k == 0))

    def lane_chunks(l, lanes):
        return [(i, i + lanes) for i in range(0, NP[l], lanes)]

    def stack_columns(ref, l, r0, rc, a, b, v, back=False):
        lanes = b - a
        at = lax.broadcasted_iota(jnp.int32, (1, lanes), 1) & (W[l] - 1)
        left = jnp.where(at == 0, 0.0, pltpu.roll(v, 1, 1))
        right = jnp.where(at == W[l] - 1, 0.0, pltpu.roll(v, lanes - 1, 1))
        for u, part in enumerate((right, v, left) if back else (left, v, right)):
            ref[pl.ds(pl.multiple_of(u * C[l] + r0, 16), rc), a:b] = part.astype(BF16)

    def stack_rows(ref, l, r0, rc, v):
        for t in range(3):
            turn = ((t - 1) * W[l]) % NP[l]
            part = pltpu.roll(v, turn, 1) if turn else v
            ref[pl.ds(pl.multiple_of(t * C[l] + r0, 16), rc), :] = part.astype(BF16)

    def conv(l, w, which, src, dst, sign=1):
        c = C[l]
        if W[l] % 128 == 0:
            span = min(1024, N[l])

            def step(i, _):
                acc = None
                for t in range(3):
                    at = pl.ds(pl.multiple_of(i * span + (1 + sign * (t - 1)) * W[l], 128), span)
                    part = jnp.dot(
                        w[l][which, t * c : (t + 1) * c, :], src[l][:, at], preferred_element_type=F32
                    )
                    acc = part if acc is None else acc + part
                dst[l][:, pl.ds(pl.multiple_of(i * span + W[l], 128), span)] = acc
                return 0

            lax.fori_loop(0, N[l] // span, step, 0)
        else:
            rows = c if c <= 384 else 96

            def step(i, _):
                acc = None
                for t in range(3):
                    at = pl.ds(pl.multiple_of(t * c + i * rows, 16), rows)
                    part = jnp.dot(w[l][which, at, :], src[l][...], preferred_element_type=F32)
                    turn = (sign * (1 - t) * W[l]) % NP[l]
                    part = pltpu.roll(part, turn, 1) if turn else part
                    acc = part if acc is None else acc + part
                dst[l][pl.ds(pl.multiple_of(i * rows, 16), rows), :] = acc
                return 0

            lax.fori_loop(0, c // rows, step, 0)

    def kernel_grad(l, src):
        c = C[l]
        if W[l] % 128 == 0:
            for t in range(3):
                kg[t * c : (t + 1) * c, 0 : 3 * c] = lax.dot_general(
                    g3[l][c : 2 * c, W[l] : W[l] + N[l]],
                    src[l][:, t * W[l] : t * W[l] + N[l]],
                    (((1,), (1,)), ((), ())),
                    preferred_element_type=F32,
                )
            return
        span = 96

        def step(i, _):
            at = pl.ds(pl.multiple_of(i * span, 16), span)
            kg[at, 0 : 3 * c] = lax.dot_general(
                t3[l][at, :], src[l][...], (((1,), (1,)), ((), ())), preferred_element_type=F32
            )
            return 0

        lax.fori_loop(0, 3 * c // span, step, 0)

    nc, ny, nx, nz = sz.nc, sz.ny, sz.nx, sz.nz
    my_core, my_y = lax.rem(me_b, nc), lax.div(me_b, nc)
    my_x, my_z = lax.rem(me_k, nx), lax.div(me_k, nx)

    def others(n, me):
        return [lax.rem(me + j, n) for j in range(1, n)]

    def remote(src, dst, send, recv, target):
        return pltpu.make_async_remote_copy(
            src_ref=src, dst_ref=dst, send_sem=send, recv_sem=recv, device_id=target, device_id_type=MESH
        )

    def sum_pack(c, l):
        n = C[l] // nb
        for q in range(nb):
            dst = part_a.at[c, q]
            for i in range(-(-3 * C[l] // 128)):
                at, rows = sz.spots[l, i]
                lanes = slice(128 * i, 128 * i + 128)
                parts = [kg[t * C[l] + q * n : t * C[l] + q * n + n, lanes] for t in range(3)]
                if rows > 3 * n:
                    parts.append(jnp.zeros((rows - 3 * n, 128), F32))
                dst[at : at + rows, :] = jnp.concatenate(parts, axis=0).astype(BF16)

    def sum_pack_unites():
        n = sz.uchan // nb
        for q in range(nb):
            dst = part_a.at[1, q]
            for j in range(3):
                for i in range(-(-C[j + 1] // 128)):
                    at, rows = sz.spots["u", j, i]
                    v = gun[j][q * n : q * n + n, 128 * i : 128 * i + 128]
                    if rows > n:
                        v = jnp.concatenate([v, jnp.zeros((rows - n, 128), F32)], axis=0)
                    dst[at : at + rows, :] = v.astype(BF16)

    def batch_copies(c, part, sending):
        rows = (slice(0, sz.early_rows), slice(sz.early_rows, sz.batch_rows))[part]
        out = []
        for other in others(nb, me_b):
            slot = me_b if sending else other
            src, dst = part_a.at[c, other, rows, :], got_a.at[c, slot, rows, :]
            sems = ra_send.at[c, part, other], ra_recv.at[c, part, slot]
            out.append(remote(src, dst, *sems, (other, me_k)))
        return out

    def part_at(x, z, n=1):
        return pl.ds(pl.multiple_of((x * nz + z) * sz.part, 16), n * sz.part)

    def x_copies(c):
        out = []
        for other in others(nx, my_x):
            src = part_s.at[c, part_at(other, 0, nz), :]
            target = (me_b, my_z * nx + other)
            out.append(remote(src, got_x.at[c], rx_send.at[c], rx_recv.at[c], target))
        return out

    def z_copies(c, sending):
        out = []
        for other in others(nz, my_z):
            slot = my_z if sending else other
            src = part_s.at[c, part_at(my_x, other), :]
            target = (me_b, other * nx + my_x)
            out.append(remote(src, got_z.at[c, slot], rz_send.at[c, other], rz_recv.at[c, slot], target))
        return out

    def back_z_copies(c, sending):
        out = []
        for other in others(nz, my_z):
            slot = my_z if sending else other
            src, dst = got_d.at[c, part_at(my_x, my_z), :], got_d.at[c, part_at(my_x, slot), :]
            target = (me_b, other * nx + my_x)
            out.append(remote(src, dst, dz_send.at[c, other], dz_recv.at[c, slot], target))
        return out

    def back_x_copies(c, sending):
        out = []
        for other in others(nx, my_x):
            slot = my_x if sending else other
            src, dst = got_d.at[c, part_at(my_x, 0, nz), :], got_d.at[c, part_at(slot, 0, nz), :]
            target = (me_b, my_z * nx + other)
            out.append(remote(src, dst, dx_send.at[c], dx_recv.at[c], target))
        return out

    def finish(pair):
        sent, received = pair
        for copy in received:
            copy.wait_recv()
        for copy in sent:
            copy.wait_send()

    def sum_level(c, l, src):
        kernel_grad(l, src)
        sum_pack(c, l)

    def sum_first(c, part):
        for copy in batch_copies(c, part, True):
            copy.start()

    def sum_second(c):
        for part in range(2):
            finish((batch_copies(c, part, True), batch_copies(c, part, False)))
        got_a[c, me_b] = part_a[c, me_b]
        v = got_a[c, 0].astype(F32)
        for b in range(1, nb):
            v = v + got_a[c, b].astype(F32)
        part_s[c, 0 : sz.batch_rows, :] = v.astype(BF16)
        for copy in x_copies(c):
            copy.start()

    def sum_third(c):
        copies = x_copies(c)
        finish((copies, copies))
        mine = part_at(my_x, 0, nz)
        if nx > 1:
            v = part_s[c, mine, :].astype(F32) + got_x[c].astype(F32)
            part_s[c, mine, :] = v.astype(BF16)
        for copy in z_copies(c, True):
            copy.start()

    def sum_fourth(c):
        finish((z_copies(c, True), z_copies(c, False)))
        got_z[c, my_z] = part_s[c, part_at(my_x, my_z), :]
        v = got_z[c, 0].astype(F32)
        for z in range(1, nz):
            v = v + got_z[c, z].astype(F32)
        got_d[c, part_at(my_x, my_z), :] = v.astype(BF16)
        for copy in back_z_copies(c, True):
            copy.start()

    def sum_fifth(c):
        finish((back_z_copies(c, True), back_z_copies(c, False)))
        for copy in back_x_copies(c, True):
            copy.start()

    def sum_last(c):
        finish((back_x_copies(c, True), back_x_copies(c, False)))
        pltpu.make_async_copy(got_d.at[c], sums_ref.at[c], out_sem.at[c]).start()

    c2 = C[2] // nb

    def pair_copies(c, step, sending):
        if not sz.pair:
            return []
        n, me = ((ny, my_y), (nc, my_core))[step]
        out = []
        for other in others(n, me):
            slot = me if sending else other
            if step == 0:
                ref, target = xb.at[c, my_core, slot], (other * nc + my_core, me_k)
            else:
                ref, target = xb.at[c, slot], (my_y * nc + other, me_k)
            out.append(remote(ref, ref, xb_send.at[c, step, other], xb_recv.at[c, step, slot], target))
        return out

    def pair_begin(c, ref):
        if sz.pair:
            xb[c, my_core, my_y] = ref[2][C[2] : 2 * C[2], :]
            for copy in pair_copies(c, 0, True):
                copy.start()

    def pair_next(c):
        finish((pair_copies(c, 0, True), pair_copies(c, 0, False)))
        for copy in pair_copies(c, 1, True):
            copy.start()

    def pair_grad_copies(c, sending):
        out = []
        for other in others(nb, me_b):
            slot = me_b if sending else other
            out.append(
                remote(gsb.at[c, other], gb.at[c, slot], gb_send.at[c, other], gb_recv.at[c, slot], (other, me_k))
            )
        return out

    def pair_grad_begin(c):
        if sz.pair:
            for q in range(nb):
                v = g3[2][C[2] + q * c2 : C[2] + (q + 1) * c2, :].astype(F32)
                gsb[c, q] = pltpu.roll(v, NP[2] - W[2], 1)[:, 0 : N[2]].astype(BF16)
            for copy in pair_grad_copies(c, True):
                copy.start()

    def nine_shifts(v, width, store):
        lanes = v.shape[1]
        lane = lax.broadcasted_iota(jnp.int32, (1, lanes), 1)
        at = lane & (width - 1)
        left = jnp.where(at == width - 1, 0.0, pltpu.roll(v, lanes - 1, 1))
        right = jnp.where(at == 0, 0.0, pltpu.roll(v, 1, 1))
        for u, part in enumerate((left, v, right)):
            store(0, u, jnp.where(lane >= lanes - width, 0.0, pltpu.roll(part, lanes - width, 1)))
            store(1, u, part)
            store(2, u, jnp.where(lane < width, 0.0, pltpu.roll(part, width, 1)))

    def pair_gradient(c):
        if not sz.pair:
            return
        finish((pair_copies(c, 1, True), pair_copies(c, 1, False)))
        finish((pair_grad_copies(c, True), pair_grad_copies(c, False)))
        gb[c, me_b] = gsb[c, me_b]

        def item(b, _):
            v = jnp.concatenate([gb[c, b].astype(F32), jnp.zeros((c2, NP[2] - N[2]), F32)], axis=1)

            def store(t, u, part):
                at = (3 * t + u) * c2
                g9b[b, at : at + c2, :] = part.astype(BF16)

            nine_shifts(pltpu.roll(v, W[2], 1), W[2], store)
            return 0

        lax.fori_loop(0, nb, item, 0)
        acc = None
        for b in range(nb):
            part = lax.dot_general(
                g9b[b], xb[c, b % nc, b // nc], (((1,), (1,)), ((), ())), preferred_element_type=F32
            )
            acc = part if acc is None else acc + part
        whole = C[2] // 128
        for i in range(whole):
            at, rows = sz.spots[2, i]
            part_s[c, at : at + rows, :] = acc[:, 128 * i : 128 * i + 128].astype(BF16)
        at, rows = sz.spots[2, whole]
        rest = acc[:, 128 * whole :]
        low, high = rest[0:rows], rest[rows:]
        high = jnp.concatenate([high, jnp.zeros((rows - high.shape[0], high.shape[1]), F32)], axis=0)
        part_s[c, at : at + rows, :] = jnp.concatenate([low, high], axis=1).astype(BF16)

    c3 = C[3] // nb
    half = c3 // 2

    def pack_pixels(ref):
        parts = []
        for q in range(nb):
            at = C[3] + q * c3
            low = pltpu.roll(ref[at : at + half, :].astype(F32), 128 - W[3], 1)
            high = pltpu.roll(ref[at + half : at + c3, :].astype(F32), 64 - W[3], 1)
            parts.append(jnp.where(lane128 < 64, low, high))
        return jnp.concatenate(parts, axis=0).astype(BF16)

    def unpack_pixels(first, second):
        first, second = first.astype(F32), second.astype(F32)
        low = jnp.where(lane128 < 64, first, pltpu.roll(second, 64, 1))
        high = jnp.where(lane128 < 64, pltpu.roll(first, 64, 1), second)
        return low, high

    def gather_copies(c, step, sending):
        if not sz.gather:
            return []
        n, me = ((nz, my_z), (nx, my_x), (ny, my_y), (nc, my_core))[step]
        out = []
        for other in others(n, me):
            slot = me if sending else other
            if step == 0:
                ref, target = xg.at[c, my_x, slot], (me_b, other * nx + my_x)
            elif step == 1:
                ref, target = xg.at[c, slot], (me_b, my_z * nx + other)
            elif step == 2:
                ref, target = xi.at[c, my_core, slot], (other * nc + my_core, me_k)
            else:
                ref, target = xi.at[c, slot], (my_y * nc + other, me_k)
            out.append(remote(ref, ref, xg_send.at[c, step, other], xg_recv.at[c, step, slot], target))
        return out

    def gather_start(c, step):
        for copy in gather_copies(c, step, True):
            copy.start()

    def gather_wait(c, step):
        finish((gather_copies(c, step, True), gather_copies(c, step, False)))

    def gather_begin(c, ref):
        if sz.gather:
            xg[c, my_x, my_z] = pack_pixels(ref[3])
            gather_start(c, 0)

    def gather_next(c, step):
        gather_wait(c, step)
        if step == 1 and sz.gather:
            for z in range(nz):
                for q in range(nb):
                    rows = slice(q * half, (q + 1) * half)
                    pair = unpack_pixels(xg[c, 0, z, rows, :], xg[c, 1, z, rows, :])
                    for i, v in enumerate(pair):
                        at = q * c3 + i * half
                        xi[c, my_core, my_y, at : at + half, 128 * z : 128 * z + 128] = v.astype(BF16)
        gather_start(c, step + 1)

    def grad_copies(c, step, sending):
        out = []
        if step == 0:
            for other in others(nb, me_b):
                slot = me_b if sending else other
                src = gs.at[c, other]
                out.append(
                    remote(src, gr.at[c, my_x, my_z, slot], g1_send.at[c, other], g1_recv.at[c, slot], (other, me_k))
                )
        elif step == 1:
            for other in others(nz, my_z):
                slot = my_z if sending else other
                src, dst = gr.at[c, my_x, my_z], gr.at[c, my_x, slot]
                target = (me_b, other * nx + my_x)
                out.append(remote(src, dst, g2_send.at[c, other], g2_recv.at[c, slot], target))
        else:
            for other in others(nx, my_x):
                slot = my_x if sending else other
                src, dst = gr.at[c, my_x], gr.at[c, slot]
                target = (me_b, my_z * nx + other)
                out.append(remote(src, dst, g3_send.at[c], g3_recv.at[c], target))
        return out

    def grad_begin(c):
        if sz.gather:
            v = pack_pixels(g3[3])
            for q in range(nb):
                gs[c, q] = v[q * half : (q + 1) * half]
            for copy in grad_copies(c, 0, True):
                copy.start()

    def grad_next(c):
        if sz.gather:
            finish((grad_copies(c, 0, True), grad_copies(c, 0, False)))
            gr[c, my_x, my_z, me_b] = gs[c, me_b]
            for copy in grad_copies(c, 1, True):
                copy.start()

    def grad_third(c):
        if sz.gather:
            finish((grad_copies(c, 1, True), grad_copies(c, 1, False)))
            for copy in grad_copies(c, 2, True):
                copy.start()

    image = nz * 128

    def coarse_copy(c, i):
        n = 3 * c3
        at = pl.ds(i * n if isinstance(i, int) else pl.multiple_of(i * n, 16), n)
        slot = i % 2 if isinstance(i, int) else lax.rem(i, 2)
        return pltpu.make_async_copy(cstage.at[slot], coarse_ref.at[c, at, :], cstage_sem.at[slot])

    def coarse_local(c, src):
        def step(i, _):
            at = pl.ds(pl.multiple_of(i * c3, 16), c3)
            cstage[0] = lax.dot_general(
                t3[3][at, :], src[3][...], (((1,), (1,)), ((), ())), preferred_element_type=F32
            )
            copy = pltpu.make_async_copy(cstage.at[0], coarse_ref.at[c, at, :], cstage_sem.at[0])
            copy.start()
            copy.wait()
            return 0

        lax.fori_loop(0, 3 * nb, step, 0)

    def coarse_gradient(c):
        if not sz.gather:
            coarse_local(c, a3 if c else x3)
            return
        gather_wait(c, 3)
        finish((grad_copies(c, 2, True), grad_copies(c, 2, False)))

        def item(b, _):
            low, high = [], []
            for z in range(nz):
                first, second = unpack_pixels(gr[c, 0, z, b], gr[c, 1, z, b])
                low.append(first)
                high.append(second)
            for i, parts in enumerate((low, high)):

                def store(t, u, part, i=i):
                    spot = pl.ds(pl.multiple_of((3 * b + u) * c3 + i * half, 16), half)
                    g9[t, spot, 0:image] = part.astype(BF16)

                nine_shifts(jnp.concatenate(parts, axis=1) if nz > 1 else parts[0], W[3], store)
            return 0

        lax.fori_loop(0, nb, item, 0)

        def step(i, _):
            acc = None
            for b in range(nb):
                part = lax.dot_general(
                    g9[i, 3 * b * c3 : 3 * (b + 1) * c3, 0:image],
                    xi[c, b % nc, b // nc],
                    (((1,), (1,)), ((), ())),
                    preferred_element_type=F32,
                )
                acc = part if acc is None else acc + part
            slot = lax.rem(i, 2)

            @pl.when(i >= 2)
            def _():
                coarse_copy(c, i - 2).wait()

            cstage[slot] = acc
            coarse_copy(c, i).start()
            return 0

        lax.fori_loop(0, 3, step, 0)
        coarse_copy(c, 1).wait()
        coarse_copy(c, 2).wait()

    def moments(arrays, group):
        for l in group:

            def body(r0, rc, lanes, l=l):
                acc = jnp.zeros((rc, 128), F32)
                for a, b in lane_chunks(l, lanes):
                    m = masks[l][1:2, a:b] > 0
                    acc = acc + fold(jnp.where(m, arrays[l][pl.ds(r0, rc), a:b], 0.0))
                stat_a[pl.ds(pl.multiple_of(OFF[l] + r0, 16), rc), :] = acc

            each(l, body)
        for l in group:
            at = slice(OFF[l], OFF[l] + C[l])
            s = jnp.sum(stat_a[at, :], axis=1, keepdims=True) * inv_local[l]
            cols[LOCAL, at, :] = jnp.broadcast_to(s, (C[l], 128))
        for l in group:

            def body(r0, rc, lanes, l=l):
                acc = jnp.zeros((rc, 128), F32)
                mean = col(LOCAL, l, r0, rc, lanes)
                for a, b in lane_chunks(l, lanes):
                    m = masks[l][1:2, a:b] > 0
                    d = jnp.where(m, arrays[l][pl.ds(r0, rc), a:b] - mean, 0.0)
                    acc = acc + fold(d * d)
                stat_b[pl.ds(pl.multiple_of(OFF[l] + r0, 16), rc), :] = acc

            each(l, body)
        return record(stat_a, stat_b, spans_of[group])

    def mean_rstd(got, group):
        mean, rstd = got[0:8] * inv_count, lax.rsqrt(got[8:16] * inv_count + EPSILON)
        to_columns([mean, rstd], cols, [MEAN, RSTD], spans_of[group])
        return rstd

    def halves(l):
        return max(1, W[l] // 128)

    def to_stage(ref, src):
        for h in range(src.shape[1] // 128):
            ref[h] = src[:, 128 * h : 128 * h + 128].astype(F32)

    for l in range(LEVELS):
        if W[l] >= 128:
            to_stage(stage, feats[l])
            for r in range(R[l]):
                for h in range(halves(l)):
                    a = (r + 1) * W[l] + 128 * h
                    xf[l][:, a : a + 128] = stage[h, pl.ds(r, C[l], stride=R[l]), :]
        else:
            v = feats[l][...].astype(F32)
            v = jnp.concatenate([v, jnp.zeros((NP[l] - N[l], C[l]), F32)], axis=0)
            xf[l][...] = pltpu.roll(v.T, W[l], 1)
    pl.semaphore_wait(barrier, nb + nk - 2)
    send_rims(0, COARSE, xf)
    send_rims(0, FINE, xf)
    to_stage(stage, ograd)
    widen(0)

    def stack_start(l):
        def body(r0, rc, lanes):
            for a, b in lane_chunks(l, lanes):
                m = masks[l][0:1, a:b] > 0
                stack_columns(x3[l], l, r0, rc, a, b, jnp.where(m, xf[l][pl.ds(r0, rc), a:b], 0.0))

        each(l, body)

    def pre_of(hat, gain, shift, l, r0, rc, lanes):
        return hat * col(gain, l, r0, rc, lanes) + col(shift, l, r0, rc, lanes)

    def first_act(l):
        def body(r0, rc, lanes):
            for a, b in lane_chunks(l, lanes):
                m = masks[l][0:1, a:b] > 0
                hat = (y1[l][pl.ds(r0, rc), a:b] - col(MEAN, l, r0, rc, lanes)) * col(RSTD, l, r0, rc, lanes)
                y1[l][pl.ds(r0, rc), a:b] = hat
                pre = pre_of(hat, GAIN1, SHIFT1, l, r0, rc, lanes)
                stack_columns(a3[l], l, r0, rc, a, b, jnp.where(m, pre * sigmoid(pre), 0.0))

        each(l, body)

    def second_act(l):
        def body(r0, rc, lanes):
            for a, b in lane_chunks(l, lanes):
                m = masks[l][0:1, a:b] > 0
                hat = (y2[l][pl.ds(r0, rc), a:b] - col(MEAN, l, r0, rc, lanes)) * col(RSTD, l, r0, rc, lanes)
                y2[l][pl.ds(r0, rc), a:b] = hat
                pre = pre_of(hat, GAIN2, SHIFT2, l, r0, rc, lanes)
                start = x3[l][pl.ds(pl.multiple_of(C[l] + r0, 16), rc), a:b].astype(F32)
                pre = jnp.where(m, pre, 0.0) + start
                p1[l][pl.ds(r0, rc), a:b] = pre
                if l:
                    br[l - 1][pl.ds(r0, rc), a:b] = (pre * sigmoid(pre)).astype(BF16)

        each(l, body)

    def second_sums(l):
        def body(r0, rc, lanes):
            acc_g = jnp.zeros((rc, 128), F32)
            acc_s = jnp.zeros((rc, 128), F32)
            for a, b in lane_chunks(l, lanes):
                m = masks[l][1:2, a:b] > 0
                pre = p1[l][pl.ds(r0, rc), a:b]
                sig = sigmoid(pre)
                d = xf[l][pl.ds(r0, rc), a:b] * (sig * (1.0 + pre * (1.0 - sig)))
                xf[l][pl.ds(r0, rc), a:b] = d
                d = jnp.where(m, d, 0.0)
                acc_s = acc_s + fold(d)
                acc_g = acc_g + fold(jnp.where(m, d * y2[l][pl.ds(r0, rc), a:b], 0.0))
            at = pl.ds(pl.multiple_of(OFF[l] + r0, 16), rc)
            stat_a[at, :] = acc_g
            stat_b[at, :] = acc_s

        each(l, body)

    def first_sums(l):
        def body(r0, rc, lanes):
            acc_g = jnp.zeros((rc, 128), F32)
            acc_s = jnp.zeros((rc, 128), F32)
            for a, b in lane_chunks(l, lanes):
                m = masks[l][1:2, a:b] > 0
                hat = y1[l][pl.ds(r0, rc), a:b]
                pre = pre_of(hat, GAIN1, SHIFT1, l, r0, rc, lanes)
                sig = sigmoid(pre)
                d = p1[l][pl.ds(r0, rc), a:b] * (sig * (1.0 + pre * (1.0 - sig)))
                d = jnp.where(m, d, 0.0)
                p1[l][pl.ds(r0, rc), a:b] = d
                acc_s = acc_s + fold(d)
                acc_g = acc_g + fold(jnp.where(m, d * hat, 0.0))
            at = pl.ds(pl.multiple_of(OFF[l] + r0, 16), rc)
            stat_a[at, :] = acc_g
            stat_b[at, :] = acc_s

        each(l, body)

    def norm_grad(l, hats, grads):
        def body(r0, rc, lanes):
            parts = []
            for a, b in lane_chunks(l, lanes):
                m = masks[l][0:1, a:b] > 0
                hat = hats[l][pl.ds(r0, rc), a:b]
                d = grads[l][pl.ds(r0, rc), a:b]
                g = col(CA, l, r0, rc, lanes) * (
                    d - col(CB, l, r0, rc, lanes) - hat * col(CC, l, r0, rc, lanes)
                )
                g = jnp.where(m, g, 0.0)
                stack_columns(g3[l], l, r0, rc, a, b, g, back=True)
                parts.append(g)
            if l in sz.stacked:
                v = parts[0] if len(parts) == 1 else jnp.concatenate(parts, axis=1)
                stack_rows(t3[l], l, r0, rc, jnp.where(masks[l][1:2, :] > 0, v, 0.0))

        each(l, body)

    def norm_columns(scale, got, group):
        to_columns(
            [scale, got[8:16] * inv_count, got[0:8] * inv_count], cols, [CA, CB, CC], spans_of[group]
        )

    def features_out(l):
        if W[l] < 128:
            v = jnp.where(masks[l][1:2, :] > 0, y1[l][...] + xf[l][...], 0.0)
            gfeat[l][...] = pltpu.roll(v, NP[l] - W[l], 1).T[0 : N[l]].astype(BF16)
            return

        def body(r0, rc, lanes):
            for r in range(R[l]):
                for h in range(halves(l)):
                    a = (r + 1) * W[l] + 128 * h
                    m = masks[l][1:2, a : a + 128] > 0
                    v = y1[l][pl.ds(r0, rc), a : a + 128] + xf[l][pl.ds(r0, rc), a : a + 128]
                    stage[h, pl.ds(r0 * R[l] + r, rc, stride=R[l]), :] = jnp.where(m, v, 0.0)

        each(l, body)
        for h in range(halves(l)):
            gfeat[l][:, 128 * h : 128 * h + 128] = stage[h].astype(BF16)

    sizes, u_sizes = (n_a, n_b), (un_a, un_b)
    fine_place = place < C[0]

    take_rims(0, COARSE, xf)
    for l in COARSE:
        stack_start(l)
    gather_begin(0, x3)
    for l in COARSE:
        conv(l, wide, 0, x3, y1)
    send_rims(1, COARSE, y1)
    ex_start(0, moments(y1, COARSE))
    take_rims(0, FINE, xf)
    stack_start(0)
    conv(0, wide, 0, x3, y1)
    send_rims(1, FINE, y1)
    ex_mid(0, sizes)
    ex_start(1, moments(y1, FINE))
    pair_begin(0, x3)
    turn(0)
    ex_mid(1, sizes)
    gather_next(0, 0)
    widen(1)
    rstd1_c = mean_rstd(ex_end(0, sizes), COARSE)
    take_rims(1, COARSE, y1)
    for l in COARSE:
        first_act(l)

    gather_begin(1, a3)
    for l in COARSE:
        conv(l, wide, 1, a3, y2)
    send_rims(2, COARSE, y2)
    ex_start(2, moments(y2, COARSE))
    rstd1_f = mean_rstd(ex_end(1, sizes), FINE)
    take_rims(1, FINE, y1)
    first_act(0)
    ex_mid(2, sizes)
    conv(0, wide, 1, a3, y2)
    send_rims(2, FINE, y2)
    ex_start(4, moments(y2, FINE))
    pair_begin(1, a3)
    pair_next(0)
    rstd2_c = mean_rstd(ex_end(2, sizes), COARSE)
    take_rims(2, COARSE, y2)
    for l in COARSE:
        second_act(l)

    UC_ = sz.uchan
    for j in range(3):
        l = j + 1
        uo[j][...] = jnp.dot(unites[j][...], br[j][...], preferred_element_type=F32)
    for j in range(3):
        l = j + 1
        m = masks[l][1:2, :] > 0
        v = jnp.where(m, uo[j][...], 0.0)
        part = fold(v)
        ustat_a[j * UC_ : (j + 1) * UC_, :] = part
        mean = jnp.sum(part, axis=1, keepdims=True) * inv_local[l]
        d = jnp.where(m, uo[j][...] - mean, 0.0)
        ustat_b[j * UC_ : (j + 1) * UC_, :] = fold(d * d)
    ex_start(3, record(ustat_a, ustat_b, u_spans))
    ex_mid(4, sizes)
    gather_next(0, 1)
    turn(1)
    ex_mid(3, u_sizes)
    gather_next(1, 0)
    pair_next(1)
    rstd2_f = mean_rstd(ex_end(4, sizes), FINE)
    take_rims(2, FINE, y2)
    second_act(0)
    got = ex_end(3, u_sizes)
    umean_p = got[0:8] * inv_ucount
    urstd_p = lax.rsqrt(got[8:16] * inv_ucount + EPSILON)
    to_columns([umean_p, urstd_p], ucols, [UMEAN, URSTD], u_spans)

    at_top = me_k == 0
    at_bottom = me_k == nk - 1
    fine = W[0]
    split = lambda v: (v.astype(BF16), (v - v.astype(BF16).astype(F32)).astype(BF16))

    def edge(l, n):
        return lax.broadcasted_iota(jnp.int32, (1, n), 1)

    for j in range(3):
        l = j + 1
        m = masks[l][0:1, :] > 0
        hat = (uo[j][...] - ucol(UMEAN, j, NP[l])) * ucol(URSTD, j, NP[l])
        uo[j][...] = hat
        norm = jnp.where(m, hat * ucol(UGAIN, j, NP[l]) + ucol(USHIFT, j, NP[l]), 0.0)
        lane = edge(l, NP[l])
        norm = jnp.where((lane < W[l]) & at_top, pltpu.roll(norm, NP[l] - W[l], 1), norm)
        norm = jnp.where((lane >= W[l] + N[l]) & at_bottom, pltpu.roll(norm, W[l], 1), norm)
        hi, lo = split(norm)
        both = jnp.concatenate([hi, lo], axis=0)
        span = max(128, W[l])
        width = tables[j].shape[1]
        for i in range(NP[l] // span):
            broad = jnp.dot(both[:, span * i : span * i + span], tables[j][...], preferred_element_type=F32)
            up[j][:, width * i : width * i + width] = broad[0:UC_] + broad[UC_:]

    blends = [blend(2 ** (j + 1), R[0]) for j in range(3)]

    def total_body(r0, rc, lanes):
        rows = pl.ds(r0, rc)
        coarse = [{}, {}, {}]
        have = [{}, {}, {}]
        for g in range(R[0]):
            a, b = (g + 1) * fine, (g + 2) * fine
            pre = p1[0][rows, a:b]
            total = pre * sigmoid(pre)
            for j in range(3):
                low, frac = blends[j][g]
                for i in (low, low + 1):
                    if i not in have[j]:
                        have[j][i] = up[j][rows, i * fine : (i + 1) * fine]
                total = total + ((1.0 - frac) * have[j][low] + frac * have[j][low + 1])
            m = masks[0][1:2, a:b] > 0
            sig = sigmoid(total)
            out = jnp.where(m, total * sig, 0.0)
            slope = sig * (1.0 + total * (1.0 - sig))
            spots = [(h, pl.ds(r0 * R[0] + g, rc, stride=R[0])) for h in range(halves(0))]
            grad = jnp.concatenate([stage[h, at, :] for h, at in spots], axis=1)
            grad = jnp.where(m, grad * slope, 0.0)
            for h, at in spots:
                stage[h, at, :] = out[:, 128 * h : 128 * h + 128]
            xf[0][rows, a:b] = grad
            for j in range(3):
                low, frac = blends[j][g]
                for i, weight in ((low, 1.0 - frac), (low + 1, frac)):
                    coarse[j][i] = weight * grad if i not in coarse[j] else coarse[j][i] + weight * grad
                done = [i for i in coarse[j] if g + 1 == R[0] or i < blends[j][g + 1][0]]
                for i in done:
                    up[j][rows, i * fine : (i + 1) * fine] = coarse[j].pop(i)

    def total_step(i, _):
        total_body(pl.multiple_of(i * 16, 16), 16, fine)
        return 0

    lax.fori_loop(0, UC_ // 16, total_step, 0)
    for h in range(halves(0)):
        united_ref[:, 128 * h : 128 * h + 128] = stage[h].astype(BF16)

    for j in range(3):
        l = j + 1
        span = max(128, W[l])
        width = tables[j].shape[1]
        parts = []
        for i in range(NP[l] // span):
            hi, lo = split(up[j][:, width * i : width * i + width])
            both = jnp.concatenate([hi, lo], axis=0)
            narrow = jnp.dot(both, tables_t[j][...], preferred_element_type=F32)
            parts.append(narrow[0:UC_] + narrow[UC_:])
        d = parts[0] if len(parts) == 1 else jnp.concatenate(parts, axis=1)
        lane = edge(l, NP[l])
        fold_top = jnp.where((lane >= W[l]) & (lane < 2 * W[l]) & at_top, pltpu.roll(d, W[l], 1), 0.0)
        fold_bottom = jnp.where(
            (lane >= N[l]) & (lane < W[l] + N[l]) & at_bottom, pltpu.roll(d, NP[l] - W[l], 1), 0.0
        )
        d = d + fold_top + fold_bottom
        d = jnp.where(masks[l][0:1, :] > 0, d, 0.0)
        ustat_a[j * UC_ : (j + 1) * UC_, :] = fold(d * uo[j][...])
        ustat_b[j * UC_ : (j + 1) * UC_, :] = fold(d)
        up[j][:, 0 : NP[l]] = d
    at = 0
    lay = []
    for j in range(3):
        l = j + 1
        n = max(2 * W[l], 128)
        lay.append((at, n))
        mid_s[0, :, at : at + n] = up[j][:, 0:n].astype(BF16)
        mid_s[1, :, at : at + n] = up[j][:, NP[l] - n : NP[l]].astype(BF16)
        at += n
    mid_s[0, :, at : at + fine] = xf[0][:, fine : 2 * fine].astype(BF16)
    mid_s[1, :, at : at + fine] = xf[0][:, N[0] : N[0] + fine].astype(BF16)
    rims_start(8, lambda i: mid_s.at[i], lambda i: mid_r.at[i])
    ex_start(5, record(ustat_a, ustat_b, u_spans))
    second_sums(0)
    ex_mid(5)
    ex_start(6, record(stat_a, stat_b, spans_of[FINE]))
    gather_next(1, 1)
    got = ex_end(5)
    totals_ref[0] = got
    rims_wait(8, lambda i: mid_s.at[i], lambda i: mid_r.at[i])
    to_columns(
        [urstd_p * ugain_p, got[8:16] * inv_ucount, got[0:8] * inv_ucount], ucols, [UA, UB, UC], u_spans
    )
    for i, lane0 in ((0, 0), (1, W[0] + N[0])):
        pre = p1[0][:, lane0 : lane0 + fine]
        sig = sigmoid(pre)
        slope = sig * (1.0 + pre * (1.0 - sig))
        xf[0][:, lane0 : lane0 + fine] = mid_r[i, :, at : at + fine].astype(F32) * slope
    for j in range(3):
        l = j + 1
        start, n = lay[j]
        lane = edge(l, n)
        above = mid_r[0, :, start : start + n].astype(F32)
        below = mid_r[1, :, start : start + n].astype(F32)
        if NP[l] == n:
            above, below = pltpu.roll(above, n // 2, 1), pltpu.roll(below, n // 2, 1)
            d = up[j][:, 0:n]
            d = d + jnp.where((lane < 2 * W[l]) & (me_k > 0), above, 0.0)
            d = d + jnp.where((lane >= n - 2 * W[l]) & (me_k < nk - 1), below, 0.0)
            up[j][:, 0:n] = d
        else:
            up[j][:, 0:n] = up[j][:, 0:n] + jnp.where((lane >= 0) & (me_k > 0), above, 0.0)
            up[j][:, NP[l] - n : NP[l]] = up[j][:, NP[l] - n : NP[l]] + jnp.where(
                (lane >= 0) & (me_k < nk - 1), below, 0.0
            )
    for j in range(3):
        l = j + 1
        d = up[j][:, 0 : NP[l]]
        g = ucol(UA, j, NP[l]) * (d - ucol(UB, j, NP[l]) - uo[j][...] * ucol(UC, j, NP[l]))
        g = jnp.where(masks[l][0:1, :] > 0, g, 0.0)
        low = g.astype(BF16)
        xf[l][...] = jnp.dot(unites[j][...].T, low, preferred_element_type=F32)
        own = jnp.where(masks[l][1:2, :] > 0, g, 0.0).astype(BF16)
        gun[j][:, 0 : C[l]] = lax.dot_general(
            own, br[j][...], (((1,), (1,)), ((), ())), preferred_element_type=F32
        )

    for l in COARSE:
        second_sums(l)
    ex_start(7, record(stat_a, stat_b, spans_of[COARSE]))
    ex_mid(6)
    got_f = ex_end(6)
    norm_columns(rstd2_f * gain2_p, got_f, FINE)
    norm_grad(0, y2, xf)
    ex_mid(7)
    conv(0, wide, 1, g3, p1, -1)
    first_sums(0)
    send_rims(3, FINE, p1)
    ex_start(8, record(stat_a, stat_b, spans_of[FINE]))
    sum_level(1, 0, a3)
    sum_pack_unites()
    sum_first(1, 0)
    got = ex_end(7)
    totals_ref[1] = jnp.where(jnp.concatenate([fine_place] * 2, axis=0), got_f, got)
    norm_columns(rstd2_c * gain2_p, got, COARSE)
    norm_grad(1, y2, xf)
    for l in sz.sum_levels[1:]:
        if l == 2:
            norm_grad(2, y2, xf)
        sum_level(1, l, a3)
    sum_first(1, 1)
    if sz.pair:
        norm_grad(2, y2, xf)
    pair_grad_begin(1)
    norm_grad(3, y2, xf)
    grad_begin(1)

    for l in COARSE:
        conv(l, wide, 1, g3, p1, -1)
    for l in COARSE:
        first_sums(l)
    send_rims(3, COARSE, p1)
    ex_start(9, record(stat_a, stat_b, spans_of[COARSE]))
    ex_mid(8)
    pair_gradient(1)
    ex_mid(9)
    sum_second(1)
    grad_next(1)
    gather_next(0, 2)
    gather_next(1, 2)
    got_f = ex_end(8)
    take_rims(3, FINE, p1)
    norm_columns(rstd1_f * gain1_p, got_f, FINE)
    norm_grad(0, y1, p1)
    sum_level(0, 0, x3)
    sum_first(0, 0)
    sum_third(1)
    grad_third(1)
    got = ex_end(9)
    totals_ref[2] = jnp.where(jnp.concatenate([fine_place] * 2, axis=0), got_f, got)
    take_rims(3, COARSE, p1)
    norm_columns(rstd1_c * gain1_p, got, COARSE)
    norm_grad(1, y1, p1)
    for l in sz.sum_levels[1:]:
        if l == 2:
            norm_grad(2, y1, p1)
        sum_level(0, l, x3)
    sum_first(0, 1)
    if sz.pair:
        norm_grad(2, y1, p1)
    pair_grad_begin(0)
    norm_grad(3, y1, p1)
    grad_begin(0)
    sum_fourth(1)

    conv(0, wide, 0, g3, y1, -1)
    features_out(0)
    pair_gradient(0)
    sum_second(0)
    grad_next(0)
    for l in (1, 2):
        conv(l, wide, 0, g3, y1, -1)
        features_out(l)
    sum_fifth(1)
    sum_third(0)
    conv(3, wide, 0, g3, y1, -1)
    features_out(3)
    grad_third(0)
    coarse_gradient(1)
    sum_fourth(0)
    coarse_gradient(0)
    sum_fifth(0)
    sum_last(1)
    sum_last(0)
    for c in range(2):
        pltpu.make_async_copy(got_d.at[c], sums_ref.at[c], out_sem.at[c]).wait()


def last_kernel(sz, nb, *refs):
    it = iter(refs)
    take = lambda n: [next(it) for _ in range(n)]
    maps = take(5)
    sums_in, totals, coarse_in = take(3)
    maps_out = take(5)
    kernels = take(4)
    unites = take(3)
    norm_gains, norm_shifts, unite_gains, unite_shifts = take(4)
    held = take(5)
    sums, coarse, in_sem, out_sem = take(4)
    C = sz.chan
    arrivals = [pltpu.make_async_copy(sums_in, sums, in_sem.at[0])]
    arrivals += [pltpu.make_async_copy(a, b, in_sem.at[1 + i]) for i, (a, b) in enumerate(zip(maps, held))]
    arrivals += [pltpu.make_async_copy(coarse_in.at[c], coarse.at[c], in_sem.at[6 + c]) for c in range(2)]
    for copy in arrivals:
        copy.start()
    leaving = [pltpu.make_async_copy(a, b, out_sem.at[i]) for i, (a, b) in enumerate(zip(held, maps_out))]
    if sz.gather:
        leaving += [
            pltpu.make_async_copy(coarse.at[c], kernels[3].at[c], out_sem.at[5 + c]) for c in range(2)
        ]

    for row, which in ((0, 2), (1, 1)):
        for k in range(sz.blocks):
            m = min(128, sz.total - 128 * k)
            for ref, base in ((norm_gains, 0), (norm_shifts, 8)):
                ref[row : row + 1, 128 * k : 128 * k + m] = totals[which, base + k : base + k + 1, 0:m]
    for ref, base in ((unite_gains, 0), (unite_shifts, 8)):
        v = jnp.concatenate([totals[0, base + k : base + k + 1, :] for k in range(sz.ublocks)], axis=1)
        for j in range(3):
            ref[j : j + 1, :] = v[:, j * sz.uchan : (j + 1) * sz.uchan]

    arrivals[0].wait()
    for i in range(5):
        arrivals[1 + i].wait()
        leaving[i].start()
    for l in range(LEVELS):
        n = C[l] // nb
        if l == 3:
            for c in range(2):
                arrivals[6 + c].wait()
                if sz.gather:
                    leaving[5 + c].start()
        for c in range(2):
            if l == 2 and sz.pair:
                at, rows = sz.spots[2, C[2] // 128]
                block = sums[c, at : at + rows, :].astype(F32)
                parts = []
                for i in range(C[2] // 128):
                    at, rows = sz.spots[2, i]
                    parts.append(sums[c, at : at + rows, :].astype(F32))
                parts.append(jnp.concatenate([block[:, 0:64], block[:, 64:128]], axis=0)[0 : 9 * n])
                v = jnp.concatenate(parts, axis=1)
            elif (l, 0) in sz.spots:
                parts = []
                for i in range(-(-3 * C[l] // 128)):
                    at, rows = sz.spots[l, i]
                    parts.append(sums[c, at : at + rows, :].astype(F32))
                v = jnp.concatenate(parts, axis=1)
            for t in range(3):
                for u in range(3):
                    at = (3 * t + u) * n
                    if l == 3 and sz.gather:
                        continue
                    if l == 3:
                        kernels[3][c, at : at + n, :] = coarse[c, t * n : (t + 1) * n, u * C[3] : (u + 1) * C[3]]
                    elif l == 2 and sz.pair:
                        kernels[2][c, t, u] = v[at : at + n]
                    else:
                        w = v[t * n : (t + 1) * n, u * C[l] : (u + 1) * C[l]]
                        if l == 0:
                            kernels[0][t, u, :, c, :] = w
                        else:
                            kernels[l][c, t, u] = w
    n = sz.uchan // nb
    for j in range(3):
        width = C[j + 1]
        for i in range(-(-width // 128)):
            at, _ = sz.spots["u", j, i]
            m = min(128, width - 128 * i)
            unites[j][:, 128 * i : 128 * i + m] = sums[1, at : at + n, 0:m].astype(F32)
    for copy in leaving:
        copy.wait()


def body(*args):
    features = args[0:4]
    blocks = args[4:8]
    unites = args[8:11]
    norm_gains, norm_shifts, unite_gains, unite_shifts, output_grad, heights, widths, item_slot = args[11:]
    nb = lax.axis_size("batch")
    nk = lax.axis_size("rows")
    sz = Sizes(features, nb, nk)
    C, R, W, N, NP = sz.chan, sz.rows, sz.width, sz.own, sz.flat

    flat = [
        f.reshape(C[l] * R[l], W[l]) if W[l] >= 128 else f.transpose(0, 2, 3, 1).reshape(N[l], C[l])
        for l, f in enumerate(features)
    ]
    ograd = output_grad.reshape(C[0] * R[0], W[0])
    blocks = [b.reshape(2, 3, 3 * C[l], C[l]) for l, b in enumerate(blocks)]

    tables = [column_table(W[l], W[0]) for l in range(1, 4)]
    operands = [heights, widths, item_slot, *flat, ograd, *blocks, *unites]
    operands += [norm_gains, norm_shifts, unite_gains, unite_shifts]
    operands += [jnp.asarray(t, BF16) for t in tables] + [jnp.asarray(t.T, BF16) for t in tables]

    shape = jax.ShapeDtypeStruct
    map_shapes = [(C[0] * R[0], W[0])]
    map_shapes += [(C[l] * R[l], W[l]) if W[l] >= 128 else (N[l], C[l]) for l in range(4)]
    outs = [shape(m, BF16) for m in map_shapes]
    outs += [shape((2, sz.sum_rows, 128), BF16)]
    outs += [shape((2, 9 * C[3] // nb, C[3]) if sz.gather else (2, 3 * C[3], 3 * C[3]), F32)]
    outs += [shape((3, 16, 128), F32)]
    vm = pltpu.VMEM
    scratch = [
        vm((3, 3 * C[l], C[l]), BF16) for l in range(3 if sz.gather else 4)
    ]
    scratch += [vm((2, 3 * C[l], 3 * C[l]), BF16) for l in range(4)]
    scratch += [vm((max(1, W[0] // 128), C[0] * R[0], 128), F32)]
    for _ in range(3):
        scratch += [vm((3 * C[l], NP[l]), BF16) for l in range(4)]
    scratch += [vm((3 * C[l], NP[l]), BF16) for l in sz.stacked]
    n = C[3] // nb
    scratch += [vm((2, 3 * n, C[3]) if sz.gather else (1, n, 3 * C[3]), F32), pltpu.SemaphoreType.DMA((2,))]
    top = C[sz.sum_levels[-1]]
    scratch += [vm((3 * top, -(-3 * top // 128) * 128), F32)]
    scratch += [vm((sz.uchan, -(-C[l] // 128) * 128), F32) for l in range(1, 4)]
    for _ in range(4):
        scratch += [vm((C[l], NP[l]), F32) for l in range(4)]
    scratch += [vm((C[l], NP[l]), BF16) for l in range(1, 4)]
    scratch += [vm((sz.uchan, NP[l]), F32) for l in range(1, 4)]
    scratch += [vm((sz.uchan, (R[l] + 2) * W[0]), F32) for l in range(1, 4)]
    scratch += [
        vm((N_COLS, sz.blocks * 128, 128), F32),
        vm((N_UCOLS, sz.ublocks * 128, 128), F32),
        vm((sz.blocks * 128, 128), F32),
        vm((sz.blocks * 128, 128), F32),
        vm((sz.ublocks * 128, 128), F32),
        vm((sz.ublocks * 128, 128), F32),
        vm((nb, 8, 128), F32),
        vm((nk, 8, 128), F32),
        vm((nb, 8, 128), F32),
        vm((nk, 8, 128), F32),
    ]
    scratch += [vm((8, NP[l]), F32) for l in range(4)]
    mid = sum(max(2 * W[l], 128) for l in range(1, 4)) + W[0]
    scratch += [
        vm((10, nb, 16, 128), F32),
        vm((10, nk, 16, 128), F32),
        vm((2, sz.rim_total, 128), BF16),
        vm((4, 2, sz.rim_total, 128), BF16),
        vm((2, sz.uchan, mid), BF16),
        vm((2, sz.uchan, mid), BF16),
        pltpu.SemaphoreType.DMA((10, nb)),
        pltpu.SemaphoreType.DMA((10, nb)),
        pltpu.SemaphoreType.DMA((10, nk)),
        pltpu.SemaphoreType.DMA((10, nk)),
        pltpu.SemaphoreType.DMA((9, 2)),
        pltpu.SemaphoreType.DMA((9, 2)),
        pltpu.SemaphoreType.DMA((4, 2)),
        pltpu.SemaphoreType.DMA((2, 9)),
        vm((8, sz.blocks * 128), F32),
        vm((8, sz.ublocks * 128), F32),
        vm((2, nb, sz.batch_rows, 128), BF16),
        vm((2, nb, sz.batch_rows, 128), BF16),
        vm((2, sz.sum_rows, 128), BF16),
        vm((2, sz.nz * sz.part, 128), BF16),
        vm((2, sz.nz, sz.part, 128), BF16),
        vm((2, sz.sum_rows, 128), BF16),
        pltpu.SemaphoreType.DMA((2,)),
    ]
    sems = pltpu.SemaphoreType.DMA
    scratch += [sems((2, 2, nb))] * 2 + [sems((2,))] * 2 + [sems((2, sz.nz))] * 4
    scratch += [sems((2,))] * 2
    if sz.gather:
        half = C[3] // nb // 2
        most = max(sz.nz, sz.nx, sz.ny, sz.nc)
        scratch += [
            vm((2, sz.nx, sz.nz, C[3] // 2, 128), BF16),
            vm((2, sz.nc, sz.ny, C[3], 128 * sz.nz), BF16),
            vm((2, nb, half, 128), BF16),
            vm((2, sz.nx, sz.nz, nb, half, 128), BF16),
            vm((3, 3 * C[3], max(C[3], 128 * sz.nz)), BF16),
            sems((2, 4, most)),
            sems((2, 4, most)),
            sems((2, nb)),
            sems((2, nb)),
            sems((2, sz.nz)),
            sems((2, sz.nz)),
            sems((2,)),
            sems((2,)),
        ]
    if sz.pair:
        c2 = C[2] // nb
        scratch += [
            vm((2, sz.nc, sz.ny, C[2], NP[2]), BF16),
            vm((2, nb, c2, N[2]), BF16),
            vm((2, nb, c2, N[2]), BF16),
            vm((nb, 9 * c2, NP[2]), BF16),
            sems((2, 2, max(sz.ny, sz.nc))),
            sems((2, 2, max(sz.ny, sz.nc))),
            sems((2, nb)),
            sems((2, nb)),
        ]
    in_vmem = pl.BlockSpec(memory_space=pltpu.VMEM)
    in_smem = pl.BlockSpec(memory_space=pltpu.SMEM)
    got = pl.pallas_call(
        functools.partial(main_kernel, sz, nb, nk),
        out_shape=outs,
        in_specs=[in_smem] * 3
        + [in_vmem] * 5
        + [pl.BlockSpec(memory_space=pl.ANY)] * 4
        + [in_vmem] * (len(operands) - 12),
        out_specs=[in_vmem] * 5
        + [pl.BlockSpec(memory_space=pl.ANY)] * 2
        + [in_vmem],
        scratch_shapes=scratch,
        compiler_params=pltpu.CompilerParams(
            collective_id=0, has_side_effects=True, vmem_limit_bytes=60 * 2**20
        ),
    )(*operands)

    maps, sums, totals = got[0:5], got[5], got[-1]
    coarse = got[6]
    if not sz.gather:
        coarse = coarse.astype(BF16).reshape(2, 3, C[3], 3 * C[3])
        coarse = lax.psum(coarse, "rows")
        coarse = lax.psum_scatter(coarse, "batch", scatter_dimension=2, tiled=True)
        coarse = coarse.astype(F32).reshape(2, 3 * C[3] // nb, 3 * C[3])
    in_any = pl.BlockSpec(memory_space=pl.ANY)
    outs = [shape(m, BF16) for m in map_shapes]
    outs += [shape((3, 3, C[0] // nb, 2, C[0]), F32)]
    outs += [shape((2, 3, 3, C[l] // nb, C[l]), F32) for l in (1, 2)]
    outs += [shape((2, 9 * C[3] // nb, C[3]), F32)]
    outs += [shape((sz.uchan // nb, C[l]), F32) for l in range(1, 4)]
    outs += [shape((2, sz.total), F32)] * 2 + [shape((3, sz.uchan), F32)] * 2
    outs = pl.pallas_call(
        functools.partial(last_kernel, sz, nb),
        out_shape=outs,
        in_specs=[in_any] * 6 + [in_vmem] + [in_any],
        out_specs=[in_any] * 5
        + [in_vmem] * 3
        + [in_any if sz.gather else in_vmem]
        + [in_vmem] * (len(outs) - 9),
        scratch_shapes=[vm(m, BF16) for m in map_shapes]
        + [
            vm(sums.shape, BF16),
            vm(coarse.shape, F32),
            pltpu.SemaphoreType.DMA((8,)),
            pltpu.SemaphoreType.DMA((7,)),
        ],
        compiler_params=pltpu.CompilerParams(vmem_limit_bytes=60 * 2**20),
    )(*maps, sums, totals, coarse)
    outs = list(outs)
    outs[5] = outs[5].transpose(3, 0, 1, 2, 4)
    outs[8] = outs[8].reshape(2, 3, 3, C[3] // nb, C[3])
    shaped = []
    for i, m in enumerate(outs[0:5]):
        l = max(i - 1, 0)
        if W[l] >= 128:
            shaped.append(m.reshape(1, C[l], R[l], W[l]))
        else:
            shaped.append(m.reshape(1, R[l], W[l], C[l]).transpose(0, 3, 1, 2))
    return (*shaped, *outs[5:])


def solution(mesh):
    image = P("batch", None, "rows", None)
    kernel = P(None, None, None, "batch", None)
    return jax.shard_map(
        body,
        mesh=mesh,
        in_specs=(image,) * 4 + (P(),) * 11 + (image,) + (P(),) * 3,
        out_specs=(image,) * 5 + (kernel,) * 4 + (P("batch", None),) * 3 + (P(),) * 4,
        check_vma=False,
    )
```

```python
import functools

import jax
import jax.numpy as jnp
import numpy as np
from jax import lax
from jax.experimental import pallas as pl
from jax.experimental.pallas import tpu as pltpu
from jax.sharding import PartitionSpec as P

EPSILON = 1e-05
LEVELS = 4
MESH = pl.DeviceIdType.MESH
F32 = jnp.float32
BF16 = jnp.bfloat16

MEAN, RSTD, GAIN1, SHIFT1, GAIN2, SHIFT2, LOCAL, N_COLS = range(8)
CA, CB, CC = MEAN, RSTD, LOCAL
UMEAN, URSTD, UGAIN, USHIFT, ULOCAL, UA, UB, UC, N_UCOLS = range(9)


class Sizes:
    def __init__(self, features, nb, nk):
        self.chan = [f.shape[1] for f in features]
        self.rows = [f.shape[2] for f in features]
        self.width = [f.shape[3] for f in features]
        self.own = [r * w for r, w in zip(self.rows, self.width)]
        self.flat = [(r + 2) * w for r, w in zip(self.rows, self.width)]
        self.off = [sum(self.chan[:l]) for l in range(LEVELS)]
        self.total = sum(self.chan)
        self.blocks = -(-self.total // 128)
        self.uchan = self.chan[0]
        self.utotal = 3 * self.uchan
        self.ublocks = -(-self.utotal // 128)
        self.rim_rows = [c * w // 128 for c, w in zip(self.chan, self.width)]
        self.rim_off = [sum(self.rim_rows[:l]) for l in range(LEVELS)]
        self.rim_total = sum(self.rim_rows)
        self.chunk = []
        for c, n, w in zip(self.chan, self.flat, self.width):
            lanes = max(x for x in range(128, 641, 128) if n % x == 0 and x % w == 0)
            rows = max(r for r in (16, 32, 48) if c % r == 0 and r * lanes <= 12288)
            self.chunk.append((rows, lanes))
        self.nc = 2 if nb % 2 == 0 else 1
        self.nx = 2 if nk % 2 == 0 else 1
        self.ny = nb // self.nc
        self.nz = nk // self.nx
        self.gather = nb * nk <= 32 and self.nx == 2 and self.nc == 2 and self.own[3] == 64
        self.pair = self.gather and self.chan[2] // nb % 16 == 0 and self.chan[2] % 128 == 64
        self.sum_levels = [0, 1] if self.pair else [0, 1, 2]
        self.stacked = [l for l in range(3 if self.gather else 4) if self.width[l] < 128]
        self.stacked = [l for l in self.stacked if not (self.pair and l == 2)]
        self.start, self.spots, self.moves = {}, {}, []

        def place(table, at, key, values, width):
            rows = -(-values // 16) * 16
            for i in range(-(-width // 128)):
                table[(*key, i)] = (at, rows)
                at += rows
            return at

        def place_kernels(table, at, levels):
            for l in levels:
                at = place(table, at, (l,), 3 * self.chan[l] // nb, 3 * self.chan[l])
            return at

        def place_unites(table, at):
            for j in range(3):
                at = place(table, at, ("u", j), self.uchan // nb, self.chan[j + 1])
            return at

        ends = [0, place_kernels(self.start, 0, [0])]
        ends.append(place_unites(self.start, ends[-1]))
        ends.append(place_kernels(self.start, ends[-1], self.sum_levels[1:]))
        self.early_rows, self.batch_rows = ends[2], ends[3]
        at = place_kernels(self.spots, 0, self.sum_levels)
        if self.pair:
            rows = 9 * self.chan[2] // nb
            for i in range(self.chan[2] // 128):
                self.spots[2, i] = (at, rows)
                at += rows
            rows = -(-rows // 32) * 16
            self.spots[2, self.chan[2] // 128] = (at, rows)
            at += rows
        rows_of = [at, place_unites(self.spots, at)]
        self.part = [-(-r // (nk * 16)) * 16 for r in rows_of]
        self.sum_rows = max(self.part) * nk
        kernels_end = ends[3] - ends[2]
        self.moves = [(0, 0, ends[1]), (ends[2], ends[1], kernels_end), (ends[1], at, ends[2] - ends[1])]


def blend(scale, rows):
    out = []
    for g in range(rows):
        num = 2 * g + 1 - scale
        low = num // (2 * scale)
        out.append((low + 1, (num - 2 * scale * low) / (2.0 * scale)))
    return out


def column_table(width, fine):
    scale = fine // width
    group = max(1, 128 // width)
    span = max(128, width)
    table = np.zeros((span, group * fine), np.float32)
    for r in range(group):
        for g in range(fine):
            num = 2 * g + 1 - scale
            low = 0 if num < 0 else num // (2 * scale)
            frac = 0.0 if num < 0 else (num - 2 * scale * low) / (2.0 * scale)
            high = min(low + 1, width - 1)
            table[r * width + low, r * fine + g] += 1.0 - frac
            table[r * width + high, r * fine + g] += frac
    return table


def sigmoid(v):
    return jax.nn.sigmoid(v)


def main_kernel(sz, nb, nk, *refs):
    it = iter(refs)
    take = lambda n: [next(it) for _ in range(n)]
    heights, widths, slots = take(3)
    feats = take(4)
    (ograd,) = take(1)
    blocks = take(4)
    unites = take(3)
    norm_gains, norm_shifts, unite_gains, unite_shifts = take(4)
    tables = take(3)
    tables_t = take(3)
    (united_ref,) = take(1)
    gfeat = take(4)
    (sums_ref,) = take(1)
    (coarse_ref,) = take(1)
    (totals_ref,) = take(1)
    raw = take(3 if sz.gather else 4)
    wide = take(4)
    (stage,) = take(1)
    x3 = take(4)
    a3 = take(4)
    g3 = take(4)
    t3 = dict(zip(sz.stacked, take(len(sz.stacked))))
    cstage, cstage_sem = take(2)
    (kg,) = take(1)
    gun = take(3)
    xf = take(4)
    y1 = take(4)
    y2 = take(4)
    p1 = take(4)
    br = take(3)
    uo = take(3)
    up = take(3)
    (cols, ucols, stat_a, stat_b, ustat_a, ustat_b, n_a, n_b, un_a, un_b) = take(10)
    masks = take(4)
    (rec_a, rec_b, rim_s, rim_r, mid_s, mid_r) = take(6)
    (sa_send, sa_recv, sb_send, sb_recv, rim_send, rim_recv) = take(6)
    raw_sem, wide_sem = take(2)
    prow, urow = take(2)
    part_a, got_a, part_s, got_x, got_z, got_d, out_sem = take(7)
    (ra_send, ra_recv, rx_send, rx_recv, rz_send, rz_recv) = take(6)
    (dz_send, dz_recv, dx_send, dx_recv) = take(4)
    if sz.gather:
        xg, xi, gs, gr, g9 = take(5)
        (xg_send, xg_recv, g1_send, g1_recv, g2_send, g2_recv, g3_send, g3_recv) = take(8)
    if sz.pair:
        xb, gsb, gb, g9b = take(4)
        (xb_send, xb_recv, gb_send, gb_recv) = take(4)

    C, R, W, N, NP, OFF = sz.chan, sz.rows, sz.width, sz.own, sz.flat, sz.off
    me_b = lax.axis_index("batch")
    me_k = lax.axis_index("rows")

    def peer_b(j):
        return lax.rem(me_b + j, nb)

    def peer_k(j):
        return lax.rem(me_k + j, nk)

    def raw_copy(l, which):
        if l == 3 and sz.gather:
            dst = g9.at[:, :, 0 : C[3]]
        else:
            dst = raw[l]
        return pltpu.make_async_copy(blocks[l].at[which], dst, raw_sem.at[l, which])

    def wide_copies(which):
        c = C[3]
        return [
            pltpu.make_async_copy(
                blocks[3].at[which, t, u * c : (u + 1) * c, :],
                wide[3].at[which, t * c : (t + 1) * c, u * c : (u + 1) * c],
                wide_sem.at[which, 3 * t + u],
            )
            for t in range(3)
            for u in range(3)
        ]

    for l in range(3):
        raw_copy(l, 0).start()
    for which in range(2):
        for copy in wide_copies(which):
            copy.start()
    raw_copy(3, 0).start()

    def widen(which):
        for copy in wide_copies(which):
            copy.wait()
        for l in range(3):
            raw_copy(l, which).wait()
            c = C[l]
            for t in range(3):
                wide[l][which, t * c : (t + 1) * c, :] = jnp.concatenate(
                    [raw[l][t, u * c : (u + 1) * c, :] for u in range(3)], axis=1
                )

    def turn(which):
        raw_copy(3, which).wait()
        for l in range(LEVELS):
            for t in range(3):
                if l == 3 and sz.gather:
                    v = g9[t, :, 0 : C[3]]
                else:
                    v = raw[l][t]
                wide[l][which, t * C[l] : (t + 1) * C[l], :] = v.T
        if which == 0:
            for l in range(LEVELS):
                raw_copy(l, 1).start()

    barrier = pltpu.get_barrier_semaphore()
    for j in range(1, nb):
        pl.semaphore_signal(barrier, inc=1, device_id=(peer_b(j), me_k), device_id_type=MESH)
    for j in range(1, nk):
        pl.semaphore_signal(barrier, inc=1, device_id=(me_b, peer_k(j)), device_id_type=MESH)

    my_h = jnp.int32(0)
    my_w = jnp.int32(0)
    slot_h, slot_w = [], []
    for b in range(nb):
        h = jnp.int32(0)
        w = jnp.int32(0)
        for i in range(nb):
            hit = (slots[i] == b).astype(jnp.int32)
            h = h + hit * heights[i]
            w = w + hit * widths[i]
        slot_h.append(h)
        slot_w.append(w)
        mine = (me_b == b).astype(jnp.int32)
        my_h = my_h + mine * h
        my_w = my_w + mine * w

    count = []
    for l in range(LEVELS):
        c = jnp.int32(0)
        for b in range(nb):
            c = c + lax.shift_right_logical(slot_h[b], l) * lax.shift_right_logical(slot_w[b], l)
        count.append(c.astype(F32))
    inv_local = []
    for l in range(LEVELS):
        inside = jnp.clip(lax.shift_right_logical(my_h, l) - me_k * R[l], 0, R[l])
        own = inside * lax.shift_right_logical(my_w, l)
        inv_local.append(1.0 / jnp.maximum(own, 1).astype(F32))
        lane = lax.broadcasted_iota(jnp.int32, (1, NP[l]), 1)
        log_w = W[l].bit_length() - 1
        row = me_k * R[l] + lax.shift_right_logical(lane, log_w) - 1
        col = lane & (W[l] - 1)
        valid = (row >= 0) & (row < lax.shift_right_logical(my_h, l))
        valid = valid & (col < lax.shift_right_logical(my_w, l))
        masks[l][0:1, :] = jnp.where(valid, 1.0, 0.0)
        masks[l][1:2, :] = jnp.where(valid & (lane >= W[l]) & (lane < W[l] + N[l]), 1.0, 0.0)

    place = lax.broadcasted_iota(jnp.int32, (8, 128), 0) * 128 + lax.broadcasted_iota(
        jnp.int32, (8, 128), 1
    )

    def by_level(values):
        out = jnp.full((8, 128), values[3])
        for l in (2, 1, 0):
            out = jnp.where(place < OFF[l + 1], jnp.full((8, 128), values[l]), out)
        return out

    def by_unite(values):
        out = jnp.full((8, 128), values[2])
        for j in (1, 0):
            out = jnp.where(place < (j + 1) * sz.uchan, jnp.full((8, 128), values[j]), out)
        return out

    inv_count = 1.0 / by_level(count)
    inv_ucount = 1.0 / by_unite(count[1:])
    for chooser, levels, na_ref, nb_ref in (
        (by_level, range(4), n_a, n_b),
        (by_unite, range(1, 4), un_a, un_b),
    ):
        span = chooser([jnp.int32(R[l]) for l in levels])
        hv = [chooser([lax.shift_right_logical(h, l) for l in levels]) for h in slot_h]
        wv = [chooser([lax.shift_right_logical(w, l) for l in levels]) for w in slot_w]
        for b in range(nb):
            na_ref[b] = (jnp.clip(hv[b] - me_k * span, 0, span) * wv[b]).astype(F32)
        for k in range(nk):
            n = jnp.zeros((8, 128), jnp.int32)
            for b in range(nb):
                n = n + jnp.clip(hv[b] - k * span, 0, span) * wv[b]
            nb_ref[k] = n.astype(F32)

    def tile(v, lanes):
        return v if lanes == 128 else jnp.concatenate([v] * (lanes // 128), axis=1)

    def col(slot, l, r0, rc, lanes):
        return tile(cols[slot, pl.ds(pl.multiple_of(OFF[l] + r0, 16), rc), :], lanes)

    def ucol(slot, j, lanes):
        return tile(ucols[slot, j * sz.uchan : (j + 1) * sz.uchan, :], lanes)

    def to_columns(packed, ref, slot_list, spans):
        full = jnp.concatenate(packed + [jnp.zeros((128 - 8 * len(packed), 128), F32)], axis=0)
        standing = full.T
        for i, slot in enumerate(slot_list):
            for lo, hi in spans:
                for k in range(lo // 128, -(-hi // 128)):
                    a, b = max(lo, 128 * k), min(hi, 128 * k + 128)
                    v = standing[a - 128 * k : b - 128 * k, 8 * i + k : 8 * i + k + 1]
                    ref[slot, a:b, :] = jnp.broadcast_to(v, (b - a, 128))

    FINE, COARSE = (0,), (1, 2, 3)
    spans_of = {FINE: [(0, C[0])], COARSE: [(C[0], sz.total)]}
    u_spans = [(0, sz.utotal)]

    prow[...] = jnp.zeros_like(prow)
    urow[...] = jnp.zeros_like(urow)
    for i in range(2):
        prow[2 * i : 2 * i + 1, 0 : sz.total] = norm_gains[i : i + 1, :]
        prow[2 * i + 1 : 2 * i + 2, 0 : sz.total] = norm_shifts[i : i + 1, :]
    for j in range(3):
        at = slice(j * sz.uchan, (j + 1) * sz.uchan)
        urow[0:1, at] = unite_gains[j : j + 1, :]
        urow[1:2, at] = unite_shifts[j : j + 1, :]
    standing = prow[...].T
    for i, slot in enumerate((GAIN1, SHIFT1, GAIN2, SHIFT2)):
        cols[slot] = jnp.broadcast_to(standing[:, i : i + 1], (sz.blocks * 128, 128))
    standing = urow[...].T
    for i, slot in enumerate((UGAIN, USHIFT)):
        ucols[slot] = jnp.broadcast_to(standing[:, i : i + 1], (sz.ublocks * 128, 128))

    def packed(ref, i, blocks):
        rows = [ref[i : i + 1, 128 * k : 128 * k + 128] for k in range(blocks)]
        return jnp.concatenate(rows + [jnp.zeros((8 - blocks, 128), F32)], axis=0)

    gain1_p, gain2_p = packed(prow, 0, sz.blocks), packed(prow, 2, sz.blocks)
    ugain_p = packed(urow, 0, sz.ublocks)
    stat_a[...] = jnp.zeros_like(stat_a)
    stat_b[...] = jnp.zeros_like(stat_b)
    ustat_a[...] = jnp.zeros_like(ustat_a)
    ustat_b[...] = jnp.zeros_like(ustat_b)

    def fold(v):
        out = v[:, 0:128]
        for i in range(1, v.shape[1] // 128):
            out = out + v[:, 128 * i : 128 * i + 128]
        return out

    lane128 = lax.broadcasted_iota(jnp.int32, (1, 128), 1)

    def record(a_ref, b_ref, spans):
        out = jnp.zeros((128, 128), F32)
        for base, ref in ((0, a_ref), (8, b_ref)):
            for lo, hi in spans:
                for k in range(lo // 128, -(-hi // 128)):
                    s = jnp.sum(ref[128 * k : 128 * k + 128, :], axis=1, keepdims=True)
                    out = jnp.where(lane128 == base + k, s, out)
        return out.T[0:16]

    def record_copies(e, which, sending):
        if which == 0:
            ref, send, recv, n, me = rec_a, sa_send, sa_recv, nb, me_b
        else:
            ref, send, recv, n, me = rec_b, sb_send, sb_recv, nk, me_k
        out = []
        for j in range(1, n):
            other = lax.rem(me + j, n)
            slot = me if sending else other
            out.append(
                pltpu.make_async_remote_copy(
                    src_ref=ref.at[e, me],
                    dst_ref=ref.at[e, slot],
                    send_sem=send.at[e, other],
                    recv_sem=recv.at[e, slot],
                    device_id=(other, me_k) if which == 0 else (me_b, other),
                    device_id_type=MESH,
                )
            )
        return out

    def record_send(e, which, rec):
        if which == 0:
            rec_a[e, me_b] = rec
        else:
            rec_b[e, me_k] = rec
        for copy in record_copies(e, which, True):
            copy.start()

    def record_total(e, which, sizes):
        for copy in record_copies(e, which, False):
            copy.wait_recv()
        for copy in record_copies(e, which, True):
            copy.wait_send()
        ref, n = ((rec_a, nb), (rec_b, nk))[which]
        if sizes is None:
            out = ref[e, 0]
            for i in range(1, n):
                out = out + ref[e, i]
            return out
        total = jnp.zeros((8, 128), F32)
        size = jnp.zeros((8, 128), F32)
        for i in range(n):
            total = total + ref[e, i, 0:8]
            size = size + sizes[which][i]
        mean = total / jnp.maximum(size, 1.0)
        spread_sum = jnp.zeros((8, 128), F32)
        for i in range(n):
            delta = ref[e, i, 0:8] / jnp.maximum(sizes[which][i], 1.0) - mean
            spread_sum = spread_sum + (ref[e, i, 8:16] + sizes[which][i] * delta * delta)
        return jnp.concatenate([total, spread_sum], axis=0)

    def ex_start(e, rec):
        record_send(e, 0, rec)

    def ex_mid(e, sizes=None):
        record_send(e, 1, record_total(e, 0, sizes))

    def ex_end(e, sizes=None):
        return record_total(e, 1, sizes)

    def rim_copies(slot, src, dst):
        up = pltpu.make_async_remote_copy(
            src_ref=src(0),
            dst_ref=dst(1),
            send_sem=rim_send.at[slot, 0],
            recv_sem=rim_recv.at[slot, 1],
            device_id=(me_b, lax.rem(me_k + nk - 1, nk)),
            device_id_type=MESH,
        )
        down = pltpu.make_async_remote_copy(
            src_ref=src(1),
            dst_ref=dst(0),
            send_sem=rim_send.at[slot, 1],
            recv_sem=rim_recv.at[slot, 0],
            device_id=(me_b, lax.rem(me_k + 1, nk)),
            device_id_type=MESH,
        )
        return up, down

    def rims_start(slot, src, dst):
        up, down = rim_copies(slot, src, dst)

        @pl.when(me_k > 0)
        def _():
            up.start()

        @pl.when(me_k < nk - 1)
        def _():
            down.start()

    def rims_wait(slot, src, dst):
        up, down = rim_copies(slot, src, dst)

        @pl.when(me_k > 0)
        def _():
            down.wait_recv()
            up.wait_send()

        @pl.when(me_k < nk - 1)
        def _():
            up.wait_recv()
            down.wait_send()

    def pack_row(ref, l, lane0):
        if W[l] >= 128:
            return jnp.concatenate(
                [ref[:, lane0 + 128 * i : lane0 + 128 * i + 128] for i in range(W[l] // 128)], axis=0
            )
        group = 128 // W[l]
        rows = C[l] // group
        base, shift = lane0 // 128 * 128, lane0 % 128
        out = None
        for g in range(group):
            v = ref[g * rows : (g + 1) * rows, base : base + 128]
            turn = (g * W[l] - shift) % 128
            v = pltpu.roll(v, turn, 1) if turn else v
            out = v if out is None else jnp.where(lane128 >= g * W[l], v, out)
        return out

    def unpack_row(ref, l, lane0, q):
        if W[l] >= 128:
            for i in range(W[l] // 128):
                ref[:, lane0 + 128 * i : lane0 + 128 * i + 128] = q[i * C[l] : (i + 1) * C[l]]
            return
        group = 128 // W[l]
        rows = C[l] // group
        base, shift = lane0 // 128 * 128, lane0 % 128
        here = (lane128 >= shift) & (lane128 < shift + W[l])
        for g in range(group):
            turn = (shift - g * W[l]) % 128
            v = pltpu.roll(q, turn, 1) if turn else q
            old = ref[g * rows : (g + 1) * rows, base : base + 128]
            ref[g * rows : (g + 1) * rows, base : base + 128] = jnp.where(here, v, old)

    def rim_span(group):
        first, last = group[0], group[-1]
        return slice(sz.rim_off[first], sz.rim_off[last] + sz.rim_rows[last])

    def rims_of(slot, group):
        at = rim_span(group)
        number = 2 * slot + (0 if group == FINE else 1)
        return number, lambda i: rim_s.at[i, at, :], lambda i: rim_r.at[slot, i, at, :]

    def send_rims(slot, group, arrays):
        for l in group:
            at = rim_span((l,))
            rim_s[0, at, :] = pack_row(arrays[l], l, W[l]).astype(BF16)
            rim_s[1, at, :] = pack_row(arrays[l], l, N[l]).astype(BF16)
        rims_start(*rims_of(slot, group))

    def take_rims(slot, group, arrays):
        rims_wait(*rims_of(slot, group))
        for l in group:
            at = rim_span((l,))
            unpack_row(arrays[l], l, 0, rim_r[slot, 0, at, :].astype(F32))
            unpack_row(arrays[l], l, W[l] + N[l], rim_r[slot, 1, at, :].astype(F32))

    def each(l, body):
        rc, lanes = sz.chunk[l]

        def step(i, _):
            body(pl.multiple_of(i * rc, rc), rc, lanes)
            return 0

        count = C[l] // rc
        lax.fori_loop(0, count, step, 0, unroll=max(k for k in range(1, 9) if count % k == 0))

    def lane_chunks(l, lanes):
        return [(i, i + lanes) for i in range(0, NP[l], lanes)]

    def stack_columns(ref, l, r0, rc, a, b, v, back=False):
        lanes = b - a
        at = lax.broadcasted_iota(jnp.int32, (1, lanes), 1) & (W[l] - 1)
        left = jnp.where(at == 0, 0.0, pltpu.roll(v, 1, 1))
        right = jnp.where(at == W[l] - 1, 0.0, pltpu.roll(v, lanes - 1, 1))
        for u, part in enumerate((right, v, left) if back else (left, v, right)):
            ref[pl.ds(pl.multiple_of(u * C[l] + r0, 16), rc), a:b] = part.astype(BF16)

    def stack_rows(ref, l, r0, rc, v):
        for t in range(3):
            turn = ((t - 1) * W[l]) % NP[l]
            part = pltpu.roll(v, turn, 1) if turn else v
            ref[pl.ds(pl.multiple_of(t * C[l] + r0, 16), rc), :] = part.astype(BF16)

    def conv(l, w, which, src, dst, sign=1):
        c = C[l]
        if W[l] % 128 == 0:
            span = min(2048, N[l])

            def step(i, _):
                acc = None
                for t in range(3):
                    at = pl.ds(pl.multiple_of(i * span + (1 + sign * (t - 1)) * W[l], 128), span)
                    part = jnp.dot(
                        w[l][which, t * c : (t + 1) * c, :], src[l][:, at], preferred_element_type=F32
                    )
                    acc = part if acc is None else acc + part
                dst[l][:, pl.ds(pl.multiple_of(i * span + W[l], 128), span)] = acc
                return 0

            lax.fori_loop(0, N[l] // span, step, 0)
        else:
            rows = c if c <= 384 else 96

            def step(i, _):
                acc = None
                for t in range(3):
                    at = pl.ds(pl.multiple_of(t * c + i * rows, 16), rows)
                    part = jnp.dot(w[l][which, at, :], src[l][...], preferred_element_type=F32)
                    turn = (sign * (1 - t) * W[l]) % NP[l]
                    part = pltpu.roll(part, turn, 1) if turn else part
                    acc = part if acc is None else acc + part
                dst[l][pl.ds(pl.multiple_of(i * rows, 16), rows), :] = acc
                return 0

            lax.fori_loop(0, c // rows, step, 0)

    def kernel_grad(l, src):
        c = C[l]
        if W[l] % 128 == 0:
            for t in range(3):
                kg[t * c : (t + 1) * c, 0 : 3 * c] = lax.dot_general(
                    g3[l][c : 2 * c, W[l] : W[l] + N[l]],
                    src[l][:, t * W[l] : t * W[l] + N[l]],
                    (((1,), (1,)), ((), ())),
                    preferred_element_type=F32,
                )
            return
        span = 96

        def step(i, _):
            at = pl.ds(pl.multiple_of(i * span, 16), span)
            kg[at, 0 : 3 * c] = lax.dot_general(
                t3[l][at, :], src[l][...], (((1,), (1,)), ((), ())), preferred_element_type=F32
            )
            return 0

        lax.fori_loop(0, 3 * c // span, step, 0)

    nc, ny, nx, nz = sz.nc, sz.ny, sz.nx, sz.nz
    my_core, my_y = lax.rem(me_b, nc), lax.div(me_b, nc)
    my_x, my_z = lax.rem(me_k, nx), lax.div(me_k, nx)

    def others(n, me):
        return [lax.rem(me + j, n) for j in range(1, n)]

    def remote(src, dst, send, recv, target):
        return pltpu.make_async_remote_copy(
            src_ref=src, dst_ref=dst, send_sem=send, recv_sem=recv, device_id=target, device_id_type=MESH
        )

    def sum_pack(c, l):
        n = C[l] // nb
        for q in range(nb):
            dst = part_a.at[c, q]
            for i in range(-(-3 * C[l] // 128)):
                at, rows = sz.start[l, i]
                lanes = slice(128 * i, 128 * i + 128)
                parts = [kg[t * C[l] + q * n : t * C[l] + q * n + n, lanes] for t in range(3)]
                if rows > 3 * n:
                    parts.append(jnp.zeros((rows - 3 * n, 128), F32))
                dst[at : at + rows, :] = jnp.concatenate(parts, axis=0).astype(BF16)

    def sum_pack_unites():
        n = sz.uchan // nb
        for q in range(nb):
            dst = part_a.at[1, q]
            for j in range(3):
                for i in range(-(-C[j + 1] // 128)):
                    at, rows = sz.start["u", j, i]
                    v = gun[j][q * n : q * n + n, 128 * i : 128 * i + 128]
                    if rows > n:
                        v = jnp.concatenate([v, jnp.zeros((rows - n, 128), F32)], axis=0)
                    dst[at : at + rows, :] = v.astype(BF16)

    def batch_copies(c, part, sending):
        rows = (slice(0, sz.early_rows), slice(sz.early_rows, sz.batch_rows))[part]
        out = []
        for other in others(nb, me_b):
            slot = me_b if sending else other
            src, dst = part_a.at[c, other, rows, :], got_a.at[c, slot, rows, :]
            sems = ra_send.at[c, part, other], ra_recv.at[c, part, slot]
            out.append(remote(src, dst, *sems, (other, me_k)))
        return out

    def part_at(c, x, z, n=1):
        return pl.ds(pl.multiple_of((x * nz + z) * sz.part[c], 16), n * sz.part[c])

    def x_copies(c):
        out = []
        for other in others(nx, my_x):
            src = part_s.at[c, part_at(c, other, 0, nz), :]
            target = (me_b, my_z * nx + other)
            out.append(remote(src, got_x.at[c, 0 : nz * sz.part[c], :], rx_send.at[c], rx_recv.at[c], target))
        return out

    def z_copies(c, sending):
        out = []
        for other in others(nz, my_z):
            slot = my_z if sending else other
            src = part_s.at[c, part_at(c, my_x, other), :]
            target = (me_b, other * nx + my_x)
            out.append(remote(src, got_z.at[c, slot, 0 : sz.part[c], :], rz_send.at[c, other], rz_recv.at[c, slot], target))
        return out

    def back_z_copies(c, sending):
        out = []
        for other in others(nz, my_z):
            slot = my_z if sending else other
            src, dst = got_d.at[c, part_at(c, my_x, my_z), :], got_d.at[c, part_at(c, my_x, slot), :]
            target = (me_b, other * nx + my_x)
            out.append(remote(src, dst, dz_send.at[c, other], dz_recv.at[c, slot], target))
        return out

    def back_x_copies(c, sending):
        out = []
        for other in others(nx, my_x):
            slot = my_x if sending else other
            src, dst = got_d.at[c, part_at(c, my_x, 0, nz), :], got_d.at[c, part_at(c, slot, 0, nz), :]
            target = (me_b, my_z * nx + other)
            out.append(remote(src, dst, dx_send.at[c], dx_recv.at[c], target))
        return out

    def finish(pair):
        sent, received = pair
        for copy in received:
            copy.wait_recv()
        for copy in sent:
            copy.wait_send()

    def sum_level(c, l, src):
        kernel_grad(l, src)
        sum_pack(c, l)

    def sum_first(c, part):
        for copy in batch_copies(c, part, True):
            copy.start()

    def sum_second(c):
        for part in range(2):
            finish((batch_copies(c, part, True), batch_copies(c, part, False)))
        got_a[c, me_b] = part_a[c, me_b]
        v = got_a[c, 0].astype(F32)
        for b in range(1, nb):
            v = v + got_a[c, b].astype(F32)
        for src, dst, rows in sz.moves[: 2 + c]:
            part_s[c, dst : dst + rows, :] = v[src : src + rows].astype(BF16)
        for copy in x_copies(c):
            copy.start()

    def sum_third(c):
        copies = x_copies(c)
        finish((copies, copies))
        mine = part_at(c, my_x, 0, nz)
        if nx > 1:
            v = part_s[c, mine, :].astype(F32) + got_x[c, 0 : nz * sz.part[c], :].astype(F32)
            part_s[c, mine, :] = v.astype(BF16)
        for copy in z_copies(c, True):
            copy.start()

    def sum_fourth(c):
        finish((z_copies(c, True), z_copies(c, False)))
        span = slice(0, sz.part[c])
        got_z[c, my_z, span, :] = part_s[c, part_at(c, my_x, my_z), :]
        v = got_z[c, 0, span, :].astype(F32)
        for z in range(1, nz):
            v = v + got_z[c, z, span, :].astype(F32)
        got_d[c, part_at(c, my_x, my_z), :] = v.astype(BF16)
        for copy in back_z_copies(c, True):
            copy.start()

    def sum_fifth(c):
        finish((back_z_copies(c, True), back_z_copies(c, False)))
        for copy in back_x_copies(c, True):
            copy.start()

    def sum_last(c):
        finish((back_x_copies(c, True), back_x_copies(c, False)))
        pltpu.make_async_copy(got_d.at[c], sums_ref.at[c], out_sem.at[c]).start()

    c2 = C[2] // nb

    def pair_copies(c, step, sending):
        if not sz.pair:
            return []
        n, me = ((ny, my_y), (nc, my_core))[step]
        out = []
        for other in others(n, me):
            slot = me if sending else other
            if step == 0:
                ref, target = xb.at[c, my_core, slot], (other * nc + my_core, me_k)
            else:
                ref, target = xb.at[c, slot], (my_y * nc + other, me_k)
            out.append(remote(ref, ref, xb_send.at[c, step, other], xb_recv.at[c, step, slot], target))
        return out

    def pair_begin(c, ref):
        if sz.pair:
            xb[c, my_core, my_y] = ref[2][C[2] : 2 * C[2], :]
            for copy in pair_copies(c, 0, True):
                copy.start()

    def pair_next(c):
        finish((pair_copies(c, 0, True), pair_copies(c, 0, False)))
        for copy in pair_copies(c, 1, True):
            copy.start()

    def pair_grad_copies(c, sending):
        out = []
        for other in others(nb, me_b):
            slot = me_b if sending else other
            out.append(
                remote(gsb.at[c, other], gb.at[c, slot], gb_send.at[c, other], gb_recv.at[c, slot], (other, me_k))
            )
        return out

    def pair_grad_begin(c):
        if sz.pair:
            for q in range(nb):
                v = g3[2][C[2] + q * c2 : C[2] + (q + 1) * c2, :].astype(F32)
                gsb[c, q] = pltpu.roll(v, NP[2] - W[2], 1)[:, 0 : N[2]].astype(BF16)
            for copy in pair_grad_copies(c, True):
                copy.start()

    def nine_shifts(v, width, store):
        lanes = v.shape[1]
        lane = lax.broadcasted_iota(jnp.int32, (1, lanes), 1)
        at = lane & (width - 1)
        left = jnp.where(at == width - 1, 0.0, pltpu.roll(v, lanes - 1, 1))
        right = jnp.where(at == 0, 0.0, pltpu.roll(v, 1, 1))
        for u, part in enumerate((left, v, right)):
            store(0, u, jnp.where(lane >= lanes - width, 0.0, pltpu.roll(part, lanes - width, 1)))
            store(1, u, part)
            store(2, u, jnp.where(lane < width, 0.0, pltpu.roll(part, width, 1)))

    def pair_gradient(c):
        if not sz.pair:
            return
        finish((pair_copies(c, 1, True), pair_copies(c, 1, False)))
        finish((pair_grad_copies(c, True), pair_grad_copies(c, False)))
        gb[c, me_b] = gsb[c, me_b]

        def item(b, _):
            v = jnp.concatenate([gb[c, b].astype(F32), jnp.zeros((c2, NP[2] - N[2]), F32)], axis=1)

            def store(t, u, part):
                at = (3 * t + u) * c2
                g9b[b, at : at + c2, :] = part.astype(BF16)

            nine_shifts(pltpu.roll(v, W[2], 1), W[2], store)
            return 0

        lax.fori_loop(0, nb, item, 0, unroll=True)
        acc = None
        for b in range(nb):
            part = lax.dot_general(
                g9b[b], xb[c, b % nc, b // nc], (((1,), (1,)), ((), ())), preferred_element_type=F32
            )
            acc = part if acc is None else acc + part
        whole = C[2] // 128
        for i in range(whole):
            at, rows = sz.spots[2, i]
            part_s[c, at : at + rows, :] = acc[:, 128 * i : 128 * i + 128].astype(BF16)
        at, rows = sz.spots[2, whole]
        rest = acc[:, 128 * whole :]
        low, high = rest[0:rows], rest[rows:]
        high = jnp.concatenate([high, jnp.zeros((rows - high.shape[0], high.shape[1]), F32)], axis=0)
        part_s[c, at : at + rows, :] = jnp.concatenate([low, high], axis=1).astype(BF16)

    c3 = C[3] // nb
    half = c3 // 2

    def pack_pixels(ref):
        parts = []
        for q in range(nb):
            at = C[3] + q * c3
            low = pltpu.roll(ref[at : at + half, :].astype(F32), 128 - W[3], 1)
            high = pltpu.roll(ref[at + half : at + c3, :].astype(F32), 64 - W[3], 1)
            parts.append(jnp.where(lane128 < 64, low, high))
        return jnp.concatenate(parts, axis=0).astype(BF16)

    def unpack_pixels(first, second):
        first, second = first.astype(F32), second.astype(F32)
        low = jnp.where(lane128 < 64, first, pltpu.roll(second, 64, 1))
        high = jnp.where(lane128 < 64, pltpu.roll(first, 64, 1), second)
        return low, high

    def gather_copies(c, step, sending):
        if not sz.gather:
            return []
        n, me = ((nz, my_z), (nx, my_x), (ny, my_y), (nc, my_core))[step]
        out = []
        for other in others(n, me):
            slot = me if sending else other
            if step == 0:
                ref, target = xg.at[c, my_x, slot], (me_b, other * nx + my_x)
            elif step == 1:
                ref, target = xg.at[c, slot], (me_b, my_z * nx + other)
            elif step == 2:
                ref, target = xi.at[c, my_core, slot], (other * nc + my_core, me_k)
            else:
                ref, target = xi.at[c, slot], (my_y * nc + other, me_k)
            out.append(remote(ref, ref, xg_send.at[c, step, other], xg_recv.at[c, step, slot], target))
        return out

    def gather_start(c, step):
        for copy in gather_copies(c, step, True):
            copy.start()

    def gather_wait(c, step):
        finish((gather_copies(c, step, True), gather_copies(c, step, False)))

    def gather_begin(c, ref):
        if sz.gather:
            xg[c, my_x, my_z] = pack_pixels(ref[3])
            gather_start(c, 0)

    def gather_next(c, step):
        gather_wait(c, step)
        if step == 1 and sz.gather:
            for z in range(nz):
                for q in range(nb):
                    rows = slice(q * half, (q + 1) * half)
                    pair = unpack_pixels(xg[c, 0, z, rows, :], xg[c, 1, z, rows, :])
                    for i, v in enumerate(pair):
                        at = q * c3 + i * half
                        xi[c, my_core, my_y, at : at + half, 128 * z : 128 * z + 128] = v.astype(BF16)
        gather_start(c, step + 1)

    def grad_copies(c, step, sending):
        out = []
        if step == 0:
            for other in others(nb, me_b):
                slot = me_b if sending else other
                src = gs.at[c, other]
                out.append(
                    remote(src, gr.at[c, my_x, my_z, slot], g1_send.at[c, other], g1_recv.at[c, slot], (other, me_k))
                )
        elif step == 1:
            for other in others(nz, my_z):
                slot = my_z if sending else other
                src, dst = gr.at[c, my_x, my_z], gr.at[c, my_x, slot]
                target = (me_b, other * nx + my_x)
                out.append(remote(src, dst, g2_send.at[c, other], g2_recv.at[c, slot], target))
        else:
            for other in others(nx, my_x):
                slot = my_x if sending else other
                src, dst = gr.at[c, my_x], gr.at[c, slot]
                target = (me_b, my_z * nx + other)
                out.append(remote(src, dst, g3_send.at[c], g3_recv.at[c], target))
        return out

    def grad_begin(c):
        if sz.gather:
            v = pack_pixels(g3[3])
            for q in range(nb):
                gs[c, q] = v[q * half : (q + 1) * half]
            for copy in grad_copies(c, 0, True):
                copy.start()

    def grad_next(c):
        if sz.gather:
            finish((grad_copies(c, 0, True), grad_copies(c, 0, False)))
            gr[c, my_x, my_z, me_b] = gs[c, me_b]
            for copy in grad_copies(c, 1, True):
                copy.start()

    def grad_third(c):
        if sz.gather:
            finish((grad_copies(c, 1, True), grad_copies(c, 1, False)))
            for copy in grad_copies(c, 2, True):
                copy.start()

    image = nz * 128

    def coarse_copy(c, i):
        n = 3 * c3
        at = pl.ds(i * n if isinstance(i, int) else pl.multiple_of(i * n, 16), n)
        slot = i % 2 if isinstance(i, int) else lax.rem(i, 2)
        return pltpu.make_async_copy(cstage.at[slot], coarse_ref.at[c, at, :], cstage_sem.at[slot])

    def coarse_local(c, src):
        def step(i, _):
            at = pl.ds(pl.multiple_of(i * c3, 16), c3)
            cstage[0] = lax.dot_general(
                t3[3][at, :], src[3][...], (((1,), (1,)), ((), ())), preferred_element_type=F32
            )
            copy = pltpu.make_async_copy(cstage.at[0], coarse_ref.at[c, at, :], cstage_sem.at[0])
            copy.start()
            copy.wait()
            return 0

        lax.fori_loop(0, 3 * nb, step, 0)

    def coarse_gradient(c):
        if not sz.gather:
            coarse_local(c, a3 if c else x3)
            return
        gather_wait(c, 3)
        finish((grad_copies(c, 2, True), grad_copies(c, 2, False)))

        def item(b, _):
            low, high = [], []
            for z in range(nz):
                first, second = unpack_pixels(gr[c, 0, z, b], gr[c, 1, z, b])
                low.append(first)
                high.append(second)
            for i, parts in enumerate((low, high)):

                def store(t, u, part, i=i):
                    spot = pl.ds(pl.multiple_of((3 * b + u) * c3 + i * half, 16), half)
                    g9[t, spot, 0:image] = part.astype(BF16)

                nine_shifts(jnp.concatenate(parts, axis=1) if nz > 1 else parts[0], W[3], store)
            return 0

        lax.fori_loop(0, nb, item, 0, unroll=True)

        def step(i, _):
            acc = None
            for b in range(nb):
                part = lax.dot_general(
                    g9[i, 3 * b * c3 : 3 * (b + 1) * c3, 0:image],
                    xi[c, b % nc, b // nc],
                    (((1,), (1,)), ((), ())),
                    preferred_element_type=F32,
                )
                acc = part if acc is None else acc + part
            slot = lax.rem(i, 2)

            @pl.when(i >= 2)
            def _():
                coarse_copy(c, i - 2).wait()

            cstage[slot] = acc
            coarse_copy(c, i).start()
            return 0

        lax.fori_loop(0, 3, step, 0)
        coarse_copy(c, 1).wait()
        coarse_copy(c, 2).wait()

    def moments(arrays, group):
        for l in group:

            def body(r0, rc, lanes, l=l):
                acc = jnp.zeros((rc, 128), F32)
                for a, b in lane_chunks(l, lanes):
                    m = masks[l][1:2, a:b] > 0
                    acc = acc + fold(jnp.where(m, arrays[l][pl.ds(r0, rc), a:b], 0.0))
                stat_a[pl.ds(pl.multiple_of(OFF[l] + r0, 16), rc), :] = acc

            each(l, body)
        for l in group:
            at = slice(OFF[l], OFF[l] + C[l])
            s = jnp.sum(stat_a[at, :], axis=1, keepdims=True) * inv_local[l]
            cols[LOCAL, at, :] = jnp.broadcast_to(s, (C[l], 128))
        for l in group:

            def body(r0, rc, lanes, l=l):
                acc = jnp.zeros((rc, 128), F32)
                mean = col(LOCAL, l, r0, rc, lanes)
                for a, b in lane_chunks(l, lanes):
                    m = masks[l][1:2, a:b] > 0
                    d = jnp.where(m, arrays[l][pl.ds(r0, rc), a:b] - mean, 0.0)
                    acc = acc + fold(d * d)
                stat_b[pl.ds(pl.multiple_of(OFF[l] + r0, 16), rc), :] = acc

            each(l, body)
        return record(stat_a, stat_b, spans_of[group])

    def mean_rstd(got, group):
        mean, rstd = got[0:8] * inv_count, lax.rsqrt(got[8:16] * inv_count + EPSILON)
        to_columns([mean, rstd], cols, [MEAN, RSTD], spans_of[group])
        return rstd

    def halves(l):
        return max(1, W[l] // 128)

    def to_stage(ref, src):
        for h in range(src.shape[1] // 128):
            ref[h] = src[:, 128 * h : 128 * h + 128].astype(F32)

    for l in range(LEVELS):
        if W[l] >= 128:
            to_stage(stage, feats[l])
            for r in range(R[l]):
                for h in range(halves(l)):
                    a = (r + 1) * W[l] + 128 * h
                    xf[l][:, a : a + 128] = stage[h, pl.ds(r, C[l], stride=R[l]), :]
        else:
            v = feats[l][...].astype(F32)
            v = jnp.concatenate([v, jnp.zeros((NP[l] - N[l], C[l]), F32)], axis=0)
            xf[l][...] = pltpu.roll(v.T, W[l], 1)
    pl.semaphore_wait(barrier, nb + nk - 2)
    send_rims(0, COARSE, xf)
    send_rims(0, FINE, xf)
    to_stage(stage, ograd)
    widen(0)

    def stack_start(l):
        def body(r0, rc, lanes):
            for a, b in lane_chunks(l, lanes):
                m = masks[l][0:1, a:b] > 0
                stack_columns(x3[l], l, r0, rc, a, b, jnp.where(m, xf[l][pl.ds(r0, rc), a:b], 0.0))

        each(l, body)

    def pre_of(hat, gain, shift, l, r0, rc, lanes):
        return hat * col(gain, l, r0, rc, lanes) + col(shift, l, r0, rc, lanes)

    def first_act(l):
        def body(r0, rc, lanes):
            for a, b in lane_chunks(l, lanes):
                m = masks[l][0:1, a:b] > 0
                hat = (y1[l][pl.ds(r0, rc), a:b] - col(MEAN, l, r0, rc, lanes)) * col(RSTD, l, r0, rc, lanes)
                y1[l][pl.ds(r0, rc), a:b] = hat
                pre = pre_of(hat, GAIN1, SHIFT1, l, r0, rc, lanes)
                stack_columns(a3[l], l, r0, rc, a, b, jnp.where(m, pre * sigmoid(pre), 0.0))

        each(l, body)

    def second_act(l):
        def body(r0, rc, lanes):
            for a, b in lane_chunks(l, lanes):
                m = masks[l][0:1, a:b] > 0
                hat = (y2[l][pl.ds(r0, rc), a:b] - col(MEAN, l, r0, rc, lanes)) * col(RSTD, l, r0, rc, lanes)
                y2[l][pl.ds(r0, rc), a:b] = hat
                pre = pre_of(hat, GAIN2, SHIFT2, l, r0, rc, lanes)
                start = x3[l][pl.ds(pl.multiple_of(C[l] + r0, 16), rc), a:b].astype(F32)
                pre = jnp.where(m, pre, 0.0) + start
                p1[l][pl.ds(r0, rc), a:b] = pre
                if l:
                    br[l - 1][pl.ds(r0, rc), a:b] = (pre * sigmoid(pre)).astype(BF16)

        each(l, body)

    def second_sums(l):
        def body(r0, rc, lanes):
            acc_g = jnp.zeros((rc, 128), F32)
            acc_s = jnp.zeros((rc, 128), F32)
            for a, b in lane_chunks(l, lanes):
                m = masks[l][1:2, a:b] > 0
                pre = p1[l][pl.ds(r0, rc), a:b]
                sig = sigmoid(pre)
                d = xf[l][pl.ds(r0, rc), a:b] * (sig * (1.0 + pre * (1.0 - sig)))
                xf[l][pl.ds(r0, rc), a:b] = d
                d = jnp.where(m, d, 0.0)
                acc_s = acc_s + fold(d)
                acc_g = acc_g + fold(jnp.where(m, d * y2[l][pl.ds(r0, rc), a:b], 0.0))
            at = pl.ds(pl.multiple_of(OFF[l] + r0, 16), rc)
            stat_a[at, :] = acc_g
            stat_b[at, :] = acc_s

        each(l, body)

    def first_sums(l):
        def body(r0, rc, lanes):
            acc_g = jnp.zeros((rc, 128), F32)
            acc_s = jnp.zeros((rc, 128), F32)
            for a, b in lane_chunks(l, lanes):
                m = masks[l][1:2, a:b] > 0
                hat = y1[l][pl.ds(r0, rc), a:b]
                pre = pre_of(hat, GAIN1, SHIFT1, l, r0, rc, lanes)
                sig = sigmoid(pre)
                d = p1[l][pl.ds(r0, rc), a:b] * (sig * (1.0 + pre * (1.0 - sig)))
                d = jnp.where(m, d, 0.0)
                p1[l][pl.ds(r0, rc), a:b] = d
                acc_s = acc_s + fold(d)
                acc_g = acc_g + fold(jnp.where(m, d * hat, 0.0))
            at = pl.ds(pl.multiple_of(OFF[l] + r0, 16), rc)
            stat_a[at, :] = acc_g
            stat_b[at, :] = acc_s

        each(l, body)

    def norm_grad(l, hats, grads):
        def body(r0, rc, lanes):
            parts = []
            for a, b in lane_chunks(l, lanes):
                m = masks[l][0:1, a:b] > 0
                hat = hats[l][pl.ds(r0, rc), a:b]
                d = grads[l][pl.ds(r0, rc), a:b]
                g = col(CA, l, r0, rc, lanes) * (
                    d - col(CB, l, r0, rc, lanes) - hat * col(CC, l, r0, rc, lanes)
                )
                g = jnp.where(m, g, 0.0)
                stack_columns(g3[l], l, r0, rc, a, b, g, back=True)
                parts.append(g)
            if l in sz.stacked:
                v = parts[0] if len(parts) == 1 else jnp.concatenate(parts, axis=1)
                stack_rows(t3[l], l, r0, rc, jnp.where(masks[l][1:2, :] > 0, v, 0.0))

        each(l, body)

    def norm_columns(scale, got, group):
        to_columns(
            [scale, got[8:16] * inv_count, got[0:8] * inv_count], cols, [CA, CB, CC], spans_of[group]
        )

    def features_out(l):
        if W[l] < 128:
            v = jnp.where(masks[l][1:2, :] > 0, y1[l][...] + xf[l][...], 0.0)
            gfeat[l][...] = pltpu.roll(v, NP[l] - W[l], 1).T[0 : N[l]].astype(BF16)
            return

        def body(r0, rc, lanes):
            for r in range(R[l]):
                for h in range(halves(l)):
                    a = (r + 1) * W[l] + 128 * h
                    m = masks[l][1:2, a : a + 128] > 0
                    v = y1[l][pl.ds(r0, rc), a : a + 128] + xf[l][pl.ds(r0, rc), a : a + 128]
                    stage[h, pl.ds(r0 * R[l] + r, rc, stride=R[l]), :] = jnp.where(m, v, 0.0)

        each(l, body)
        for h in range(halves(l)):
            gfeat[l][:, 128 * h : 128 * h + 128] = stage[h].astype(BF16)

    sizes, u_sizes = (n_a, n_b), (un_a, un_b)
    fine_place = place < C[0]

    take_rims(0, COARSE, xf)
    for l in COARSE:
        stack_start(l)
    gather_begin(0, x3)
    for l in COARSE:
        conv(l, wide, 0, x3, y1)
    send_rims(1, COARSE, y1)
    ex_start(0, moments(y1, COARSE))
    take_rims(0, FINE, xf)
    stack_start(0)
    conv(0, wide, 0, x3, y1)
    send_rims(1, FINE, y1)
    ex_mid(0, sizes)
    ex_start(1, moments(y1, FINE))
    pair_begin(0, x3)
    turn(0)
    ex_mid(1, sizes)
    gather_next(0, 0)
    widen(1)
    rstd1_c = mean_rstd(ex_end(0, sizes), COARSE)
    take_rims(1, COARSE, y1)
    for l in COARSE:
        first_act(l)

    gather_begin(1, a3)
    for l in COARSE:
        conv(l, wide, 1, a3, y2)
    send_rims(2, COARSE, y2)
    ex_start(2, moments(y2, COARSE))
    rstd1_f = mean_rstd(ex_end(1, sizes), FINE)
    take_rims(1, FINE, y1)
    first_act(0)
    ex_mid(2, sizes)
    conv(0, wide, 1, a3, y2)
    send_rims(2, FINE, y2)
    ex_start(4, moments(y2, FINE))
    pair_begin(1, a3)
    pair_next(0)
    rstd2_c = mean_rstd(ex_end(2, sizes), COARSE)
    take_rims(2, COARSE, y2)
    for l in COARSE:
        second_act(l)

    UC_ = sz.uchan
    for j in range(3):
        l = j + 1
        uo[j][...] = jnp.dot(unites[j][...], br[j][...], preferred_element_type=F32)
    for j in range(3):
        l = j + 1
        m = masks[l][1:2, :] > 0
        v = jnp.where(m, uo[j][...], 0.0)
        part = fold(v)
        ustat_a[j * UC_ : (j + 1) * UC_, :] = part
        mean = jnp.sum(part, axis=1, keepdims=True) * inv_local[l]
        d = jnp.where(m, uo[j][...] - mean, 0.0)
        ustat_b[j * UC_ : (j + 1) * UC_, :] = fold(d * d)
    ex_start(3, record(ustat_a, ustat_b, u_spans))
    ex_mid(4, sizes)
    gather_next(0, 1)
    turn(1)
    ex_mid(3, u_sizes)
    gather_next(1, 0)
    pair_next(1)
    rstd2_f = mean_rstd(ex_end(4, sizes), FINE)
    take_rims(2, FINE, y2)
    second_act(0)
    got = ex_end(3, u_sizes)
    umean_p = got[0:8] * inv_ucount
    urstd_p = lax.rsqrt(got[8:16] * inv_ucount + EPSILON)
    to_columns([umean_p, urstd_p], ucols, [UMEAN, URSTD], u_spans)

    at_top = me_k == 0
    at_bottom = me_k == nk - 1
    fine = W[0]
    split = lambda v: (v.astype(BF16), (v - v.astype(BF16).astype(F32)).astype(BF16))

    def edge(l, n):
        return lax.broadcasted_iota(jnp.int32, (1, n), 1)

    for j in range(3):
        l = j + 1
        m = masks[l][0:1, :] > 0
        hat = (uo[j][...] - ucol(UMEAN, j, NP[l])) * ucol(URSTD, j, NP[l])
        uo[j][...] = hat
        norm = jnp.where(m, hat * ucol(UGAIN, j, NP[l]) + ucol(USHIFT, j, NP[l]), 0.0)
        lane = edge(l, NP[l])
        norm = jnp.where((lane < W[l]) & at_top, pltpu.roll(norm, NP[l] - W[l], 1), norm)
        norm = jnp.where((lane >= W[l] + N[l]) & at_bottom, pltpu.roll(norm, W[l], 1), norm)
        hi, lo = split(norm)
        both = jnp.concatenate([hi, lo], axis=0)
        span = max(128, W[l])
        width = tables[j].shape[1]
        for i in range(NP[l] // span):
            broad = jnp.dot(both[:, span * i : span * i + span], tables[j][...], preferred_element_type=F32)
            up[j][:, width * i : width * i + width] = broad[0:UC_] + broad[UC_:]

    blends = [blend(2 ** (j + 1), R[0]) for j in range(3)]

    def total_body(r0, rc, lanes):
        rows = pl.ds(r0, rc)
        coarse = [{}, {}, {}]
        have = [{}, {}, {}]
        for g in range(R[0]):
            a, b = (g + 1) * fine, (g + 2) * fine
            pre = p1[0][rows, a:b]
            total = pre * sigmoid(pre)
            for j in range(3):
                low, frac = blends[j][g]
                for i in (low, low + 1):
                    if i not in have[j]:
                        have[j][i] = up[j][rows, i * fine : (i + 1) * fine]
                total = total + ((1.0 - frac) * have[j][low] + frac * have[j][low + 1])
            m = masks[0][1:2, a:b] > 0
            sig = sigmoid(total)
            out = jnp.where(m, total * sig, 0.0)
            slope = sig * (1.0 + total * (1.0 - sig))
            spots = [(h, pl.ds(r0 * R[0] + g, rc, stride=R[0])) for h in range(halves(0))]
            grad = jnp.concatenate([stage[h, at, :] for h, at in spots], axis=1)
            grad = jnp.where(m, grad * slope, 0.0)
            for h, at in spots:
                stage[h, at, :] = out[:, 128 * h : 128 * h + 128]
            xf[0][rows, a:b] = grad
            for j in range(3):
                low, frac = blends[j][g]
                for i, weight in ((low, 1.0 - frac), (low + 1, frac)):
                    coarse[j][i] = weight * grad if i not in coarse[j] else coarse[j][i] + weight * grad
                done = [i for i in coarse[j] if g + 1 == R[0] or i < blends[j][g + 1][0]]
                for i in done:
                    up[j][rows, i * fine : (i + 1) * fine] = coarse[j].pop(i)

    def total_step(i, _):
        total_body(pl.multiple_of(i * 16, 16), 16, fine)
        return 0

    lax.fori_loop(0, UC_ // 16, total_step, 0)
    for h in range(halves(0)):
        united_ref[:, 128 * h : 128 * h + 128] = stage[h].astype(BF16)

    for j in range(3):
        l = j + 1
        span = max(128, W[l])
        width = tables[j].shape[1]
        parts = []
        for i in range(NP[l] // span):
            hi, lo = split(up[j][:, width * i : width * i + width])
            both = jnp.concatenate([hi, lo], axis=0)
            narrow = jnp.dot(both, tables_t[j][...], preferred_element_type=F32)
            parts.append(narrow[0:UC_] + narrow[UC_:])
        d = parts[0] if len(parts) == 1 else jnp.concatenate(parts, axis=1)
        lane = edge(l, NP[l])
        fold_top = jnp.where((lane >= W[l]) & (lane < 2 * W[l]) & at_top, pltpu.roll(d, W[l], 1), 0.0)
        fold_bottom = jnp.where(
            (lane >= N[l]) & (lane < W[l] + N[l]) & at_bottom, pltpu.roll(d, NP[l] - W[l], 1), 0.0
        )
        d = d + fold_top + fold_bottom
        d = jnp.where(masks[l][0:1, :] > 0, d, 0.0)
        ustat_a[j * UC_ : (j + 1) * UC_, :] = fold(d * uo[j][...])
        ustat_b[j * UC_ : (j + 1) * UC_, :] = fold(d)
        up[j][:, 0 : NP[l]] = d
    at = 0
    lay = []
    for j in range(3):
        l = j + 1
        n = max(2 * W[l], 128)
        lay.append((at, n))
        mid_s[0, :, at : at + n] = up[j][:, 0:n].astype(BF16)
        mid_s[1, :, at : at + n] = up[j][:, NP[l] - n : NP[l]].astype(BF16)
        at += n
    mid_s[0, :, at : at + fine] = xf[0][:, fine : 2 * fine].astype(BF16)
    mid_s[1, :, at : at + fine] = xf[0][:, N[0] : N[0] + fine].astype(BF16)
    rims_start(8, lambda i: mid_s.at[i], lambda i: mid_r.at[i])
    ex_start(5, record(ustat_a, ustat_b, u_spans))
    second_sums(0)
    ex_mid(5)
    ex_start(6, record(stat_a, stat_b, spans_of[FINE]))
    gather_next(1, 1)
    got = ex_end(5)
    totals_ref[0] = got
    rims_wait(8, lambda i: mid_s.at[i], lambda i: mid_r.at[i])
    to_columns(
        [urstd_p * ugain_p, got[8:16] * inv_ucount, got[0:8] * inv_ucount], ucols, [UA, UB, UC], u_spans
    )
    for i, lane0 in ((0, 0), (1, W[0] + N[0])):
        pre = p1[0][:, lane0 : lane0 + fine]
        sig = sigmoid(pre)
        slope = sig * (1.0 + pre * (1.0 - sig))
        xf[0][:, lane0 : lane0 + fine] = mid_r[i, :, at : at + fine].astype(F32) * slope
    for j in range(3):
        l = j + 1
        start, n = lay[j]
        lane = edge(l, n)
        above = mid_r[0, :, start : start + n].astype(F32)
        below = mid_r[1, :, start : start + n].astype(F32)
        if NP[l] == n:
            above, below = pltpu.roll(above, n // 2, 1), pltpu.roll(below, n // 2, 1)
            d = up[j][:, 0:n]
            d = d + jnp.where((lane < 2 * W[l]) & (me_k > 0), above, 0.0)
            d = d + jnp.where((lane >= n - 2 * W[l]) & (me_k < nk - 1), below, 0.0)
            up[j][:, 0:n] = d
        else:
            up[j][:, 0:n] = up[j][:, 0:n] + jnp.where((lane >= 0) & (me_k > 0), above, 0.0)
            up[j][:, NP[l] - n : NP[l]] = up[j][:, NP[l] - n : NP[l]] + jnp.where(
                (lane >= 0) & (me_k < nk - 1), below, 0.0
            )
    for j in range(3):
        l = j + 1
        d = up[j][:, 0 : NP[l]]
        g = ucol(UA, j, NP[l]) * (d - ucol(UB, j, NP[l]) - uo[j][...] * ucol(UC, j, NP[l]))
        g = jnp.where(masks[l][0:1, :] > 0, g, 0.0)
        low = g.astype(BF16)
        xf[l][...] = jnp.dot(unites[j][...].T, low, preferred_element_type=F32)
        own = jnp.where(masks[l][1:2, :] > 0, g, 0.0).astype(BF16)
        gun[j][:, 0 : C[l]] = lax.dot_general(
            own, br[j][...], (((1,), (1,)), ((), ())), preferred_element_type=F32
        )

    for l in COARSE:
        second_sums(l)
    ex_start(7, record(stat_a, stat_b, spans_of[COARSE]))
    ex_mid(6)
    got_f = ex_end(6)
    norm_columns(rstd2_f * gain2_p, got_f, FINE)
    norm_grad(0, y2, xf)
    ex_mid(7)
    conv(0, wide, 1, g3, p1, -1)
    first_sums(0)
    send_rims(3, FINE, p1)
    ex_start(8, record(stat_a, stat_b, spans_of[FINE]))
    sum_level(1, 0, a3)
    sum_pack_unites()
    sum_first(1, 0)
    got = ex_end(7)
    totals_ref[1] = jnp.where(jnp.concatenate([fine_place] * 2, axis=0), got_f, got)
    norm_columns(rstd2_c * gain2_p, got, COARSE)
    norm_grad(1, y2, xf)
    for l in sz.sum_levels[1:]:
        if l == 2:
            norm_grad(2, y2, xf)
        sum_level(1, l, a3)
    sum_first(1, 1)
    if sz.pair:
        norm_grad(2, y2, xf)
    pair_grad_begin(1)
    norm_grad(3, y2, xf)
    grad_begin(1)

    for l in COARSE:
        conv(l, wide, 1, g3, p1, -1)
    for l in COARSE:
        first_sums(l)
    send_rims(3, COARSE, p1)
    ex_start(9, record(stat_a, stat_b, spans_of[COARSE]))
    ex_mid(8)
    pair_gradient(1)
    ex_mid(9)
    sum_second(1)
    grad_next(1)
    gather_next(0, 2)
    gather_next(1, 2)
    got_f = ex_end(8)
    take_rims(3, FINE, p1)
    norm_columns(rstd1_f * gain1_p, got_f, FINE)
    norm_grad(0, y1, p1)
    sum_level(0, 0, x3)
    sum_first(0, 0)
    got = ex_end(9)
    totals_ref[2] = jnp.where(jnp.concatenate([fine_place] * 2, axis=0), got_f, got)
    take_rims(3, COARSE, p1)
    norm_columns(rstd1_c * gain1_p, got, COARSE)
    norm_grad(3, y1, p1)
    grad_begin(0)
    norm_grad(2, y1, p1)
    pair_grad_begin(0)
    sum_third(1)
    norm_grad(1, y1, p1)
    for l in sz.sum_levels[1:]:
        sum_level(0, l, x3)
    sum_first(0, 1)
    grad_third(1)
    conv(0, wide, 0, g3, y1, -1)
    features_out(0)
    grad_next(0)
    pair_gradient(0)
    sum_second(0)
    conv(1, wide, 0, g3, y1, -1)
    features_out(1)
    grad_third(0)
    sum_third(0)
    sum_fourth(1)
    conv(2, wide, 0, g3, y1, -1)
    features_out(2)
    conv(3, wide, 0, g3, y1, -1)
    features_out(3)
    coarse_gradient(1)
    sum_fourth(0)
    sum_fifth(1)
    coarse_gradient(0)
    sum_fifth(0)
    sum_last(1)
    sum_last(0)
    for c in range(2):
        pltpu.make_async_copy(got_d.at[c], sums_ref.at[c], out_sem.at[c]).wait()


def last_kernel(sz, nb, *refs):
    it = iter(refs)
    take = lambda n: [next(it) for _ in range(n)]
    maps = take(5)
    sums_in, totals, coarse_in = take(3)
    maps_out = take(5)
    kernels = take(4)
    unites = take(3)
    norm_gains, norm_shifts, unite_gains, unite_shifts = take(4)
    held = take(5)
    sums, coarse, in_sem, out_sem = take(4)
    C = sz.chan
    arrivals = [pltpu.make_async_copy(sums_in, sums, in_sem.at[0])]
    arrivals += [pltpu.make_async_copy(a, b, in_sem.at[1 + i]) for i, (a, b) in enumerate(zip(maps, held))]
    arrivals += [pltpu.make_async_copy(coarse_in.at[c], coarse.at[c], in_sem.at[6 + c]) for c in range(2)]
    for copy in arrivals:
        copy.start()
    leaving = [pltpu.make_async_copy(a, b, out_sem.at[i]) for i, (a, b) in enumerate(zip(held, maps_out))]
    if sz.gather:
        leaving += [
            pltpu.make_async_copy(coarse.at[c], kernels[3].at[c], out_sem.at[5 + c]) for c in range(2)
        ]

    for row, which in ((0, 2), (1, 1)):
        for k in range(sz.blocks):
            m = min(128, sz.total - 128 * k)
            for ref, base in ((norm_gains, 0), (norm_shifts, 8)):
                ref[row : row + 1, 128 * k : 128 * k + m] = totals[which, base + k : base + k + 1, 0:m]
    for ref, base in ((unite_gains, 0), (unite_shifts, 8)):
        v = jnp.concatenate([totals[0, base + k : base + k + 1, :] for k in range(sz.ublocks)], axis=1)
        for j in range(3):
            ref[j : j + 1, :] = v[:, j * sz.uchan : (j + 1) * sz.uchan]

    arrivals[0].wait()
    for i in range(5):
        arrivals[1 + i].wait()
        leaving[i].start()
    for l in range(LEVELS):
        n = C[l] // nb
        if l == 3:
            for c in range(2):
                arrivals[6 + c].wait()
                if sz.gather:
                    leaving[5 + c].start()
        for c in range(2):
            if l == 2 and sz.pair:
                at, rows = sz.spots[2, C[2] // 128]
                block = sums[c, at : at + rows, :].astype(F32)
                parts = []
                for i in range(C[2] // 128):
                    at, rows = sz.spots[2, i]
                    parts.append(sums[c, at : at + rows, :].astype(F32))
                parts.append(jnp.concatenate([block[:, 0:64], block[:, 64:128]], axis=0)[0 : 9 * n])
                v = jnp.concatenate(parts, axis=1)
            elif (l, 0) in sz.spots:
                parts = []
                for i in range(-(-3 * C[l] // 128)):
                    at, rows = sz.spots[l, i]
                    parts.append(sums[c, at : at + rows, :].astype(F32))
                v = jnp.concatenate(parts, axis=1)
            for t in range(3):
                for u in range(3):
                    at = (3 * t + u) * n
                    if l == 3 and sz.gather:
                        continue
                    if l == 3:
                        kernels[3][c, at : at + n, :] = coarse[c, t * n : (t + 1) * n, u * C[3] : (u + 1) * C[3]]
                    elif l == 2 and sz.pair:
                        kernels[2][c, t, u] = v[at : at + n]
                    else:
                        w = v[t * n : (t + 1) * n, u * C[l] : (u + 1) * C[l]]
                        if l == 0:
                            kernels[0][t, u, :, c, :] = w
                        else:
                            kernels[l][c, t, u] = w
    n = sz.uchan // nb
    for j in range(3):
        width = C[j + 1]
        for i in range(-(-width // 128)):
            at, _ = sz.spots["u", j, i]
            m = min(128, width - 128 * i)
            unites[j][:, 128 * i : 128 * i + m] = sums[1, at : at + n, 0:m].astype(F32)
    for copy in leaving:
        copy.wait()


def body(*args):
    features = args[0:4]
    blocks = args[4:8]
    unites = args[8:11]
    norm_gains, norm_shifts, unite_gains, unite_shifts, output_grad, heights, widths, item_slot = args[11:]
    nb = lax.axis_size("batch")
    nk = lax.axis_size("rows")
    sz = Sizes(features, nb, nk)
    C, R, W, N, NP = sz.chan, sz.rows, sz.width, sz.own, sz.flat

    flat = [
        f.reshape(C[l] * R[l], W[l]) if W[l] >= 128 else f.transpose(0, 2, 3, 1).reshape(N[l], C[l])
        for l, f in enumerate(features)
    ]
    ograd = output_grad.reshape(C[0] * R[0], W[0])
    blocks = [b.reshape(2, 3, 3 * C[l], C[l]) for l, b in enumerate(blocks)]

    tables = [column_table(W[l], W[0]) for l in range(1, 4)]
    operands = [heights, widths, item_slot, *flat, ograd, *blocks, *unites]
    operands += [norm_gains, norm_shifts, unite_gains, unite_shifts]
    operands += [jnp.asarray(t, BF16) for t in tables] + [jnp.asarray(t.T, BF16) for t in tables]

    shape = jax.ShapeDtypeStruct
    map_shapes = [(C[0] * R[0], W[0])]
    map_shapes += [(C[l] * R[l], W[l]) if W[l] >= 128 else (N[l], C[l]) for l in range(4)]
    outs = [shape(m, BF16) for m in map_shapes]
    outs += [shape((2, sz.sum_rows, 128), BF16)]
    outs += [shape((2, 9 * C[3] // nb, C[3]) if sz.gather else (2, 3 * C[3], 3 * C[3]), F32)]
    outs += [shape((3, 16, 128), F32)]
    vm = pltpu.VMEM
    scratch = [
        vm((3, 3 * C[l], C[l]), BF16) for l in range(3 if sz.gather else 4)
    ]
    scratch += [vm((2, 3 * C[l], 3 * C[l]), BF16) for l in range(4)]
    scratch += [vm((max(1, W[0] // 128), C[0] * R[0], 128), F32)]
    for _ in range(3):
        scratch += [vm((3 * C[l], NP[l]), BF16) for l in range(4)]
    scratch += [vm((3 * C[l], NP[l]), BF16) for l in sz.stacked]
    n = C[3] // nb
    scratch += [vm((2, 3 * n, C[3]) if sz.gather else (1, n, 3 * C[3]), F32), pltpu.SemaphoreType.DMA((2,))]
    top = C[sz.sum_levels[-1]]
    scratch += [vm((3 * top, -(-3 * top // 128) * 128), F32)]
    scratch += [vm((sz.uchan, -(-C[l] // 128) * 128), F32) for l in range(1, 4)]
    for _ in range(4):
        scratch += [vm((C[l], NP[l]), F32) for l in range(4)]
    scratch += [vm((C[l], NP[l]), BF16) for l in range(1, 4)]
    scratch += [vm((sz.uchan, NP[l]), F32) for l in range(1, 4)]
    scratch += [vm((sz.uchan, (R[l] + 2) * W[0]), F32) for l in range(1, 4)]
    scratch += [
        vm((N_COLS, sz.blocks * 128, 128), F32),
        vm((N_UCOLS, sz.ublocks * 128, 128), F32),
        vm((sz.blocks * 128, 128), F32),
        vm((sz.blocks * 128, 128), F32),
        vm((sz.ublocks * 128, 128), F32),
        vm((sz.ublocks * 128, 128), F32),
        vm((nb, 8, 128), F32),
        vm((nk, 8, 128), F32),
        vm((nb, 8, 128), F32),
        vm((nk, 8, 128), F32),
    ]
    scratch += [vm((8, NP[l]), F32) for l in range(4)]
    mid = sum(max(2 * W[l], 128) for l in range(1, 4)) + W[0]
    scratch += [
        vm((10, nb, 16, 128), F32),
        vm((10, nk, 16, 128), F32),
        vm((2, sz.rim_total, 128), BF16),
        vm((4, 2, sz.rim_total, 128), BF16),
        vm((2, sz.uchan, mid), BF16),
        vm((2, sz.uchan, mid), BF16),
        pltpu.SemaphoreType.DMA((10, nb)),
        pltpu.SemaphoreType.DMA((10, nb)),
        pltpu.SemaphoreType.DMA((10, nk)),
        pltpu.SemaphoreType.DMA((10, nk)),
        pltpu.SemaphoreType.DMA((9, 2)),
        pltpu.SemaphoreType.DMA((9, 2)),
        pltpu.SemaphoreType.DMA((4, 2)),
        pltpu.SemaphoreType.DMA((2, 9)),
        vm((8, sz.blocks * 128), F32),
        vm((8, sz.ublocks * 128), F32),
        vm((2, nb, sz.batch_rows, 128), BF16),
        vm((2, nb, sz.batch_rows, 128), BF16),
        vm((2, sz.sum_rows, 128), BF16),
        vm((2, sz.nz * max(sz.part), 128), BF16),
        vm((2, sz.nz, max(sz.part), 128), BF16),
        vm((2, sz.sum_rows, 128), BF16),
        pltpu.SemaphoreType.DMA((2,)),
    ]
    sems = pltpu.SemaphoreType.DMA
    scratch += [sems((2, 2, nb))] * 2 + [sems((2,))] * 2 + [sems((2, sz.nz))] * 4
    scratch += [sems((2,))] * 2
    if sz.gather:
        half = C[3] // nb // 2
        most = max(sz.nz, sz.nx, sz.ny, sz.nc)
        scratch += [
            vm((2, sz.nx, sz.nz, C[3] // 2, 128), BF16),
            vm((2, sz.nc, sz.ny, C[3], 128 * sz.nz), BF16),
            vm((2, nb, half, 128), BF16),
            vm((2, sz.nx, sz.nz, nb, half, 128), BF16),
            vm((3, 3 * C[3], max(C[3], 128 * sz.nz)), BF16),
            sems((2, 4, most)),
            sems((2, 4, most)),
            sems((2, nb)),
            sems((2, nb)),
            sems((2, sz.nz)),
            sems((2, sz.nz)),
            sems((2,)),
            sems((2,)),
        ]
    if sz.pair:
        c2 = C[2] // nb
        scratch += [
            vm((2, sz.nc, sz.ny, C[2], NP[2]), BF16),
            vm((2, nb, c2, N[2]), BF16),
            vm((2, nb, c2, N[2]), BF16),
            vm((nb, 9 * c2, NP[2]), BF16),
            sems((2, 2, max(sz.ny, sz.nc))),
            sems((2, 2, max(sz.ny, sz.nc))),
            sems((2, nb)),
            sems((2, nb)),
        ]
    in_vmem = pl.BlockSpec(memory_space=pltpu.VMEM)
    in_smem = pl.BlockSpec(memory_space=pltpu.SMEM)
    got = pl.pallas_call(
        functools.partial(main_kernel, sz, nb, nk),
        out_shape=outs,
        in_specs=[in_smem] * 3
        + [in_vmem] * 5
        + [pl.BlockSpec(memory_space=pl.ANY)] * 4
        + [in_vmem] * (len(operands) - 12),
        out_specs=[in_vmem] * 5
        + [pl.BlockSpec(memory_space=pl.ANY)] * 2
        + [in_vmem],
        scratch_shapes=scratch,
        compiler_params=pltpu.CompilerParams(
            collective_id=0, has_side_effects=True, vmem_limit_bytes=60 * 2**20
        ),
    )(*operands)

    maps, sums, totals = got[0:5], got[5], got[-1]
    coarse = got[6]
    if not sz.gather:
        coarse = coarse.astype(BF16).reshape(2, 3, C[3], 3 * C[3])
        coarse = lax.psum(coarse, "rows")
        coarse = lax.psum_scatter(coarse, "batch", scatter_dimension=2, tiled=True)
        coarse = coarse.astype(F32).reshape(2, 3 * C[3] // nb, 3 * C[3])
    in_any = pl.BlockSpec(memory_space=pl.ANY)
    outs = [shape(m, BF16) for m in map_shapes]
    outs += [shape((3, 3, C[0] // nb, 2, C[0]), F32)]
    outs += [shape((2, 3, 3, C[l] // nb, C[l]), F32) for l in (1, 2)]
    outs += [shape((2, 9 * C[3] // nb, C[3]), F32)]
    outs += [shape((sz.uchan // nb, C[l]), F32) for l in range(1, 4)]
    outs += [shape((2, sz.total), F32)] * 2 + [shape((3, sz.uchan), F32)] * 2
    outs = pl.pallas_call(
        functools.partial(last_kernel, sz, nb),
        out_shape=outs,
        in_specs=[in_any] * 6 + [in_vmem] + [in_any],
        out_specs=[in_any] * 5
        + [in_vmem] * 3
        + [in_any if sz.gather else in_vmem]
        + [in_vmem] * (len(outs) - 9),
        scratch_shapes=[vm(m, BF16) for m in map_shapes]
        + [
            vm(sums.shape, BF16),
            vm(coarse.shape, F32),
            pltpu.SemaphoreType.DMA((8,)),
            pltpu.SemaphoreType.DMA((7,)),
        ],
        compiler_params=pltpu.CompilerParams(vmem_limit_bytes=60 * 2**20),
    )(*maps, sums, totals, coarse)
    outs = list(outs)
    outs[5] = outs[5].transpose(3, 0, 1, 2, 4)
    outs[8] = outs[8].reshape(2, 3, 3, C[3] // nb, C[3])
    shaped = []
    for i, m in enumerate(outs[0:5]):
        l = max(i - 1, 0)
        if W[l] >= 128:
            shaped.append(m.reshape(1, C[l], R[l], W[l]))
        else:
            shaped.append(m.reshape(1, R[l], W[l], C[l]).transpose(0, 3, 1, 2))
    return (*shaped, *outs[5:])


def solution(mesh):
    image = P("batch", None, "rows", None)
    kernel = P(None, None, None, "batch", None)
    return jax.shard_map(
        body,
        mesh=mesh,
        in_specs=(image,) * 4 + (P(),) * 11 + (image,) + (P(),) * 3,
        out_specs=(image,) * 5 + (kernel,) * 4 + (P("batch", None),) * 3 + (P(),) * 4,
        check_vma=False,
    )
```

```python
import functools

import jax
import jax.numpy as jnp
import numpy as np
from jax import lax
from jax.experimental import pallas as pl
from jax.experimental.pallas import tpu as pltpu
from jax.sharding import PartitionSpec as P

EPSILON = 1e-05
LEVELS = 4
MESH = pl.DeviceIdType.MESH
F32 = jnp.float32
BF16 = jnp.bfloat16

MEAN, RSTD, GAIN1, SHIFT1, GAIN2, SHIFT2, LOCAL, N_COLS = range(8)
CA, CB, CC = MEAN, RSTD, LOCAL
UMEAN, URSTD, UGAIN, USHIFT, ULOCAL, UA, UB, UC, N_UCOLS = range(9)


class Sizes:
    def __init__(self, features, nb, nk):
        self.chan = [f.shape[1] for f in features]
        self.rows = [f.shape[2] for f in features]
        self.width = [f.shape[3] for f in features]
        self.own = [r * w for r, w in zip(self.rows, self.width)]
        self.flat = [(r + 2) * w for r, w in zip(self.rows, self.width)]
        self.off = [sum(self.chan[:l]) for l in range(LEVELS)]
        self.total = sum(self.chan)
        self.blocks = -(-self.total // 128)
        self.uchan = self.chan[0]
        self.utotal = 3 * self.uchan
        self.ublocks = -(-self.utotal // 128)
        self.rim_rows = [c * w // 128 for c, w in zip(self.chan, self.width)]
        self.rim_off = [sum(self.rim_rows[:l]) for l in range(LEVELS)]
        self.rim_total = sum(self.rim_rows)
        self.chunk = []
        for c, n, w in zip(self.chan, self.flat, self.width):
            lanes = max(x for x in range(128, 641, 128) if n % x == 0 and x % w == 0)
            rows = max(r for r in (16, 32, 48) if c % r == 0 and r * lanes <= 12288)
            self.chunk.append((rows, lanes))
        self.nc = 2 if nb % 2 == 0 else 1
        self.nx = 2 if nk % 2 == 0 else 1
        self.ny = nb // self.nc
        self.nz = nk // self.nx
        self.gather = nb * nk <= 32 and self.nx == 2 and self.nc == 2 and self.own[3] == 64
        self.pair = self.gather and self.chan[2] // nb % 16 == 0 and self.chan[2] % 128 == 64
        self.sum_levels = [0, 1] if self.pair else [0, 1, 2]
        self.stacked = [l for l in range(3 if self.gather else 4) if self.width[l] < 128]
        self.stacked = [l for l in self.stacked if not (self.pair and l == 2)]
        self.start, self.spots, self.moves = {}, {}, []

        def place(table, at, key, values, width):
            rows = -(-values // 16) * 16
            for i in range(-(-width // 128)):
                table[(*key, i)] = (at, rows)
                at += rows
            return at

        def place_kernels(table, at, levels):
            for l in levels:
                at = place(table, at, (l,), 3 * self.chan[l] // nb, 3 * self.chan[l])
            return at

        def place_unites(table, at):
            for j in range(3):
                at = place(table, at, ("u", j), self.uchan // nb, self.chan[j + 1])
            return at

        ends = [0, place_kernels(self.start, 0, [0])]
        ends.append(place_unites(self.start, ends[-1]))
        ends.append(place_kernels(self.start, ends[-1], self.sum_levels[1:]))
        self.early_rows, self.batch_rows = ends[2], ends[3]
        at = place_kernels(self.spots, 0, self.sum_levels)
        if self.pair:
            rows = 9 * self.chan[2] // nb
            for i in range(self.chan[2] // 128):
                self.spots[2, i] = (at, rows)
                at += rows
            rows = -(-rows // 32) * 16
            self.spots[2, self.chan[2] // 128] = (at, rows)
            at += rows
        rows_of = [at, place_unites(self.spots, at)]
        self.part = [-(-r // (nk * 16)) * 16 for r in rows_of]
        self.sum_rows = max(self.part) * nk
        kernels_end = ends[3] - ends[2]
        self.moves = [(0, 0, ends[1]), (ends[2], ends[1], kernels_end), (ends[1], at, ends[2] - ends[1])]


def blend(scale, rows):
    out = []
    for g in range(rows):
        num = 2 * g + 1 - scale
        low = num // (2 * scale)
        out.append((low + 1, (num - 2 * scale * low) / (2.0 * scale)))
    return out


def column_table(width, fine):
    scale = fine // width
    group = max(1, 128 // width)
    span = max(128, width)
    table = np.zeros((span, group * fine), np.float32)
    for r in range(group):
        for g in range(fine):
            num = 2 * g + 1 - scale
            low = 0 if num < 0 else num // (2 * scale)
            frac = 0.0 if num < 0 else (num - 2 * scale * low) / (2.0 * scale)
            high = min(low + 1, width - 1)
            table[r * width + low, r * fine + g] += 1.0 - frac
            table[r * width + high, r * fine + g] += frac
    return table


def sigmoid(v):
    return jax.nn.sigmoid(v)


def main_kernel(sz, nb, nk, *refs):
    it = iter(refs)
    take = lambda n: [next(it) for _ in range(n)]
    heights, widths, slots = take(3)
    feats = take(4)
    (ograd,) = take(1)
    blocks = take(4)
    unites = take(3)
    norm_gains, norm_shifts, unite_gains, unite_shifts = take(4)
    tables = take(3)
    tables_t = take(3)
    map_outs = take(5)
    (sums_ref,) = take(1)
    (coarse_ref,) = take(1)
    (totals_ref,) = take(1)
    raw = take(3 if sz.gather else 4)
    wide = take(4)
    (stage,) = take(1)
    x3 = take(4)
    a3 = take(4)
    g3 = take(4)
    t3 = dict(zip(sz.stacked, take(len(sz.stacked))))
    cstage, cstage_sem = take(2)
    (kg,) = take(1)
    gun = take(3)
    xf = take(4)
    y1 = take(4)
    y2 = take(4)
    p1 = take(4)
    br = take(3)
    uo = take(3)
    up = take(3)
    (cols, ucols, stat_a, stat_b, ustat_a, ustat_b, n_a, n_b, un_a, un_b) = take(10)
    masks = take(4)
    (rec_a, rec_b, rim_s, rim_r, mid_s, mid_r) = take(6)
    (sa_send, sa_recv, sb_send, sb_recv, rim_send, rim_recv) = take(6)
    raw_sem, wide_sem = take(2)
    united_ref, *gfeat = take(5)
    (map_sem,) = take(1)

    def map_copy(i):
        return pltpu.make_async_copy(([united_ref] + gfeat)[i], map_outs[i], map_sem.at[i])

    prow, urow = take(2)
    part_a, got_a, part_s, got_x, got_z, got_d, out_sem = take(7)
    (ra_send, ra_recv, rx_send, rx_recv, rz_send, rz_recv) = take(6)
    (dz_send, dz_recv, dx_send, dx_recv) = take(4)
    if sz.gather:
        xg, xi, gs, gr, g9 = take(5)
        (xg_send, xg_recv, g1_send, g1_recv, g2_send, g2_recv, g3_send, g3_recv) = take(8)
    if sz.pair:
        xb, gsb, gb, g9b = take(4)
        (xb_send, xb_recv, gb_send, gb_recv) = take(4)

    C, R, W, N, NP, OFF = sz.chan, sz.rows, sz.width, sz.own, sz.flat, sz.off
    me_b = lax.axis_index("batch")
    me_k = lax.axis_index("rows")

    def peer_b(j):
        return lax.rem(me_b + j, nb)

    def peer_k(j):
        return lax.rem(me_k + j, nk)

    def raw_copy(l, which):
        if l == 3 and sz.gather:
            dst = g9.at[:, :, 0 : C[3]]
        else:
            dst = raw[l]
        return pltpu.make_async_copy(blocks[l].at[which], dst, raw_sem.at[l, which])

    def wide_copies(which):
        c = C[3]
        return [
            pltpu.make_async_copy(
                blocks[3].at[which, t, u * c : (u + 1) * c, :],
                wide[3].at[which, t * c : (t + 1) * c, u * c : (u + 1) * c],
                wide_sem.at[which, 3 * t + u],
            )
            for t in range(3)
            for u in range(3)
        ]

    for l in range(3):
        raw_copy(l, 0).start()
    for which in range(2):
        for copy in wide_copies(which):
            copy.start()
    raw_copy(3, 0).start()

    def widen(which):
        for copy in wide_copies(which):
            copy.wait()
        for l in range(3):
            raw_copy(l, which).wait()
            c = C[l]
            for t in range(3):
                wide[l][which, t * c : (t + 1) * c, :] = jnp.concatenate(
                    [raw[l][t, u * c : (u + 1) * c, :] for u in range(3)], axis=1
                )

    def turn(which):
        raw_copy(3, which).wait()
        for l in range(LEVELS):
            for t in range(3):
                if l == 3 and sz.gather:
                    v = g9[t, :, 0 : C[3]]
                else:
                    v = raw[l][t]
                wide[l][which, t * C[l] : (t + 1) * C[l], :] = v.T
        if which == 0:
            for l in range(LEVELS):
                raw_copy(l, 1).start()

    barrier = pltpu.get_barrier_semaphore()
    for j in range(1, nb):
        pl.semaphore_signal(barrier, inc=1, device_id=(peer_b(j), me_k), device_id_type=MESH)
    for j in range(1, nk):
        pl.semaphore_signal(barrier, inc=1, device_id=(me_b, peer_k(j)), device_id_type=MESH)

    my_h = jnp.int32(0)
    my_w = jnp.int32(0)
    slot_h, slot_w = [], []
    for b in range(nb):
        h = jnp.int32(0)
        w = jnp.int32(0)
        for i in range(nb):
            hit = (slots[i] == b).astype(jnp.int32)
            h = h + hit * heights[i]
            w = w + hit * widths[i]
        slot_h.append(h)
        slot_w.append(w)
        mine = (me_b == b).astype(jnp.int32)
        my_h = my_h + mine * h
        my_w = my_w + mine * w

    count = []
    for l in range(LEVELS):
        c = jnp.int32(0)
        for b in range(nb):
            c = c + lax.shift_right_logical(slot_h[b], l) * lax.shift_right_logical(slot_w[b], l)
        count.append(c.astype(F32))
    inv_local = []
    for l in range(LEVELS):
        inside = jnp.clip(lax.shift_right_logical(my_h, l) - me_k * R[l], 0, R[l])
        own = inside * lax.shift_right_logical(my_w, l)
        inv_local.append(1.0 / jnp.maximum(own, 1).astype(F32))
        lane = lax.broadcasted_iota(jnp.int32, (1, NP[l]), 1)
        log_w = W[l].bit_length() - 1
        row = me_k * R[l] + lax.shift_right_logical(lane, log_w) - 1
        col = lane & (W[l] - 1)
        valid = (row >= 0) & (row < lax.shift_right_logical(my_h, l))
        valid = valid & (col < lax.shift_right_logical(my_w, l))
        masks[l][0:1, :] = jnp.where(valid, 1.0, 0.0)
        masks[l][1:2, :] = jnp.where(valid & (lane >= W[l]) & (lane < W[l] + N[l]), 1.0, 0.0)

    place = lax.broadcasted_iota(jnp.int32, (8, 128), 0) * 128 + lax.broadcasted_iota(
        jnp.int32, (8, 128), 1
    )

    def by_level(values):
        out = jnp.full((8, 128), values[3])
        for l in (2, 1, 0):
            out = jnp.where(place < OFF[l + 1], jnp.full((8, 128), values[l]), out)
        return out

    def by_unite(values):
        out = jnp.full((8, 128), values[2])
        for j in (1, 0):
            out = jnp.where(place < (j + 1) * sz.uchan, jnp.full((8, 128), values[j]), out)
        return out

    inv_count = 1.0 / by_level(count)
    inv_ucount = 1.0 / by_unite(count[1:])
    for chooser, levels, na_ref, nb_ref in (
        (by_level, range(4), n_a, n_b),
        (by_unite, range(1, 4), un_a, un_b),
    ):
        span = chooser([jnp.int32(R[l]) for l in levels])
        hv = [chooser([lax.shift_right_logical(h, l) for l in levels]) for h in slot_h]
        wv = [chooser([lax.shift_right_logical(w, l) for l in levels]) for w in slot_w]
        for b in range(nb):
            na_ref[b] = (jnp.clip(hv[b] - me_k * span, 0, span) * wv[b]).astype(F32)
        for k in range(nk):
            n = jnp.zeros((8, 128), jnp.int32)
            for b in range(nb):
                n = n + jnp.clip(hv[b] - k * span, 0, span) * wv[b]
            nb_ref[k] = n.astype(F32)

    def tile(v, lanes):
        return v if lanes == 128 else jnp.concatenate([v] * (lanes // 128), axis=1)

    def col(slot, l, r0, rc, lanes):
        return tile(cols[slot, pl.ds(pl.multiple_of(OFF[l] + r0, 16), rc), :], lanes)

    def ucol(slot, j, lanes):
        return tile(ucols[slot, j * sz.uchan : (j + 1) * sz.uchan, :], lanes)

    def to_columns(packed, ref, slot_list, spans):
        full = jnp.concatenate(packed + [jnp.zeros((128 - 8 * len(packed), 128), F32)], axis=0)
        standing = full.T
        for i, slot in enumerate(slot_list):
            for lo, hi in spans:
                for k in range(lo // 128, -(-hi // 128)):
                    a, b = max(lo, 128 * k), min(hi, 128 * k + 128)
                    v = standing[a - 128 * k : b - 128 * k, 8 * i + k : 8 * i + k + 1]
                    ref[slot, a:b, :] = jnp.broadcast_to(v, (b - a, 128))

    FINE, COARSE = (0,), (1, 2, 3)
    spans_of = {FINE: [(0, C[0])], COARSE: [(C[0], sz.total)]}
    u_spans = [(0, sz.utotal)]

    prow[...] = jnp.zeros_like(prow)
    urow[...] = jnp.zeros_like(urow)
    for i in range(2):
        prow[2 * i : 2 * i + 1, 0 : sz.total] = norm_gains[i : i + 1, :]
        prow[2 * i + 1 : 2 * i + 2, 0 : sz.total] = norm_shifts[i : i + 1, :]
    for j in range(3):
        at = slice(j * sz.uchan, (j + 1) * sz.uchan)
        urow[0:1, at] = unite_gains[j : j + 1, :]
        urow[1:2, at] = unite_shifts[j : j + 1, :]
    standing = prow[...].T
    for i, slot in enumerate((GAIN1, SHIFT1, GAIN2, SHIFT2)):
        cols[slot] = jnp.broadcast_to(standing[:, i : i + 1], (sz.blocks * 128, 128))
    standing = urow[...].T
    for i, slot in enumerate((UGAIN, USHIFT)):
        ucols[slot] = jnp.broadcast_to(standing[:, i : i + 1], (sz.ublocks * 128, 128))

    def packed(ref, i, blocks):
        rows = [ref[i : i + 1, 128 * k : 128 * k + 128] for k in range(blocks)]
        return jnp.concatenate(rows + [jnp.zeros((8 - blocks, 128), F32)], axis=0)

    gain1_p, gain2_p = packed(prow, 0, sz.blocks), packed(prow, 2, sz.blocks)
    ugain_p = packed(urow, 0, sz.ublocks)
    stat_a[...] = jnp.zeros_like(stat_a)
    stat_b[...] = jnp.zeros_like(stat_b)
    ustat_a[...] = jnp.zeros_like(ustat_a)
    ustat_b[...] = jnp.zeros_like(ustat_b)

    def fold(v):
        out = v[:, 0:128]
        for i in range(1, v.shape[1] // 128):
            out = out + v[:, 128 * i : 128 * i + 128]
        return out

    lane128 = lax.broadcasted_iota(jnp.int32, (1, 128), 1)

    def record(a_ref, b_ref, spans):
        out = jnp.zeros((128, 128), F32)
        for base, ref in ((0, a_ref), (8, b_ref)):
            for lo, hi in spans:
                for k in range(lo // 128, -(-hi // 128)):
                    s = jnp.sum(ref[128 * k : 128 * k + 128, :], axis=1, keepdims=True)
                    out = jnp.where(lane128 == base + k, s, out)
        return out.T[0:16]

    def record_copies(e, which, sending):
        if which == 0:
            ref, send, recv, n, me = rec_a, sa_send, sa_recv, nb, me_b
        else:
            ref, send, recv, n, me = rec_b, sb_send, sb_recv, nk, me_k
        out = []
        for j in range(1, n):
            other = lax.rem(me + j, n)
            slot = me if sending else other
            out.append(
                pltpu.make_async_remote_copy(
                    src_ref=ref.at[e, me],
                    dst_ref=ref.at[e, slot],
                    send_sem=send.at[e, other],
                    recv_sem=recv.at[e, slot],
                    device_id=(other, me_k) if which == 0 else (me_b, other),
                    device_id_type=MESH,
                )
            )
        return out

    def record_send(e, which, rec):
        if which == 0:
            rec_a[e, me_b] = rec
        else:
            rec_b[e, me_k] = rec
        for copy in record_copies(e, which, True):
            copy.start()

    def record_total(e, which, sizes):
        for copy in record_copies(e, which, False):
            copy.wait_recv()
        for copy in record_copies(e, which, True):
            copy.wait_send()
        ref, n = ((rec_a, nb), (rec_b, nk))[which]
        if sizes is None:
            out = ref[e, 0]
            for i in range(1, n):
                out = out + ref[e, i]
            return out
        total = jnp.zeros((8, 128), F32)
        size = jnp.zeros((8, 128), F32)
        for i in range(n):
            total = total + ref[e, i, 0:8]
            size = size + sizes[which][i]
        mean = total / jnp.maximum(size, 1.0)
        spread_sum = jnp.zeros((8, 128), F32)
        for i in range(n):
            delta = ref[e, i, 0:8] / jnp.maximum(sizes[which][i], 1.0) - mean
            spread_sum = spread_sum + (ref[e, i, 8:16] + sizes[which][i] * delta * delta)
        return jnp.concatenate([total, spread_sum], axis=0)

    def ex_start(e, rec):
        record_send(e, 0, rec)

    def ex_mid(e, sizes=None):
        record_send(e, 1, record_total(e, 0, sizes))

    def ex_end(e, sizes=None):
        return record_total(e, 1, sizes)

    def rim_copies(slot, src, dst):
        up = pltpu.make_async_remote_copy(
            src_ref=src(0),
            dst_ref=dst(1),
            send_sem=rim_send.at[slot, 0],
            recv_sem=rim_recv.at[slot, 1],
            device_id=(me_b, lax.rem(me_k + nk - 1, nk)),
            device_id_type=MESH,
        )
        down = pltpu.make_async_remote_copy(
            src_ref=src(1),
            dst_ref=dst(0),
            send_sem=rim_send.at[slot, 1],
            recv_sem=rim_recv.at[slot, 0],
            device_id=(me_b, lax.rem(me_k + 1, nk)),
            device_id_type=MESH,
        )
        return up, down

    def rims_start(slot, src, dst):
        up, down = rim_copies(slot, src, dst)

        @pl.when(me_k > 0)
        def _():
            up.start()

        @pl.when(me_k < nk - 1)
        def _():
            down.start()

    def rims_wait(slot, src, dst):
        up, down = rim_copies(slot, src, dst)

        @pl.when(me_k > 0)
        def _():
            down.wait_recv()
            up.wait_send()

        @pl.when(me_k < nk - 1)
        def _():
            up.wait_recv()
            down.wait_send()

    def pack_row(ref, l, lane0):
        if W[l] >= 128:
            return jnp.concatenate(
                [ref[:, lane0 + 128 * i : lane0 + 128 * i + 128] for i in range(W[l] // 128)], axis=0
            )
        group = 128 // W[l]
        rows = C[l] // group
        base, shift = lane0 // 128 * 128, lane0 % 128
        out = None
        for g in range(group):
            v = ref[g * rows : (g + 1) * rows, base : base + 128]
            turn = (g * W[l] - shift) % 128
            v = pltpu.roll(v, turn, 1) if turn else v
            out = v if out is None else jnp.where(lane128 >= g * W[l], v, out)
        return out

    def unpack_row(ref, l, lane0, q):
        if W[l] >= 128:
            for i in range(W[l] // 128):
                ref[:, lane0 + 128 * i : lane0 + 128 * i + 128] = q[i * C[l] : (i + 1) * C[l]]
            return
        group = 128 // W[l]
        rows = C[l] // group
        base, shift = lane0 // 128 * 128, lane0 % 128
        here = (lane128 >= shift) & (lane128 < shift + W[l])
        for g in range(group):
            turn = (shift - g * W[l]) % 128
            v = pltpu.roll(q, turn, 1) if turn else q
            old = ref[g * rows : (g + 1) * rows, base : base + 128]
            ref[g * rows : (g + 1) * rows, base : base + 128] = jnp.where(here, v, old)

    def rim_span(group):
        first, last = group[0], group[-1]
        return slice(sz.rim_off[first], sz.rim_off[last] + sz.rim_rows[last])

    def rims_of(slot, group):
        at = rim_span(group)
        number = 2 * slot + (0 if group == FINE else 1)
        return number, lambda i: rim_s.at[i, at, :], lambda i: rim_r.at[slot, i, at, :]

    def send_rims(slot, group, arrays):
        for l in group:
            at = rim_span((l,))
            rim_s[0, at, :] = pack_row(arrays[l], l, W[l]).astype(BF16)
            rim_s[1, at, :] = pack_row(arrays[l], l, N[l]).astype(BF16)
        rims_start(*rims_of(slot, group))

    def take_rims(slot, group, arrays):
        rims_wait(*rims_of(slot, group))
        for l in group:
            at = rim_span((l,))
            unpack_row(arrays[l], l, 0, rim_r[slot, 0, at, :].astype(F32))
            unpack_row(arrays[l], l, W[l] + N[l], rim_r[slot, 1, at, :].astype(F32))

    def each(l, body):
        rc, lanes = sz.chunk[l]

        def step(i, _):
            body(pl.multiple_of(i * rc, rc), rc, lanes)
            return 0

        count = C[l] // rc
        lax.fori_loop(0, count, step, 0, unroll=max(k for k in range(1, 9) if count % k == 0))

    def lane_chunks(l, lanes):
        return [(i, i + lanes) for i in range(0, NP[l], lanes)]

    def stack_columns(ref, l, r0, rc, a, b, v, back=False):
        lanes = b - a
        at = lax.broadcasted_iota(jnp.int32, (1, lanes), 1) & (W[l] - 1)
        left = jnp.where(at == 0, 0.0, pltpu.roll(v, 1, 1))
        right = jnp.where(at == W[l] - 1, 0.0, pltpu.roll(v, lanes - 1, 1))
        for u, part in enumerate((right, v, left) if back else (left, v, right)):
            ref[pl.ds(pl.multiple_of(u * C[l] + r0, 16), rc), a:b] = part.astype(BF16)

    def stack_rows(ref, l, r0, rc, v):
        for t in range(3):
            turn = ((t - 1) * W[l]) % NP[l]
            part = pltpu.roll(v, turn, 1) if turn else v
            ref[pl.ds(pl.multiple_of(t * C[l] + r0, 16), rc), :] = part.astype(BF16)

    def conv(l, w, which, src, dst, sign=1):
        c = C[l]
        if W[l] % 128 == 0:
            span = min(2048, N[l])

            def step(i, _):
                acc = None
                for t in range(3):
                    at = pl.ds(pl.multiple_of(i * span + (1 + sign * (t - 1)) * W[l], 128), span)
                    part = jnp.dot(
                        w[l][which, t * c : (t + 1) * c, :], src[l][:, at], preferred_element_type=F32
                    )
                    acc = part if acc is None else acc + part
                dst[l][:, pl.ds(pl.multiple_of(i * span + W[l], 128), span)] = acc
                return 0

            lax.fori_loop(0, N[l] // span, step, 0)
        else:
            rows = c if c <= 384 else 96

            def step(i, _):
                acc = None
                for t in range(3):
                    at = pl.ds(pl.multiple_of(t * c + i * rows, 16), rows)
                    part = jnp.dot(w[l][which, at, :], src[l][...], preferred_element_type=F32)
                    turn = (sign * (1 - t) * W[l]) % NP[l]
                    part = pltpu.roll(part, turn, 1) if turn else part
                    acc = part if acc is None else acc + part
                dst[l][pl.ds(pl.multiple_of(i * rows, 16), rows), :] = acc
                return 0

            lax.fori_loop(0, c // rows, step, 0)

    def kernel_grad(l, src):
        c = C[l]
        if W[l] % 128 == 0:
            for t in range(3):
                kg[t * c : (t + 1) * c, 0 : 3 * c] = lax.dot_general(
                    g3[l][c : 2 * c, W[l] : W[l] + N[l]],
                    src[l][:, t * W[l] : t * W[l] + N[l]],
                    (((1,), (1,)), ((), ())),
                    preferred_element_type=F32,
                )
            return
        span = 96

        def step(i, _):
            at = pl.ds(pl.multiple_of(i * span, 16), span)
            kg[at, 0 : 3 * c] = lax.dot_general(
                t3[l][at, :], src[l][...], (((1,), (1,)), ((), ())), preferred_element_type=F32
            )
            return 0

        lax.fori_loop(0, 3 * c // span, step, 0)

    nc, ny, nx, nz = sz.nc, sz.ny, sz.nx, sz.nz
    my_core, my_y = lax.rem(me_b, nc), lax.div(me_b, nc)
    my_x, my_z = lax.rem(me_k, nx), lax.div(me_k, nx)

    def others(n, me):
        return [lax.rem(me + j, n) for j in range(1, n)]

    def remote(src, dst, send, recv, target):
        return pltpu.make_async_remote_copy(
            src_ref=src, dst_ref=dst, send_sem=send, recv_sem=recv, device_id=target, device_id_type=MESH
        )

    def sum_pack(c, l):
        n = C[l] // nb
        for q in range(nb):
            dst = part_a.at[c, q]
            for i in range(-(-3 * C[l] // 128)):
                at, rows = sz.start[l, i]
                lanes = slice(128 * i, 128 * i + 128)
                parts = [kg[t * C[l] + q * n : t * C[l] + q * n + n, lanes] for t in range(3)]
                if rows > 3 * n:
                    parts.append(jnp.zeros((rows - 3 * n, 128), F32))
                dst[at : at + rows, :] = jnp.concatenate(parts, axis=0).astype(BF16)

    def sum_pack_unites():
        n = sz.uchan // nb
        for q in range(nb):
            dst = part_a.at[1, q]
            for j in range(3):
                for i in range(-(-C[j + 1] // 128)):
                    at, rows = sz.start["u", j, i]
                    v = gun[j][q * n : q * n + n, 128 * i : 128 * i + 128]
                    if rows > n:
                        v = jnp.concatenate([v, jnp.zeros((rows - n, 128), F32)], axis=0)
                    dst[at : at + rows, :] = v.astype(BF16)

    def batch_copies(c, part, sending):
        rows = (slice(0, sz.early_rows), slice(sz.early_rows, sz.batch_rows))[part]
        out = []
        for other in others(nb, me_b):
            slot = me_b if sending else other
            src, dst = part_a.at[c, other, rows, :], got_a.at[c, slot, rows, :]
            sems = ra_send.at[c, part, other], ra_recv.at[c, part, slot]
            out.append(remote(src, dst, *sems, (other, me_k)))
        return out

    def part_at(c, x, z, n=1):
        return pl.ds(pl.multiple_of((x * nz + z) * sz.part[c], 16), n * sz.part[c])

    def x_copies(c):
        out = []
        for other in others(nx, my_x):
            src = part_s.at[c, part_at(c, other, 0, nz), :]
            target = (me_b, my_z * nx + other)
            out.append(remote(src, got_x.at[c, 0 : nz * sz.part[c], :], rx_send.at[c], rx_recv.at[c], target))
        return out

    def z_copies(c, sending):
        out = []
        for other in others(nz, my_z):
            slot = my_z if sending else other
            src = part_s.at[c, part_at(c, my_x, other), :]
            target = (me_b, other * nx + my_x)
            out.append(remote(src, got_z.at[c, slot, 0 : sz.part[c], :], rz_send.at[c, other], rz_recv.at[c, slot], target))
        return out

    def back_z_copies(c, sending):
        out = []
        for other in others(nz, my_z):
            slot = my_z if sending else other
            src, dst = got_d.at[c, part_at(c, my_x, my_z), :], got_d.at[c, part_at(c, my_x, slot), :]
            target = (me_b, other * nx + my_x)
            out.append(remote(src, dst, dz_send.at[c, other], dz_recv.at[c, slot], target))
        return out

    def back_x_copies(c, sending):
        out = []
        for other in others(nx, my_x):
            slot = my_x if sending else other
            src, dst = got_d.at[c, part_at(c, my_x, 0, nz), :], got_d.at[c, part_at(c, slot, 0, nz), :]
            target = (me_b, my_z * nx + other)
            out.append(remote(src, dst, dx_send.at[c], dx_recv.at[c], target))
        return out

    def finish(pair):
        sent, received = pair
        for copy in received:
            copy.wait_recv()
        for copy in sent:
            copy.wait_send()

    def sum_level(c, l, src):
        kernel_grad(l, src)
        sum_pack(c, l)

    def sum_first(c, part):
        for copy in batch_copies(c, part, True):
            copy.start()

    def sum_second(c):
        for part in range(2):
            finish((batch_copies(c, part, True), batch_copies(c, part, False)))
        got_a[c, me_b] = part_a[c, me_b]
        v = got_a[c, 0].astype(F32)
        for b in range(1, nb):
            v = v + got_a[c, b].astype(F32)
        for src, dst, rows in sz.moves[: 2 + c]:
            part_s[c, dst : dst + rows, :] = v[src : src + rows].astype(BF16)
        for copy in x_copies(c):
            copy.start()

    def sum_third(c):
        copies = x_copies(c)
        finish((copies, copies))
        mine = part_at(c, my_x, 0, nz)
        if nx > 1:
            v = part_s[c, mine, :].astype(F32) + got_x[c, 0 : nz * sz.part[c], :].astype(F32)
            part_s[c, mine, :] = v.astype(BF16)
        for copy in z_copies(c, True):
            copy.start()

    def sum_fourth(c):
        finish((z_copies(c, True), z_copies(c, False)))
        span = slice(0, sz.part[c])
        got_z[c, my_z, span, :] = part_s[c, part_at(c, my_x, my_z), :]
        v = got_z[c, 0, span, :].astype(F32)
        for z in range(1, nz):
            v = v + got_z[c, z, span, :].astype(F32)
        got_d[c, part_at(c, my_x, my_z), :] = v.astype(BF16)
        for copy in back_z_copies(c, True):
            copy.start()

    def sum_fifth(c):
        finish((back_z_copies(c, True), back_z_copies(c, False)))
        for copy in back_x_copies(c, True):
            copy.start()

    def sum_last(c):
        finish((back_x_copies(c, True), back_x_copies(c, False)))
        pltpu.make_async_copy(got_d.at[c], sums_ref.at[c], out_sem.at[c]).start()

    c2 = C[2] // nb

    def pair_copies(c, step, sending):
        if not sz.pair:
            return []
        n, me = ((ny, my_y), (nc, my_core))[step]
        out = []
        for other in others(n, me):
            slot = me if sending else other
            if step == 0:
                ref, target = xb.at[c, my_core, slot], (other * nc + my_core, me_k)
            else:
                ref, target = xb.at[c, slot], (my_y * nc + other, me_k)
            out.append(remote(ref, ref, xb_send.at[c, step, other], xb_recv.at[c, step, slot], target))
        return out

    def pair_begin(c, ref):
        if sz.pair:
            xb[c, my_core, my_y] = ref[2][C[2] : 2 * C[2], :]
            for copy in pair_copies(c, 0, True):
                copy.start()

    def pair_next(c):
        finish((pair_copies(c, 0, True), pair_copies(c, 0, False)))
        for copy in pair_copies(c, 1, True):
            copy.start()

    def pair_grad_copies(c, sending):
        out = []
        for other in others(nb, me_b):
            slot = me_b if sending else other
            out.append(
                remote(gsb.at[c, other], gb.at[c, slot], gb_send.at[c, other], gb_recv.at[c, slot], (other, me_k))
            )
        return out

    def pair_grad_begin(c):
        if sz.pair:
            for q in range(nb):
                v = g3[2][C[2] + q * c2 : C[2] + (q + 1) * c2, :].astype(F32)
                gsb[c, q] = pltpu.roll(v, NP[2] - W[2], 1)[:, 0 : N[2]].astype(BF16)
            for copy in pair_grad_copies(c, True):
                copy.start()

    def nine_shifts(v, width, store):
        lanes = v.shape[1]
        lane = lax.broadcasted_iota(jnp.int32, (1, lanes), 1)
        at = lane & (width - 1)
        left = jnp.where(at == width - 1, 0.0, pltpu.roll(v, lanes - 1, 1))
        right = jnp.where(at == 0, 0.0, pltpu.roll(v, 1, 1))
        for u, part in enumerate((left, v, right)):
            store(0, u, jnp.where(lane >= lanes - width, 0.0, pltpu.roll(part, lanes - width, 1)))
            store(1, u, part)
            store(2, u, jnp.where(lane < width, 0.0, pltpu.roll(part, width, 1)))

    def pair_gradient(c):
        if not sz.pair:
            return
        finish((pair_copies(c, 1, True), pair_copies(c, 1, False)))
        finish((pair_grad_copies(c, True), pair_grad_copies(c, False)))
        gb[c, me_b] = gsb[c, me_b]

        def item(b, _):
            v = jnp.concatenate([gb[c, b].astype(F32), jnp.zeros((c2, NP[2] - N[2]), F32)], axis=1)

            def store(t, u, part):
                at = (3 * t + u) * c2
                g9b[b, at : at + c2, :] = part.astype(BF16)

            nine_shifts(pltpu.roll(v, W[2], 1), W[2], store)
            return 0

        lax.fori_loop(0, nb, item, 0, unroll=True)
        acc = None
        for b in range(nb):
            part = lax.dot_general(
                g9b[b], xb[c, b % nc, b // nc], (((1,), (1,)), ((), ())), preferred_element_type=F32
            )
            acc = part if acc is None else acc + part
        whole = C[2] // 128
        for i in range(whole):
            at, rows = sz.spots[2, i]
            part_s[c, at : at + rows, :] = acc[:, 128 * i : 128 * i + 128].astype(BF16)
        at, rows = sz.spots[2, whole]
        rest = acc[:, 128 * whole :]
        low, high = rest[0:rows], rest[rows:]
        high = jnp.concatenate([high, jnp.zeros((rows - high.shape[0], high.shape[1]), F32)], axis=0)
        part_s[c, at : at + rows, :] = jnp.concatenate([low, high], axis=1).astype(BF16)

    c3 = C[3] // nb
    half = c3 // 2

    def pack_pixels(ref):
        parts = []
        for q in range(nb):
            at = C[3] + q * c3
            low = pltpu.roll(ref[at : at + half, :].astype(F32), 128 - W[3], 1)
            high = pltpu.roll(ref[at + half : at + c3, :].astype(F32), 64 - W[3], 1)
            parts.append(jnp.where(lane128 < 64, low, high))
        return jnp.concatenate(parts, axis=0).astype(BF16)

    def unpack_pixels(first, second):
        first, second = first.astype(F32), second.astype(F32)
        low = jnp.where(lane128 < 64, first, pltpu.roll(second, 64, 1))
        high = jnp.where(lane128 < 64, pltpu.roll(first, 64, 1), second)
        return low, high

    def gather_copies(c, step, sending):
        if not sz.gather:
            return []
        n, me = ((nz, my_z), (nx, my_x), (ny, my_y), (nc, my_core))[step]
        out = []
        for other in others(n, me):
            slot = me if sending else other
            if step == 0:
                ref, target = xg.at[c, my_x, slot], (me_b, other * nx + my_x)
            elif step == 1:
                ref, target = xg.at[c, slot], (me_b, my_z * nx + other)
            elif step == 2:
                ref, target = xi.at[c, my_core, slot], (other * nc + my_core, me_k)
            else:
                ref, target = xi.at[c, slot], (my_y * nc + other, me_k)
            out.append(remote(ref, ref, xg_send.at[c, step, other], xg_recv.at[c, step, slot], target))
        return out

    def gather_start(c, step):
        for copy in gather_copies(c, step, True):
            copy.start()

    def gather_wait(c, step):
        finish((gather_copies(c, step, True), gather_copies(c, step, False)))

    def gather_begin(c, ref):
        if sz.gather:
            xg[c, my_x, my_z] = pack_pixels(ref[3])
            gather_start(c, 0)

    def gather_next(c, step):
        gather_wait(c, step)
        if step == 1 and sz.gather:
            for z in range(nz):
                for q in range(nb):
                    rows = slice(q * half, (q + 1) * half)
                    pair = unpack_pixels(xg[c, 0, z, rows, :], xg[c, 1, z, rows, :])
                    for i, v in enumerate(pair):
                        at = q * c3 + i * half
                        xi[c, my_core, my_y, at : at + half, 128 * z : 128 * z + 128] = v.astype(BF16)
        gather_start(c, step + 1)

    def grad_copies(c, step, sending):
        out = []
        if step == 0:
            for other in others(nb, me_b):
                slot = me_b if sending else other
                src = gs.at[c, other]
                out.append(
                    remote(src, gr.at[c, my_x, my_z, slot], g1_send.at[c, other], g1_recv.at[c, slot], (other, me_k))
                )
        elif step == 1:
            for other in others(nz, my_z):
                slot = my_z if sending else other
                src, dst = gr.at[c, my_x, my_z], gr.at[c, my_x, slot]
                target = (me_b, other * nx + my_x)
                out.append(remote(src, dst, g2_send.at[c, other], g2_recv.at[c, slot], target))
        else:
            for other in others(nx, my_x):
                slot = my_x if sending else other
                src, dst = gr.at[c, my_x], gr.at[c, slot]
                target = (me_b, my_z * nx + other)
                out.append(remote(src, dst, g3_send.at[c], g3_recv.at[c], target))
        return out

    def grad_begin(c):
        if sz.gather:
            v = pack_pixels(g3[3])
            for q in range(nb):
                gs[c, q] = v[q * half : (q + 1) * half]
            for copy in grad_copies(c, 0, True):
                copy.start()

    def grad_next(c):
        if sz.gather:
            finish((grad_copies(c, 0, True), grad_copies(c, 0, False)))
            gr[c, my_x, my_z, me_b] = gs[c, me_b]
            for copy in grad_copies(c, 1, True):
                copy.start()

    def grad_third(c):
        if sz.gather:
            finish((grad_copies(c, 1, True), grad_copies(c, 1, False)))
            for copy in grad_copies(c, 2, True):
                copy.start()

    image = nz * 128

    def coarse_copy(c, i):
        n = 3 * c3
        at = pl.ds(i * n if isinstance(i, int) else pl.multiple_of(i * n, 16), n)
        slot = i % 2 if isinstance(i, int) else lax.rem(i, 2)
        return pltpu.make_async_copy(cstage.at[slot], coarse_ref.at[c, at, :], cstage_sem.at[slot])

    def coarse_local(c, src):
        def step(i, _):
            at = pl.ds(pl.multiple_of(i * c3, 16), c3)
            cstage[0] = lax.dot_general(
                t3[3][at, :], src[3][...], (((1,), (1,)), ((), ())), preferred_element_type=F32
            )
            copy = pltpu.make_async_copy(cstage.at[0], coarse_ref.at[c, at, :], cstage_sem.at[0])
            copy.start()
            copy.wait()
            return 0

        lax.fori_loop(0, 3 * nb, step, 0)

    def coarse_gradient(c):
        if not sz.gather:
            coarse_local(c, a3 if c else x3)
            return
        gather_wait(c, 3)
        finish((grad_copies(c, 2, True), grad_copies(c, 2, False)))

        def item(b, _):
            low, high = [], []
            for z in range(nz):
                first, second = unpack_pixels(gr[c, 0, z, b], gr[c, 1, z, b])
                low.append(first)
                high.append(second)
            for i, parts in enumerate((low, high)):

                def store(t, u, part, i=i):
                    spot = pl.ds(pl.multiple_of((3 * b + u) * c3 + i * half, 16), half)
                    g9[t, spot, 0:image] = part.astype(BF16)

                nine_shifts(jnp.concatenate(parts, axis=1) if nz > 1 else parts[0], W[3], store)
            return 0

        lax.fori_loop(0, nb, item, 0, unroll=True)

        def step(i, _):
            acc = None
            for b in range(nb):
                part = lax.dot_general(
                    g9[i, 3 * b * c3 : 3 * (b + 1) * c3, 0:image],
                    xi[c, b % nc, b // nc],
                    (((1,), (1,)), ((), ())),
                    preferred_element_type=F32,
                )
                acc = part if acc is None else acc + part
            slot = lax.rem(i, 2)

            @pl.when(i >= 2)
            def _():
                coarse_copy(c, i - 2).wait()

            cstage[slot] = acc
            coarse_copy(c, i).start()
            return 0

        lax.fori_loop(0, 3, step, 0)
        coarse_copy(c, 1).wait()
        coarse_copy(c, 2).wait()

    def moments(arrays, group):
        for l in group:

            def body(r0, rc, lanes, l=l):
                acc = jnp.zeros((rc, 128), F32)
                for a, b in lane_chunks(l, lanes):
                    m = masks[l][1:2, a:b] > 0
                    acc = acc + fold(jnp.where(m, arrays[l][pl.ds(r0, rc), a:b], 0.0))
                stat_a[pl.ds(pl.multiple_of(OFF[l] + r0, 16), rc), :] = acc

            each(l, body)
        for l in group:
            at = slice(OFF[l], OFF[l] + C[l])
            s = jnp.sum(stat_a[at, :], axis=1, keepdims=True) * inv_local[l]
            cols[LOCAL, at, :] = jnp.broadcast_to(s, (C[l], 128))
        for l in group:

            def body(r0, rc, lanes, l=l):
                acc = jnp.zeros((rc, 128), F32)
                mean = col(LOCAL, l, r0, rc, lanes)
                for a, b in lane_chunks(l, lanes):
                    m = masks[l][1:2, a:b] > 0
                    d = jnp.where(m, arrays[l][pl.ds(r0, rc), a:b] - mean, 0.0)
                    acc = acc + fold(d * d)
                stat_b[pl.ds(pl.multiple_of(OFF[l] + r0, 16), rc), :] = acc

            each(l, body)
        return record(stat_a, stat_b, spans_of[group])

    def mean_rstd(got, group):
        mean, rstd = got[0:8] * inv_count, lax.rsqrt(got[8:16] * inv_count + EPSILON)
        to_columns([mean, rstd], cols, [MEAN, RSTD], spans_of[group])
        return rstd

    def halves(l):
        return max(1, W[l] // 128)

    def to_stage(ref, src):
        for h in range(src.shape[1] // 128):
            ref[h] = src[:, 128 * h : 128 * h + 128].astype(F32)

    for l in range(LEVELS):
        if W[l] >= 128:
            to_stage(stage, feats[l])
            for r in range(R[l]):
                for h in range(halves(l)):
                    a = (r + 1) * W[l] + 128 * h
                    xf[l][:, a : a + 128] = stage[h, pl.ds(r, C[l], stride=R[l]), :]
        else:
            v = feats[l][...].astype(F32)
            v = jnp.concatenate([v, jnp.zeros((NP[l] - N[l], C[l]), F32)], axis=0)
            xf[l][...] = pltpu.roll(v.T, W[l], 1)
    pl.semaphore_wait(barrier, nb + nk - 2)
    send_rims(0, COARSE, xf)
    send_rims(0, FINE, xf)
    to_stage(stage, ograd)
    widen(0)

    def stack_start(l):
        def body(r0, rc, lanes):
            for a, b in lane_chunks(l, lanes):
                m = masks[l][0:1, a:b] > 0
                stack_columns(x3[l], l, r0, rc, a, b, jnp.where(m, xf[l][pl.ds(r0, rc), a:b], 0.0))

        each(l, body)

    def pre_of(hat, gain, shift, l, r0, rc, lanes):
        return hat * col(gain, l, r0, rc, lanes) + col(shift, l, r0, rc, lanes)

    def first_act(l):
        def body(r0, rc, lanes):
            for a, b in lane_chunks(l, lanes):
                m = masks[l][0:1, a:b] > 0
                hat = (y1[l][pl.ds(r0, rc), a:b] - col(MEAN, l, r0, rc, lanes)) * col(RSTD, l, r0, rc, lanes)
                y1[l][pl.ds(r0, rc), a:b] = hat
                pre = pre_of(hat, GAIN1, SHIFT1, l, r0, rc, lanes)
                stack_columns(a3[l], l, r0, rc, a, b, jnp.where(m, pre * sigmoid(pre), 0.0))

        each(l, body)

    def second_act(l):
        def body(r0, rc, lanes):
            for a, b in lane_chunks(l, lanes):
                m = masks[l][0:1, a:b] > 0
                hat = (y2[l][pl.ds(r0, rc), a:b] - col(MEAN, l, r0, rc, lanes)) * col(RSTD, l, r0, rc, lanes)
                y2[l][pl.ds(r0, rc), a:b] = hat
                pre = pre_of(hat, GAIN2, SHIFT2, l, r0, rc, lanes)
                start = x3[l][pl.ds(pl.multiple_of(C[l] + r0, 16), rc), a:b].astype(F32)
                pre = jnp.where(m, pre, 0.0) + start
                p1[l][pl.ds(r0, rc), a:b] = pre
                if l:
                    br[l - 1][pl.ds(r0, rc), a:b] = (pre * sigmoid(pre)).astype(BF16)

        each(l, body)

    def second_sums(l):
        def body(r0, rc, lanes):
            acc_g = jnp.zeros((rc, 128), F32)
            acc_s = jnp.zeros((rc, 128), F32)
            for a, b in lane_chunks(l, lanes):
                m = masks[l][1:2, a:b] > 0
                pre = p1[l][pl.ds(r0, rc), a:b]
                sig = sigmoid(pre)
                d = xf[l][pl.ds(r0, rc), a:b] * (sig * (1.0 + pre * (1.0 - sig)))
                xf[l][pl.ds(r0, rc), a:b] = d
                d = jnp.where(m, d, 0.0)
                acc_s = acc_s + fold(d)
                acc_g = acc_g + fold(jnp.where(m, d * y2[l][pl.ds(r0, rc), a:b], 0.0))
            at = pl.ds(pl.multiple_of(OFF[l] + r0, 16), rc)
            stat_a[at, :] = acc_g
            stat_b[at, :] = acc_s

        each(l, body)

    def first_sums(l):
        def body(r0, rc, lanes):
            acc_g = jnp.zeros((rc, 128), F32)
            acc_s = jnp.zeros((rc, 128), F32)
            for a, b in lane_chunks(l, lanes):
                m = masks[l][1:2, a:b] > 0
                hat = y1[l][pl.ds(r0, rc), a:b]
                pre = pre_of(hat, GAIN1, SHIFT1, l, r0, rc, lanes)
                sig = sigmoid(pre)
                d = p1[l][pl.ds(r0, rc), a:b] * (sig * (1.0 + pre * (1.0 - sig)))
                d = jnp.where(m, d, 0.0)
                p1[l][pl.ds(r0, rc), a:b] = d
                acc_s = acc_s + fold(d)
                acc_g = acc_g + fold(jnp.where(m, d * hat, 0.0))
            at = pl.ds(pl.multiple_of(OFF[l] + r0, 16), rc)
            stat_a[at, :] = acc_g
            stat_b[at, :] = acc_s

        each(l, body)

    def norm_grad(l, hats, grads):
        def body(r0, rc, lanes):
            parts = []
            for a, b in lane_chunks(l, lanes):
                m = masks[l][0:1, a:b] > 0
                hat = hats[l][pl.ds(r0, rc), a:b]
                d = grads[l][pl.ds(r0, rc), a:b]
                g = col(CA, l, r0, rc, lanes) * (
                    d - col(CB, l, r0, rc, lanes) - hat * col(CC, l, r0, rc, lanes)
                )
                g = jnp.where(m, g, 0.0)
                stack_columns(g3[l], l, r0, rc, a, b, g, back=True)
                parts.append(g)
            if l in sz.stacked:
                v = parts[0] if len(parts) == 1 else jnp.concatenate(parts, axis=1)
                stack_rows(t3[l], l, r0, rc, jnp.where(masks[l][1:2, :] > 0, v, 0.0))

        each(l, body)

    def norm_columns(scale, got, group):
        to_columns(
            [scale, got[8:16] * inv_count, got[0:8] * inv_count], cols, [CA, CB, CC], spans_of[group]
        )

    def features_out(l):
        if W[l] < 128:
            v = jnp.where(masks[l][1:2, :] > 0, y1[l][...] + xf[l][...], 0.0)
            gfeat[l][...] = pltpu.roll(v, NP[l] - W[l], 1).T[0 : N[l]].astype(BF16)
            map_copy(1 + l).start()
            return

        def body(r0, rc, lanes):
            for r in range(R[l]):
                for h in range(halves(l)):
                    a = (r + 1) * W[l] + 128 * h
                    m = masks[l][1:2, a : a + 128] > 0
                    v = y1[l][pl.ds(r0, rc), a : a + 128] + xf[l][pl.ds(r0, rc), a : a + 128]
                    stage[h, pl.ds(r0 * R[l] + r, rc, stride=R[l]), :] = jnp.where(m, v, 0.0)

        each(l, body)
        for h in range(halves(l)):
            gfeat[l][:, 128 * h : 128 * h + 128] = stage[h].astype(BF16)
        map_copy(1 + l).start()

    sizes, u_sizes = (n_a, n_b), (un_a, un_b)
    fine_place = place < C[0]

    take_rims(0, COARSE, xf)
    for l in COARSE:
        stack_start(l)
    gather_begin(0, x3)
    for l in COARSE:
        conv(l, wide, 0, x3, y1)
    send_rims(1, COARSE, y1)
    ex_start(0, moments(y1, COARSE))
    take_rims(0, FINE, xf)
    stack_start(0)
    conv(0, wide, 0, x3, y1)
    send_rims(1, FINE, y1)
    ex_mid(0, sizes)
    ex_start(1, moments(y1, FINE))
    pair_begin(0, x3)
    turn(0)
    ex_mid(1, sizes)
    gather_next(0, 0)
    widen(1)
    rstd1_c = mean_rstd(ex_end(0, sizes), COARSE)
    take_rims(1, COARSE, y1)
    for l in COARSE:
        first_act(l)

    gather_begin(1, a3)
    for l in COARSE:
        conv(l, wide, 1, a3, y2)
    send_rims(2, COARSE, y2)
    ex_start(2, moments(y2, COARSE))
    rstd1_f = mean_rstd(ex_end(1, sizes), FINE)
    take_rims(1, FINE, y1)
    first_act(0)
    ex_mid(2, sizes)
    conv(0, wide, 1, a3, y2)
    send_rims(2, FINE, y2)
    ex_start(4, moments(y2, FINE))
    pair_begin(1, a3)
    pair_next(0)
    rstd2_c = mean_rstd(ex_end(2, sizes), COARSE)
    take_rims(2, COARSE, y2)
    for l in COARSE:
        second_act(l)

    UC_ = sz.uchan
    for j in range(3):
        l = j + 1
        uo[j][...] = jnp.dot(unites[j][...], br[j][...], preferred_element_type=F32)
    for j in range(3):
        l = j + 1
        m = masks[l][1:2, :] > 0
        v = jnp.where(m, uo[j][...], 0.0)
        part = fold(v)
        ustat_a[j * UC_ : (j + 1) * UC_, :] = part
        mean = jnp.sum(part, axis=1, keepdims=True) * inv_local[l]
        d = jnp.where(m, uo[j][...] - mean, 0.0)
        ustat_b[j * UC_ : (j + 1) * UC_, :] = fold(d * d)
    ex_start(3, record(ustat_a, ustat_b, u_spans))
    ex_mid(4, sizes)
    gather_next(0, 1)
    turn(1)
    ex_mid(3, u_sizes)
    gather_next(1, 0)
    pair_next(1)
    rstd2_f = mean_rstd(ex_end(4, sizes), FINE)
    take_rims(2, FINE, y2)
    second_act(0)
    got = ex_end(3, u_sizes)
    umean_p = got[0:8] * inv_ucount
    urstd_p = lax.rsqrt(got[8:16] * inv_ucount + EPSILON)
    to_columns([umean_p, urstd_p], ucols, [UMEAN, URSTD], u_spans)

    at_top = me_k == 0
    at_bottom = me_k == nk - 1
    fine = W[0]
    split = lambda v: (v.astype(BF16), (v - v.astype(BF16).astype(F32)).astype(BF16))

    def edge(l, n):
        return lax.broadcasted_iota(jnp.int32, (1, n), 1)

    for j in range(3):
        l = j + 1
        m = masks[l][0:1, :] > 0
        hat = (uo[j][...] - ucol(UMEAN, j, NP[l])) * ucol(URSTD, j, NP[l])
        uo[j][...] = hat
        norm = jnp.where(m, hat * ucol(UGAIN, j, NP[l]) + ucol(USHIFT, j, NP[l]), 0.0)
        lane = edge(l, NP[l])
        norm = jnp.where((lane < W[l]) & at_top, pltpu.roll(norm, NP[l] - W[l], 1), norm)
        norm = jnp.where((lane >= W[l] + N[l]) & at_bottom, pltpu.roll(norm, W[l], 1), norm)
        hi, lo = split(norm)
        both = jnp.concatenate([hi, lo], axis=0)
        span = max(128, W[l])
        width = tables[j].shape[1]
        for i in range(NP[l] // span):
            broad = jnp.dot(both[:, span * i : span * i + span], tables[j][...], preferred_element_type=F32)
            up[j][:, width * i : width * i + width] = broad[0:UC_] + broad[UC_:]

    blends = [blend(2 ** (j + 1), R[0]) for j in range(3)]

    def total_body(r0, rc, lanes):
        rows = pl.ds(r0, rc)
        coarse = [{}, {}, {}]
        have = [{}, {}, {}]
        for g in range(R[0]):
            a, b = (g + 1) * fine, (g + 2) * fine
            pre = p1[0][rows, a:b]
            total = pre * sigmoid(pre)
            for j in range(3):
                low, frac = blends[j][g]
                for i in (low, low + 1):
                    if i not in have[j]:
                        have[j][i] = up[j][rows, i * fine : (i + 1) * fine]
                total = total + ((1.0 - frac) * have[j][low] + frac * have[j][low + 1])
            m = masks[0][1:2, a:b] > 0
            sig = sigmoid(total)
            out = jnp.where(m, total * sig, 0.0)
            slope = sig * (1.0 + total * (1.0 - sig))
            spots = [(h, pl.ds(r0 * R[0] + g, rc, stride=R[0])) for h in range(halves(0))]
            grad = jnp.concatenate([stage[h, at, :] for h, at in spots], axis=1)
            grad = jnp.where(m, grad * slope, 0.0)
            for h, at in spots:
                stage[h, at, :] = out[:, 128 * h : 128 * h + 128]
            xf[0][rows, a:b] = grad
            for j in range(3):
                low, frac = blends[j][g]
                for i, weight in ((low, 1.0 - frac), (low + 1, frac)):
                    coarse[j][i] = weight * grad if i not in coarse[j] else coarse[j][i] + weight * grad
                done = [i for i in coarse[j] if g + 1 == R[0] or i < blends[j][g + 1][0]]
                for i in done:
                    up[j][rows, i * fine : (i + 1) * fine] = coarse[j].pop(i)

    def total_step(i, _):
        total_body(pl.multiple_of(i * 16, 16), 16, fine)
        return 0

    lax.fori_loop(0, UC_ // 16, total_step, 0)
    for h in range(halves(0)):
        united_ref[:, 128 * h : 128 * h + 128] = stage[h].astype(BF16)
    map_copy(0).start()

    for j in range(3):
        l = j + 1
        span = max(128, W[l])
        width = tables[j].shape[1]
        parts = []
        for i in range(NP[l] // span):
            hi, lo = split(up[j][:, width * i : width * i + width])
            both = jnp.concatenate([hi, lo], axis=0)
            narrow = jnp.dot(both, tables_t[j][...], preferred_element_type=F32)
            parts.append(narrow[0:UC_] + narrow[UC_:])
        d = parts[0] if len(parts) == 1 else jnp.concatenate(parts, axis=1)
        lane = edge(l, NP[l])
        fold_top = jnp.where((lane >= W[l]) & (lane < 2 * W[l]) & at_top, pltpu.roll(d, W[l], 1), 0.0)
        fold_bottom = jnp.where(
            (lane >= N[l]) & (lane < W[l] + N[l]) & at_bottom, pltpu.roll(d, NP[l] - W[l], 1), 0.0
        )
        d = d + fold_top + fold_bottom
        d = jnp.where(masks[l][0:1, :] > 0, d, 0.0)
        ustat_a[j * UC_ : (j + 1) * UC_, :] = fold(d * uo[j][...])
        ustat_b[j * UC_ : (j + 1) * UC_, :] = fold(d)
        up[j][:, 0 : NP[l]] = d
    at = 0
    lay = []
    for j in range(3):
        l = j + 1
        n = max(2 * W[l], 128)
        lay.append((at, n))
        mid_s[0, :, at : at + n] = up[j][:, 0:n].astype(BF16)
        mid_s[1, :, at : at + n] = up[j][:, NP[l] - n : NP[l]].astype(BF16)
        at += n
    mid_s[0, :, at : at + fine] = xf[0][:, fine : 2 * fine].astype(BF16)
    mid_s[1, :, at : at + fine] = xf[0][:, N[0] : N[0] + fine].astype(BF16)
    rims_start(8, lambda i: mid_s.at[i], lambda i: mid_r.at[i])
    ex_start(5, record(ustat_a, ustat_b, u_spans))
    second_sums(0)
    ex_mid(5)
    ex_start(6, record(stat_a, stat_b, spans_of[FINE]))
    gather_next(1, 1)
    got = ex_end(5)
    totals_ref[0] = got
    rims_wait(8, lambda i: mid_s.at[i], lambda i: mid_r.at[i])
    to_columns(
        [urstd_p * ugain_p, got[8:16] * inv_ucount, got[0:8] * inv_ucount], ucols, [UA, UB, UC], u_spans
    )
    for i, lane0 in ((0, 0), (1, W[0] + N[0])):
        pre = p1[0][:, lane0 : lane0 + fine]
        sig = sigmoid(pre)
        slope = sig * (1.0 + pre * (1.0 - sig))
        xf[0][:, lane0 : lane0 + fine] = mid_r[i, :, at : at + fine].astype(F32) * slope
    for j in range(3):
        l = j + 1
        start, n = lay[j]
        lane = edge(l, n)
        above = mid_r[0, :, start : start + n].astype(F32)
        below = mid_r[1, :, start : start + n].astype(F32)
        if NP[l] == n:
            above, below = pltpu.roll(above, n // 2, 1), pltpu.roll(below, n // 2, 1)
            d = up[j][:, 0:n]
            d = d + jnp.where((lane < 2 * W[l]) & (me_k > 0), above, 0.0)
            d = d + jnp.where((lane >= n - 2 * W[l]) & (me_k < nk - 1), below, 0.0)
            up[j][:, 0:n] = d
        else:
            up[j][:, 0:n] = up[j][:, 0:n] + jnp.where((lane >= 0) & (me_k > 0), above, 0.0)
            up[j][:, NP[l] - n : NP[l]] = up[j][:, NP[l] - n : NP[l]] + jnp.where(
                (lane >= 0) & (me_k < nk - 1), below, 0.0
            )
    for j in range(3):
        l = j + 1
        d = up[j][:, 0 : NP[l]]
        g = ucol(UA, j, NP[l]) * (d - ucol(UB, j, NP[l]) - uo[j][...] * ucol(UC, j, NP[l]))
        g = jnp.where(masks[l][0:1, :] > 0, g, 0.0)
        low = g.astype(BF16)
        xf[l][...] = jnp.dot(unites[j][...].T, low, preferred_element_type=F32)
        own = jnp.where(masks[l][1:2, :] > 0, g, 0.0).astype(BF16)
        gun[j][:, 0 : C[l]] = lax.dot_general(
            own, br[j][...], (((1,), (1,)), ((), ())), preferred_element_type=F32
        )

    for l in COARSE:
        second_sums(l)
    ex_start(7, record(stat_a, stat_b, spans_of[COARSE]))
    ex_mid(6)
    got_f = ex_end(6)
    norm_columns(rstd2_f * gain2_p, got_f, FINE)
    norm_grad(0, y2, xf)
    ex_mid(7)
    conv(0, wide, 1, g3, p1, -1)
    first_sums(0)
    send_rims(3, FINE, p1)
    ex_start(8, record(stat_a, stat_b, spans_of[FINE]))
    sum_level(1, 0, a3)
    sum_pack_unites()
    sum_first(1, 0)
    got = ex_end(7)
    totals_ref[1] = jnp.where(jnp.concatenate([fine_place] * 2, axis=0), got_f, got)
    norm_columns(rstd2_c * gain2_p, got, COARSE)
    norm_grad(1, y2, xf)
    for l in sz.sum_levels[1:]:
        if l == 2:
            norm_grad(2, y2, xf)
        sum_level(1, l, a3)
    sum_first(1, 1)
    if sz.pair:
        norm_grad(2, y2, xf)
    pair_grad_begin(1)
    norm_grad(3, y2, xf)
    grad_begin(1)

    for l in COARSE:
        conv(l, wide, 1, g3, p1, -1)
    for l in COARSE:
        first_sums(l)
    send_rims(3, COARSE, p1)
    ex_start(9, record(stat_a, stat_b, spans_of[COARSE]))
    ex_mid(8)
    pair_gradient(1)
    ex_mid(9)
    sum_second(1)
    grad_next(1)
    gather_next(0, 2)
    gather_next(1, 2)
    got_f = ex_end(8)
    take_rims(3, FINE, p1)
    norm_columns(rstd1_f * gain1_p, got_f, FINE)
    norm_grad(0, y1, p1)
    sum_level(0, 0, x3)
    sum_first(0, 0)
    got = ex_end(9)
    totals_ref[2] = jnp.where(jnp.concatenate([fine_place] * 2, axis=0), got_f, got)
    take_rims(3, COARSE, p1)
    norm_columns(rstd1_c * gain1_p, got, COARSE)
    norm_grad(3, y1, p1)
    grad_begin(0)
    norm_grad(2, y1, p1)
    pair_grad_begin(0)
    sum_third(1)
    norm_grad(1, y1, p1)
    for l in sz.sum_levels[1:]:
        sum_level(0, l, x3)
    sum_first(0, 1)
    grad_third(1)
    conv(0, wide, 0, g3, y1, -1)
    features_out(0)
    grad_next(0)
    pair_gradient(0)
    sum_second(0)
    conv(1, wide, 0, g3, y1, -1)
    features_out(1)
    grad_third(0)
    sum_third(0)
    sum_fourth(1)
    conv(2, wide, 0, g3, y1, -1)
    features_out(2)
    conv(3, wide, 0, g3, y1, -1)
    features_out(3)
    coarse_gradient(1)
    sum_fourth(0)
    sum_fifth(1)
    coarse_gradient(0)
    sum_fifth(0)
    sum_last(1)
    sum_last(0)
    for c in range(2):
        pltpu.make_async_copy(got_d.at[c], sums_ref.at[c], out_sem.at[c]).wait()
    for i in range(5):
        map_copy(i).wait()


def last_kernel(sz, nb, *refs):
    it = iter(refs)
    take = lambda n: [next(it) for _ in range(n)]
    maps = take(5)
    sums_in, totals, coarse_in = take(3)
    maps_out = take(5)
    kernels = take(4)
    unites = take(3)
    norm_gains, norm_shifts, unite_gains, unite_shifts = take(4)
    held = take(5)
    sums, coarse, in_sem, out_sem = take(4)
    C = sz.chan
    arrivals = [pltpu.make_async_copy(sums_in, sums, in_sem.at[0])]
    arrivals += [pltpu.make_async_copy(a, b, in_sem.at[1 + i]) for i, (a, b) in enumerate(zip(maps, held))]
    arrivals += [pltpu.make_async_copy(coarse_in.at[c], coarse.at[c], in_sem.at[6 + c]) for c in range(2)]
    for copy in arrivals:
        copy.start()
    leaving = [pltpu.make_async_copy(a, b, out_sem.at[i]) for i, (a, b) in enumerate(zip(held, maps_out))]
    if sz.gather:
        leaving += [
            pltpu.make_async_copy(coarse.at[c], kernels[3].at[c], out_sem.at[5 + c]) for c in range(2)
        ]

    for row, which in ((0, 2), (1, 1)):
        for k in range(sz.blocks):
            m = min(128, sz.total - 128 * k)
            for ref, base in ((norm_gains, 0), (norm_shifts, 8)):
                ref[row : row + 1, 128 * k : 128 * k + m] = totals[which, base + k : base + k + 1, 0:m]
    for ref, base in ((unite_gains, 0), (unite_shifts, 8)):
        v = jnp.concatenate([totals[0, base + k : base + k + 1, :] for k in range(sz.ublocks)], axis=1)
        for j in range(3):
            ref[j : j + 1, :] = v[:, j * sz.uchan : (j + 1) * sz.uchan]

    arrivals[0].wait()
    for i in range(5):
        arrivals[1 + i].wait()
        leaving[i].start()
    for l in range(LEVELS):
        n = C[l] // nb
        if l == 3:
            for c in range(2):
                arrivals[6 + c].wait()
                if sz.gather:
                    leaving[5 + c].start()
        for c in range(2):
            if l == 2 and sz.pair:
                at, rows = sz.spots[2, C[2] // 128]
                block = sums[c, at : at + rows, :].astype(F32)
                parts = []
                for i in range(C[2] // 128):
                    at, rows = sz.spots[2, i]
                    parts.append(sums[c, at : at + rows, :].astype(F32))
                parts.append(jnp.concatenate([block[:, 0:64], block[:, 64:128]], axis=0)[0 : 9 * n])
                v = jnp.concatenate(parts, axis=1)
            elif (l, 0) in sz.spots:
                parts = []
                for i in range(-(-3 * C[l] // 128)):
                    at, rows = sz.spots[l, i]
                    parts.append(sums[c, at : at + rows, :].astype(F32))
                v = jnp.concatenate(parts, axis=1)
            for t in range(3):
                for u in range(3):
                    at = (3 * t + u) * n
                    if l == 3 and sz.gather:
                        continue
                    if l == 3:
                        kernels[3][c, at : at + n, :] = coarse[c, t * n : (t + 1) * n, u * C[3] : (u + 1) * C[3]]
                    elif l == 2 and sz.pair:
                        kernels[2][c, t, u] = v[at : at + n]
                    else:
                        w = v[t * n : (t + 1) * n, u * C[l] : (u + 1) * C[l]]
                        if l == 0:
                            kernels[0][t, u, :, c, :] = w
                        else:
                            kernels[l][c, t, u] = w
    n = sz.uchan // nb
    for j in range(3):
        width = C[j + 1]
        for i in range(-(-width // 128)):
            at, _ = sz.spots["u", j, i]
            m = min(128, width - 128 * i)
            unites[j][:, 128 * i : 128 * i + m] = sums[1, at : at + n, 0:m].astype(F32)
    for copy in leaving:
        copy.wait()


def body(*args):
    features = args[0:4]
    blocks = args[4:8]
    unites = args[8:11]
    norm_gains, norm_shifts, unite_gains, unite_shifts, output_grad, heights, widths, item_slot = args[11:]
    nb = lax.axis_size("batch")
    nk = lax.axis_size("rows")
    sz = Sizes(features, nb, nk)
    C, R, W, N, NP = sz.chan, sz.rows, sz.width, sz.own, sz.flat

    flat = [
        f.reshape(C[l] * R[l], W[l]) if W[l] >= 128 else f.transpose(0, 2, 3, 1).reshape(N[l], C[l])
        for l, f in enumerate(features)
    ]
    ograd = output_grad.reshape(C[0] * R[0], W[0])
    blocks = [b.reshape(2, 3, 3 * C[l], C[l]) for l, b in enumerate(blocks)]

    tables = [column_table(W[l], W[0]) for l in range(1, 4)]
    operands = [heights, widths, item_slot, *flat, ograd, *blocks, *unites]
    operands += [norm_gains, norm_shifts, unite_gains, unite_shifts]
    operands += [jnp.asarray(t, BF16) for t in tables] + [jnp.asarray(t.T, BF16) for t in tables]

    shape = jax.ShapeDtypeStruct
    map_shapes = [(C[0] * R[0], W[0])]
    map_shapes += [(C[l] * R[l], W[l]) if W[l] >= 128 else (N[l], C[l]) for l in range(4)]
    outs = [shape(m, BF16) for m in map_shapes]
    outs += [shape((2, sz.sum_rows, 128), BF16)]
    outs += [shape((2, 9 * C[3] // nb, C[3]) if sz.gather else (2, 3 * C[3], 3 * C[3]), F32)]
    outs += [shape((3, 16, 128), F32)]
    vm = pltpu.VMEM
    scratch = [
        vm((3, 3 * C[l], C[l]), BF16) for l in range(3 if sz.gather else 4)
    ]
    scratch += [vm((2, 3 * C[l], 3 * C[l]), BF16) for l in range(4)]
    scratch += [vm((max(1, W[0] // 128), C[0] * R[0], 128), F32)]
    for _ in range(3):
        scratch += [vm((3 * C[l], NP[l]), BF16) for l in range(4)]
    scratch += [vm((3 * C[l], NP[l]), BF16) for l in sz.stacked]
    n = C[3] // nb
    scratch += [vm((2, 3 * n, C[3]) if sz.gather else (1, n, 3 * C[3]), F32), pltpu.SemaphoreType.DMA((2,))]
    top = C[sz.sum_levels[-1]]
    scratch += [vm((3 * top, -(-3 * top // 128) * 128), F32)]
    scratch += [vm((sz.uchan, -(-C[l] // 128) * 128), F32) for l in range(1, 4)]
    for _ in range(4):
        scratch += [vm((C[l], NP[l]), F32) for l in range(4)]
    scratch += [vm((C[l], NP[l]), BF16) for l in range(1, 4)]
    scratch += [vm((sz.uchan, NP[l]), F32) for l in range(1, 4)]
    scratch += [vm((sz.uchan, (R[l] + 2) * W[0]), F32) for l in range(1, 4)]
    scratch += [
        vm((N_COLS, sz.blocks * 128, 128), F32),
        vm((N_UCOLS, sz.ublocks * 128, 128), F32),
        vm((sz.blocks * 128, 128), F32),
        vm((sz.blocks * 128, 128), F32),
        vm((sz.ublocks * 128, 128), F32),
        vm((sz.ublocks * 128, 128), F32),
        vm((nb, 8, 128), F32),
        vm((nk, 8, 128), F32),
        vm((nb, 8, 128), F32),
        vm((nk, 8, 128), F32),
    ]
    scratch += [vm((8, NP[l]), F32) for l in range(4)]
    mid = sum(max(2 * W[l], 128) for l in range(1, 4)) + W[0]
    scratch += [
        vm((10, nb, 16, 128), F32),
        vm((10, nk, 16, 128), F32),
        vm((2, sz.rim_total, 128), BF16),
        vm((4, 2, sz.rim_total, 128), BF16),
        vm((2, sz.uchan, mid), BF16),
        vm((2, sz.uchan, mid), BF16),
        pltpu.SemaphoreType.DMA((10, nb)),
        pltpu.SemaphoreType.DMA((10, nb)),
        pltpu.SemaphoreType.DMA((10, nk)),
        pltpu.SemaphoreType.DMA((10, nk)),
        pltpu.SemaphoreType.DMA((9, 2)),
        pltpu.SemaphoreType.DMA((9, 2)),
        pltpu.SemaphoreType.DMA((4, 2)),
        pltpu.SemaphoreType.DMA((2, 9)),
        *[vm(m, BF16) for m in map_shapes],
        pltpu.SemaphoreType.DMA((5,)),
        vm((8, sz.blocks * 128), F32),
        vm((8, sz.ublocks * 128), F32),
        vm((2, nb, sz.batch_rows, 128), BF16),
        vm((2, nb, sz.batch_rows, 128), BF16),
        vm((2, sz.sum_rows, 128), BF16),
        vm((2, sz.nz * max(sz.part), 128), BF16),
        vm((2, sz.nz, max(sz.part), 128), BF16),
        vm((2, sz.sum_rows, 128), BF16),
        pltpu.SemaphoreType.DMA((2,)),
    ]
    sems = pltpu.SemaphoreType.DMA
    scratch += [sems((2, 2, nb))] * 2 + [sems((2,))] * 2 + [sems((2, sz.nz))] * 4
    scratch += [sems((2,))] * 2
    if sz.gather:
        half = C[3] // nb // 2
        most = max(sz.nz, sz.nx, sz.ny, sz.nc)
        scratch += [
            vm((2, sz.nx, sz.nz, C[3] // 2, 128), BF16),
            vm((2, sz.nc, sz.ny, C[3], 128 * sz.nz), BF16),
            vm((2, nb, half, 128), BF16),
            vm((2, sz.nx, sz.nz, nb, half, 128), BF16),
            vm((3, 3 * C[3], max(C[3], 128 * sz.nz)), BF16),
            sems((2, 4, most)),
            sems((2, 4, most)),
            sems((2, nb)),
            sems((2, nb)),
            sems((2, sz.nz)),
            sems((2, sz.nz)),
            sems((2,)),
            sems((2,)),
        ]
    if sz.pair:
        c2 = C[2] // nb
        scratch += [
            vm((2, sz.nc, sz.ny, C[2], NP[2]), BF16),
            vm((2, nb, c2, N[2]), BF16),
            vm((2, nb, c2, N[2]), BF16),
            vm((nb, 9 * c2, NP[2]), BF16),
            sems((2, 2, max(sz.ny, sz.nc))),
            sems((2, 2, max(sz.ny, sz.nc))),
            sems((2, nb)),
            sems((2, nb)),
        ]
    in_vmem = pl.BlockSpec(memory_space=pltpu.VMEM)
    in_smem = pl.BlockSpec(memory_space=pltpu.SMEM)
    got = pl.pallas_call(
        functools.partial(main_kernel, sz, nb, nk),
        out_shape=outs,
        in_specs=[in_smem] * 3
        + [in_vmem] * 5
        + [pl.BlockSpec(memory_space=pl.ANY)] * 4
        + [in_vmem] * (len(operands) - 12),
        out_specs=[pl.BlockSpec(memory_space=pl.ANY)] * 7
        + [in_vmem],
        scratch_shapes=scratch,
        compiler_params=pltpu.CompilerParams(
            collective_id=0, has_side_effects=True, vmem_limit_bytes=60 * 2**20
        ),
    )(*operands)

    maps, sums, totals = got[0:5], got[5], got[-1]
    coarse = got[6]
    if not sz.gather:
        coarse = coarse.astype(BF16).reshape(2, 3, C[3], 3 * C[3])
        coarse = lax.psum(coarse, "rows")
        coarse = lax.psum_scatter(coarse, "batch", scatter_dimension=2, tiled=True)
        coarse = coarse.astype(F32).reshape(2, 3 * C[3] // nb, 3 * C[3])
    in_any = pl.BlockSpec(memory_space=pl.ANY)
    outs = [shape(m, BF16) for m in map_shapes]
    outs += [shape((3, 3, C[0] // nb, 2, C[0]), F32)]
    outs += [shape((2, 3, 3, C[l] // nb, C[l]), F32) for l in (1, 2)]
    outs += [shape((2, 9 * C[3] // nb, C[3]), F32)]
    outs += [shape((sz.uchan // nb, C[l]), F32) for l in range(1, 4)]
    outs += [shape((2, sz.total), F32)] * 2 + [shape((3, sz.uchan), F32)] * 2
    outs = pl.pallas_call(
        functools.partial(last_kernel, sz, nb),
        out_shape=outs,
        in_specs=[in_any] * 6 + [in_vmem] + [in_any],
        out_specs=[in_any] * 5
        + [in_vmem] * 3
        + [in_any if sz.gather else in_vmem]
        + [in_vmem] * (len(outs) - 9),
        scratch_shapes=[vm(m, BF16) for m in map_shapes]
        + [
            vm(sums.shape, BF16),
            vm(coarse.shape, F32),
            pltpu.SemaphoreType.DMA((8,)),
            pltpu.SemaphoreType.DMA((7,)),
        ],
        compiler_params=pltpu.CompilerParams(vmem_limit_bytes=60 * 2**20),
    )(*maps, sums, totals, coarse)
    outs = list(outs)
    outs[5] = outs[5].transpose(3, 0, 1, 2, 4)
    outs[8] = outs[8].reshape(2, 3, 3, C[3] // nb, C[3])
    shaped = []
    for i, m in enumerate(outs[0:5]):
        l = max(i - 1, 0)
        if W[l] >= 128:
            shaped.append(m.reshape(1, C[l], R[l], W[l]))
        else:
            shaped.append(m.reshape(1, R[l], W[l], C[l]).transpose(0, 3, 1, 2))
    return (*shaped, *outs[5:])


def solution(mesh):
    image = P("batch", None, "rows", None)
    kernel = P(None, None, None, "batch", None)
    return jax.shard_map(
        body,
        mesh=mesh,
        in_specs=(image,) * 4 + (P(),) * 11 + (image,) + (P(),) * 3,
        out_specs=(image,) * 5 + (kernel,) * 4 + (P("batch", None),) * 3 + (P(),) * 4,
        check_vma=False,
    )
```
